32 devices in a mesh: ctx: 8 (over y, x, core), head: 4 (over z).
Axes of the slice: x: 2, y: 2, z: 4, core: 2. Of those that a mesh axis runs over, the one named last changes fastest.
Arguments:
- tokens: bfloat16 [2048, 2048], P('ctx'), may hold values from -6 to 6
- qkv_weight: bfloat16 [2048, 3, 16, 128], P(None, None, 'head'), may hold values from -0.125 to 0.125
- small_weight: bfloat16 [2048, 16, 15], P(None, 'head'), may hold values from -0.125 to 0.125
- head_param: float32 [16, 2], P('head'), as said below
- norm_gain: float32 [128], replicated, may hold values from 0.1 to 1.9
- out_weight: bfloat16 [16, 128, 2048], P('head'), may hold values from -0.125 to 0.125
- grad_out: bfloat16 [2048, 2048], P('ctx'), may hold values from -6 to 6
Outputs:
- layer_out: bfloat16 [2048, 2048], P('ctx', 'head')
- grad_tokens: bfloat16 [2048, 2048], P('ctx', 'head')
The draws below stay inside these ranges and needn't reach their ends.
Inputs may be any that keep to these rules, and one draw needn't show every extreme that they name: `head_param`: column 0 holds each head's decay rate, positive; column 1 a bias added before the write strength's sigmoid.
All inputs are finite; a program needn't handle non-finite values.
Results may differ from the reference program's by a relative error of at most 0.017.
Values may be sent and summed in bfloat16 or wider, within the bound.
No kernel may reach another device: no remote copies, remote signals or barrier semaphores. Data moves between devices by JAX's collectives and lax.ppermute only.
A program may use at most 128 MiB of HBM per device.

```python
import jax
import jax.numpy as jnp
from jax import lax

D = 2048
H = 16
DK = 128
BLOCK = 64
LV = 13
TOKENS = 2048
NS = 15
N_HEAD = 4


def draw_head_param(key, part):
    key_rate, key_bias = jax.random.split(jax.random.fold_in(key, 7))
    slow_end = jnp.log(0.5 / TOKENS)
    fast_end = jnp.log(0.05)
    share_pos = jax.random.uniform(key_rate, (H,), jnp.float32)
    decay_rate = jnp.exp(slow_end + share_pos * (fast_end - slow_end))
    write_bias = jnp.log(64.0 * decay_rate) + jax.random.uniform(key_bias, (H,), jnp.float32, -0.5, 0.5)
    return jnp.stack([decay_rate, write_bias], 1)


def steps_of(key, extent, cuts, smallest, top_value):
    gain, own = 1.0, jax.random.fold_in(key, 6)
    for dim, parts in cuts:
        heights = jnp.exp(jax.random.uniform(jax.random.fold_in(own, dim), (parts,), jnp.float32, smallest / len(cuts), top_value / len(cuts)))
        gain = gain * jnp.repeat(heights, extent[dim] // parts).reshape([-1 if axis == dim else 1 for axis in range(len(extent))])
    return gain


def gaussian(key, extent, scale, bound, cuts=(), kind=jnp.bfloat16):
    factor_of = steps_of(key, extent, cuts, -0.22, 0.18) if cuts else 1.0
    array = jax.random.normal(key, extent, jnp.float32) * scale * factor_of
    return jnp.minimum(jnp.maximum(array, -bound), bound).astype(kind)


def setup_inputs(seed: int = 0) -> dict:
    key_of = jax.random.split(jax.random.key(seed), 8)
    return {
        "tokens": gaussian(key_of[0], (TOKENS, D), 1.0, 6.0, ((0, 8),)),
        "qkv_weight": gaussian(key_of[1], (D, 3, H, DK), D ** -0.5, 0.125, ((2, 4),)),
        "small_weight": gaussian(key_of[2], (D, H, NS), D ** -0.5, 0.125, ((1, 4),)),
        "head_param": draw_head_param(jax.random.fold_in(key_of[7], 71), 0),
        "norm_gain": jnp.clip(1.0 + 0.18 * jax.random.normal(key_of[4], (DK,), jnp.float32), 0.1, 1.9),
        "out_weight": gaussian(key_of[5], (H, DK, D), (H * DK) ** -0.5, 0.125, ((0, 4),)),
        "grad_out": gaussian(key_of[6], (TOKENS, D), 1.0, 6.0, ((0, 8),)),
    }


def mat_mul(left, right):
    return jnp.matmul(left, right, precision=lax.Precision.HIGHEST)

def flip_last(array_in):
    return jnp.swapaxes(array_in, -1, -2)

def unit_scale(values):
    return values * lax.rsqrt(lax.optimization_barrier(jnp.sum(values * values, -1, keepdims=True)) + 1e-06)

def block_pieces(q_in, k_in, v_in, beta_w, decay_log):
    length = q_in.shape[-2]
    cum_log = jnp.cumsum(decay_log, axis=-1)
    row_id = lax.broadcasted_iota(jnp.int32, (length, length), 0)
    col_id = lax.broadcasted_iota(jnp.int32, (length, length), 1)
    inclusive = row_id >= col_id
    strict = row_id > col_id
    spread = cum_log[..., :, None] - cum_log[..., None, :]
    decay_mat = jnp.where(inclusive, jnp.exp(jnp.where(inclusive, spread, 0.0)), 0.0)
    key_gram = mat_mul(k_in, flip_last(k_in))
    lower_part = jnp.where(strict, beta_w[..., :, None] * decay_mat * key_gram, 0.0)
    system = lower_part + jnp.eye(length, dtype=jnp.float32)
    growth = jnp.exp(cum_log)
    right_side = jnp.concatenate([beta_w[..., None] * v_in, (beta_w * growth)[..., None] * k_in], -1)
    solved = jax.scipy.linalg.solve_triangular(system, right_side, lower=True, unit_diagonal=True)
    value_dim = v_in.shape[-1]
    new_values = solved[..., :value_dim]
    key_mix = solved[..., value_dim:]
    scores = mat_mul(q_in, flip_last(k_in)) * decay_mat
    intra_out = mat_mul(scores, new_values)
    query_mix = growth[..., None] * q_in - mat_mul(scores, key_mix)
    tail_decay = jnp.exp(cum_log[..., -1:] - cum_log)
    tail_keys = tail_decay[..., None] * k_in
    eye_key = jnp.eye(k_in.shape[-1], dtype=jnp.float32)
    transit = jnp.exp(cum_log[..., -1])[..., None, None] * eye_key - mat_mul(flip_last(key_mix), tail_keys)
    own_state = mat_mul(flip_last(new_values), tail_keys)
    return (intra_out, query_mix, transit, own_state)

def butterfly(transit, own_state):
    total_count = transit.shape[0]
    eye_key = jnp.eye(transit.shape[-1], dtype=jnp.float32)
    prefix = jnp.broadcast_to(eye_key, transit.shape)
    block_a = transit
    block_u = own_state
    found_all = []
    block_len = 1
    while block_len < total_count:
        pair_count = total_count // (2 * block_len)
        split_a = block_a.reshape((pair_count, 2) + block_a.shape[1:])
        split_u = block_u.reshape((pair_count, 2) + block_u.shape[1:])
        split_p = prefix.reshape((pair_count, 2, block_len) + prefix.shape[1:])
        low_a = split_a[:, 0]
        high_a = split_a[:, 1]
        low_u = split_u[:, 0]
        high_u = split_u[:, 1]
        upper_p = split_p[:, 1]
        arriving = mat_mul(low_u[:, None], upper_p)
        moved_p = mat_mul(low_a[:, None], upper_p)
        found_all.append(jnp.stack([jnp.zeros_like(arriving), arriving], 1).reshape(own_state.shape))
        prefix = jnp.stack([split_p[:, 0], moved_p], 1).reshape(prefix.shape)
        block_a = mat_mul(low_a, high_a)
        block_u = mat_mul(low_u, high_a) + high_u
        block_len = block_len * 2
    return (found_all, prefix, block_a[0], block_u[0])

def head_output(q_raw, k_raw, v_raw, gate_pre, decay_rate, write_bias, norm_gain):
    token_count = q_raw.shape[0]
    block_count = token_count // BLOCK

    def to_blocks(tensor):
        return tensor.reshape((block_count, BLOCK) + tensor.shape[1:])
    beta_w = jax.nn.sigmoid(gate_pre[:, LV + 1] + write_bias)
    decay_log = -decay_rate * jax.nn.sigmoid(gate_pre[:, LV])
    weights = to_blocks(jax.nn.softplus(gate_pre[:, :LV]))
    intra_out, query_mix, transit, own_state = block_pieces(to_blocks(unit_scale(q_raw)), to_blocks(unit_scale(k_raw)), to_blocks(v_raw), to_blocks(beta_w), to_blocks(decay_log))
    found_all, prefix, block_a, block_u = butterfly(transit, own_state)
    summed = weights[..., 0:1] * intra_out
    for level_no in range(len(found_all)):
        summed = summed + weights[..., level_no + 1:level_no + 2] * mat_mul(query_mix, flip_last(found_all[level_no]))
    summed = summed.reshape(token_count, q_raw.shape[1])
    return summed * lax.rsqrt(lax.optimization_barrier(jnp.mean(summed * summed, -1, keepdims=True)) + 1e-06) * norm_gain

def reference(tokens, qkv_weight, small_weight, head_param, norm_gain, out_weight, grad_out):
    token_count = tokens.shape[0]
    proj = jnp.dot(tokens.astype(jnp.float32), qkv_weight.reshape(D, 3 * H * DK).astype(jnp.float32), preferred_element_type=jnp.float32)
    proj = proj.reshape(token_count, 3, H, DK)
    gate_pre = jnp.dot(tokens.astype(jnp.float32), small_weight.reshape(D, H * NS).astype(jnp.float32), preferred_element_type=jnp.float32)
    gate_pre = gate_pre.reshape(token_count, H, NS)

    def one_head(packed):
        return head_output(packed[0], packed[1], packed[2], packed[3], packed[4], packed[5], norm_gain)
    saved_head = jax.checkpoint(one_head)

    def core_all(q_all, k_all, v_all, gate_all):
        return lax.map(saved_head, (q_all, k_all, v_all, gate_all, head_param[:, 0], head_param[:, 1]))
    q_all = jnp.transpose(proj[:, 0], (1, 0, 2))
    k_all = jnp.transpose(proj[:, 1], (1, 0, 2))
    v_all = jnp.transpose(proj[:, 2], (1, 0, 2))
    gate_all = jnp.transpose(gate_pre, (1, 0, 2))
    normed, pull_back = jax.vjp(core_all, q_all, k_all, v_all, gate_all)
    normed_low = jnp.transpose(normed.astype(jnp.bfloat16), (1, 0, 2))
    group_size = H // N_HEAD
    layer_sum = jnp.zeros((token_count, D), jnp.float32)
    for group_no in range(N_HEAD):
        first = group_no * group_size
        partial_value = jnp.dot(normed_low[:, first:first + group_size].reshape(token_count, group_size * DK).astype(jnp.float32), out_weight[first:first + group_size].reshape(group_size * DK, D).astype(jnp.float32), preferred_element_type=jnp.float32)
        layer_sum = layer_sum + lax.optimization_barrier(partial_value.astype(jnp.bfloat16)).astype(jnp.float32)
    grad_normed = jnp.dot(grad_out.astype(jnp.float32), out_weight.reshape(H * DK, D).T.astype(jnp.float32), preferred_element_type=jnp.float32)
    grad_normed = jnp.transpose(grad_normed.reshape(token_count, H, DK), (1, 0, 2))
    grad_q, grad_k, grad_v, grad_gate = pull_back(grad_normed)
    grad_proj = jnp.stack([grad_q, grad_k, grad_v], 0)
    grad_proj = jnp.transpose(grad_proj, (2, 0, 1, 3)).astype(jnp.bfloat16)
    grad_gate = jnp.transpose(grad_gate, (1, 0, 2)).astype(jnp.bfloat16)
    grad_sum = jnp.zeros((token_count, D), jnp.float32)
    for group_no in range(N_HEAD):
        first = group_no * group_size
        partial_value = jnp.dot(grad_proj[:, :, first:first + group_size].reshape(token_count, 3 * group_size * DK).astype(jnp.float32), qkv_weight[:, :, first:first + group_size].reshape(D, 3 * group_size * DK).T.astype(jnp.float32), preferred_element_type=jnp.float32)
        partial_value = partial_value + jnp.dot(grad_gate[:, first:first + group_size].reshape(token_count, group_size * NS).astype(jnp.float32), small_weight[:, first:first + group_size].reshape(D, group_size * NS).T.astype(jnp.float32), preferred_element_type=jnp.float32)
        grad_sum = grad_sum + lax.optimization_barrier(partial_value.astype(jnp.bfloat16)).astype(jnp.float32)
    return (layer_sum.astype(jnp.bfloat16), grad_sum.astype(jnp.bfloat16))
```

```python
import functools

import jax
import jax.numpy as jnp
from jax import lax
from jax.experimental import pallas as pl
from jax.experimental.pallas import tpu as pltpu
from jax.sharding import PartitionSpec as P

BLOCK = 64
LANES = 128
EPS = 1e-06
VMEM_BYTES = 58 * 1024 * 1024
F32 = jnp.float32
BF16 = jnp.bfloat16
WHOLE = pl.BlockSpec(memory_space=pltpu.VMEM)
SCALARS = pl.BlockSpec(memory_space=pltpu.SMEM)
PARAMS = pltpu.CompilerParams(vmem_limit_bytes=VMEM_BYTES)


def contract(left, right, dim_left, dim_right):
    return lax.dot_general(
        left.astype(BF16),
        right.astype(BF16),
        (((dim_left,), (dim_right,)), ((), ())),
        preferred_element_type=F32,
    )


def mm(left, right):
    return contract(left, right, 1, 0)


def mm_nt(left, right):
    return contract(left, right, 1, 1)


def mm_tn(left, right):
    return contract(left, right, 0, 0)


def split(values):
    high = values.astype(BF16)
    return high, (values - high.astype(F32)).astype(BF16)


def mm_nt_fine(left, right):
    left_high, left_low = split(left)
    right_high, right_low = split(right)
    return mm_nt(left_high, right_high) + (mm_nt(left_low, right_high) + mm_nt(left_high, right_low))


def mm_full(left, right):
    return jnp.dot(left, right, precision=lax.Precision.HIGHEST, preferred_element_type=F32)


def pair_ids(count):
    row_id = lax.broadcasted_iota(jnp.int32, (count, count), 0)
    col_id = lax.broadcasted_iota(jnp.int32, (count, count), 1)
    return row_id, col_id


def row_sum(values):
    return jnp.sum(values, 1, keepdims=True)


def col_sum(values):
    return jnp.sum(values, 0, keepdims=True)


def lane_of(rows):
    return lax.broadcasted_iota(jnp.int32, (rows, LANES), 1)


def decay_of(pack, pack_t, col, inclusive):
    spread = pack[:, col : col + 1] - pack_t[col : col + 1, :]
    return jnp.where(inclusive, jnp.exp(jnp.minimum(spread, 0.0)), 0.0)


def level_mix(pack, head, heads, bits, apart):
    block_bit = BLOCK.bit_length() - 1
    mix = pack[:, head : head + 1]
    mixed = jnp.broadcast_to(mix, apart.shape)
    for level in range(1, bits + 1):
        col = level * heads + head
        here = (apart >> (block_bit + level - 1)) >= 1
        mixed = jnp.where(here, pack[:, col : col + 1], mixed)
    return mixed


def project_body(
    sizes, hp_ref, tokens_ref, w_ref, small_ref, wr_ref, qkv_ref, gate_ref, pack_ref, pack_t_ref,
    trans_ref, mixed_ref, pair_ref, wide, acc, gate_acc
):
    heads, levels, steps = sizes
    step = pl.program_id(0)
    rows = tokens_ref.shape[0]
    depth = tokens_ref.shape[1]
    cols = 3 * heads
    wide[...] = w_ref[...].astype(F32)
    for col in range(cols):
        part = wide[pl.ds(col, depth, stride=cols), :]
        wr_ref[:, col * LANES : (col + 1) * LANES] = part.astype(BF16)
    own = jnp.dot(tokens_ref[...], wr_ref[...], preferred_element_type=F32)
    own_gate = mm_nt(tokens_ref[...], small_ref[...])

    @pl.when(step == 0)
    def _():
        acc[...] = own
        gate_acc[...] = own_gate

    @pl.when(step > 0)
    def _():
        acc[...] += own
        gate_acc[...] += own_gate

    @pl.when(step == steps - 1)
    def _():
        local_summary(
            heads, levels, hp_ref, acc, gate_acc, qkv_ref, gate_ref, pack_ref, pack_t_ref,
            trans_ref, mixed_ref, pair_ref
        )


def local_summary(
    heads, levels, hp_ref, acc, gate_acc, qkv_ref, gate_ref, pack_ref, pack_t_ref, trans_ref,
    mixed_ref, pair_ref
):
    rows = acc.shape[0]
    decay_col = levels * heads
    beta_col = decay_col + heads
    norm_col = beta_col + heads
    gate = gate_acc[...]
    gate_ref[...] = gate
    lane = lane_of(rows)
    lane_row = lane_of(1)
    rate = jnp.zeros((1, LANES), F32)
    bias = jnp.zeros((1, LANES), F32)
    for head in range(heads):
        rate = jnp.where(lane_row == decay_col + head, hp_ref[head, 0], rate)
        bias = jnp.where(lane_row == beta_col + head, hp_ref[head, 1], bias)
    switch = jax.nn.sigmoid(gate + bias)
    lam = jnp.maximum(gate, 0.0) + jnp.log1p(jnp.exp(-jnp.abs(gate)))
    row_id, col_id = pair_ids(rows)
    inclusive = row_id >= col_id
    strict = row_id > col_id
    apart = row_id ^ col_id
    cum = mm_full(inclusive.astype(F32), -rate * switch)
    pack = jnp.where(lane < decay_col, lam, jnp.where(lane < beta_col, cum, switch))
    q_all, k_all, v_all = [], [], []
    for head in range(heads):
        for part in range(2):
            col = (part * heads + head) * LANES
            raw = acc[:, col : col + LANES]
            scale = lax.rsqrt(row_sum(raw * raw) + EPS)
            unit = raw * scale
            qkv_ref[part, head] = unit
            pack = jnp.where(lane == norm_col + part * heads + head, scale, pack)
            if part == 1:
                k_all.append(unit)
        col = (2 * heads + head) * LANES
        v_all.append(acc[:, col : col + LANES])
        qkv_ref[2, head] = v_all[head]
    pack_ref[...] = pack
    pack_t = pack.T
    pack_t_ref[...] = pack_t
    eye = (row_id == col_id).astype(F32)
    lower_all, trans_all = [], []
    for head in range(heads):
        decay = decay_of(pack, pack_t, decay_col + head, inclusive)
        beta = pack[:, beta_col + head : beta_col + head + 1]
        gram = mm_nt(k_all[head], k_all[head])
        lower = jnp.where(strict, beta * decay * gram, 0.0)
        lower_all.append(lower)
        trans_all.append((eye - jnp.where(apart == 1, lower, 0.0)).astype(BF16))
    for bit in range(1, rows.bit_length() - 1):
        here = (apart >> bit) == 1
        for head in range(heads):
            trans = trans_all[head]
            edge = jnp.where(here, lower_all[head], 0.0)
            trans_all[head] = trans - mm(mm(trans, edge), trans).astype(BF16)
    for head in range(heads):
        trans = trans_all[head]
        lower = lower_all[head]
        high = lower.astype(BF16)
        rest = eye - trans.astype(F32) - mm(high, trans) - mm(lower - high.astype(F32), trans)
        trans_all[head] = (trans.astype(F32) + mm(trans, rest)).astype(BF16)
        trans_ref[head] = trans_all[head]
    eye_key = eye[:LANES, :LANES]
    for head in range(heads):
        cum_col = pack[:, decay_col + head : decay_col + head + 1]
        beta = pack[:, beta_col + head : beta_col + head + 1]
        last = cum_col[rows - 1 : rows, :]
        tail = jnp.exp(last - cum_col) * k_all[head]
        mixed = mm_tn(trans_all[head], tail)
        mixed_ref[head] = mixed
        grown = (beta * jnp.exp(cum_col)) * k_all[head]
        pair_ref[head, :LANES] = (jnp.exp(last) * eye_key - mm_tn(grown, mixed)).astype(BF16)
        pair_ref[head, LANES:] = mm_tn(beta * v_all[head], mixed).astype(BF16)


def project(tokens, flat_w, small_t, head_param, heads, levels):
    rows, width = tokens.shape
    steps = 4
    depth = width // steps
    cols = 3 * heads
    key = flat_w.shape[1]
    fixed = lambda *shape: pl.BlockSpec(shape, lambda step: (0,) * len(shape))
    out_shape = (
        jax.ShapeDtypeStruct((width, cols * key), BF16),
        jax.ShapeDtypeStruct((3, heads, rows, key), F32),
        jax.ShapeDtypeStruct((rows, LANES), F32),
        jax.ShapeDtypeStruct((rows, LANES), F32),
        jax.ShapeDtypeStruct((LANES, rows), F32),
        jax.ShapeDtypeStruct((heads, rows, rows), BF16),
        jax.ShapeDtypeStruct((heads, rows, key), F32),
        jax.ShapeDtypeStruct((heads, 2 * key, key), BF16),
    )
    out_specs = (pl.BlockSpec((depth, cols * key), lambda step: (step, 0)),) + tuple(
        fixed(*shape.shape) for shape in out_shape[1:]
    )
    return pl.pallas_call(
        functools.partial(project_body, (heads, levels, steps)),
        grid=(steps,),
        out_shape=out_shape,
        in_specs=[
            SCALARS,
            pl.BlockSpec((rows, depth), lambda step: (0, step)),
            pl.BlockSpec((depth * cols, key), lambda step: (step, 0)),
            pl.BlockSpec((LANES, depth), lambda step: (0, step)),
        ],
        out_specs=out_specs,
        scratch_shapes=[
            pltpu.VMEM((depth * cols, key), F32),
            pltpu.VMEM((rows, cols * key), F32),
            pltpu.VMEM((rows, LANES), F32),
        ],
        compiler_params=PARAMS,
        name="project",
    )(head_param, tokens, flat_w, small_t)


def local_body(sizes, qkv_ref, pack_ref, pack_t_ref, trans_ref, attn_ref, local_ref, hat_ref):
    heads, levels, bits = sizes
    rows = pack_ref.shape[0]
    decay_col = levels * heads
    beta_col = decay_col + heads
    pack = pack_ref[...]
    pack_t = pack_t_ref[...]
    row_id, col_id = pair_ids(rows)
    inclusive = row_id >= col_id
    apart = row_id ^ col_id
    for head in range(heads):
        q_in, k_in, v_in = qkv_ref[0, head], qkv_ref[1, head], qkv_ref[2, head]
        decay = decay_of(pack, pack_t, decay_col + head, inclusive)
        scores = mm_nt_fine(q_in, k_in) * decay
        attn = mm(scores, trans_ref[head])
        attn_ref[head] = attn.astype(BF16)
        attn = attn * pack_t[beta_col + head : beta_col + head + 1, :]
        mix = level_mix(pack, head, heads, bits, apart)
        growth = jnp.exp(pack[:, decay_col + head : decay_col + head + 1])
        local_ref[head] = mm(attn * mix, v_in)
        hat_ref[head] = growth * q_in - mm(attn, growth * k_in)


def local_part(qkv, pack, pack_t, trans, levels, bits):
    heads, rows, key = qkv.shape[1:]
    return pl.pallas_call(
        functools.partial(local_body, (heads, levels, bits)),
        out_shape=(
            jax.ShapeDtypeStruct((heads, rows, rows), BF16),
            jax.ShapeDtypeStruct((heads, rows, key), F32),
            jax.ShapeDtypeStruct((heads, rows, key), F32),
        ),
        in_specs=[WHOLE] * 4,
        out_specs=(WHOLE,) * 3,
        compiler_params=PARAMS,
        name="local_part",
    )(qkv, pack, pack_t, trans)


def join_body(bit, place_ref, own_ref, other_ref, out_ref):
    heads = own_ref.shape[0]
    key = own_ref.shape[2]
    upper = ((place_ref[0] >> bit) & 1) == 1
    for head in range(heads):
        own, other = own_ref[head], other_ref[head]
        low = jnp.where(upper, other, own)
        high = jnp.where(upper, own, other)
        moved = mm(low, high[:key])
        out_ref[head, :key] = moved[:key].astype(BF16)
        out_ref[head, key:] = (moved[key:] + high[key:].astype(F32)).astype(BF16)


def join(bit, place, own, other):
    return pl.pallas_call(
        functools.partial(join_body, bit),
        out_shape=jax.ShapeDtypeStruct(own.shape, BF16),
        in_specs=[SCALARS, WHOLE, WHOLE],
        out_specs=WHOLE,
        compiler_params=PARAMS,
        name="join",
    )(place, own, other)


def cross_body(sizes, place_ref, gain_ref, pack_ref, local_ref, hat_ref, grad_ref, *refs):
    heads, bits, far = sizes
    others = refs[:far]
    normed_ref, dout_ref, dhat_ref, dfar_ref = refs[far : far + 4]
    sends = refs[far + 4 :]
    rows = pack_ref.shape[0]
    key = hat_ref.shape[2]
    place = place_ref[0]
    pack = pack_ref[...]
    gain = gain_ref[...]
    lane = lane_of(rows)
    dfar = jnp.zeros((rows, LANES), F32)
    eye_key = jnp.where(pair_ids(key)[0] == pair_ids(key)[1], 1.0, 0.0).astype(BF16)
    uppers = [((place >> bit) & 1) == 1 for bit in range(far)]
    for head in range(heads):
        prefix = eye_key
        prefixes, found = [], []
        for bit in range(far):
            prefixes.append(prefix)
            moved = mm(others[bit][head], prefix)
            found.append(jnp.where(uppers[bit], moved[key:], 0.0).astype(BF16))
            prefix = jnp.where(uppers[bit], moved[:key].astype(BF16), prefix)
        hat = hat_ref[head].astype(BF16)
        summed = local_ref[head]
        reached, weights = [], []
        for bit in range(far):
            col = (bits + 1 + bit) * heads + head
            weights.append(pack[:, col : col + 1])
            reached.append(mm_nt(hat, found[bit]))
            summed = summed + weights[bit] * reached[bit]
        scale = lax.rsqrt(jnp.mean(summed * summed, -1, keepdims=True) + EPS)
        unit = summed * scale
        normed_ref[:, head * key : (head + 1) * key] = (unit * gain).astype(BF16)
        pulled = grad_ref[:, head * key : (head + 1) * key] * gain
        dout = scale * (pulled - unit * jnp.mean(pulled * unit, -1, keepdims=True))
        dout_ref[head] = dout
        dhat = jnp.zeros((rows, key), F32)
        dfound = []
        for bit in range(far):
            col = (bits + 1 + bit) * heads + head
            dfar = jnp.where(lane == col, row_sum(dout * reached[bit]), dfar)
            spread = (weights[bit] * dout).astype(BF16)
            dhat = dhat + mm(spread, found[bit])
            dfound.append(mm_tn(spread, hat))
        dhat_ref[head] = dhat
        dprefix = jnp.zeros((key, key), F32)
        for bit in reversed(range(far)):
            dfree = jnp.where(uppers[bit], dfound[bit], 0.0)
            if bit == far - 1:
                sends[bit][head] = mm_nt(dfree, prefixes[bit]).astype(BF16)
                if bit > 0:
                    dprefix = mm_tn(others[bit][head, key:], dfree)
            else:
                both = jnp.concatenate([jnp.where(uppers[bit], dprefix, 0.0), dfree], 0)
                sends[bit][head] = mm_nt(both, prefixes[bit]).astype(BF16)
                if bit > 0:
                    moved = mm_tn(others[bit][head], both)
                    dprefix = jnp.where(uppers[bit], moved, dprefix)
    dfar_ref[...] = dfar


def cross(place, gain, pack, local_out, hat, grad_normed, others, bits):
    heads, rows, key = hat.shape
    far = len(others)
    sends = tuple(
        jax.ShapeDtypeStruct((heads, (1 if bit == far - 1 else 2) * key, key), BF16)
        for bit in range(far)
    )
    out_shape = (
        jax.ShapeDtypeStruct((rows, heads * key), BF16),
        jax.ShapeDtypeStruct((heads, rows, key), F32),
        jax.ShapeDtypeStruct((heads, rows, key), F32),
        jax.ShapeDtypeStruct((rows, LANES), F32),
    ) + sends
    return pl.pallas_call(
        functools.partial(cross_body, (heads, bits, far)),
        out_shape=out_shape,
        in_specs=[SCALARS] + [WHOLE] * (5 + far),
        out_specs=(WHOLE,) * len(out_shape),
        compiler_params=PARAMS,
        name="cross",
    )(place, gain, pack, local_out, hat, grad_normed, *others)


def spread_body(count, place_ref, left_ref, right_ref, *out_refs):
    size = out_refs[0].shape[1]
    for shift in range(count):
        dest = lax.rem(place_ref[1] + shift, count)
        cols = pl.ds(pl.multiple_of(dest * size, size), size)
        out_refs[shift][...] = jnp.dot(
            left_ref[...], right_ref[:, cols], preferred_element_type=F32
        ).astype(BF16)


def spread_out(place, left, right, count):
    size = right.shape[1] // count
    return pl.pallas_call(
        functools.partial(spread_body, count),
        out_shape=(jax.ShapeDtypeStruct((left.shape[0], size), BF16),) * count,
        in_specs=[SCALARS, WHOLE, WHOLE],
        out_specs=(WHOLE,) * count,
        compiler_params=PARAMS,
        name="spread_out",
    )(place, left, right)


def lower_pull(dlower, beta, decay, gram, strict, k_in):
    dlower = jnp.where(strict, dlower, 0.0)
    shaped = dlower * decay
    dbeta = row_sum(shaped * gram)
    dgram = shaped * beta
    both = dgram * gram
    dkey = mm(dgram, k_in) + mm_tn(dgram, k_in)
    return dbeta, row_sum(both), col_sum(both), dkey


def pull_body(
    sizes, qkv_ref, pack_ref, pack_t_ref, trans_ref, attn_ref, dout_ref, dhat_ref,
    dqkv_ref, dgrown_ref, dcol_ref, drow_ref
):
    heads, levels, bits = sizes
    rows = pack_ref.shape[0]
    decay_col = levels * heads
    beta_col = decay_col + heads
    block_bit = BLOCK.bit_length() - 1
    pack = pack_ref[...]
    pack_t = pack_t_ref[...]
    row_id, col_id = pair_ids(rows)
    inclusive = row_id >= col_id
    strict = row_id > col_id
    apart = row_id ^ col_id
    lane = lane_of(rows)
    dcol = jnp.zeros((rows, LANES), F32)
    dbeta_rows, dcum_rows = [], []
    for head in range(heads):
        q_in, k_in, v_in = qkv_ref[0, head], qkv_ref[1, head], qkv_ref[2, head]
        decay = decay_of(pack, pack_t, decay_col + head, inclusive)
        beta = pack[:, beta_col + head : beta_col + head + 1]
        beta_row = pack_t[beta_col + head : beta_col + head + 1, :]
        growth = jnp.exp(pack[:, decay_col + head : decay_col + head + 1])
        mix = level_mix(pack, head, heads, bits, apart)
        attn_low = attn_ref[head]
        attn0 = attn_low.astype(F32)
        attn = attn0 * beta_row
        dout = dout_ref[head].astype(BF16)
        dhat = dhat_ref[head]
        gram = mm_nt(k_in, k_in)
        scores = mm_nt(q_in, k_in) * decay
        rest = dout_ref[head] - dout.astype(F32)
        dprod = mm_nt(dout, v_in) + mm_nt(rest, v_in)
        dv = mm_tn(attn * mix, dout)
        touched = dprod * attn
        for level in range(bits + 1):
            if level == 0:
                here = (apart >> block_bit) == 0
            else:
                here = (apart >> (block_bit + level - 1)) == 1
            dcol = jnp.where(
                lane == level * heads + head, row_sum(jnp.where(here, touched, 0.0)), dcol
            )
        dattn = dprod * mix - mm_nt(dhat, growth * k_in)
        dattn0 = dattn * beta_row
        dbeta_rows.append(col_sum(dattn * attn0))
        dscore = mm_nt(dattn0, trans_ref[head])
        dlower = -mm_tn(attn_low, dscore)
        dgrown = -beta * mm_tn(attn_low, dhat)
        dprobs = dscore * decay
        dq = growth * dhat + mm(dprobs, k_in)
        dk = mm_tn(dprobs, q_in)
        shift = dscore * scores
        dbeta, dcum_col, dcum_row, dk_lower = lower_pull(dlower, beta, decay, gram, strict, k_in)
        dcum_col = dcum_col + row_sum(shift) + growth * row_sum(q_in * dhat)
        dcum_rows.append(-dcum_row - col_sum(shift))
        dqkv_ref[0, head] = dq
        dqkv_ref[1, head] = dk + dk_lower
        dqkv_ref[2, head] = dv
        dgrown_ref[head] = dgrown
        dcol = jnp.where(lane == beta_col + head, dbeta, dcol)
        dcol = jnp.where(lane == decay_col + head, dcum_col, dcol)
    dcol_ref[...] = dcol
    drow_ref[...] = jnp.concatenate(dcum_rows + dbeta_rows, 0)


def pull_local(qkv, pack, pack_t, trans, attn, dout, dhat, levels, bits):
    heads, rows, key = qkv.shape[1:]
    out_shape = (
        jax.ShapeDtypeStruct((3, heads, rows, key), F32),
        jax.ShapeDtypeStruct((heads, rows, key), F32),
        jax.ShapeDtypeStruct((rows, LANES), F32),
        jax.ShapeDtypeStruct((2 * heads, rows), F32),
    )
    return pl.pallas_call(
        functools.partial(pull_body, (heads, levels, bits)),
        out_shape=out_shape,
        in_specs=[WHOLE] * 7,
        out_specs=(WHOLE,) * len(out_shape),
        compiler_params=PARAMS,
        name="pull_local",
    )(qkv, pack, pack_t, trans, attn, dout, dhat)


def finish_body(sizes, place_ref, hp_ref, *refs):
    heads, levels, far, count = sizes
    (qkv_ref, gate_ref, pack_ref, pack_t_ref, trans_ref, mixed_ref, dqkv_ref, dgrown_ref,
     dcol_ref, drow_ref, dfar_ref, small_ref, wr_ref) = refs[:13]
    others = refs[13 : 13 + far]
    arrived = refs[13 + far : 13 + 2 * far]
    out_refs = refs[13 + 2 * far : 13 + 2 * far + count]
    dproj, wr, sem = refs[13 + 2 * far + count :]
    rows = pack_ref.shape[0]
    key = qkv_ref.shape[3]
    fetch = pltpu.make_async_copy(wr_ref, wr, sem)
    fetch.start()
    decay_col = levels * heads
    beta_col = decay_col + heads
    norm_col = beta_col + heads
    place = place_ref[0]
    uppers = [((place >> bit) & 1) == 1 for bit in range(far)]
    pack = pack_ref[...]
    pack_t = pack_t_ref[...]
    row_id, col_id = pair_ids(rows)
    inclusive = row_id >= col_id
    strict = row_id > col_id
    lane = lane_of(rows)
    last_row = lax.broadcasted_iota(jnp.int32, (rows, 1), 0) == rows - 1
    eye_key = (pair_ids(key)[0] == pair_ids(key)[1]).astype(F32)
    dcol = jnp.where(lane < decay_col, dcol_ref[...] + dfar_ref[...], dcol_ref[...])
    dcum_rows, dcum_cols = [], []
    for head in range(heads):
        q_in, k_in, v_in = qkv_ref[0, head], qkv_ref[1, head], qkv_ref[2, head]
        decay = decay_of(pack, pack_t, decay_col + head, inclusive)
        beta = pack[:, beta_col + head : beta_col + head + 1]
        cum_col = pack[:, decay_col + head : decay_col + head + 1]
        growth = jnp.exp(cum_col)
        last = cum_col[rows - 1 : rows, :]
        tail = jnp.exp(last - cum_col)
        gram = mm_nt(k_in, k_in)
        dpair = jnp.zeros((2 * key, key), F32)
        for bit in reversed(range(far)):
            other = others[bit][head]
            if bit == far - 1:
                got = jnp.concatenate(
                    [jnp.zeros((key, key), F32), arrived[bit][head].astype(F32)], 0
                )
                dpair = jnp.where(uppers[bit], 0.0, got)
            else:
                as_low = mm_nt(dpair, other[:key]) + arrived[bit][head].astype(F32)
                as_high = jnp.concatenate([mm_tn(other, dpair), dpair[key:]], 0)
                dpair = jnp.where(uppers[bit], as_high, as_low)
        mixed = mixed_ref[head]
        grown = growth * k_in
        dmixed = mm(v_in, dpair[key:]) - mm(grown, dpair[:key])
        moved = mm_nt(beta * mixed, dpair)
        dgrown = dgrown_ref[head] - moved[:, :key]
        dv = dqkv_ref[2, head] + moved[:, key:]
        dbeta_more = row_sum(mixed * dmixed)
        dtail = mm(trans_ref[head], beta * dmixed)
        dbeta, dcum_col, dcum_row, dk_lower = lower_pull(
            -mm_nt(mixed, dtail), beta, decay, gram, strict, k_in
        )
        dcum_rows.append(-dcum_row)
        tail_pull = tail * row_sum(k_in * dtail)
        at_last = col_sum(tail_pull) + jnp.exp(last) * col_sum(row_sum(dpair[:key] * eye_key))
        dcum_col = dcum_col + growth * row_sum(k_in * dgrown) - tail_pull
        dcum_col = dcum_col + jnp.where(last_row, at_last, 0.0)
        dk = dqkv_ref[1, head] + dk_lower + growth * dgrown + tail * dtail
        dq = dqkv_ref[0, head]
        dcol = dcol + jnp.where(lane == beta_col + head, dbeta + dbeta_more, 0.0)
        dcol = dcol + jnp.where(lane == decay_col + head, dcum_col, 0.0)
        for part, unit, dunit in ((0, q_in, dq), (1, k_in, dk)):
            at = norm_col + part * heads + head
            scale = pack[:, at : at + 1]
            back = scale * (dunit - unit * row_sum(unit * dunit))
            col = (part * heads + head) * key
            dproj[:, col : col + key] = back.astype(BF16)
        col = (2 * heads + head) * key
        dproj[:, col : col + key] = dv.astype(BF16)
    drow = drow_ref[...]
    drow = drow + jnp.concatenate(dcum_rows + [jnp.zeros((heads, rows), F32)], 0)
    drow = jnp.concatenate(
        [jnp.zeros((decay_col, rows), F32), drow,
         jnp.zeros((LANES - norm_col, rows), F32)], 0
    )
    dcol = dcol + drow.T
    lane_row = lane_of(1)
    rate = jnp.zeros((1, LANES), F32)
    bias = jnp.zeros((1, LANES), F32)
    for head in range(heads):
        rate = jnp.where(lane_row == decay_col + head, hp_ref[head, 0], rate)
        bias = jnp.where(lane_row == beta_col + head, hp_ref[head, 1], bias)
    switch = jax.nn.sigmoid(gate_ref[...] + bias)
    dlog = mm_full((row_id <= col_id).astype(F32), dcol)
    slope = switch * (1.0 - switch)
    dgate = jnp.where(
        lane < decay_col,
        dcol * switch,
        jnp.where(lane < beta_col, -rate * dlog * slope, dcol * slope),
    )
    dgate = jnp.where(lane < norm_col, dgate, 0.0).astype(BF16)
    fetch.wait()
    size = out_refs[0].shape[1]
    for shift in range(count):
        dest = lax.rem(place_ref[1] + shift, count)
        span = pl.ds(pl.multiple_of(dest * size, size), size)
        part = mm_nt(dproj[...], wr[span, :]) + mm(dgate, small_ref[:, span])
        out_refs[shift][...] = part.astype(BF16)


def finish(place, head_param, arrays, wr, others, arrived, levels, count):
    heads, rows, key = arrays[0].shape[1:]
    width = wr.shape[0]
    far = len(others)
    return pl.pallas_call(
        functools.partial(finish_body, (heads, levels, far, count)),
        out_shape=(jax.ShapeDtypeStruct((rows, width // count), BF16),) * count,
        in_specs=[SCALARS, SCALARS]
        + [WHOLE] * len(arrays)
        + [pl.BlockSpec(memory_space=pl.ANY)]
        + [WHOLE] * (2 * far),
        out_specs=(WHOLE,) * count,
        scratch_shapes=[
            pltpu.VMEM((rows, wr.shape[1]), BF16),
            pltpu.VMEM(wr.shape, BF16),
            pltpu.SemaphoreType.DMA,
        ],
        compiler_params=PARAMS,
        name="finish",
    )(place, head_param, *arrays, wr, *others, *arrived)


def swap(value, axis, bit):
    size = lax.axis_size(axis)
    return lax.ppermute(value, axis, [(at, at ^ (1 << bit)) for at in range(size)])


def scatter_sum(parts, axis):
    count = lax.axis_size(axis)
    total = parts[0].astype(F32)
    for shift in range(1, count):
        got = lax.ppermute(parts[shift], axis, [(at, (at + shift) % count) for at in range(count)])
        total = total + got.astype(F32)
    return total.astype(BF16)


def on_device(tokens, qkv_weight, small_weight, head_param, norm_gain, out_weight, grad_out):
    rows, width = tokens.shape
    heads, key = qkv_weight.shape[2:]
    cols = small_weight.shape[2]
    levels = cols - 2
    bits = (rows // BLOCK).bit_length() - 1
    far = lax.axis_size("ctx").bit_length() - 1
    count = lax.axis_size("head")
    place = jnp.stack([lax.axis_index("ctx"), lax.axis_index("head")]).astype(jnp.int32)
    flat_w = qkv_weight.reshape(width * 3 * heads, key)
    small_t = jnp.transpose(small_weight, (2, 1, 0)).reshape(cols * heads, width)
    small_t = jnp.pad(small_t, ((0, LANES - cols * heads), (0, 0)))
    flat_out = out_weight.reshape(heads * key, width)
    gain = norm_gain.reshape(1, key)

    wr, qkv, gate, pack, pack_t, trans, mixed, pair = project(
        tokens, flat_w, small_t, head_param, heads, levels
    )
    attn, local_out, hat = local_part(qkv, pack, pack_t, trans, levels, bits)
    grad_normed = lax.dot_general(
        grad_out, flat_out, (((1,), (1,)), ((), ())), preferred_element_type=F32
    )
    others = []
    for bit in range(far):
        others.append(swap(pair, "ctx", bit))
        if bit < far - 1:
            pair = join(bit, place, pair, others[bit])
    normed, dout, dhat, dfar, *sends = cross(
        place, gain, pack, local_out, hat, grad_normed, others, bits
    )
    arrived = []
    for bit in range(far):
        got = [swap(value, "ctx", bit) for value in sends]
        arrived.append(got[0])
        sends = [
            (mine.astype(F32) + more.astype(F32)).astype(BF16)
            for mine, more in zip(sends[1:], got[1:])
        ]
    layer_out = scatter_sum(spread_out(place, normed, flat_out, count), "head")
    dqkv, dgrown, dcol, drow = pull_local(
        qkv, pack, pack_t, trans, attn, dout, dhat, levels, bits
    )
    arrays = (qkv, gate, pack, pack_t, trans, mixed, dqkv, dgrown, dcol, drow, dfar, small_t)
    parts = finish(place, head_param, arrays, wr, others, arrived, levels, count)
    return layer_out, scatter_sum(parts, "head")


def solution(mesh):
    placed = (
        P("ctx", None),
        P(None, None, "head", None),
        P(None, "head", None),
        P("head", None),
        P(),
        P("head", None, None),
        P("ctx", None),
    )
    return jax.shard_map(
        on_device,
        mesh=mesh,
        in_specs=placed,
        out_specs=(P("ctx", "head"), P("ctx", "head")),
        check_vma=False,
    )
```

```python
import functools

import jax
import jax.numpy as jnp
from jax import lax
from jax.experimental import pallas as pl
from jax.experimental.pallas import tpu as pltpu
from jax.sharding import PartitionSpec as P

BLOCK = 64
LANES = 128
EPS = 1e-06
VMEM_BYTES = 28 * 1024 * 1024
F32 = jnp.float32
BF16 = jnp.bfloat16
WHOLE = pl.BlockSpec(memory_space=pltpu.VMEM)
SCALARS = pl.BlockSpec(memory_space=pltpu.SMEM)
PARAMS = pltpu.CompilerParams(vmem_limit_bytes=VMEM_BYTES)


def contract(left, right, dim_left, dim_right):
    return lax.dot_general(
        left.astype(BF16),
        right.astype(BF16),
        (((dim_left,), (dim_right,)), ((), ())),
        preferred_element_type=F32,
    )


def mm(left, right):
    return contract(left, right, 1, 0)


def mm_nt(left, right):
    return contract(left, right, 1, 1)


def mm_tn(left, right):
    return contract(left, right, 0, 0)


def split(values):
    high = values.astype(BF16)
    return high, (values - high.astype(F32)).astype(BF16)


def mm_nt_fine(left, right):
    left_high, left_low = split(left)
    right_high, right_low = split(right)
    return mm_nt(left_high, right_high) + (mm_nt(left_low, right_high) + mm_nt(left_high, right_low))


def mm_full(left, right):
    return jnp.dot(left, right, precision=lax.Precision.HIGHEST, preferred_element_type=F32)


def pair_ids(count):
    row_id = lax.broadcasted_iota(jnp.int32, (count, count), 0)
    col_id = lax.broadcasted_iota(jnp.int32, (count, count), 1)
    return row_id, col_id


def row_sum(values):
    return jnp.sum(values, 1, keepdims=True)


def col_sum(values):
    return jnp.sum(values, 0, keepdims=True)


def lane_of(rows):
    return lax.broadcasted_iota(jnp.int32, (rows, LANES), 1)


def decay_of(pack, pack_t, col, inclusive):
    spread = pack[:, col : col + 1] - pack_t[col : col + 1, :]
    return jnp.where(inclusive, jnp.exp(jnp.minimum(spread, 0.0)), 0.0)


def kept(shape, dtype):
    return pltpu.VMEM(shape, dtype)


def pin(values):
    return [pltpu.with_memory_space_constraint(value, pltpu.VMEM) for value in values]


def local_call(body, name, out_shape, scalars, arrays, scratch=(), remote=()):
    return pl.pallas_call(
        body,
        out_shape=tuple(out_shape),
        in_specs=[SCALARS] * len(scalars)
        + [WHOLE] * len(arrays)
        + [pl.BlockSpec(memory_space=pl.ANY)] * len(remote),
        out_specs=(WHOLE,) * len(out_shape),
        scratch_shapes=list(scratch),
        compiler_params=PARAMS,
        name=name,
    )(*scalars, *pin(arrays), *remote)


def column(pack, at):
    return pack[:, at : at + 1]


def level_mix(pack, head, heads, bits, apart):
    block_bit = BLOCK.bit_length() - 1
    mixed = jnp.broadcast_to(column(pack, head), apart.shape)
    for level in range(1, bits + 1):
        here = (apart >> (block_bit + level - 1)) >= 1
        mixed = jnp.where(here, column(pack, level * heads + head), mixed)
    return mixed


def head_rows(hp_ref, heads, decay_col, beta_col):
    lane_row = lane_of(1)
    rate = jnp.zeros((1, LANES), F32)
    bias = jnp.zeros((1, LANES), F32)
    for head in range(heads):
        rate = jnp.where(lane_row == decay_col + head, hp_ref[0, head], rate)
        bias = jnp.where(lane_row == beta_col + head, hp_ref[1, head], bias)
    return rate, bias


def project_body(sizes, hp_ref, tokens_hbm, w_hbm, small_hbm, *refs):
    heads, levels, chunks = sizes
    (wr_ref, small_ref, qkv_ref, gate_ref, pack_ref, pack_t_ref, trans_ref, mixed_t_ref,
     decay_ref, base_ref, lower_ref, pair_ref) = refs[:12]
    tokens, wide_in, wide_even, wide_odd, small_in, small_wide, acc, sems = refs[12:]
    rows, width = tokens.shape
    depth = width // chunks
    cols = 3 * heads
    fetch_tokens = pltpu.make_async_copy(tokens_hbm, tokens, sems.at[chunks])
    fetch_small = pltpu.make_async_copy(small_hbm, small_in, sems.at[chunks + 1])
    fetches = []
    for chunk in range(chunks):
        span = pl.ds(chunk * depth * cols, depth * cols)
        fetches.append(
            pltpu.make_async_copy(w_hbm.at[span, :], wide_in.at[span, :], sems.at[chunk])
        )
    fetches[0].start()
    fetch_tokens.start()
    fetch_small.start()
    for fetch in fetches[1:]:
        fetch.start()
    for chunk in range(chunks):
        fetches[chunk].wait()
        at = chunk * depth
        wide = wide_odd if chunk % 2 else wide_even
        wide[...] = wide_in[at * cols : (at + depth) * cols, :].astype(F32)
        for col in range(cols):
            part = wide[pl.ds(col, depth, stride=cols), :]
            wr_ref[at : at + depth, col * LANES : (col + 1) * LANES] = part.astype(BF16)
        if chunk == 0:
            fetch_tokens.wait()
        own = jnp.dot(
            tokens[:, at : at + depth], wr_ref[at : at + depth, :], preferred_element_type=F32
        )
        if chunk == 0:
            acc[...] = own
        else:
            acc[...] += own
    fetch_small.wait()
    small_rows = small_in.shape[0] * heads
    for level in range(small_in.shape[0]):
        small_wide[level * heads : (level + 1) * heads, :] = small_in[level].astype(F32)
    small_wide[small_rows:, :] = jnp.zeros((LANES - small_rows, width), F32)
    small_ref[...] = small_wide[...].astype(BF16)
    gate = mm_nt(tokens[...], small_ref[...])
    decay_col = levels * heads
    beta_col = decay_col + heads
    norm_col = beta_col + heads
    gate_ref[...] = gate
    lane = lane_of(rows)
    rate, bias = head_rows(hp_ref, heads, decay_col, beta_col)
    switch = jax.nn.sigmoid(gate + bias)
    lam = jnp.maximum(gate, 0.0) + jnp.log1p(jnp.exp(-jnp.abs(gate)))
    row_id, col_id = pair_ids(rows)
    inclusive = row_id >= col_id
    strict = row_id > col_id
    apart = row_id ^ col_id
    cum = mm_full(inclusive.astype(F32), -rate * switch)
    pack = jnp.where(lane < decay_col, lam, jnp.where(lane < beta_col, cum, switch))
    k_all, v_all = [], []
    for head in range(heads):
        for part in range(2):
            col = (part * heads + head) * LANES
            raw = acc[:, col : col + LANES]
            scale = lax.rsqrt(row_sum(raw * raw) + EPS)
            unit = raw * scale
            qkv_ref[part, head] = unit
            pack = jnp.where(lane == norm_col + part * heads + head, scale, pack)
            if part == 1:
                k_all.append(unit)
        col = (2 * heads + head) * LANES
        v_all.append(acc[:, col : col + LANES])
        qkv_ref[2, head] = v_all[head]
    pack_ref[...] = pack
    pack_t = pack.T
    pack_t_ref[...] = pack_t
    eye = (row_id == col_id).astype(F32)
    lower_all, trans_all = [], []
    for head in range(heads):
        decay = decay_of(pack, pack_t, decay_col + head, inclusive)
        decay_ref[head] = decay
        gram = mm_nt(k_all[head], k_all[head])
        base = jnp.where(strict, decay * gram, 0.0)
        base_ref[head] = base
        lower = column(pack, beta_col + head) * base
        lower_ref[head] = lower
        lower_all.append(lower)
        trans_all.append((eye - jnp.where(apart == 1, lower, 0.0)).astype(BF16))
    for bit in range(1, rows.bit_length() - 1):
        here = (apart >> bit) == 1
        edge = [jnp.where(here, lower, 0.0) for lower in lower_all]
        half = [mm(trans, part) for trans, part in zip(trans_all, edge)]
        trans_all = [
            trans - mm(part, trans).astype(BF16) for trans, part in zip(trans_all, half)
        ]
    rest_all = []
    for trans, lower in zip(trans_all, lower_all):
        high, low = split(lower)
        rest_all.append(eye - trans.astype(F32) - mm(high, trans) - mm(low, trans))
    trans_all = [
        (trans.astype(F32) + mm(trans, rest)).astype(BF16)
        for trans, rest in zip(trans_all, rest_all)
    ]
    mixed_all = []
    for head in range(heads):
        trans_ref[head] = trans_all[head]
        cum_row = pack_t[decay_col + head : decay_col + head + 1, :]
        tail_t = k_all[head].T * jnp.exp(cum_row[:, rows - 1 :] - cum_row)
        mixed_all.append(mm(tail_t, trans_all[head]))
    eye_key = eye[:LANES, :LANES]
    for head in range(heads):
        mixed_t_ref[head] = mixed_all[head]
        cum_col = column(pack, decay_col + head)
        beta = column(pack, beta_col + head)
        grown = (beta * jnp.exp(cum_col)) * k_all[head]
        both = jnp.concatenate([-grown, beta * v_all[head]], 1)
        pair = mm(mixed_all[head], both)
        last = jnp.exp(cum_col[rows - 1 : rows, :])
        pair_ref[head, :, :LANES] = (last * eye_key + pair[:, :LANES]).astype(BF16)
        pair_ref[head, :, LANES:] = pair[:, LANES:].astype(BF16)


def project(tokens, flat_w, small, head_param, heads, levels):
    rows, width = tokens.shape
    chunks = 8
    cols = 3 * heads
    key = flat_w.shape[1]
    square = (heads, rows, rows)
    out_shape = (
        kept((width, cols * key), BF16),
        kept((LANES, width), BF16),
        kept((3, heads, rows, key), F32),
        kept((rows, LANES), F32),
        kept((rows, LANES), F32),
        kept((LANES, rows), F32),
        kept(square, BF16),
        kept((heads, key, rows), F32),
        kept(square, F32),
        kept(square, F32),
        kept(square, F32),
        kept((heads, key, 2 * key), BF16),
    )
    scratch = [
        pltpu.VMEM(tokens.shape, BF16),
        pltpu.VMEM(flat_w.shape, BF16),
        pltpu.VMEM((width // chunks * cols, key), F32),
        pltpu.VMEM((width // chunks * cols, key), F32),
        pltpu.VMEM(small.shape, BF16),
        pltpu.VMEM((LANES, width), F32),
        pltpu.VMEM((rows, cols * key), F32),
        pltpu.SemaphoreType.DMA((chunks + 2,)),
    ]
    return local_call(
        functools.partial(project_body, (heads, levels, chunks)), "project", out_shape,
        [head_param], [], scratch, [tokens, flat_w, small],
    )


def local_body(sizes, qkv_ref, pack_ref, pack_t_ref, trans_ref, mixed_t_ref, decay_ref, *outs):
    heads, levels, bits = sizes
    (attn_ref, attn_t_ref, prod_t_ref, scores_ref, mix_ref, mixed_ref, local_ref, hat_ref,
     hat_t_ref) = outs
    rows = pack_ref.shape[0]
    decay_col = levels * heads
    beta_col = decay_col + heads
    pack = pack_ref[...]
    pack_t = pack_t_ref[...]
    row_id, col_id = pair_ids(rows)
    apart = row_id ^ col_id
    for head in range(heads):
        scores = mm_nt_fine(qkv_ref[0, head], qkv_ref[1, head]) * decay_ref[head]
        scores_ref[head] = scores.astype(BF16)
        mix_ref[head] = level_mix(pack, head, heads, bits, apart)
        mixed_ref[head] = mixed_t_ref[head].T.astype(BF16)
    for head in range(heads):
        attn = mm(scores_ref[head], trans_ref[head])
        attn_ref[head] = attn.astype(BF16)
        attn_t_ref[head] = attn.T.astype(BF16)
        attn = attn * pack_t[beta_col + head : beta_col + head + 1, :]
        prod = attn * mix_ref[head]
        prod_t_ref[head] = prod.T.astype(BF16)
        growth = jnp.exp(column(pack, decay_col + head))
        local_ref[head] = mm(prod, qkv_ref[2, head])
        hat = growth * qkv_ref[0, head] - mm(attn, growth * qkv_ref[1, head])
        hat_ref[head] = hat.astype(BF16)
        hat_t_ref[head] = hat.T.astype(BF16)


def local_part(qkv, pack, pack_t, trans, mixed_t, decay, levels, bits):
    heads, rows, key = qkv.shape[1:]
    square = (heads, rows, rows)
    out_shape = (
        kept(square, BF16),
        kept(square, BF16),
        kept(square, BF16),
        kept(square, BF16),
        kept(square, F32),
        kept((heads, rows, key), BF16),
        kept((heads, rows, key), F32),
        kept((heads, rows, key), BF16),
        kept((heads, key, rows), BF16),
    )
    return local_call(
        functools.partial(local_body, (heads, levels, bits)), "local_part", out_shape,
        [], [qkv, pack, pack_t, trans, mixed_t, decay],
    )


def join_pair(upper, own, other):
    key = own.shape[0]
    low = jnp.where(upper, other, own)
    high = jnp.where(upper, own, other)
    moved = mm(high[:, :key], low)
    late = jnp.concatenate([jnp.zeros((key, key), F32), high[:, key:].astype(F32)], 1)
    return (moved + late).astype(BF16)


def join_body(bit, place_ref, own_ref, other_ref, out_ref):
    upper = ((place_ref[0] >> bit) & 1) == 1
    for head in range(own_ref.shape[0]):
        out_ref[head] = join_pair(upper, own_ref[head], other_ref[head])


def join(bit, place, own, other):
    return local_call(
        functools.partial(join_body, bit), "join", [kept(own.shape, BF16)], [place], [own, other]
    )[0]


def gather_node(head, bit, first, near, uppers):
    if bit == 0:
        return near[first][head]
    own = gather_node(head, bit - 1, first, near, uppers)
    other = gather_node(head, bit - 1, first ^ (1 << (bit - 1)), near, uppers)
    return join_pair(uppers[bit], own, other)


def cross_body(sizes, place_ref, gain_ref, pack_ref, local_ref, hat_ref, hat_t_ref, grad_ref, *refs):
    heads, bits, far, near_count = sizes
    first_ref = refs[0]
    near = (None,) + refs[1 : near_count + 1]
    refs = refs[near_count + 1 :]
    normed_ref, dout_ref, dhat_ref, dfar_ref = refs[:4]
    nodes = refs[4 : 4 + far - 2]
    sends = refs[4 + max(far - 2, 0) :]
    rows = pack_ref.shape[0]
    key = hat_ref.shape[2]
    place = place_ref[0]
    pack = pack_ref[...]
    gain = gain_ref[...]
    lane = lane_of(rows)
    all_heads = range(heads)
    uppers = [((place >> bit) & 1) == 1 for bit in range(far)]
    others = []
    for bit in range(far):
        if bit == 0:
            others.append([first_ref[head] for head in all_heads])
        elif bit == 1:
            others.append([near[1][head] for head in all_heads])
        else:
            others.append(
                [gather_node(head, bit - 1, 1 << (bit - 1), near, uppers) for head in all_heads]
            )
            for head in all_heads:
                nodes[bit - 2][head] = others[bit][head]
    eye_key = jnp.where(pair_ids(key)[0] == pair_ids(key)[1], 1.0, 0.0).astype(BF16)
    prefix = [eye_key for head in all_heads]
    prefixes, found = [], []
    for bit in range(far):
        prefixes.append(prefix)
        moved = [mm(prefix[head], others[bit][head]) for head in all_heads]
        found.append([jnp.where(uppers[bit], m[:, key:], 0.0).astype(BF16) for m in moved])
        prefix = [
            jnp.where(uppers[bit], moved[head][:, :key].astype(BF16), prefix[head])
            for head in all_heads
        ]
    found = [jnp.concatenate([found[bit][head] for bit in range(far)], 1) for head in all_heads]
    reached = [mm(hat_ref[head], found[head]) for head in all_heads]
    dfar = jnp.zeros((rows, LANES), F32)
    spread = []
    for head in all_heads:
        summed = local_ref[head]
        weights, parts = [], []
        for bit in range(far):
            weights.append(column(pack, (bits + 1 + bit) * heads + head))
            parts.append(reached[head][:, bit * key : (bit + 1) * key])
            summed = summed + weights[bit] * parts[bit]
        scale = lax.rsqrt(jnp.mean(summed * summed, -1, keepdims=True) + EPS)
        unit = summed * scale
        normed_ref[:, head * key : (head + 1) * key] = (unit * gain).astype(BF16)
        pulled = grad_ref[:, head * key : (head + 1) * key] * gain
        dout = scale * (pulled - unit * jnp.mean(pulled * unit, -1, keepdims=True))
        dout_ref[head] = dout
        for bit in range(far):
            col = (bits + 1 + bit) * heads + head
            dfar = jnp.where(lane == col, row_sum(dout * parts[bit]), dfar)
        spread.append(
            jnp.concatenate([(weights[bit] * dout).astype(BF16) for bit in range(far)], 1)
        )
    dfar_ref[...] = dfar
    dfound = [mm(hat_t_ref[head], spread[head]) for head in all_heads]
    for head in all_heads:
        dhat_ref[head] = mm_nt(spread[head], found[head])
    dprefix = [jnp.zeros((key, key), F32) for head in all_heads]
    for bit in reversed(range(far)):
        dfree = [
            jnp.where(uppers[bit], d[:, bit * key : (bit + 1) * key], 0.0) for d in dfound
        ]
        both = [
            jnp.concatenate([jnp.where(uppers[bit], dprefix[head], 0.0), dfree[head]], 1)
            for head in all_heads
        ]
        for head in all_heads:
            if bit == far - 1:
                sends[bit][head] = mm_tn(prefixes[bit][head], dfree[head]).astype(BF16)
            else:
                sends[bit][head] = mm_tn(prefixes[bit][head], both[head]).astype(BF16)
        if bit > 0:
            moved = [mm_nt(both[head], others[bit][head]) for head in all_heads]
            dprefix = [
                jnp.where(uppers[bit], moved[head], dprefix[head]) for head in all_heads
            ]


def cross(place, gain, pack, local_out, hat, hat_t, grad_normed, first, near, bits, far):
    heads, rows, key = hat.shape
    nodes = tuple(kept(first.shape, BF16) for bit in range(2, far))
    sends = tuple(
        kept((heads, key, (1 if bit == far - 1 else 2) * key), BF16) for bit in range(far)
    )
    out_shape = (
        kept((rows, heads * key), BF16),
        kept((heads, rows, key), F32),
        kept((heads, rows, key), F32),
        kept((rows, LANES), F32),
    ) + nodes + sends
    got = local_call(
        functools.partial(cross_body, (heads, bits, far, len(near))), "cross", out_shape,
        [place], [gain, pack, local_out, hat, hat_t, grad_normed, first, *near],
    )
    return got[:4], got[4 : 4 + len(nodes)], got[4 + len(nodes) :]


def spread_body(count, place_ref, left_ref, right_ref, *out_refs):
    size = out_refs[0].shape[1]
    for shift in range(count):
        dest = lax.rem(place_ref[1] + shift, count)
        cols = pl.ds(pl.multiple_of(dest * size, size), size)
        out_refs[shift][...] = jnp.dot(
            left_ref[...], right_ref[:, cols], preferred_element_type=F32
        ).astype(BF16)


def spread_out(place, left, right, count):
    out = kept((left.shape[0], right.shape[1] // count), BF16)
    return local_call(
        functools.partial(spread_body, count), "spread_out", [out] * count, [place], [left, right]
    )


def add_body(*refs):
    count = len(refs) // 3
    for at in range(count):
        left, right = refs[at][...].astype(F32), refs[count + at][...].astype(F32)
        refs[2 * count + at][...] = (left + right).astype(BF16)


def add_all(left, right):
    out_shape = [kept(value.shape, BF16) for value in left]
    return local_call(add_body, "add_all", out_shape, [], [*left, *right])


def lower_pull(dlower, base, lower, beta, decay, strict, k_in):
    dlower = jnp.where(strict, dlower, 0.0)
    dbeta = row_sum(dlower * base)
    dgram = dlower * (beta * decay)
    dkey = mm(dgram, k_in) + mm_tn(dgram, k_in)
    return dbeta, beta * dbeta, col_sum(dlower * lower), dkey


def pull_body(sizes, *refs):
    heads, levels, bits = sizes
    (qkv_ref, pack_ref, pack_t_ref, trans_ref, attn_ref, attn_t_ref, prod_t_ref, scores_ref,
     mix_ref, decay_ref, base_ref, lower_ref, dout_ref, dhat_ref) = refs[:14]
    dqkv_ref, dgrown_ref, dcol_ref, drow_ref = refs[14:]
    rows = pack_ref.shape[0]
    decay_col = levels * heads
    beta_col = decay_col + heads
    block_bit = BLOCK.bit_length() - 1
    pack = pack_ref[...]
    pack_t = pack_t_ref[...]
    row_id, col_id = pair_ids(rows)
    strict = row_id > col_id
    apart = row_id ^ col_id
    lane = lane_of(rows)
    all_heads = range(heads)
    dcol = jnp.zeros((rows, LANES), F32)
    dbeta_rows, dcum_rows, dattn_all = [], [], []
    for head in all_heads:
        high, low = split(dout_ref[head])
        v_in = qkv_ref[2, head].astype(BF16)
        dprod = mm_nt(high, v_in) + mm_nt(low, v_in)
        dqkv_ref[2, head] = mm(prod_t_ref[head], high)
        beta_row = pack_t[beta_col + head : beta_col + head + 1, :]
        growth = jnp.exp(column(pack, decay_col + head))
        attn0 = attn_ref[head].astype(F32)
        touched = dprod * (attn0 * beta_row)
        for level in range(bits + 1):
            if level == 0:
                here = (apart >> block_bit) == 0
            else:
                here = (apart >> (block_bit + level - 1)) == 1
            dcol = jnp.where(
                lane == level * heads + head, row_sum(jnp.where(here, touched, 0.0)), dcol
            )
        dattn = dprod * mix_ref[head] - mm_nt(dhat_ref[head], growth * qkv_ref[1, head])
        dbeta_rows.append(col_sum(dattn * attn0))
        dattn_all.append((dattn * beta_row).astype(BF16))
    dscore_all = [mm_nt(dattn_all[head], trans_ref[head]) for head in all_heads]
    moved_all = []
    for head in all_heads:
        both = jnp.concatenate(
            [dscore_all[head].astype(BF16), dhat_ref[head].astype(BF16)], 1
        )
        moved_all.append(mm(attn_t_ref[head], both))
    for head in all_heads:
        q_in, k_in = qkv_ref[0, head], qkv_ref[1, head]
        beta = column(pack, beta_col + head)
        growth = jnp.exp(column(pack, decay_col + head))
        dscore = dscore_all[head]
        dprobs = dscore * decay_ref[head]
        shift = dscore * scores_ref[head].astype(F32)
        dgrown_ref[head] = -beta * moved_all[head][:, rows:]
        dbeta, dcum_col, dcum_row, dk_lower = lower_pull(
            -moved_all[head][:, :rows], base_ref[head], lower_ref[head], beta, decay_ref[head],
            strict, k_in
        )
        dhat = dhat_ref[head]
        dqkv_ref[0, head] = growth * dhat + mm(dprobs, k_in)
        dqkv_ref[1, head] = mm_tn(dprobs, q_in) + dk_lower
        dcum_col = dcum_col + row_sum(shift) + growth * row_sum(q_in * dhat)
        dcum_rows.append(-dcum_row - col_sum(shift))
        dcol = jnp.where(lane == beta_col + head, dbeta, dcol)
        dcol = jnp.where(lane == decay_col + head, dcum_col, dcol)
    dcol_ref[...] = dcol
    drow_ref[...] = jnp.concatenate(dcum_rows + dbeta_rows, 0)


def pull_local(arrays, levels, bits):
    heads, rows, key = arrays[0].shape[1:]
    out_shape = (
        kept((3, heads, rows, key), F32),
        kept((heads, rows, key), F32),
        kept((rows, LANES), F32),
        kept((2 * heads, rows), F32),
    )
    return local_call(
        functools.partial(pull_body, (heads, levels, bits)), "pull_local", out_shape, [], arrays
    )


def finish_body(sizes, place_ref, hp_ref, *refs):
    heads, levels, far, count, arrived_counts = sizes
    (qkv_ref, gate_ref, pack_ref, trans_ref, mixed_ref, decay_ref, base_ref, lower_ref,
     dqkv_ref, dgrown_ref, dcol_ref, drow_ref, dfar_ref, small_ref, wr_ref) = refs[:15]
    others = refs[15 : 15 + far]
    refs = refs[15 + far :]
    arrived = []
    for found in arrived_counts:
        arrived.append(refs[:found])
        refs = refs[found:]
    out_refs = refs[:count]
    (dproj,) = refs[count:]
    rows = pack_ref.shape[0]
    key = qkv_ref.shape[3]
    decay_col = levels * heads
    beta_col = decay_col + heads
    norm_col = beta_col + heads
    place = place_ref[0]
    all_heads = range(heads)
    uppers = [((place >> bit) & 1) == 1 for bit in range(far)]
    pack = pack_ref[...]
    row_id, col_id = pair_ids(rows)
    strict = row_id > col_id
    lane = lane_of(rows)
    last_row = lax.broadcasted_iota(jnp.int32, (rows, 1), 0) == rows - 1
    eye_key = (pair_ids(key)[0] == pair_ids(key)[1]).astype(F32)
    dpair = [jnp.zeros((key, 2 * key), F32) for head in all_heads]
    for bit in reversed(range(far)):
        for head in all_heads:
            got = arrived[bit][0][head].astype(F32)
            for more in arrived[bit][1:]:
                got = got + more[head].astype(F32)
            other = others[bit][head]
            if bit == far - 1:
                got = jnp.concatenate([jnp.zeros((key, key), F32), got], 1)
                dpair[head] = jnp.where(uppers[bit], 0.0, got)
            else:
                as_low = mm_tn(other[:, :key], dpair[head]) + got
                as_high = mm_nt(dpair[head], other)
                as_high = jnp.concatenate([as_high, dpair[head][:, key:]], 1)
                dpair[head] = jnp.where(uppers[bit], as_high, as_low)
    moved_all, dmixed_all = [], []
    for head in all_heads:
        beta = column(pack, beta_col + head)
        growth = jnp.exp(column(pack, decay_col + head))
        both = jnp.concatenate([-growth * qkv_ref[1, head], qkv_ref[2, head]], 1)
        dmixed_all.append(mm_nt(both, dpair[head]))
        moved_all.append(mm(beta * mixed_ref[head].astype(F32), dpair[head]))
    dtail_all = [
        mm(trans_ref[head], column(pack, beta_col + head) * dmixed_all[head])
        for head in all_heads
    ]
    dlower_all = [-mm_nt(mixed_ref[head], dtail_all[head]) for head in all_heads]
    dcol = jnp.where(lane < decay_col, dcol_ref[...] + dfar_ref[...], dcol_ref[...])
    dcum_rows = []
    for head in all_heads:
        q_in, k_in = qkv_ref[0, head], qkv_ref[1, head]
        beta = column(pack, beta_col + head)
        cum_col = column(pack, decay_col + head)
        growth = jnp.exp(cum_col)
        last = cum_col[rows - 1 : rows, :]
        tail = jnp.exp(last - cum_col)
        dgrown = dgrown_ref[head] - moved_all[head][:, :key]
        dv = dqkv_ref[2, head] + moved_all[head][:, key:]
        dbeta_more = row_sum(mixed_ref[head].astype(F32) * dmixed_all[head])
        dtail = dtail_all[head]
        dbeta, dcum_col, dcum_row, dk_lower = lower_pull(
            dlower_all[head], base_ref[head], lower_ref[head], beta, decay_ref[head], strict, k_in
        )
        dcum_rows.append(-dcum_row)
        tail_pull = tail * row_sum(k_in * dtail)
        trace = col_sum(row_sum(dpair[head][:, :key] * eye_key))
        at_last = col_sum(tail_pull) + jnp.exp(last) * trace
        dcum_col = dcum_col + growth * row_sum(k_in * dgrown) - tail_pull
        dcum_col = dcum_col + jnp.where(last_row, at_last, 0.0)
        dk = dqkv_ref[1, head] + dk_lower + growth * dgrown + tail * dtail
        dq = dqkv_ref[0, head]
        dcol = dcol + jnp.where(lane == beta_col + head, dbeta + dbeta_more, 0.0)
        dcol = dcol + jnp.where(lane == decay_col + head, dcum_col, 0.0)
        for part, unit, dunit in ((0, q_in, dq), (1, k_in, dk)):
            scale = column(pack, norm_col + part * heads + head)
            back = scale * (dunit - unit * row_sum(unit * dunit))
            col = (part * heads + head) * key
            dproj[:, col : col + key] = back.astype(BF16)
        col = (2 * heads + head) * key
        dproj[:, col : col + key] = dv.astype(BF16)
    drow = drow_ref[...]
    drow = drow + jnp.concatenate(dcum_rows + [jnp.zeros((heads, rows), F32)], 0)
    drow = jnp.concatenate(
        [jnp.zeros((decay_col, rows), F32), drow,
         jnp.zeros((LANES - norm_col, rows), F32)], 0
    )
    dcol = dcol + drow.T
    rate, bias = head_rows(hp_ref, heads, decay_col, beta_col)
    switch = jax.nn.sigmoid(gate_ref[...] + bias)
    dlog = mm_full((row_id <= col_id).astype(F32), dcol)
    slope = switch * (1.0 - switch)
    dgate = jnp.where(
        lane < decay_col,
        dcol * switch,
        jnp.where(lane < beta_col, -rate * dlog * slope, dcol * slope),
    )
    dgate = jnp.where(lane < norm_col, dgate, 0.0).astype(BF16)
    size = out_refs[0].shape[1]
    for shift in range(count):
        dest = lax.rem(place_ref[1] + shift, count)
        span = pl.ds(pl.multiple_of(dest * size, size), size)
        part = mm_nt(dproj[...], wr_ref[span, :]) + mm(dgate, small_ref[:, span])
        out_refs[shift][...] = part.astype(BF16)


def finish(place, head_param, arrays, others, arrived, levels, count):
    rows = arrays[0].shape[2]
    width, cols = arrays[-1].shape
    far = len(others)
    counts = tuple(len(group) for group in arrived)
    heads = arrays[0].shape[1]
    flat = [value for group in arrived for value in group]
    return local_call(
        functools.partial(finish_body, (heads, levels, far, count, counts)), "finish",
        [kept((rows, width // count), BF16)] * count,
        [place, head_param], [*arrays, *others, *flat], [pltpu.VMEM((rows, cols), BF16)],
    )


def swap(value, axis, mask):
    size = lax.axis_size(axis)
    return lax.ppermute(value, axis, [(at, at ^ mask) for at in range(size)])


def scatter_sum(parts, axis):
    count = lax.axis_size(axis)
    total = parts[0].astype(F32)
    for shift in range(1, count):
        got = lax.ppermute(parts[shift], axis, [(at, (at + shift) % count) for at in range(count)])
        total = total + got.astype(F32)
    return total.astype(BF16)


def on_device(tokens, qkv_weight, small_weight, head_param, norm_gain, out_weight, grad_out):
    rows, width = tokens.shape
    heads, key = qkv_weight.shape[2:]
    levels = small_weight.shape[2] - 2
    bits = (rows // BLOCK).bit_length() - 1
    size = lax.axis_size("ctx")
    far = size.bit_length() - 1
    count = lax.axis_size("head")
    place = jnp.stack([lax.axis_index("ctx"), lax.axis_index("head")]).astype(jnp.int32)
    flat_w = qkv_weight.reshape(width * 3 * heads, key)
    small = jnp.transpose(small_weight, (2, 1, 0))
    rates = head_param.T
    flat_out = out_weight.reshape(heads * key, width)
    gain = norm_gain.reshape(1, key)

    (wr, small_t, qkv, gate, pack, pack_t, trans, mixed_t, decay, base, lower, pair) = project(
        tokens, flat_w, small, rates, heads, levels
    )
    first = swap(pair, "ctx", 1)
    node = join(0, place, pair, first)
    near = [swap(node, "ctx", 2 * at) for at in range(1, size // 2)]
    (attn, attn_t, prod_t, scores, mix, mixed, local_out, hat, hat_t) = local_part(
        qkv, pack, pack_t, trans, mixed_t, decay, levels, bits
    )
    grad_normed = lax.dot_general(
        grad_out, flat_out, (((1,), (1,)), ((), ())), preferred_element_type=F32
    )
    (normed, dout, dhat, dfar), nodes, sends = cross(
        place, gain, pack, local_out, hat, hat_t, grad_normed, first, near, bits, far
    )
    others = [first, near[0], *nodes]
    got = [swap(value, "ctx", 1) for value in sends]
    arrived = [[got[0]]]
    sums = add_all(sends[1:], got[1:])
    for bit in range(1, far):
        half = 1 << (bit - 1)
        arrived.append([swap(sums[bit - 1], "ctx", 2 * at) for at in range(half, 2 * half)])
    layer_out = scatter_sum(spread_out(place, normed, flat_out, count), "head")
    dqkv, dgrown, dcol, drow = pull_local(
        [qkv, pack, pack_t, trans, attn, attn_t, prod_t, scores, mix, decay, base, lower, dout,
         dhat],
        levels, bits,
    )
    arrays = [qkv, gate, pack, trans, mixed, decay, base, lower, dqkv, dgrown, dcol, drow, dfar,
              small_t, wr]
    parts = finish(place, rates, arrays, others, arrived, levels, count)
    return layer_out, scatter_sum(parts, "head")


def solution(mesh):
    placed = (
        P("ctx", None),
        P(None, None, "head", None),
        P(None, "head", None),
        P("head", None),
        P(),
        P("head", None, None),
        P("ctx", None),
    )
    return jax.shard_map(
        on_device,
        mesh=mesh,
        in_specs=placed,
        out_specs=(P("ctx", "head"), P("ctx", "head")),
        check_vma=False,
    )
```

```python
import functools

import jax
import jax.numpy as jnp
from jax import lax
from jax.experimental import pallas as pl
from jax.experimental.pallas import tpu as pltpu
from jax.sharding import PartitionSpec as P

BLOCK = 64
LANES = 128
EPS = 1e-06
MIB = 1024 * 1024
F32 = jnp.float32
BF16 = jnp.bfloat16
WHOLE = pl.BlockSpec(memory_space=pltpu.VMEM)
SCALARS = pl.BlockSpec(memory_space=pltpu.SMEM)
HBM = pl.BlockSpec(memory_space=pltpu.HBM)


def contract(left, right, dim_left, dim_right):
    return lax.dot_general(
        left.astype(BF16),
        right.astype(BF16),
        (((dim_left,), (dim_right,)), ((), ())),
        preferred_element_type=F32,
    )


def mm(left, right):
    return contract(left, right, 1, 0)


def mm_nt(left, right):
    return contract(left, right, 1, 1)


def mm_tn(left, right):
    return contract(left, right, 0, 0)


def split(values):
    high = values.astype(BF16)
    return high, (values - high.astype(F32)).astype(BF16)


def mm_nt_fine(left, right):
    left_high, left_low = split(left)
    right_high, right_low = split(right)
    return mm_nt(left_high, right_high) + (mm_nt(left_low, right_high) + mm_nt(left_high, right_low))


def mm_full(left, right):
    return jnp.dot(left, right, precision=lax.Precision.HIGHEST, preferred_element_type=F32)


def pair_ids(count):
    row_id = lax.broadcasted_iota(jnp.int32, (count, count), 0)
    col_id = lax.broadcasted_iota(jnp.int32, (count, count), 1)
    return row_id, col_id


def row_sum(values):
    return jnp.sum(values, 1, keepdims=True)


def col_sum(values):
    return jnp.sum(values, 0, keepdims=True)


def lane_of(rows):
    return lax.broadcasted_iota(jnp.int32, (rows, LANES), 1)


def decay_of(pack, pack_t, col, inclusive):
    spread = pack[:, col : col + 1] - pack_t[col : col + 1, :]
    return jnp.where(inclusive, jnp.exp(jnp.minimum(spread, 0.0)), 0.0)


def kept(shape, dtype):
    return pltpu.VMEM(shape, dtype)


def pin(values, space):
    return [pltpu.with_memory_space_constraint(value, space) for value in values]


def local_call(body, name, limit, out_shape, scalars, arrays, scratch=(), remote=()):
    return pl.pallas_call(
        body,
        out_shape=tuple(out_shape),
        in_specs=[SCALARS] * len(scalars)
        + [WHOLE] * len(arrays)
        + [HBM] * len(remote),
        out_specs=(WHOLE,) * len(out_shape),
        scratch_shapes=list(scratch),
        compiler_params=pltpu.CompilerParams(vmem_limit_bytes=limit * MIB),
        name=name,
    )(*scalars, *pin(arrays, pltpu.VMEM), *pin(remote, pltpu.HBM))


def column(pack, at):
    return pack[:, at : at + 1]


def level_mix(pack, head, heads, bits, apart):
    block_bit = BLOCK.bit_length() - 1
    mixed = jnp.broadcast_to(column(pack, head), apart.shape)
    for level in range(1, bits + 1):
        here = (apart >> (block_bit + level - 1)) >= 1
        mixed = jnp.where(here, column(pack, level * heads + head), mixed)
    return mixed


def head_rows(hp_ref, heads, decay_col, beta_col):
    lane_row = lane_of(1)
    rate = jnp.zeros((1, LANES), F32)
    bias = jnp.zeros((1, LANES), F32)
    for head in range(heads):
        rate = jnp.where(lane_row == decay_col + head, hp_ref[0:1, head : head + 1], rate)
        bias = jnp.where(lane_row == beta_col + head, hp_ref[1:2, head : head + 1], bias)
    return rate, bias


def project_body(sizes, hp_hbm, tokens_hbm, w_hbm, small_hbm, *refs):
    heads, levels, chunks = sizes
    (wr_ref, small_ref, qkv_ref, gate_ref, pack_ref, pack_t_ref, trans_ref, mixed_t_ref,
     decay_ref, base_ref, lower_ref, rates_ref, pair_ref) = refs[:13]
    tokens, wide_in, wide_even, wide_odd, small_in, small_wide, acc, hp_ref, sems = refs[13:]
    rows, width = tokens.shape
    depth = width // chunks
    cols = 3 * heads
    fetch_tokens = pltpu.make_async_copy(tokens_hbm, tokens, sems.at[chunks])
    fetch_small = pltpu.make_async_copy(small_hbm, small_in, sems.at[chunks + 1])
    fetch_rates = pltpu.make_async_copy(hp_hbm, hp_ref, sems.at[chunks + 2])
    fetches = []
    for chunk in range(chunks):
        span = pl.ds(chunk * depth * cols, depth * cols)
        fetches.append(
            pltpu.make_async_copy(w_hbm.at[span, :], wide_in.at[span, :], sems.at[chunk])
        )
    fetches[0].start()
    fetch_tokens.start()
    fetch_small.start()
    fetch_rates.start()
    for fetch in fetches[1:]:
        fetch.start()
    for chunk in range(chunks):
        fetches[chunk].wait()
        at = chunk * depth
        wide = wide_odd if chunk % 2 else wide_even
        wide[...] = wide_in[at * cols : (at + depth) * cols, :].astype(F32)
        for col in range(cols):
            part = wide[pl.ds(col, depth, stride=cols), :]
            wr_ref[at : at + depth, col * LANES : (col + 1) * LANES] = part.astype(BF16)
        if chunk == 0:
            fetch_tokens.wait()
        own = jnp.dot(
            tokens[:, at : at + depth], wr_ref[at : at + depth, :], preferred_element_type=F32
        )
        if chunk == 0:
            acc[...] = own
        else:
            acc[...] += own
    fetch_small.wait()
    small_rows = small_in.shape[0] * heads
    for level in range(small_in.shape[0]):
        small_wide[level * heads : (level + 1) * heads, :] = small_in[level].astype(F32)
    small_wide[small_rows:, :] = jnp.zeros((LANES - small_rows, width), F32)
    small_ref[...] = small_wide[...].astype(BF16)
    gate = mm_nt(tokens[...], small_ref[...])
    decay_col = levels * heads
    beta_col = decay_col + heads
    norm_col = beta_col + heads
    gate_ref[...] = gate
    lane = lane_of(rows)
    fetch_rates.wait()
    rate, bias = head_rows(hp_ref, heads, decay_col, beta_col)
    rates_ref[0:1, :] = rate
    rates_ref[1:2, :] = bias
    switch = jax.nn.sigmoid(gate + bias)
    lam = jnp.maximum(gate, 0.0) + jnp.log1p(jnp.exp(-jnp.abs(gate)))
    row_id, col_id = pair_ids(rows)
    inclusive = row_id >= col_id
    strict = row_id > col_id
    apart = row_id ^ col_id
    cum = mm_full(inclusive.astype(F32), -rate * switch)
    pack = jnp.where(lane < decay_col, lam, jnp.where(lane < beta_col, cum, switch))
    k_all, v_all = [], []
    for head in range(heads):
        for part in range(2):
            col = (part * heads + head) * LANES
            raw = acc[:, col : col + LANES]
            scale = lax.rsqrt(row_sum(raw * raw) + EPS)
            unit = raw * scale
            qkv_ref[part, head] = unit
            pack = jnp.where(lane == norm_col + part * heads + head, scale, pack)
            if part == 1:
                k_all.append(unit)
        col = (2 * heads + head) * LANES
        v_all.append(acc[:, col : col + LANES])
        qkv_ref[2, head] = v_all[head]
    pack_ref[...] = pack
    pack_t = pack.T
    pack_t_ref[...] = pack_t
    eye = (row_id == col_id).astype(F32)
    lower_all, trans_all = [], []
    for head in range(heads):
        decay = decay_of(pack, pack_t, decay_col + head, inclusive)
        decay_ref[head] = decay
        gram = mm_nt(k_all[head], k_all[head])
        base = jnp.where(strict, decay * gram, 0.0)
        base_ref[head] = base
        lower = column(pack, beta_col + head) * base
        lower_ref[head] = lower
        lower_all.append(lower)
        trans_all.append((eye - jnp.where(apart == 1, lower, 0.0)).astype(BF16))
    for bit in range(1, rows.bit_length() - 1):
        here = (apart >> bit) == 1
        edge = [jnp.where(here, lower, 0.0) for lower in lower_all]
        half = [mm(trans, part) for trans, part in zip(trans_all, edge)]
        trans_all = [
            trans - mm(part, trans).astype(BF16) for trans, part in zip(trans_all, half)
        ]
    rest_all = []
    for trans, lower in zip(trans_all, lower_all):
        high, low = split(lower)
        rest_all.append(eye - trans.astype(F32) - mm(high, trans) - mm(low, trans))
    trans_all = [
        (trans.astype(F32) + mm(trans, rest)).astype(BF16)
        for trans, rest in zip(trans_all, rest_all)
    ]
    mixed_all = []
    for head in range(heads):
        trans_ref[head] = trans_all[head]
        cum_row = pack_t[decay_col + head : decay_col + head + 1, :]
        tail_t = k_all[head].T * jnp.exp(cum_row[:, rows - 1 :] - cum_row)
        mixed_all.append(mm(tail_t, trans_all[head]))
    eye_key = eye[:LANES, :LANES]
    for head in range(heads):
        mixed_t_ref[head] = mixed_all[head]
        cum_col = column(pack, decay_col + head)
        beta = column(pack, beta_col + head)
        grown = (beta * jnp.exp(cum_col)) * k_all[head]
        both = jnp.concatenate([-grown, beta * v_all[head]], 1)
        pair = mm(mixed_all[head], both)
        last = jnp.exp(cum_col[rows - 1 : rows, :])
        pair_ref[head, :, :LANES] = (last * eye_key + pair[:, :LANES]).astype(BF16)
        pair_ref[head, :, LANES:] = pair[:, LANES:].astype(BF16)


def project(tokens, flat_w, small, head_param, heads, levels):
    rows, width = tokens.shape
    chunks = 8
    cols = 3 * heads
    key = flat_w.shape[1]
    square = (heads, rows, rows)
    out_shape = (
        kept((width, cols * key), BF16),
        kept((LANES, width), BF16),
        kept((3, heads, rows, key), F32),
        kept((rows, LANES), F32),
        kept((rows, LANES), F32),
        kept((LANES, rows), F32),
        kept(square, BF16),
        kept((heads, key, rows), F32),
        kept(square, F32),
        kept(square, F32),
        kept(square, F32),
        kept((2, LANES), F32),
        kept((heads, key, 2 * key), BF16),
    )
    scratch = [
        pltpu.VMEM(tokens.shape, BF16),
        pltpu.VMEM(flat_w.shape, BF16),
        pltpu.VMEM((width // chunks * cols, key), F32),
        pltpu.VMEM((width // chunks * cols, key), F32),
        pltpu.VMEM(small.shape, BF16),
        pltpu.VMEM((LANES, width), F32),
        pltpu.VMEM((rows, cols * key), F32),
        pltpu.VMEM(head_param.shape, F32),
        pltpu.SemaphoreType.DMA((chunks + 3,)),
    ]
    return local_call(
        functools.partial(project_body, (heads, levels, chunks)), "project", 22, out_shape,
        [], [], scratch, [head_param, tokens, flat_w, small],
    )


def local_body(sizes, qkv_ref, pack_ref, pack_t_ref, trans_ref, mixed_t_ref, decay_ref, *outs):
    heads, levels, bits = sizes
    (attn_ref, attn_t_ref, prod_t_ref, scores_ref, mix_ref, mixed_ref, local_ref, hat_ref,
     hat_t_ref) = outs
    rows = pack_ref.shape[0]
    decay_col = levels * heads
    beta_col = decay_col + heads
    pack = pack_ref[...]
    pack_t = pack_t_ref[...]
    row_id, col_id = pair_ids(rows)
    apart = row_id ^ col_id
    for head in range(heads):
        scores = mm_nt_fine(qkv_ref[0, head], qkv_ref[1, head]) * decay_ref[head]
        scores_ref[head] = scores.astype(BF16)
        mix_ref[head] = level_mix(pack, head, heads, bits, apart)
        mixed_ref[head] = mixed_t_ref[head].T.astype(BF16)
    for head in range(heads):
        attn = mm(scores_ref[head], trans_ref[head])
        attn_ref[head] = attn.astype(BF16)
        attn_t_ref[head] = attn.T.astype(BF16)
        attn = attn * pack_t[beta_col + head : beta_col + head + 1, :]
        prod = attn * mix_ref[head]
        prod_t_ref[head] = prod.T.astype(BF16)
        growth = jnp.exp(column(pack, decay_col + head))
        local_ref[head] = mm(prod, qkv_ref[2, head])
        hat = growth * qkv_ref[0, head] - mm(attn, growth * qkv_ref[1, head])
        hat_ref[head] = hat.astype(BF16)
        hat_t_ref[head] = hat.T.astype(BF16)


def local_part(qkv, pack, pack_t, trans, mixed_t, decay, levels, bits):
    heads, rows, key = qkv.shape[1:]
    square = (heads, rows, rows)
    out_shape = (
        kept(square, BF16),
        kept(square, BF16),
        kept(square, BF16),
        kept(square, BF16),
        kept(square, F32),
        kept((heads, rows, key), BF16),
        kept((heads, rows, key), F32),
        kept((heads, rows, key), BF16),
        kept((heads, key, rows), BF16),
    )
    return local_call(
        functools.partial(local_body, (heads, levels, bits)), "local_part", 10, out_shape,
        [], [qkv, pack, pack_t, trans, mixed_t, decay],
    )


def join_pair(upper, own, other):
    key = own.shape[0]
    low = jnp.where(upper, other, own)
    high = jnp.where(upper, own, other)
    moved = mm(high[:, :key], low)
    late = jnp.concatenate([jnp.zeros((key, key), F32), high[:, key:].astype(F32)], 1)
    return (moved + late).astype(BF16)


def join_body(place_ref, own_ref, other_ref, out_ref):
    half = out_ref.shape[0]
    upper = (place_ref[0] & 1) == 1
    for slot in range(half):
        head = (place_ref[0] & 1) * half + slot
        out_ref[slot] = join_pair(upper, own_ref[head], other_ref[head])


def join_half(place, own, other):
    half = (own.shape[0] // 2,) + own.shape[1:]
    return local_call(join_body, "join_half", 6, [kept(half, BF16)], [place], [own, other])[0]


def gather_node(head, bit, first, near, uppers):
    if bit == 0:
        mine, theirs = near[first]
        half = mine.shape[0]
        here = uppers[0] if head >= half else jnp.logical_not(uppers[0])
        return jnp.where(here, mine[head % half], theirs[head % half])
    own = gather_node(head, bit - 1, first, near, uppers)
    other = gather_node(head, bit - 1, first ^ (1 << (bit - 1)), near, uppers)
    return join_pair(uppers[bit], own, other)


def reach_body(
    sizes, place_ref, gain_ref, pack_ref, local_ref, hat_ref, grad_ref, weight_ref, *refs
):
    heads, bits, far, count, near_count = sizes
    first_ref = refs[0]
    near = [None] + [(refs[1 + at], refs[1 + near_count + at]) for at in range(near_count)]
    refs = refs[2 * near_count + 1 :]
    out_refs = refs[:count]
    dout_ref, found_ref, prefix_ref, dfar_ref = refs[count : count + 4]
    nodes = refs[count + 4 : -1]
    normed_ref = refs[-1]
    rows = pack_ref.shape[0]
    key = hat_ref.shape[2]
    pack = pack_ref[...]
    gain = gain_ref[...]
    lane = lane_of(rows)
    all_heads = range(heads)
    uppers = [((place_ref[0] >> bit) & 1) == 1 for bit in range(far)]
    others = []
    for bit in range(far):
        if bit == 0:
            others.append([first_ref[head] for head in all_heads])
        else:
            others.append(
                [gather_node(head, bit - 1, 1 << (bit - 1), near, uppers) for head in all_heads]
            )
            for head in all_heads:
                nodes[bit - 1][head] = others[bit][head]
    eye_key = jnp.where(pair_ids(key)[0] == pair_ids(key)[1], 1.0, 0.0).astype(BF16)
    prefix = [eye_key for head in all_heads]
    found = []
    for bit in range(far):
        for head in all_heads:
            prefix_ref[head, bit] = prefix[head]
        moved = [mm(prefix[head], others[bit][head]) for head in all_heads]
        found.append([jnp.where(uppers[bit], m[:, key:], 0.0).astype(BF16) for m in moved])
        prefix = [
            jnp.where(uppers[bit], moved[head][:, :key].astype(BF16), prefix[head])
            for head in all_heads
        ]
    found = [jnp.concatenate([found[bit][head] for bit in range(far)], 1) for head in all_heads]
    reached = [mm(hat_ref[head], found[head]) for head in all_heads]
    dfar = jnp.zeros((rows, LANES), F32)
    for head in all_heads:
        found_ref[head] = found[head]
        summed = local_ref[head]
        parts = []
        for bit in range(far):
            parts.append(reached[head][:, bit * key : (bit + 1) * key])
            summed = summed + column(pack, (bits + 1 + bit) * heads + head) * parts[bit]
        scale = lax.rsqrt(jnp.mean(summed * summed, -1, keepdims=True) + EPS)
        unit = summed * scale
        normed_ref[:, head * key : (head + 1) * key] = (unit * gain).astype(BF16)
        pulled = grad_ref[:, head * key : (head + 1) * key] * gain
        dout = scale * (pulled - unit * jnp.mean(pulled * unit, -1, keepdims=True))
        dout_ref[head] = dout
        for bit in range(far):
            col = (bits + 1 + bit) * heads + head
            dfar = jnp.where(lane == col, row_sum(dout * parts[bit]), dfar)
    dfar_ref[...] = dfar
    size = out_refs[0].shape[1]
    for shift in range(count):
        dest = lax.rem(place_ref[1] + shift, count)
        cols = pl.ds(pl.multiple_of(dest * size, size), size)
        out_refs[shift][...] = jnp.dot(
            normed_ref[...], weight_ref[:, cols], preferred_element_type=F32
        ).astype(BF16)


def reach(place, arrays, first, near, bits, far, count):
    gain, pack, local_out, hat, grad_normed, weight = arrays
    heads, rows, key = hat.shape
    nodes = tuple(kept(first.shape, BF16) for bit in range(1, far))
    out_shape = (kept((rows, weight.shape[1] // count), BF16),) * count + (
        kept((heads, rows, key), F32),
        kept((heads, key, far * key), BF16),
        kept((heads, far, key, key), BF16),
        kept((rows, LANES), F32),
    ) + nodes
    mine, theirs = near
    got = local_call(
        functools.partial(reach_body, (heads, bits, far, count, len(mine))), "reach", 10, out_shape,
        [place], [*arrays, first, *mine, *theirs], [pltpu.VMEM((rows, heads * key), BF16)],
    )
    parts, got = got[:count], got[count:]
    return parts, got[:4], got[4:]


def return_body(sizes, place_ref, pack_ref, hat_t_ref, dout_ref, found_ref, prefix_ref, *refs):
    heads, bits, far = sizes
    others = refs[:far]
    dhat_ref = refs[far]
    sends = refs[far + 1 :]
    key = hat_t_ref.shape[1]
    pack = pack_ref[...]
    all_heads = range(heads)
    uppers = [((place_ref[0] >> bit) & 1) == 1 for bit in range(far)]
    spread = []
    for head in all_heads:
        parts = []
        for bit in range(far):
            weight = column(pack, (bits + 1 + bit) * heads + head)
            parts.append((weight * dout_ref[head]).astype(BF16))
        spread.append(jnp.concatenate(parts, 1))
    dfound = [mm(hat_t_ref[head], spread[head]) for head in all_heads]
    for head in all_heads:
        dhat_ref[head] = mm_nt(spread[head], found_ref[head])
    dprefix = [jnp.zeros((key, key), F32) for head in all_heads]
    for bit in reversed(range(far)):
        dfree = [
            jnp.where(uppers[bit], d[:, bit * key : (bit + 1) * key], 0.0) for d in dfound
        ]
        both = [
            jnp.concatenate([jnp.where(uppers[bit], dprefix[head], 0.0), dfree[head]], 1)
            for head in all_heads
        ]
        for head in all_heads:
            sent = dfree[head] if bit == far - 1 else both[head]
            sends[bit][head] = mm_tn(prefix_ref[head, bit], sent).astype(BF16)
        if bit > 0:
            moved = [mm_nt(both[head], others[bit][head]) for head in all_heads]
            dprefix = [
                jnp.where(uppers[bit], moved[head], dprefix[head]) for head in all_heads
            ]


def return_states(place, pack, hat_t, dout, found, prefix, others, bits):
    heads, rows, key = dout.shape
    far = len(others)
    sends = tuple(
        kept((heads, key, (1 if bit == far - 1 else 2) * key), BF16) for bit in range(far)
    )
    got = local_call(
        functools.partial(return_body, (heads, bits, far)), "return_states", 8,
        (kept(dout.shape, F32),) + sends, [place], [pack, hat_t, dout, found, prefix, *others],
    )
    return got[0], got[1:]


def add_body(*refs):
    count = len(refs) // 3
    for at in range(count):
        left, right = refs[at][...].astype(F32), refs[count + at][...].astype(F32)
        refs[2 * count + at][...] = (left + right).astype(BF16)


def add_all(left, right):
    out_shape = [kept(value.shape, BF16) for value in left]
    return local_call(add_body, "add_all", 6, out_shape, [], [*left, *right])


def lower_pull(dlower, base, lower, beta, decay, strict, k_in):
    dlower = jnp.where(strict, dlower, 0.0)
    dbeta = row_sum(dlower * base)
    dgram = dlower * (beta * decay)
    dkey = mm(dgram, k_in) + mm_tn(dgram, k_in)
    return dbeta, beta * dbeta, col_sum(dlower * lower), dkey


def pull_body(sizes, *refs):
    heads, levels, bits = sizes
    (qkv_ref, pack_ref, pack_t_ref, trans_ref, attn_ref, attn_t_ref, prod_t_ref, scores_ref,
     mix_ref, decay_ref, base_ref, lower_ref, dout_ref, dhat_ref) = refs[:14]
    dqkv_ref, dgrown_ref, dcol_ref, drow_ref = refs[14:]
    rows = pack_ref.shape[0]
    decay_col = levels * heads
    beta_col = decay_col + heads
    block_bit = BLOCK.bit_length() - 1
    pack = pack_ref[...]
    pack_t = pack_t_ref[...]
    row_id, col_id = pair_ids(rows)
    strict = row_id > col_id
    apart = row_id ^ col_id
    lane = lane_of(rows)
    all_heads = range(heads)
    dcol = jnp.zeros((rows, LANES), F32)
    dbeta_rows, dcum_rows, dattn_all = [], [], []
    for head in all_heads:
        high, low = split(dout_ref[head])
        v_in = qkv_ref[2, head].astype(BF16)
        dprod = mm_nt(high, v_in) + mm_nt(low, v_in)
        dqkv_ref[2, head] = mm(prod_t_ref[head], high)
        beta_row = pack_t[beta_col + head : beta_col + head + 1, :]
        growth = jnp.exp(column(pack, decay_col + head))
        attn0 = attn_ref[head].astype(F32)
        touched = dprod * (attn0 * beta_row)
        for level in range(bits + 1):
            if level == 0:
                here = (apart >> block_bit) == 0
            else:
                here = (apart >> (block_bit + level - 1)) == 1
            dcol = jnp.where(
                lane == level * heads + head, row_sum(jnp.where(here, touched, 0.0)), dcol
            )
        dattn = dprod * mix_ref[head] - mm_nt(dhat_ref[head], growth * qkv_ref[1, head])
        dbeta_rows.append(col_sum(dattn * attn0))
        dattn_all.append((dattn * beta_row).astype(BF16))
    dscore_all = [mm_nt(dattn_all[head], trans_ref[head]) for head in all_heads]
    moved_all = []
    for head in all_heads:
        both = jnp.concatenate(
            [dscore_all[head].astype(BF16), dhat_ref[head].astype(BF16)], 1
        )
        moved_all.append(mm(attn_t_ref[head], both))
    for head in all_heads:
        q_in, k_in = qkv_ref[0, head], qkv_ref[1, head]
        beta = column(pack, beta_col + head)
        growth = jnp.exp(column(pack, decay_col + head))
        dscore = dscore_all[head]
        dprobs = dscore * decay_ref[head]
        shift = dscore * scores_ref[head].astype(F32)
        dgrown_ref[head] = -beta * moved_all[head][:, rows:]
        dbeta, dcum_col, dcum_row, dk_lower = lower_pull(
            -moved_all[head][:, :rows], base_ref[head], lower_ref[head], beta, decay_ref[head],
            strict, k_in
        )
        dhat = dhat_ref[head]
        dqkv_ref[0, head] = growth * dhat + mm(dprobs, k_in)
        dqkv_ref[1, head] = mm_tn(dprobs, q_in) + dk_lower
        dcum_col = dcum_col + row_sum(shift) + growth * row_sum(q_in * dhat)
        dcum_rows.append(-dcum_row - col_sum(shift))
        dcol = jnp.where(lane == beta_col + head, dbeta, dcol)
        dcol = jnp.where(lane == decay_col + head, dcum_col, dcol)
    dcol_ref[...] = dcol
    drow_ref[...] = jnp.concatenate(dcum_rows + dbeta_rows, 0)


def pull_local(arrays, levels, bits):
    heads, rows, key = arrays[0].shape[1:]
    out_shape = (
        kept((3, heads, rows, key), F32),
        kept((heads, rows, key), F32),
        kept((rows, LANES), F32),
        kept((2 * heads, rows), F32),
    )
    return local_call(
        functools.partial(pull_body, (heads, levels, bits)), "pull_local", 12, out_shape, [], arrays
    )


def finish_body(sizes, place_ref, *refs):
    heads, levels, far, count, arrived_counts = sizes
    (qkv_ref, gate_ref, pack_ref, trans_ref, mixed_ref, decay_ref, base_ref, lower_ref,
     dqkv_ref, dgrown_ref, dcol_ref, drow_ref, dfar_ref, rates_ref, small_ref, wr_ref) = refs[:16]
    others = refs[16 : 16 + far]
    refs = refs[16 + far :]
    arrived = []
    for found in arrived_counts:
        arrived.append(refs[:found])
        refs = refs[found:]
    out_refs = refs[:count]
    (dproj,) = refs[count:]
    rows = pack_ref.shape[0]
    key = qkv_ref.shape[3]
    decay_col = levels * heads
    beta_col = decay_col + heads
    norm_col = beta_col + heads
    place = place_ref[0]
    all_heads = range(heads)
    uppers = [((place >> bit) & 1) == 1 for bit in range(far)]
    pack = pack_ref[...]
    row_id, col_id = pair_ids(rows)
    strict = row_id > col_id
    lane = lane_of(rows)
    last_row = lax.broadcasted_iota(jnp.int32, (rows, 1), 0) == rows - 1
    eye_key = (pair_ids(key)[0] == pair_ids(key)[1]).astype(F32)
    dpair = [jnp.zeros((key, 2 * key), F32) for head in all_heads]
    for bit in reversed(range(far)):
        for head in all_heads:
            got = arrived[bit][0][head].astype(F32)
            for more in arrived[bit][1:]:
                got = got + more[head].astype(F32)
            other = others[bit][head]
            if bit == far - 1:
                got = jnp.concatenate([jnp.zeros((key, key), F32), got], 1)
                dpair[head] = jnp.where(uppers[bit], 0.0, got)
            else:
                as_low = mm_tn(other[:, :key], dpair[head]) + got
                as_high = mm_nt(dpair[head], other)
                as_high = jnp.concatenate([as_high, dpair[head][:, key:]], 1)
                dpair[head] = jnp.where(uppers[bit], as_high, as_low)
    moved_all, dmixed_all = [], []
    for head in all_heads:
        beta = column(pack, beta_col + head)
        growth = jnp.exp(column(pack, decay_col + head))
        both = jnp.concatenate([-growth * qkv_ref[1, head], qkv_ref[2, head]], 1)
        dmixed_all.append(mm_nt(both, dpair[head]))
        moved_all.append(mm(beta * mixed_ref[head].astype(F32), dpair[head]))
    dtail_all = [
        mm(trans_ref[head], column(pack, beta_col + head) * dmixed_all[head])
        for head in all_heads
    ]
    dlower_all = [-mm_nt(mixed_ref[head], dtail_all[head]) for head in all_heads]
    dcol = jnp.where(lane < decay_col, dcol_ref[...] + dfar_ref[...], dcol_ref[...])
    dcum_rows = []
    for head in all_heads:
        q_in, k_in = qkv_ref[0, head], qkv_ref[1, head]
        beta = column(pack, beta_col + head)
        cum_col = column(pack, decay_col + head)
        growth = jnp.exp(cum_col)
        last = cum_col[rows - 1 : rows, :]
        tail = jnp.exp(last - cum_col)
        dgrown = dgrown_ref[head] - moved_all[head][:, :key]
        dv = dqkv_ref[2, head] + moved_all[head][:, key:]
        dbeta_more = row_sum(mixed_ref[head].astype(F32) * dmixed_all[head])
        dtail = dtail_all[head]
        dbeta, dcum_col, dcum_row, dk_lower = lower_pull(
            dlower_all[head], base_ref[head], lower_ref[head], beta, decay_ref[head], strict, k_in
        )
        dcum_rows.append(-dcum_row)
        tail_pull = tail * row_sum(k_in * dtail)
        trace = col_sum(row_sum(dpair[head][:, :key] * eye_key))
        at_last = col_sum(tail_pull) + jnp.exp(last) * trace
        dcum_col = dcum_col + growth * row_sum(k_in * dgrown) - tail_pull
        dcum_col = dcum_col + jnp.where(last_row, at_last, 0.0)
        dk = dqkv_ref[1, head] + dk_lower + growth * dgrown + tail * dtail
        dq = dqkv_ref[0, head]
        dcol = dcol + jnp.where(lane == beta_col + head, dbeta + dbeta_more, 0.0)
        dcol = dcol + jnp.where(lane == decay_col + head, dcum_col, 0.0)
        for part, unit, dunit in ((0, q_in, dq), (1, k_in, dk)):
            scale = column(pack, norm_col + part * heads + head)
            back = scale * (dunit - unit * row_sum(unit * dunit))
            col = (part * heads + head) * key
            dproj[:, col : col + key] = back.astype(BF16)
        col = (2 * heads + head) * key
        dproj[:, col : col + key] = dv.astype(BF16)
    drow = drow_ref[...]
    drow = drow + jnp.concatenate(dcum_rows + [jnp.zeros((heads, rows), F32)], 0)
    drow = jnp.concatenate(
        [jnp.zeros((decay_col, rows), F32), drow,
         jnp.zeros((LANES - norm_col, rows), F32)], 0
    )
    dcol = dcol + drow.T
    rate, bias = rates_ref[0:1, :], rates_ref[1:2, :]
    switch = jax.nn.sigmoid(gate_ref[...] + bias)
    dlog = mm_full((row_id <= col_id).astype(F32), dcol)
    slope = switch * (1.0 - switch)
    dgate = jnp.where(
        lane < decay_col,
        dcol * switch,
        jnp.where(lane < beta_col, -rate * dlog * slope, dcol * slope),
    )
    dgate = jnp.where(lane < norm_col, dgate, 0.0).astype(BF16)
    size = out_refs[0].shape[1]
    for shift in range(count):
        dest = lax.rem(place_ref[1] + shift, count)
        span = pl.ds(pl.multiple_of(dest * size, size), size)
        part = mm_nt(dproj[...], wr_ref[span, :]) + mm(dgate, small_ref[:, span])
        out_refs[shift][...] = part.astype(BF16)


def finish(place, arrays, others, arrived, levels, count):
    rows = arrays[0].shape[2]
    width, cols = arrays[-1].shape
    far = len(others)
    counts = tuple(len(group) for group in arrived)
    heads = arrays[0].shape[1]
    flat = [value for group in arrived for value in group]
    return local_call(
        functools.partial(finish_body, (heads, levels, far, count, counts)), "finish", 12,
        [kept((rows, width // count), BF16)] * count,
        [place], [*arrays, *others, *flat], [pltpu.VMEM((rows, cols), BF16)],
    )


def swap(value, axis, mask):
    size = lax.axis_size(axis)
    return lax.ppermute(value, axis, [(at, at ^ mask) for at in range(size)])


def scatter_sum(parts, axis):
    count = lax.axis_size(axis)
    total = parts[0].astype(F32)
    for shift in range(1, count):
        got = lax.ppermute(parts[shift], axis, [(at, (at + shift) % count) for at in range(count)])
        total = total + got.astype(F32)
    return total.astype(BF16)


def on_device(tokens, qkv_weight, small_weight, head_param, norm_gain, out_weight, grad_out):
    rows, width = tokens.shape
    heads, key = qkv_weight.shape[2:]
    levels = small_weight.shape[2] - 2
    bits = (rows // BLOCK).bit_length() - 1
    size = lax.axis_size("ctx")
    far = size.bit_length() - 1
    count = lax.axis_size("head")
    place = jnp.stack([lax.axis_index("ctx"), lax.axis_index("head")]).astype(jnp.int32)
    flat_w = qkv_weight.reshape(width * 3 * heads, key)
    small = jnp.transpose(small_weight, (2, 1, 0))
    rates = head_param.T
    flat_out = out_weight.reshape(heads * key, width)
    gain = norm_gain.reshape(1, key)

    (wr, small_t, qkv, gate, pack, pack_t, trans, mixed_t, decay, base, lower, rates_row,
     pair) = project(
        tokens, flat_w, small, rates, heads, levels
    )
    first = swap(pair, "ctx", 1)
    node = join_half(place, pair, first)
    mine = [swap(node, "ctx", 2 * at) for at in range(1, size // 2)]
    (attn, attn_t, prod_t, scores, mix, mixed, local_out, hat, hat_t) = local_part(
        qkv, pack, pack_t, trans, mixed_t, decay, levels, bits
    )
    grad_normed = lax.dot_general(
        grad_out, flat_out, (((1,), (1,)), ((), ())), preferred_element_type=F32
    )
    mine, local_out, grad_normed = lax.optimization_barrier((mine, local_out, grad_normed))
    theirs = [swap(value, "ctx", 1) for value in mine]
    out_parts, (dout, found, prefix, dfar), nodes = reach(
        place, [gain, pack, local_out, hat, grad_normed, flat_out], first, (mine, theirs),
        bits, far, count
    )
    layer_out = scatter_sum(out_parts, "head")
    others = [first, *nodes]
    dhat, sends = return_states(place, pack, hat_t, dout, found, prefix, others, bits)
    got = [swap(value, "ctx", 1) for value in sends]
    arrived = [[got[0]]]
    sums = add_all(sends[1:], got[1:])
    for bit in range(1, far):
        half = 1 << (bit - 1)
        arrived.append([swap(sums[bit - 1], "ctx", 2 * at) for at in range(half, 2 * half)])
    dqkv, dgrown, dcol, drow = pull_local(
        [qkv, pack, pack_t, trans, attn, attn_t, prod_t, scores, mix, decay, base, lower, dout,
         dhat],
        levels, bits,
    )
    arrays = [qkv, gate, pack, trans, mixed, decay, base, lower, dqkv, dgrown, dcol, drow, dfar,
              rates_row, small_t, wr]
    parts = finish(place, arrays, others, arrived, levels, count)
    return layer_out, scatter_sum(parts, "head")


def solution(mesh):
    placed = (
        P("ctx", None),
        P(None, None, "head", None),
        P(None, "head", None),
        P("head", None),
        P(),
        P("head", None, None),
        P("ctx", None),
    )
    return jax.shard_map(
        on_device,
        mesh=mesh,
        in_specs=placed,
        out_specs=(P("ctx", "head"), P("ctx", "head")),
        check_vma=False,
    )
```

```python
import functools

import jax
import jax.numpy as jnp
from jax import lax
from jax.experimental import pallas as pl
from jax.experimental.pallas import tpu as pltpu
from jax.sharding import PartitionSpec as P

BLOCK = 64
LANES = 128
EPS = 1e-06
MIB = 1024 * 1024
F32 = jnp.float32
BF16 = jnp.bfloat16
WHOLE = pl.BlockSpec(memory_space=pltpu.VMEM)
SCALARS = pl.BlockSpec(memory_space=pltpu.SMEM)
HBM = pl.BlockSpec(memory_space=pltpu.HBM)


def contract(left, right, dim_left, dim_right):
    return lax.dot_general(
        left.astype(BF16),
        right.astype(BF16),
        (((dim_left,), (dim_right,)), ((), ())),
        preferred_element_type=F32,
    )


def mm(left, right):
    return contract(left, right, 1, 0)


def mm_nt(left, right):
    return contract(left, right, 1, 1)


def mm_tn(left, right):
    return contract(left, right, 0, 0)


def split(values):
    high = values.astype(BF16)
    return high, (values - high.astype(F32)).astype(BF16)


def mm_nt_fine(left, right):
    left_high, left_low = split(left)
    right_high, right_low = split(right)
    return mm_nt(left_high, right_high) + (mm_nt(left_low, right_high) + mm_nt(left_high, right_low))


def mm_full(left, right):
    return jnp.dot(left, right, precision=lax.Precision.HIGHEST, preferred_element_type=F32)


def pair_ids(count):
    row_id = lax.broadcasted_iota(jnp.int32, (count, count), 0)
    col_id = lax.broadcasted_iota(jnp.int32, (count, count), 1)
    return row_id, col_id


def row_sum(values):
    return jnp.sum(values, 1, keepdims=True)


def col_sum(values):
    return jnp.sum(values, 0, keepdims=True)


def lane_of(rows):
    return lax.broadcasted_iota(jnp.int32, (rows, LANES), 1)


def decay_of(pack, pack_t, col, inclusive):
    spread = pack[:, col : col + 1] - pack_t[col : col + 1, :]
    return jnp.where(inclusive, jnp.exp(jnp.minimum(spread, 0.0)), 0.0)


def kept(shape, dtype):
    return pltpu.VMEM(shape, dtype)


def pin(values, space):
    return [pltpu.with_memory_space_constraint(value, space) for value in values]


def local_call(body, name, limit, out_shape, scalars, arrays, scratch=(), remote=()):
    return pl.pallas_call(
        body,
        out_shape=tuple(out_shape),
        in_specs=[SCALARS] * len(scalars)
        + [WHOLE] * len(arrays)
        + [HBM] * len(remote),
        out_specs=(WHOLE,) * len(out_shape),
        scratch_shapes=list(scratch),
        compiler_params=pltpu.CompilerParams(vmem_limit_bytes=limit * MIB),
        name=name,
    )(*scalars, *pin(arrays, pltpu.VMEM), *pin(remote, pltpu.HBM))


def column(pack, at):
    return pack[:, at : at + 1]


def level_mix(pack, head, heads, bits, apart):
    block_bit = BLOCK.bit_length() - 1
    mixed = jnp.broadcast_to(column(pack, head), apart.shape)
    for level in range(1, bits + 1):
        here = (apart >> (block_bit + level - 1)) >= 1
        mixed = jnp.where(here, column(pack, level * heads + head), mixed)
    return mixed


def head_rows(hp_ref, heads, decay_col, beta_col):
    lane_row = lane_of(1)
    rate = jnp.zeros((1, LANES), F32)
    bias = jnp.zeros((1, LANES), F32)
    for head in range(heads):
        rate = jnp.where(lane_row == decay_col + head, hp_ref[0:1, head : head + 1], rate)
        bias = jnp.where(lane_row == beta_col + head, hp_ref[1:2, head : head + 1], bias)
    return rate, bias


def project_body(sizes, place_ref, hp_hbm, tokens_hbm, w_hbm, small_hbm, *refs):
    heads, levels, chunks = sizes
    (wr_ref, small_ref, qkv_ref, gate_ref, pack_ref, pack_t_ref, trans_ref, mixed_t_ref,
     decay_ref, base_ref, lower_ref, rates_ref, pair_ref) = refs[:13]
    tokens, wide_in, wide_even, wide_odd, small_in, small_wide, acc, hp_ref, sems = refs[13:]
    rows, width = tokens.shape
    depth = width // chunks
    cols = 3 * heads
    fetch_tokens = pltpu.make_async_copy(tokens_hbm, tokens, sems.at[chunks])
    fetch_small = pltpu.make_async_copy(small_hbm, small_in, sems.at[chunks + 1])
    fetch_rates = pltpu.make_async_copy(hp_hbm, hp_ref, sems.at[chunks + 2])
    fetches = []
    for chunk in range(chunks):
        span = pl.ds(chunk * depth * cols, depth * cols)
        fetches.append(
            pltpu.make_async_copy(w_hbm.at[span, :], wide_in.at[span, :], sems.at[chunk])
        )
    fetches[0].start()
    fetch_tokens.start()
    fetch_small.start()
    fetch_rates.start()
    for fetch in fetches[1:]:
        fetch.start()
    for chunk in range(chunks):
        fetches[chunk].wait()
        at = chunk * depth
        wide = wide_odd if chunk % 2 else wide_even
        wide[...] = wide_in[at * cols : (at + depth) * cols, :].astype(F32)
        for col in range(cols):
            part = wide[pl.ds(col, depth, stride=cols), :]
            wr_ref[at : at + depth, col * LANES : (col + 1) * LANES] = part.astype(BF16)
        if chunk == 0:
            fetch_tokens.wait()
        own = jnp.dot(
            tokens[:, at : at + depth], wr_ref[at : at + depth, :], preferred_element_type=F32
        )
        if chunk == 0:
            acc[...] = own
        else:
            acc[...] += own
    fetch_small.wait()
    small_rows = small_in.shape[0] * heads
    for level in range(small_in.shape[0]):
        small_wide[level * heads : (level + 1) * heads, :] = small_in[level].astype(F32)
    small_wide[small_rows:, :] = jnp.zeros((LANES - small_rows, width), F32)
    small_ref[...] = small_wide[...].astype(BF16)
    gate = mm_nt(tokens[...], small_ref[...])
    decay_col = levels * heads
    beta_col = decay_col + heads
    norm_col = beta_col + heads
    gate_ref[...] = gate
    lane = lane_of(rows)
    fetch_rates.wait()
    rate, bias = head_rows(hp_ref, heads, decay_col, beta_col)
    rates_ref[0:1, :] = rate
    rates_ref[1:2, :] = bias
    switch = jax.nn.sigmoid(gate + bias)
    lam = jnp.maximum(gate, 0.0) + jnp.log1p(jnp.exp(-jnp.abs(gate)))
    row_id, col_id = pair_ids(rows)
    inclusive = row_id >= col_id
    strict = row_id > col_id
    apart = row_id ^ col_id
    cum = mm_full(inclusive.astype(F32), -rate * switch)
    pack = jnp.where(lane < decay_col, lam, jnp.where(lane < beta_col, cum, switch))
    k_all, v_all = [], []
    for head in range(heads):
        for part in range(2):
            col = (part * heads + head) * LANES
            raw = acc[:, col : col + LANES]
            scale = lax.rsqrt(row_sum(raw * raw) + EPS)
            unit = raw * scale
            qkv_ref[part, head] = unit
            pack = jnp.where(lane == norm_col + part * heads + head, scale, pack)
            if part == 1:
                k_all.append(unit)
        col = (2 * heads + head) * LANES
        v_all.append(acc[:, col : col + LANES])
        qkv_ref[2, head] = v_all[head]
    pack_ref[...] = pack
    pack_t = pack.T
    pack_t_ref[...] = pack_t
    eye = (row_id == col_id).astype(F32)
    lower_all, trans_all = [], []
    for head in range(heads):
        decay = decay_of(pack, pack_t, decay_col + head, inclusive)
        decay_ref[head] = decay
        gram = mm_nt(k_all[head], k_all[head])
        base = jnp.where(strict, decay * gram, 0.0)
        base_ref[head] = base
        lower = column(pack, beta_col + head) * base
        lower_ref[head] = lower
        lower_all.append(lower)
        trans_all.append((eye - jnp.where(apart == 1, lower, 0.0)).astype(BF16))
    for bit in range(1, rows.bit_length() - 1):
        here = (apart >> bit) == 1
        edge = [jnp.where(here, lower, 0.0) for lower in lower_all]
        half = [mm(trans, part) for trans, part in zip(trans_all, edge)]
        trans_all = [
            trans - mm(part, trans).astype(BF16) for trans, part in zip(trans_all, half)
        ]
    rest_all = []
    for trans, lower in zip(trans_all, lower_all):
        high, low = split(lower)
        rest_all.append(eye - trans.astype(F32) - mm(high, trans) - mm(low, trans))
    trans_all = [
        (trans.astype(F32) + mm(trans, rest)).astype(BF16)
        for trans, rest in zip(trans_all, rest_all)
    ]
    mixed_all = []
    for head in range(heads):
        trans_ref[head] = trans_all[head]
        cum_row = pack_t[decay_col + head : decay_col + head + 1, :]
        tail_t = k_all[head].T * jnp.exp(cum_row[:, rows - 1 :] - cum_row)
        mixed_all.append(mm(tail_t, trans_all[head]))
    eye_key = eye[:LANES, :LANES]
    for head in range(heads):
        mixed_t_ref[head] = mixed_all[head]
        cum_col = column(pack, decay_col + head)
        beta = column(pack, beta_col + head)
        grown = (beta * jnp.exp(cum_col)) * k_all[head]
        both = jnp.concatenate([-grown, beta * v_all[head]], 1)
        pair = mm(mixed_all[head], both)
        last = jnp.exp(cum_col[rows - 1 : rows, :])
        pair_ref[head, :, :LANES] = (last * eye_key + pair[:, :LANES]).astype(BF16)
        pair_ref[head, :, LANES:] = pair[:, LANES:].astype(BF16)


def project(place, tokens, flat_w, small, head_param, heads, levels):
    rows, width = tokens.shape
    chunks = 8
    cols = 3 * heads
    key = flat_w.shape[1]
    square = (heads, rows, rows)
    out_shape = (
        kept((width, cols * key), BF16),
        kept((LANES, width), BF16),
        kept((3, heads, rows, key), F32),
        kept((rows, LANES), F32),
        kept((rows, LANES), F32),
        kept((LANES, rows), F32),
        kept(square, BF16),
        kept((heads, key, rows), F32),
        kept(square, F32),
        kept(square, F32),
        kept(square, F32),
        kept((2, LANES), F32),
        kept((heads, key, 2 * key), BF16),
    )
    scratch = [
        pltpu.VMEM(tokens.shape, BF16),
        pltpu.VMEM(flat_w.shape, BF16),
        pltpu.VMEM((width // chunks * cols, key), F32),
        pltpu.VMEM((width // chunks * cols, key), F32),
        pltpu.VMEM(small.shape, BF16),
        pltpu.VMEM((LANES, width), F32),
        pltpu.VMEM((rows, cols * key), F32),
        pltpu.VMEM(head_param.shape, F32),
        pltpu.SemaphoreType.DMA((chunks + 3,)),
    ]
    return local_call(
        functools.partial(project_body, (heads, levels, chunks)), "project", 22, out_shape,
        [place], [], scratch, [head_param, tokens, flat_w, small],
    )


def local_body(
    sizes, qkv_ref, pack_ref, pack_t_ref, trans_ref, mixed_t_ref, decay_ref, grad_ref, weight_ref, *outs
):
    heads, levels, bits = sizes
    (attn_ref, attn_t_ref, prod_t_ref, scores_ref, mix_ref, mixed_ref, local_ref, hat_ref,
     hat_t_ref, grad_normed_ref) = outs
    grad_normed_ref[...] = mm_nt(grad_ref[...], weight_ref[...])
    rows = pack_ref.shape[0]
    decay_col = levels * heads
    beta_col = decay_col + heads
    pack = pack_ref[...]
    pack_t = pack_t_ref[...]
    row_id, col_id = pair_ids(rows)
    apart = row_id ^ col_id
    for head in range(heads):
        scores = mm_nt_fine(qkv_ref[0, head], qkv_ref[1, head]) * decay_ref[head]
        scores_ref[head] = scores.astype(BF16)
        mix_ref[head] = level_mix(pack, head, heads, bits, apart)
        mixed_ref[head] = mixed_t_ref[head].T.astype(BF16)
    for head in range(heads):
        attn = mm(scores_ref[head], trans_ref[head])
        attn_ref[head] = attn.astype(BF16)
        attn_t_ref[head] = attn.T.astype(BF16)
        attn = attn * pack_t[beta_col + head : beta_col + head + 1, :]
        prod = attn * mix_ref[head]
        prod_t_ref[head] = prod.T.astype(BF16)
        growth = jnp.exp(column(pack, decay_col + head))
        local_ref[head] = mm(prod, qkv_ref[2, head])
        hat = growth * qkv_ref[0, head] - mm(attn, growth * qkv_ref[1, head])
        hat_ref[head] = hat.astype(BF16)
        hat_t_ref[head] = hat.T.astype(BF16)


def local_part(arrays, levels, bits):
    heads, rows, key = arrays[0].shape[1:]
    square = (heads, rows, rows)
    out_shape = (
        kept(square, BF16),
        kept(square, BF16),
        kept(square, BF16),
        kept(square, BF16),
        kept(square, F32),
        kept((heads, rows, key), BF16),
        kept((heads, rows, key), F32),
        kept((heads, rows, key), BF16),
        kept((heads, key, rows), BF16),
        kept((rows, heads * key), F32),
    )
    return local_call(
        functools.partial(local_body, (heads, levels, bits)), "local_part", 10, out_shape,
        [], arrays,
    )


def join_pair(upper, own, other):
    key = own.shape[0]
    low = jnp.where(upper, other, own)
    high = jnp.where(upper, own, other)
    moved = mm(high[:, :key], low)
    late = jnp.concatenate([jnp.zeros((key, key), F32), high[:, key:].astype(F32)], 1)
    return (moved + late).astype(BF16)


def join_body(place_ref, own_ref, other_ref, out_ref):
    half = out_ref.shape[0]
    upper = (place_ref[0] & 1) == 1
    for slot in range(half):
        head = (place_ref[0] & 1) * half + slot
        out_ref[slot] = join_pair(upper, own_ref[head], other_ref[head])


def join_half(place, own, other):
    half = (own.shape[0] // 2,) + own.shape[1:]
    return local_call(join_body, "join_half", 6, [kept(half, BF16)], [place], [own, other])[0]


def gather_node(head, bit, first, near, uppers):
    if bit == 0:
        mine, theirs = near[first]
        half = mine.shape[0]
        here = uppers[0] if head >= half else jnp.logical_not(uppers[0])
        return jnp.where(here, mine[head % half], theirs[head % half])
    own = gather_node(head, bit - 1, first, near, uppers)
    other = gather_node(head, bit - 1, first ^ (1 << (bit - 1)), near, uppers)
    return join_pair(uppers[bit], own, other)


def reach_body(
    sizes, place_ref, gain_ref, pack_ref, local_ref, hat_ref, grad_ref, weight_ref, *refs
):
    heads, bits, far, near_count = sizes
    first_ref = refs[0]
    near = [None] + [(refs[1 + at], refs[1 + near_count + at]) for at in range(near_count)]
    refs = refs[2 * near_count + 1 :]
    out_ref, dout_ref, found_ref, prefix_ref, dfar_ref = refs[:5]
    nodes = refs[5:-1]
    normed_ref = refs[-1]
    rows = pack_ref.shape[0]
    key = hat_ref.shape[2]
    pack = pack_ref[...]
    gain = gain_ref[...]
    lane = lane_of(rows)
    all_heads = range(heads)
    uppers = [((place_ref[0] >> bit) & 1) == 1 for bit in range(far)]
    others = []
    for bit in range(far):
        if bit == 0:
            others.append([first_ref[head] for head in all_heads])
        else:
            others.append(
                [gather_node(head, bit - 1, 1 << (bit - 1), near, uppers) for head in all_heads]
            )
            for head in all_heads:
                nodes[bit - 1][head] = others[bit][head]
    eye_key = jnp.where(pair_ids(key)[0] == pair_ids(key)[1], 1.0, 0.0).astype(BF16)
    prefix = [eye_key for head in all_heads]
    found = []
    for bit in range(far):
        for head in all_heads:
            prefix_ref[head, bit] = prefix[head]
        moved = [mm(prefix[head], others[bit][head]) for head in all_heads]
        found.append([jnp.where(uppers[bit], m[:, key:], 0.0).astype(BF16) for m in moved])
        prefix = [
            jnp.where(uppers[bit], moved[head][:, :key].astype(BF16), prefix[head])
            for head in all_heads
        ]
    found = [jnp.concatenate([found[bit][head] for bit in range(far)], 1) for head in all_heads]
    reached = [mm(hat_ref[head], found[head]) for head in all_heads]
    dfar = jnp.zeros((rows, LANES), F32)
    for head in all_heads:
        found_ref[head] = found[head]
        summed = local_ref[head]
        parts = []
        for bit in range(far):
            parts.append(reached[head][:, bit * key : (bit + 1) * key])
            summed = summed + column(pack, (bits + 1 + bit) * heads + head) * parts[bit]
        scale = lax.rsqrt(jnp.mean(summed * summed, -1, keepdims=True) + EPS)
        unit = summed * scale
        normed_ref[:, head * key : (head + 1) * key] = (unit * gain).astype(BF16)
        pulled = grad_ref[:, head * key : (head + 1) * key] * gain
        dout = scale * (pulled - unit * jnp.mean(pulled * unit, -1, keepdims=True))
        dout_ref[head] = dout
        for bit in range(far):
            col = (bits + 1 + bit) * heads + head
            dfar = jnp.where(lane == col, row_sum(dout * parts[bit]), dfar)
    dfar_ref[...] = dfar
    out_ref[...] = jnp.dot(
        normed_ref[...], weight_ref[...], preferred_element_type=F32
    ).astype(BF16)


def reach(place, arrays, first, near, bits, far):
    gain, pack, local_out, hat, grad_normed, weight = arrays
    heads, rows, key = hat.shape
    nodes = tuple(kept(first.shape, BF16) for bit in range(1, far))
    out_shape = (
        jax.ShapeDtypeStruct((rows, weight.shape[1]), BF16),
        kept((heads, rows, key), F32),
        kept((heads, key, far * key), BF16),
        kept((heads, far, key, key), BF16),
        kept((rows, LANES), F32),
    ) + nodes
    mine, theirs = near
    got = local_call(
        functools.partial(reach_body, (heads, bits, far, len(mine))), "reach", 10, out_shape,
        [place], [*arrays, first, *mine, *theirs], [pltpu.VMEM((rows, heads * key), BF16)],
    )
    return got[:5], got[5:]


def return_body(sizes, place_ref, pack_ref, hat_t_ref, dout_ref, found_ref, prefix_ref, *refs):
    heads, bits, far = sizes
    others = refs[:far]
    dhat_ref = refs[far]
    sends = refs[far + 1 :]
    key = hat_t_ref.shape[1]
    pack = pack_ref[...]
    all_heads = range(heads)
    uppers = [((place_ref[0] >> bit) & 1) == 1 for bit in range(far)]
    spread = []
    for head in all_heads:
        parts = []
        for bit in range(far):
            weight = column(pack, (bits + 1 + bit) * heads + head)
            parts.append((weight * dout_ref[head]).astype(BF16))
        spread.append(jnp.concatenate(parts, 1))
    dfound = [mm(hat_t_ref[head], spread[head]) for head in all_heads]
    for head in all_heads:
        dhat_ref[head] = mm_nt(spread[head], found_ref[head])
    dprefix = [jnp.zeros((key, key), F32) for head in all_heads]
    for bit in reversed(range(far)):
        dfree = [
            jnp.where(uppers[bit], d[:, bit * key : (bit + 1) * key], 0.0) for d in dfound
        ]
        both = [
            jnp.concatenate([jnp.where(uppers[bit], dprefix[head], 0.0), dfree[head]], 1)
            for head in all_heads
        ]
        for head in all_heads:
            sent = dfree[head] if bit == far - 1 else both[head]
            sends[bit][head] = mm_tn(prefix_ref[head, bit], sent).astype(BF16)
        if bit > 0:
            moved = [mm_nt(both[head], others[bit][head]) for head in all_heads]
            dprefix = [
                jnp.where(uppers[bit], moved[head], dprefix[head]) for head in all_heads
            ]


def return_states(place, pack, hat_t, dout, found, prefix, others, bits):
    heads, rows, key = dout.shape
    far = len(others)
    sends = tuple(
        kept((heads, key, (1 if bit == far - 1 else 2) * key), BF16) for bit in range(far)
    )
    got = local_call(
        functools.partial(return_body, (heads, bits, far)), "return_states", 8,
        (kept(dout.shape, F32),) + sends, [place], [pack, hat_t, dout, found, prefix, *others],
    )
    return got[0], got[1:]


def add_body(*refs):
    count = len(refs) // 3
    for at in range(count):
        left, right = refs[at][...].astype(F32), refs[count + at][...].astype(F32)
        refs[2 * count + at][...] = (left + right).astype(BF16)


def add_all(left, right):
    out_shape = [kept(value.shape, BF16) for value in left]
    return local_call(add_body, "add_all", 6, out_shape, [], [*left, *right])


def lower_pull(dlower, base, lower, beta, decay, strict, k_in):
    dlower = jnp.where(strict, dlower, 0.0)
    dbeta = row_sum(dlower * base)
    dgram = dlower * (beta * decay)
    dkey = mm(dgram, k_in) + mm_tn(dgram, k_in)
    return dbeta, beta * dbeta, col_sum(dlower * lower), dkey


def pull_body(sizes, *refs):
    heads, levels, bits = sizes
    (qkv_ref, pack_ref, pack_t_ref, trans_ref, attn_ref, attn_t_ref, prod_t_ref, scores_ref,
     mix_ref, decay_ref, base_ref, lower_ref, dout_ref, dhat_ref) = refs[:14]
    dqkv_ref, dgrown_ref, dcol_ref, drow_ref = refs[14:]
    rows = pack_ref.shape[0]
    decay_col = levels * heads
    beta_col = decay_col + heads
    block_bit = BLOCK.bit_length() - 1
    pack = pack_ref[...]
    pack_t = pack_t_ref[...]
    row_id, col_id = pair_ids(rows)
    strict = row_id > col_id
    apart = row_id ^ col_id
    lane = lane_of(rows)
    all_heads = range(heads)
    dcol = jnp.zeros((rows, LANES), F32)
    dbeta_rows, dcum_rows, dattn_all = [], [], []
    for head in all_heads:
        high, low = split(dout_ref[head])
        v_in = qkv_ref[2, head].astype(BF16)
        dprod = mm_nt(high, v_in) + mm_nt(low, v_in)
        dqkv_ref[2, head] = mm(prod_t_ref[head], high)
        beta_row = pack_t[beta_col + head : beta_col + head + 1, :]
        growth = jnp.exp(column(pack, decay_col + head))
        attn0 = attn_ref[head].astype(F32)
        touched = dprod * (attn0 * beta_row)
        for level in range(bits + 1):
            if level == 0:
                here = (apart >> block_bit) == 0
            else:
                here = (apart >> (block_bit + level - 1)) == 1
            dcol = jnp.where(
                lane == level * heads + head, row_sum(jnp.where(here, touched, 0.0)), dcol
            )
        dattn = dprod * mix_ref[head] - mm_nt(dhat_ref[head], growth * qkv_ref[1, head])
        dbeta_rows.append(col_sum(dattn * attn0))
        dattn_all.append((dattn * beta_row).astype(BF16))
    dscore_all = [mm_nt(dattn_all[head], trans_ref[head]) for head in all_heads]
    moved_all = []
    for head in all_heads:
        both = jnp.concatenate(
            [dscore_all[head].astype(BF16), dhat_ref[head].astype(BF16)], 1
        )
        moved_all.append(mm(attn_t_ref[head], both))
    for head in all_heads:
        q_in, k_in = qkv_ref[0, head], qkv_ref[1, head]
        beta = column(pack, beta_col + head)
        growth = jnp.exp(column(pack, decay_col + head))
        dscore = dscore_all[head]
        dprobs = dscore * decay_ref[head]
        shift = dscore * scores_ref[head].astype(F32)
        dgrown_ref[head] = -beta * moved_all[head][:, rows:]
        dbeta, dcum_col, dcum_row, dk_lower = lower_pull(
            -moved_all[head][:, :rows], base_ref[head], lower_ref[head], beta, decay_ref[head],
            strict, k_in
        )
        dhat = dhat_ref[head]
        dqkv_ref[0, head] = growth * dhat + mm(dprobs, k_in)
        dqkv_ref[1, head] = mm_tn(dprobs, q_in) + dk_lower
        dcum_col = dcum_col + row_sum(shift) + growth * row_sum(q_in * dhat)
        dcum_rows.append(-dcum_row - col_sum(shift))
        dcol = jnp.where(lane == beta_col + head, dbeta, dcol)
        dcol = jnp.where(lane == decay_col + head, dcum_col, dcol)
    dcol_ref[...] = dcol
    drow_ref[...] = jnp.concatenate(dcum_rows + dbeta_rows, 0)


def pull_local(arrays, levels, bits):
    heads, rows, key = arrays[0].shape[1:]
    out_shape = (
        kept((3, heads, rows, key), F32),
        kept((heads, rows, key), F32),
        kept((rows, LANES), F32),
        kept((2 * heads, rows), F32),
    )
    return local_call(
        functools.partial(pull_body, (heads, levels, bits)), "pull_local", 12, out_shape, [], arrays
    )


def finish_body(sizes, place_ref, *refs):
    heads, levels, far, count, arrived_counts = sizes
    (qkv_ref, gate_ref, pack_ref, trans_ref, mixed_ref, decay_ref, base_ref, lower_ref,
     dqkv_ref, dgrown_ref, dcol_ref, drow_ref, dfar_ref, rates_ref, small_ref, wr_ref) = refs[:16]
    others = refs[16 : 16 + far]
    refs = refs[16 + far :]
    arrived = []
    for found in arrived_counts:
        arrived.append(refs[:found])
        refs = refs[found:]
    out_ref, dproj = refs
    rows = pack_ref.shape[0]
    key = qkv_ref.shape[3]
    decay_col = levels * heads
    beta_col = decay_col + heads
    norm_col = beta_col + heads
    place = place_ref[0]
    all_heads = range(heads)
    uppers = [((place >> bit) & 1) == 1 for bit in range(far)]
    pack = pack_ref[...]
    row_id, col_id = pair_ids(rows)
    strict = row_id > col_id
    lane = lane_of(rows)
    last_row = lax.broadcasted_iota(jnp.int32, (rows, 1), 0) == rows - 1
    eye_key = (pair_ids(key)[0] == pair_ids(key)[1]).astype(F32)
    dpair = [jnp.zeros((key, 2 * key), F32) for head in all_heads]
    for bit in reversed(range(far)):
        for head in all_heads:
            got = arrived[bit][0][head].astype(F32)
            for more in arrived[bit][1:]:
                got = got + more[head].astype(F32)
            other = others[bit][head]
            if bit == far - 1:
                got = jnp.concatenate([jnp.zeros((key, key), F32), got], 1)
                dpair[head] = jnp.where(uppers[bit], 0.0, got)
            else:
                as_low = mm_tn(other[:, :key], dpair[head]) + got
                as_high = mm_nt(dpair[head], other)
                as_high = jnp.concatenate([as_high, dpair[head][:, key:]], 1)
                dpair[head] = jnp.where(uppers[bit], as_high, as_low)
    moved_all, dmixed_all = [], []
    for head in all_heads:
        beta = column(pack, beta_col + head)
        growth = jnp.exp(column(pack, decay_col + head))
        both = jnp.concatenate([-growth * qkv_ref[1, head], qkv_ref[2, head]], 1)
        dmixed_all.append(mm_nt(both, dpair[head]))
        moved_all.append(mm(beta * mixed_ref[head].astype(F32), dpair[head]))
    dtail_all = [
        mm(trans_ref[head], column(pack, beta_col + head) * dmixed_all[head])
        for head in all_heads
    ]
    dlower_all = [-mm_nt(mixed_ref[head], dtail_all[head]) for head in all_heads]
    dcol = jnp.where(lane < decay_col, dcol_ref[...] + dfar_ref[...], dcol_ref[...])
    dcum_rows = []
    for head in all_heads:
        q_in, k_in = qkv_ref[0, head], qkv_ref[1, head]
        beta = column(pack, beta_col + head)
        cum_col = column(pack, decay_col + head)
        growth = jnp.exp(cum_col)
        last = cum_col[rows - 1 : rows, :]
        tail = jnp.exp(last - cum_col)
        dgrown = dgrown_ref[head] - moved_all[head][:, :key]
        dv = dqkv_ref[2, head] + moved_all[head][:, key:]
        dbeta_more = row_sum(mixed_ref[head].astype(F32) * dmixed_all[head])
        dtail = dtail_all[head]
        dbeta, dcum_col, dcum_row, dk_lower = lower_pull(
            dlower_all[head], base_ref[head], lower_ref[head], beta, decay_ref[head], strict, k_in
        )
        dcum_rows.append(-dcum_row)
        tail_pull = tail * row_sum(k_in * dtail)
        trace = col_sum(row_sum(dpair[head][:, :key] * eye_key))
        at_last = col_sum(tail_pull) + jnp.exp(last) * trace
        dcum_col = dcum_col + growth * row_sum(k_in * dgrown) - tail_pull
        dcum_col = dcum_col + jnp.where(last_row, at_last, 0.0)
        dk = dqkv_ref[1, head] + dk_lower + growth * dgrown + tail * dtail
        dq = dqkv_ref[0, head]
        dcol = dcol + jnp.where(lane == beta_col + head, dbeta + dbeta_more, 0.0)
        dcol = dcol + jnp.where(lane == decay_col + head, dcum_col, 0.0)
        for part, unit, dunit in ((0, q_in, dq), (1, k_in, dk)):
            scale = column(pack, norm_col + part * heads + head)
            back = scale * (dunit - unit * row_sum(unit * dunit))
            col = (part * heads + head) * key
            dproj[:, col : col + key] = back.astype(BF16)
        col = (2 * heads + head) * key
        dproj[:, col : col + key] = dv.astype(BF16)
    drow = drow_ref[...]
    drow = drow + jnp.concatenate(dcum_rows + [jnp.zeros((heads, rows), F32)], 0)
    drow = jnp.concatenate(
        [jnp.zeros((decay_col, rows), F32), drow,
         jnp.zeros((LANES - norm_col, rows), F32)], 0
    )
    dcol = dcol + drow.T
    rate, bias = rates_ref[0:1, :], rates_ref[1:2, :]
    switch = jax.nn.sigmoid(gate_ref[...] + bias)
    dlog = mm_full((row_id <= col_id).astype(F32), dcol)
    slope = switch * (1.0 - switch)
    dgate = jnp.where(
        lane < decay_col,
        dcol * switch,
        jnp.where(lane < beta_col, -rate * dlog * slope, dcol * slope),
    )
    dgate = jnp.where(lane < norm_col, dgate, 0.0).astype(BF16)
    size = out_ref.shape[2]
    for dest in range(count):
        span = slice(dest * size, (dest + 1) * size)
        part = mm_nt(dproj[...], wr_ref[span, :]) + mm(dgate, small_ref[:, span])
        out_ref[dest] = part.astype(BF16)


def finish(place, arrays, others, arrived, levels, count):
    rows = arrays[0].shape[2]
    width, cols = arrays[-1].shape
    far = len(others)
    counts = tuple(len(group) for group in arrived)
    heads = arrays[0].shape[1]
    flat = [value for group in arrived for value in group]
    return local_call(
        functools.partial(finish_body, (heads, levels, far, count, counts)), "finish", 12,
        [kept((count, rows, width // count), BF16)],
        [place], [*arrays, *others, *flat], [pltpu.VMEM((rows, cols), BF16)],
    )[0]


def swap(value, axis, mask):
    size = lax.axis_size(axis)
    return lax.ppermute(value, axis, [(at, at ^ mask) for at in range(size)])


def sum_body(parts_ref, out_ref):
    total = parts_ref[0].astype(F32)
    for at in range(1, parts_ref.shape[0]):
        total = total + parts_ref[at].astype(F32)
    out_ref[...] = total.astype(BF16)


def scatter_sum(parts, axis):
    parts = lax.all_to_all(parts, axis, 0, 0)
    out_shape = [jax.ShapeDtypeStruct(parts.shape[1:], BF16)]
    return local_call(sum_body, "scatter_sum", 6, out_shape, [], [parts])[0]


def on_device(tokens, qkv_weight, small_weight, head_param, norm_gain, out_weight, grad_out):
    rows, width = tokens.shape
    heads, key = qkv_weight.shape[2:]
    levels = small_weight.shape[2] - 2
    bits = (rows // BLOCK).bit_length() - 1
    size = lax.axis_size("ctx")
    far = size.bit_length() - 1
    count = lax.axis_size("head")
    place = jnp.stack([lax.axis_index("ctx"), lax.axis_index("head")]).astype(jnp.int32)
    flat_w = qkv_weight.reshape(width * 3 * heads, key)
    small = jnp.transpose(small_weight, (2, 1, 0))
    rates = head_param.T
    flat_out = out_weight.reshape(heads * key, width)
    gain = norm_gain.reshape(1, key)

    (wr, small_t, qkv, gate, pack, pack_t, trans, mixed_t, decay, base, lower, rates_row,
     pair) = project(
        place, tokens, flat_w, small, rates, heads, levels
    )
    first = swap(pair, "ctx", 1)
    node = join_half(place, pair, first)
    mine = [swap(node, "ctx", 2 * at) for at in range(1, size // 2)]
    (attn, attn_t, prod_t, scores, mix, mixed, local_out, hat, hat_t, grad_normed) = local_part(
        [qkv, pack, pack_t, trans, mixed_t, decay, grad_out, flat_out], levels, bits
    )
    mine, local_out, grad_normed = lax.optimization_barrier((mine, local_out, grad_normed))
    theirs = [swap(value, "ctx", 1) for value in mine]
    (out_part, dout, found, prefix, dfar), nodes = reach(
        place, [gain, pack, local_out, hat, grad_normed, flat_out], first, (mine, theirs),
        bits, far
    )
    layer_out = lax.psum_scatter(out_part, "head", scatter_dimension=1, tiled=True)
    others = [first, *nodes]
    dhat, sends = return_states(place, pack, hat_t, dout, found, prefix, others, bits)
    got = [swap(value, "ctx", 1) for value in sends]
    arrived = [[got[0]]]
    sums = add_all(sends[1:], got[1:])
    for bit in range(1, far):
        half = 1 << (bit - 1)
        arrived.append([swap(sums[bit - 1], "ctx", 2 * at) for at in range(half, 2 * half)])
    dqkv, dgrown, dcol, drow = pull_local(
        [qkv, pack, pack_t, trans, attn, attn_t, prod_t, scores, mix, decay, base, lower, dout,
         dhat],
        levels, bits,
    )
    arrays = [qkv, gate, pack, trans, mixed, decay, base, lower, dqkv, dgrown, dcol, drow, dfar,
              rates_row, small_t, wr]
    parts = finish(place, arrays, others, arrived, levels, count)
    return layer_out, scatter_sum(parts, "head")


def solution(mesh):
    placed = (
        P("ctx", None),
        P(None, None, "head", None),
        P(None, "head", None),
        P("head", None),
        P(),
        P("head", None, None),
        P("ctx", None),
    )
    return jax.shard_map(
        on_device,
        mesh=mesh,
        in_specs=placed,
        out_specs=(P("ctx", "head"), P("ctx", "head")),
        check_vma=False,
    )
```

```python
import functools

import jax
import jax.numpy as jnp
from jax import lax
from jax.experimental import pallas as pl
from jax.experimental.pallas import tpu as pltpu
from jax.sharding import PartitionSpec as P

BLOCK = 64
LANES = 128
EPS = 1e-06
MIB = 1024 * 1024
F32 = jnp.float32
BF16 = jnp.bfloat16
WHOLE = pl.BlockSpec(memory_space=pltpu.VMEM)
SCALARS = pl.BlockSpec(memory_space=pltpu.SMEM)
HBM = pl.BlockSpec(memory_space=pltpu.HBM)


def contract(left, right, dim_left, dim_right):
    return lax.dot_general(
        left.astype(BF16),
        right.astype(BF16),
        (((dim_left,), (dim_right,)), ((), ())),
        preferred_element_type=F32,
    )


def mm(left, right):
    return contract(left, right, 1, 0)


def mm_nt(left, right):
    return contract(left, right, 1, 1)


def mm_tn(left, right):
    return contract(left, right, 0, 0)


def split(values):
    high = values.astype(BF16)
    return high, (values - high.astype(F32)).astype(BF16)


def mm_nt_fine(left, right):
    left_high, left_low = split(left)
    right_high, right_low = split(right)
    return mm_nt(left_high, right_high) + (mm_nt(left_low, right_high) + mm_nt(left_high, right_low))


def mm_full(left, right):
    return jnp.dot(left, right, precision=lax.Precision.HIGHEST, preferred_element_type=F32)


def pair_ids(count):
    row_id = lax.broadcasted_iota(jnp.int32, (count, count), 0)
    col_id = lax.broadcasted_iota(jnp.int32, (count, count), 1)
    return row_id, col_id


def row_sum(values):
    return jnp.sum(values, 1, keepdims=True)


def col_sum(values):
    return jnp.sum(values, 0, keepdims=True)


def lane_of(rows):
    return lax.broadcasted_iota(jnp.int32, (rows, LANES), 1)


def decay_of(pack, pack_t, col, inclusive):
    spread = pack[:, col : col + 1] - pack_t[col : col + 1, :]
    return jnp.where(inclusive, jnp.exp(jnp.minimum(spread, 0.0)), 0.0)


def kept(shape, dtype):
    return pltpu.VMEM(shape, dtype)


def stored(shape, dtype):
    return pltpu.HBM(shape, dtype)


def pin(values, space):
    return [pltpu.with_memory_space_constraint(value, space) for value in values]


def local_call(
    body, name, limit, out_shape, scalars, arrays, scratch=(), remote=(), out_specs=None
):
    return pl.pallas_call(
        body,
        out_shape=tuple(out_shape),
        in_specs=[SCALARS] * len(scalars)
        + [WHOLE] * len(arrays)
        + [HBM] * len(remote),
        out_specs=tuple(out_specs or [WHOLE] * len(out_shape)),
        scratch_shapes=list(scratch),
        compiler_params=pltpu.CompilerParams(vmem_limit_bytes=limit * MIB),
        name=name,
    )(*scalars, *pin(arrays, pltpu.VMEM), *pin(remote, pltpu.HBM))


def column(pack, at):
    return pack[:, at : at + 1]


def level_mix(pack, head, heads, bits, apart):
    block_bit = BLOCK.bit_length() - 1
    mixed = jnp.broadcast_to(column(pack, head), apart.shape)
    for level in range(1, bits + 1):
        here = (apart >> (block_bit + level - 1)) >= 1
        mixed = jnp.where(here, column(pack, level * heads + head), mixed)
    return mixed


def head_rows(hp_ref, heads, decay_col, beta_col):
    lane_row = lane_of(1)
    rate = jnp.zeros((1, LANES), F32)
    bias = jnp.zeros((1, LANES), F32)
    for head in range(heads):
        rate = jnp.where(lane_row == decay_col + head, hp_ref[0:1, head : head + 1], rate)
        bias = jnp.where(lane_row == beta_col + head, hp_ref[1:2, head : head + 1], bias)
    return rate, bias


def merge_blocks(trans_all, edge_all, levels, first):
    if first:
        powers = [edge.astype(BF16) for edge in edge_all]
        trans_all = [trans - power for trans, power in zip(trans_all, powers)]
    else:
        powers = [mm(edge, trans).astype(BF16) for edge, trans in zip(edge_all, trans_all)]
        yield
        trans_all = [
            trans - mm(trans, power).astype(BF16) for trans, power in zip(trans_all, powers)
        ]
    for level in range(1, levels):
        powers = [mm(power, power).astype(BF16) for power in powers]
        yield
        trans_all = [
            trans + mm(trans, power).astype(BF16) for trans, power in zip(trans_all, powers)
        ]
    return trans_all


def invert(lower_all, eye, apart, rows):
    trans_all = [eye.astype(BF16) for lower in lower_all]
    bits = rows.bit_length() - 1
    start = 0
    while start < bits:
        levels = min(2 if bits - start == 2 else 3, bits - start)
        here = jnp.logical_and((apart >> start) >= 1, (apart >> (start + levels)) == 0)
        edge_all = [jnp.where(here, lower, 0.0) for lower in lower_all]
        trans_all = yield from merge_blocks(trans_all, edge_all, levels, start == 0)
        start += levels
        yield
    rest_all = []
    for trans, lower in zip(trans_all, lower_all):
        high, low = split(lower)
        rest_all.append(eye - trans.astype(F32) - mm(high, trans) - mm(low, trans))
    yield
    return [
        (trans.astype(F32) + mm(trans, rest)).astype(BF16)
        for trans, rest in zip(trans_all, rest_all)
    ]


def project_body(sizes, place_ref, hp_hbm, tokens_hbm, w_hbm, small_hbm, *refs):
    heads, levels, chunks = sizes
    (wr_hbm, small_ref, qkv_ref, gate_ref, pack_ref, pack_t_ref, trans_ref, mixed_t_ref,
     decay_ref, base_ref, lower_ref, rates_ref, pair_ref) = refs[:13]
    tokens, wide_in, wide, wr, small_in, small_wide, acc, hp_ref, sems = refs[13:]
    rows, width = tokens.shape
    depth = width // chunks
    cols = 3 * heads
    fetch_tokens = pltpu.make_async_copy(tokens_hbm, tokens, sems.at[chunks])
    fetch_small = pltpu.make_async_copy(small_hbm, small_in, sems.at[chunks + 1])
    fetch_rates = pltpu.make_async_copy(hp_hbm, hp_ref, sems.at[chunks + 2])
    keep_weight = pltpu.make_async_copy(wr, wr_hbm, sems.at[chunks + 3])
    fetches = []
    for chunk in range(chunks):
        span = pl.ds(chunk * depth * cols, depth * cols)
        fetches.append(
            pltpu.make_async_copy(w_hbm.at[span, :], wide_in.at[span, :], sems.at[chunk])
        )
    fetch_small.start()
    fetch_rates.start()
    fetch_tokens.start()
    for fetch in fetches:
        fetch.start()
    decay_col = levels * heads
    beta_col = decay_col + heads
    norm_col = beta_col + heads
    lane = lane_of(rows)
    row_id, col_id = pair_ids(rows)
    inclusive = row_id >= col_id
    strict = row_id > col_id
    apart = row_id ^ col_id
    eye = (row_id == col_id).astype(F32)
    fetch_small.wait()
    small_rows = small_in.shape[0] * heads
    for level in range(small_in.shape[0]):
        small_wide[level * heads : (level + 1) * heads, :] = small_in[level].astype(F32)
    small_wide[small_rows:, :] = jnp.zeros((LANES - small_rows, width), F32)
    small_ref[...] = small_wide[...].astype(BF16)
    fetch_rates.wait()
    rate, bias = head_rows(hp_ref, heads, decay_col, beta_col)
    rates_ref[0:1, :] = rate
    rates_ref[1:2, :] = bias
    fetch_tokens.wait()
    gate = mm_nt(tokens[...], small_ref[...])
    gate_ref[...] = gate
    switch = jax.nn.sigmoid(gate + bias)
    lam = jnp.maximum(gate, 0.0) + jnp.log1p(jnp.exp(-jnp.abs(gate)))
    cum = mm_full(inclusive.astype(F32), -rate * switch)
    pack = jnp.where(lane < decay_col, lam, jnp.where(lane < beta_col, cum, switch))
    pack_t = pack.T
    pack_t_ref[...] = pack_t

    def extract(chunk, part):
        at = chunk * depth
        for col in range(part * heads, (part + 1) * heads):
            value = wide[pl.ds(at * cols + col, depth, stride=cols), :]
            wr[at : at + depth, col * LANES : (col + 1) * LANES] = value.astype(BF16)

    def multiply(part, first, last):
        span = slice((part * heads) * LANES, (part + 1) * heads * LANES)
        own = jnp.dot(
            tokens[:, first * depth : last * depth], wr[first * depth : last * depth, span],
            preferred_element_type=F32,
        )
        if first == 0:
            acc[:, span] = own
        else:
            acc[:, span] += own

    for chunk in range(chunks):
        fetches[chunk].wait()
        at = chunk * depth * cols
        wide[at : at + depth * cols, :] = wide_in[at : at + depth * cols, :].astype(F32)
        extract(chunk, 1)
        if chunk % 2 == 1:
            multiply(1, chunk - 1, chunk + 1)

    def unit_of(part, head):
        col = (part * heads + head) * LANES
        raw = acc[:, col : col + LANES]
        scale = lax.rsqrt(row_sum(raw * raw) + EPS)
        qkv_ref[part, head] = raw * scale
        return raw * scale, jnp.where(lane == norm_col + part * heads + head, scale, 0.0)

    scales = jnp.zeros((rows, LANES), F32)
    k_all, lower_all = [], []
    for head in range(heads):
        unit, scale = unit_of(1, head)
        k_all.append(unit)
        scales = scales + scale
        decay = decay_of(pack, pack_t, decay_col + head, inclusive)
        decay_ref[head] = decay.astype(BF16)
        base = jnp.where(strict, decay * mm_nt(unit, unit), 0.0)
        base_ref[head] = base.astype(BF16)
        lower = column(pack, beta_col + head) * base
        lower_ref[head] = lower.astype(BF16)
        lower_all.append(lower)

    def later():
        for part in (2, 0):
            for chunk in range(chunks):
                extract(chunk, part)
                if chunk % 4 == 3:
                    multiply(part, chunk - 3, chunk + 1)
                if chunk % 2 == 1:
                    yield

    chain, filler = invert(lower_all, eye, apart, rows), later()
    while True:
        try:
            next(chain)
        except StopIteration as stop:
            trans_all = stop.value
            break
        next(filler, None)
    for _ in filler:
        pass
    keep_weight.start()
    mixed_all = []
    for head in range(heads):
        trans_ref[head] = trans_all[head]
        cum_row = pack_t[decay_col + head : decay_col + head + 1, :]
        tail_t = k_all[head].T * jnp.exp(cum_row[:, rows - 1 :] - cum_row)
        mixed_all.append(mm(tail_t, trans_all[head]).astype(BF16))
    eye_key = eye[:LANES, :LANES]
    for head in range(heads):
        mixed_t_ref[head] = mixed_all[head]
        col = (2 * heads + head) * LANES
        v_in = acc[:, col : col + LANES]
        qkv_ref[2, head] = v_in
        cum_col = column(pack, decay_col + head)
        beta = column(pack, beta_col + head)
        grown = (beta * jnp.exp(cum_col)) * k_all[head]
        both = jnp.concatenate([-grown, beta * v_in], 1)
        pair = mm(mixed_all[head], both)
        last = jnp.exp(cum_col[rows - 1 : rows, :])
        pair_ref[head, :, :LANES] = (last * eye_key + pair[:, :LANES]).astype(BF16)
        pair_ref[head, :, LANES:] = pair[:, LANES:].astype(BF16)
    for head in range(heads):
        scales = scales + unit_of(0, head)[1]
    pack_ref[...] = jnp.where(lane < norm_col, pack, scales)
    keep_weight.wait()


def project(place, tokens, flat_w, small, head_param, heads, levels):
    rows, width = tokens.shape
    chunks = 8
    cols = 3 * heads
    key = flat_w.shape[1]
    square = (heads, rows, rows)
    out_shape = (
        stored((width, cols * key), BF16),
        kept((LANES, width), BF16),
        kept((3, heads, rows, key), F32),
        kept((rows, LANES), F32),
        kept((rows, LANES), F32),
        kept((LANES, rows), F32),
        kept(square, BF16),
        kept((heads, key, rows), BF16),
        kept(square, BF16),
        kept(square, BF16),
        kept(square, BF16),
        kept((2, LANES), F32),
        kept((heads, key, 2 * key), BF16),
    )
    scratch = [
        pltpu.VMEM(tokens.shape, BF16),
        pltpu.VMEM(flat_w.shape, BF16),
        pltpu.VMEM(flat_w.shape, F32),
        pltpu.VMEM((width, cols * key), BF16),
        pltpu.VMEM(small.shape, BF16),
        pltpu.VMEM((LANES, width), F32),
        pltpu.VMEM((rows, cols * key), F32),
        pltpu.VMEM(head_param.shape, F32),
        pltpu.SemaphoreType.DMA((chunks + 4,)),
    ]
    return local_call(
        functools.partial(project_body, (heads, levels, chunks)), "project", 36, out_shape,
        [place], [], scratch, [head_param, tokens, flat_w, small], [HBM] + [WHOLE] * 12,
    )


def local_body(
    sizes, qkv_ref, pack_ref, pack_t_ref, trans_ref, mixed_t_ref, decay_ref, grad_ref, weight_ref, *outs
):
    heads, levels, bits = sizes
    (attn_ref, attn_t_ref, prod_t_ref, scores_ref, mix_ref, mixed_ref, local_ref, hat_ref,
     hat_t_ref, grad_normed_ref) = outs
    grad_normed_ref[...] = mm_nt(grad_ref[...], weight_ref[...])
    rows = pack_ref.shape[0]
    decay_col = levels * heads
    beta_col = decay_col + heads
    pack = pack_ref[...]
    pack_t = pack_t_ref[...]
    row_id, col_id = pair_ids(rows)
    apart = row_id ^ col_id
    for head in range(heads):
        scores = mm_nt_fine(qkv_ref[0, head], qkv_ref[1, head]) * decay_ref[head].astype(F32)
        scores_ref[head] = scores.astype(BF16)
        mix_ref[head] = level_mix(pack, head, heads, bits, apart).astype(BF16)
        mixed_ref[head] = mixed_t_ref[head].astype(F32).T.astype(BF16)
    for head in range(heads):
        attn = mm(scores_ref[head], trans_ref[head])
        attn_ref[head] = attn.astype(BF16)
        attn_t_ref[head] = attn.T.astype(BF16)
        attn = attn * pack_t[beta_col + head : beta_col + head + 1, :]
        prod = attn * mix_ref[head].astype(F32)
        prod_t_ref[head] = prod.T.astype(BF16)
        growth = jnp.exp(column(pack, decay_col + head))
        local_ref[head] = mm(prod, qkv_ref[2, head])
        hat = growth * qkv_ref[0, head] - mm(attn, growth * qkv_ref[1, head])
        hat_ref[head] = hat.astype(BF16)
        hat_t_ref[head] = hat.T.astype(BF16)


def local_part(arrays, levels, bits):
    heads, rows, key = arrays[0].shape[1:]
    square = (heads, rows, rows)
    out_shape = (
        kept(square, BF16),
        kept(square, BF16),
        kept(square, BF16),
        kept(square, BF16),
        kept(square, BF16),
        kept((heads, rows, key), BF16),
        kept((heads, rows, key), F32),
        kept((heads, rows, key), BF16),
        kept((heads, key, rows), BF16),
        kept((rows, heads * key), F32),
    )
    return local_call(
        functools.partial(local_body, (heads, levels, bits)), "local_part", 10, out_shape,
        [], arrays,
    )


def join_pair(upper, own, other):
    key = own.shape[0]
    low = jnp.where(upper, other, own)
    high = jnp.where(upper, own, other)
    moved = mm(high[:, :key], low)
    late = jnp.concatenate([jnp.zeros((key, key), F32), high[:, key:].astype(F32)], 1)
    return (moved + late).astype(BF16)


def join_body(place_ref, own_ref, other_ref, out_ref):
    half = out_ref.shape[0]
    upper = (place_ref[0] & 1) == 1
    for slot in range(half):
        head = (place_ref[0] & 1) * half + slot
        out_ref[slot] = join_pair(upper, own_ref[head], other_ref[head])


def join_half(place, own, other):
    half = (own.shape[0] // 2,) + own.shape[1:]
    return local_call(join_body, "join_half", 6, [kept(half, BF16)], [place], [own, other])[0]


def gather_node(head, bit, first, near, uppers):
    if bit == 0:
        mine, theirs = near[first]
        half = mine.shape[0]
        here = uppers[0] if head >= half else jnp.logical_not(uppers[0])
        return jnp.where(here, mine[head % half], theirs[head % half])
    own = gather_node(head, bit - 1, first, near, uppers)
    other = gather_node(head, bit - 1, first ^ (1 << (bit - 1)), near, uppers)
    return join_pair(uppers[bit], own, other)


def reach_body(
    sizes, place_ref, gain_ref, pack_ref, local_ref, hat_ref, grad_ref, weight_ref, *refs
):
    heads, bits, far, count, near_count = sizes
    first_ref = refs[0]
    near = [None] + [(refs[1 + at], refs[1 + near_count + at]) for at in range(near_count)]
    refs = refs[2 * near_count + 1 :]
    out_refs = refs[:2]
    dout_ref, found_ref, prefix_ref, dfar_ref = refs[2:6]
    nodes = refs[6:-1]
    normed_ref = refs[-1]
    rows = pack_ref.shape[0]
    key = hat_ref.shape[2]
    pack = pack_ref[...]
    gain = gain_ref[...]
    lane = lane_of(rows)
    all_heads = range(heads)
    uppers = [((place_ref[0] >> bit) & 1) == 1 for bit in range(far)]
    others = []
    for bit in range(far):
        if bit == 0:
            others.append([first_ref[head] for head in all_heads])
        else:
            others.append(
                [gather_node(head, bit - 1, 1 << (bit - 1), near, uppers) for head in all_heads]
            )
            for head in all_heads:
                nodes[bit - 1][head] = others[bit][head]
    eye_key = jnp.where(pair_ids(key)[0] == pair_ids(key)[1], 1.0, 0.0).astype(BF16)
    prefix = [eye_key for head in all_heads]
    found = []
    for bit in range(far):
        for head in all_heads:
            prefix_ref[head, bit] = prefix[head]
        moved = [mm(prefix[head], others[bit][head]) for head in all_heads]
        found.append([jnp.where(uppers[bit], m[:, key:], 0.0).astype(BF16) for m in moved])
        prefix = [
            jnp.where(uppers[bit], moved[head][:, :key].astype(BF16), prefix[head])
            for head in all_heads
        ]
    found = [jnp.concatenate([found[bit][head] for bit in range(far)], 1) for head in all_heads]
    reached = [mm(hat_ref[head], found[head]) for head in all_heads]
    dfar = jnp.zeros((rows, LANES), F32)
    for head in all_heads:
        found_ref[head] = found[head]
        summed = local_ref[head]
        parts = []
        for bit in range(far):
            parts.append(reached[head][:, bit * key : (bit + 1) * key])
            summed = summed + column(pack, (bits + 1 + bit) * heads + head) * parts[bit]
        scale = lax.rsqrt(jnp.mean(summed * summed, -1, keepdims=True) + EPS)
        unit = summed * scale
        normed_ref[:, head * key : (head + 1) * key] = (unit * gain).astype(BF16)
        pulled = grad_ref[:, head * key : (head + 1) * key] * gain
        dout = scale * (pulled - unit * jnp.mean(pulled * unit, -1, keepdims=True))
        dout_ref[head] = dout
        for bit in range(far):
            col = (bits + 1 + bit) * heads + head
            dfar = jnp.where(lane == col, row_sum(dout * parts[bit]), dfar)
    dfar_ref[...] = dfar
    size = weight_ref.shape[1] // count
    for mask in range(count):
        dest = place_ref[1] ^ mask
        cols = pl.ds(pl.multiple_of(dest * size, size), size)
        out_refs[mask % 2][mask // 2] = jnp.dot(
            normed_ref[...], weight_ref[:, cols], preferred_element_type=F32
        ).astype(BF16)


def reach(place, arrays, first, near, bits, far, count):
    gain, pack, local_out, hat, grad_normed, weight = arrays
    heads, rows, key = hat.shape
    nodes = tuple(kept(first.shape, BF16) for bit in range(1, far))
    size = weight.shape[1] // count
    out_shape = (kept((count // 2, rows, size), BF16),) * 2 + (
        kept((heads, rows, key), F32),
        kept((heads, key, far * key), BF16),
        kept((heads, far, key, key), BF16),
        kept((rows, LANES), F32),
    ) + nodes
    mine, theirs = near
    got = local_call(
        functools.partial(reach_body, (heads, bits, far, count, len(mine))), "reach", 10, out_shape,
        [place], [*arrays, first, *mine, *theirs], [pltpu.VMEM((rows, heads * key), BF16)],
    )
    return got[:2], got[2:6], got[6:]


def return_body(sizes, place_ref, pack_ref, hat_t_ref, dout_ref, found_ref, prefix_ref, *refs):
    heads, bits, far = sizes
    others = refs[:far]
    dhat_ref = refs[far]
    sends = refs[far + 1 :]
    key = hat_t_ref.shape[1]
    pack = pack_ref[...]
    all_heads = range(heads)
    uppers = [((place_ref[0] >> bit) & 1) == 1 for bit in range(far)]
    spread = []
    for head in all_heads:
        parts = []
        for bit in range(far):
            weight = column(pack, (bits + 1 + bit) * heads + head)
            parts.append((weight * dout_ref[head]).astype(BF16))
        spread.append(jnp.concatenate(parts, 1))
    dfound = [mm(hat_t_ref[head], spread[head]) for head in all_heads]
    for head in all_heads:
        dhat_ref[head] = mm_nt(spread[head], found_ref[head])
    dprefix = [jnp.zeros((key, key), F32) for head in all_heads]
    for bit in reversed(range(far)):
        dfree = [
            jnp.where(uppers[bit], d[:, bit * key : (bit + 1) * key], 0.0) for d in dfound
        ]
        both = [
            jnp.concatenate([jnp.where(uppers[bit], dprefix[head], 0.0), dfree[head]], 1)
            for head in all_heads
        ]
        for head in all_heads:
            sent = dfree[head] if bit == far - 1 else both[head]
            sends[bit][head] = mm_tn(prefix_ref[head, bit], sent).astype(BF16)
        if bit > 0:
            moved = [mm_nt(both[head], others[bit][head]) for head in all_heads]
            dprefix = [
                jnp.where(uppers[bit], moved[head], dprefix[head]) for head in all_heads
            ]


def return_states(place, pack, hat_t, dout, found, prefix, others, bits):
    heads, rows, key = dout.shape
    far = len(others)
    sends = tuple(
        kept((heads, key, (1 if bit == far - 1 else 2) * key), BF16) for bit in range(far)
    )
    got = local_call(
        functools.partial(return_body, (heads, bits, far)), "return_states", 8,
        (kept(dout.shape, F32),) + sends, [place], [pack, hat_t, dout, found, prefix, *others],
    )
    return got[0], got[1:]


def add_body(*refs):
    count = len(refs) // 3
    for at in range(count):
        left, right = refs[at][...].astype(F32), refs[count + at][...].astype(F32)
        refs[2 * count + at][...] = (left + right).astype(BF16)


def add_all(left, right):
    out_shape = [kept(value.shape, BF16) for value in left]
    return local_call(add_body, "add_all", 6, out_shape, [], [*left, *right])


def lower_pull(dlower, base, lower, beta, decay, strict, k_in):
    dlower = jnp.where(strict, dlower, 0.0)
    dbeta = row_sum(dlower * base.astype(F32))
    dgram = dlower * (beta * decay)
    dkey = mm(dgram, k_in) + mm_tn(dgram, k_in)
    return dbeta, beta * dbeta, col_sum(dlower * lower.astype(F32)), dkey


def pull_body(sizes, *refs):
    heads, levels, bits = sizes
    (qkv_ref, pack_ref, pack_t_ref, trans_ref, attn_ref, attn_t_ref, prod_t_ref, scores_ref,
     mix_ref, decay_ref, base_ref, lower_ref, dout_ref, dhat_ref) = refs[:14]
    dqkv_ref, dgrown_ref, dcol_ref, drow_ref = refs[14:]
    rows = pack_ref.shape[0]
    decay_col = levels * heads
    beta_col = decay_col + heads
    block_bit = BLOCK.bit_length() - 1
    pack = pack_ref[...]
    pack_t = pack_t_ref[...]
    row_id, col_id = pair_ids(rows)
    strict = row_id > col_id
    apart = row_id ^ col_id
    lane = lane_of(rows)
    all_heads = range(heads)
    dcol = jnp.zeros((rows, LANES), F32)
    dbeta_rows, dcum_rows, dattn_all = [], [], []
    for head in all_heads:
        high, low = split(dout_ref[head])
        v_in = qkv_ref[2, head].astype(BF16)
        dprod = mm_nt(high, v_in) + mm_nt(low, v_in)
        dqkv_ref[2, head] = mm(prod_t_ref[head], high)
        beta_row = pack_t[beta_col + head : beta_col + head + 1, :]
        growth = jnp.exp(column(pack, decay_col + head))
        attn0 = attn_ref[head].astype(F32)
        touched = dprod * (attn0 * beta_row)
        for level in range(bits + 1):
            if level == 0:
                here = (apart >> block_bit) == 0
            else:
                here = (apart >> (block_bit + level - 1)) == 1
            dcol = jnp.where(
                lane == level * heads + head, row_sum(jnp.where(here, touched, 0.0)), dcol
            )
        dattn = dprod * mix_ref[head].astype(F32) - mm_nt(dhat_ref[head], growth * qkv_ref[1, head])
        dbeta_rows.append(col_sum(dattn * attn0))
        dattn_all.append((dattn * beta_row).astype(BF16))
    dscore_all = [mm_nt(dattn_all[head], trans_ref[head]) for head in all_heads]
    moved_all = []
    for head in all_heads:
        both = jnp.concatenate(
            [dscore_all[head].astype(BF16), dhat_ref[head].astype(BF16)], 1
        )
        moved_all.append(mm(attn_t_ref[head], both))
    for head in all_heads:
        q_in, k_in = qkv_ref[0, head], qkv_ref[1, head]
        beta = column(pack, beta_col + head)
        growth = jnp.exp(column(pack, decay_col + head))
        dscore = dscore_all[head]
        decay = decay_ref[head].astype(F32)
        dprobs = dscore * decay
        shift = dscore * scores_ref[head].astype(F32)
        dgrown_ref[head] = -beta * moved_all[head][:, rows:]
        dbeta, dcum_col, dcum_row, dk_lower = lower_pull(
            -moved_all[head][:, :rows], base_ref[head], lower_ref[head], beta, decay, strict, k_in
        )
        dhat = dhat_ref[head]
        dqkv_ref[0, head] = growth * dhat + mm(dprobs, k_in)
        dqkv_ref[1, head] = mm_tn(dprobs, q_in) + dk_lower
        dcum_col = dcum_col + row_sum(shift) + growth * row_sum(q_in * dhat)
        dcum_rows.append(-dcum_row - col_sum(shift))
        dcol = jnp.where(lane == beta_col + head, dbeta, dcol)
        dcol = jnp.where(lane == decay_col + head, dcum_col, dcol)
    dcol_ref[...] = dcol
    drow_ref[...] = jnp.concatenate(dcum_rows + dbeta_rows, 0)


def pull_local(arrays, levels, bits):
    heads, rows, key = arrays[0].shape[1:]
    out_shape = (
        kept((3, heads, rows, key), F32),
        kept((heads, rows, key), F32),
        kept((rows, LANES), F32),
        kept((2 * heads, rows), F32),
    )
    return local_call(
        functools.partial(pull_body, (heads, levels, bits)), "pull_local", 12, out_shape, [], arrays
    )


def finish_body(sizes, place_ref, *refs):
    heads, levels, far, count, arrived_counts = sizes
    (qkv_ref, gate_ref, pack_ref, trans_ref, mixed_ref, decay_ref, base_ref, lower_ref,
     dqkv_ref, dgrown_ref, dcol_ref, drow_ref, dfar_ref, rates_ref, small_ref) = refs[:15]
    others = refs[15 : 15 + far]
    refs = refs[15 + far :]
    arrived = []
    for found in arrived_counts:
        arrived.append(refs[:found])
        refs = refs[found:]
    wr_hbm = refs[0]
    out_refs = refs[1 : 1 + count]
    dproj, wr_ref, sem = refs[1 + count :]
    fetch = pltpu.make_async_copy(wr_hbm, wr_ref, sem)
    fetch.start()
    rows = pack_ref.shape[0]
    key = qkv_ref.shape[3]
    decay_col = levels * heads
    beta_col = decay_col + heads
    norm_col = beta_col + heads
    place = place_ref[0]
    all_heads = range(heads)
    uppers = [((place >> bit) & 1) == 1 for bit in range(far)]
    pack = pack_ref[...]
    row_id, col_id = pair_ids(rows)
    strict = row_id > col_id
    lane = lane_of(rows)
    last_row = lax.broadcasted_iota(jnp.int32, (rows, 1), 0) == rows - 1
    eye_key = (pair_ids(key)[0] == pair_ids(key)[1]).astype(F32)
    dpair = [jnp.zeros((key, 2 * key), F32) for head in all_heads]
    for bit in reversed(range(far)):
        for head in all_heads:
            got = arrived[bit][0][head].astype(F32)
            for more in arrived[bit][1:]:
                got = got + more[head].astype(F32)
            other = others[bit][head]
            if bit == far - 1:
                got = jnp.concatenate([jnp.zeros((key, key), F32), got], 1)
                dpair[head] = jnp.where(uppers[bit], 0.0, got)
            else:
                as_low = mm_tn(other[:, :key], dpair[head]) + got
                as_high = mm_nt(dpair[head], other)
                as_high = jnp.concatenate([as_high, dpair[head][:, key:]], 1)
                dpair[head] = jnp.where(uppers[bit], as_high, as_low)
    moved_all, dmixed_all = [], []
    for head in all_heads:
        beta = column(pack, beta_col + head)
        growth = jnp.exp(column(pack, decay_col + head))
        both = jnp.concatenate([-growth * qkv_ref[1, head], qkv_ref[2, head]], 1)
        dmixed_all.append(mm_nt(both, dpair[head]))
        moved_all.append(mm(beta * mixed_ref[head].astype(F32), dpair[head]))
    dtail_all = [
        mm(trans_ref[head], column(pack, beta_col + head) * dmixed_all[head])
        for head in all_heads
    ]
    dlower_all = [-mm_nt(mixed_ref[head], dtail_all[head]) for head in all_heads]
    dcol = jnp.where(lane < decay_col, dcol_ref[...] + dfar_ref[...], dcol_ref[...])
    dcum_rows = []
    for head in all_heads:
        q_in, k_in = qkv_ref[0, head], qkv_ref[1, head]
        beta = column(pack, beta_col + head)
        cum_col = column(pack, decay_col + head)
        growth = jnp.exp(cum_col)
        last = cum_col[rows - 1 : rows, :]
        tail = jnp.exp(last - cum_col)
        dgrown = dgrown_ref[head] - moved_all[head][:, :key]
        dv = dqkv_ref[2, head] + moved_all[head][:, key:]
        dbeta_more = row_sum(mixed_ref[head].astype(F32) * dmixed_all[head])
        dtail = dtail_all[head]
        dbeta, dcum_col, dcum_row, dk_lower = lower_pull(
            dlower_all[head], base_ref[head], lower_ref[head], beta, decay_ref[head].astype(F32),
            strict, k_in
        )
        dcum_rows.append(-dcum_row)
        tail_pull = tail * row_sum(k_in * dtail)
        trace = col_sum(row_sum(dpair[head][:, :key] * eye_key))
        at_last = col_sum(tail_pull) + jnp.exp(last) * trace
        dcum_col = dcum_col + growth * row_sum(k_in * dgrown) - tail_pull
        dcum_col = dcum_col + jnp.where(last_row, at_last, 0.0)
        dk = dqkv_ref[1, head] + dk_lower + growth * dgrown + tail * dtail
        dq = dqkv_ref[0, head]
        dcol = dcol + jnp.where(lane == beta_col + head, dbeta + dbeta_more, 0.0)
        dcol = dcol + jnp.where(lane == decay_col + head, dcum_col, 0.0)
        for part, unit, dunit in ((0, q_in, dq), (1, k_in, dk)):
            scale = column(pack, norm_col + part * heads + head)
            back = scale * (dunit - unit * row_sum(unit * dunit))
            col = (part * heads + head) * key
            dproj[:, col : col + key] = back.astype(BF16)
        col = (2 * heads + head) * key
        dproj[:, col : col + key] = dv.astype(BF16)
    drow = drow_ref[...]
    drow = drow + jnp.concatenate(dcum_rows + [jnp.zeros((heads, rows), F32)], 0)
    drow = jnp.concatenate(
        [jnp.zeros((decay_col, rows), F32), drow,
         jnp.zeros((LANES - norm_col, rows), F32)], 0
    )
    dcol = dcol + drow.T
    rate, bias = rates_ref[0:1, :], rates_ref[1:2, :]
    switch = jax.nn.sigmoid(gate_ref[...] + bias)
    dlog = mm_full((row_id <= col_id).astype(F32), dcol)
    slope = switch * (1.0 - switch)
    dgate = jnp.where(
        lane < decay_col,
        dcol * switch,
        jnp.where(lane < beta_col, -rate * dlog * slope, dcol * slope),
    )
    dgate = jnp.where(lane < norm_col, dgate, 0.0).astype(BF16)
    fetch.wait()
    size = out_refs[0].shape[1]
    for shift in range(count):
        dest = lax.rem(place_ref[1] + shift, count)
        span = pl.ds(pl.multiple_of(dest * size, size), size)
        part = mm_nt(dproj[...], wr_ref[span, :]) + mm(dgate, small_ref[:, span])
        out_refs[shift][...] = part.astype(BF16)


def finish(place, arrays, others, arrived, wr, levels, count):
    rows = arrays[0].shape[2]
    width, cols = wr.shape
    far = len(others)
    counts = tuple(len(group) for group in arrived)
    heads = arrays[0].shape[1]
    flat = [value for group in arrived for value in group]
    scratch = [
        pltpu.VMEM((rows, cols), BF16), pltpu.VMEM(wr.shape, BF16), pltpu.SemaphoreType.DMA
    ]
    return local_call(
        functools.partial(finish_body, (heads, levels, far, count, counts)), "finish", 16,
        [kept((rows, width // count), BF16)] * count,
        [place], [*arrays, *others, *flat], scratch, [wr],
    )


def swap(value, axis, mask):
    size = lax.axis_size(axis)
    return lax.ppermute(value, axis, [(at, at ^ mask) for at in range(size)])


def sum_body(*refs):
    total = refs[0][...].astype(F32)
    for ref in refs[1:-1]:
        total = total + ref[...].astype(F32)
    refs[-1][...] = total.astype(BF16)


def sum_all(values, keep):
    out = kept if keep else jax.ShapeDtypeStruct
    return local_call(sum_body, "sum_all", 6, [out(values[0].shape, BF16)], [], values)[0]


def shift_sum(parts, axis):
    count = lax.axis_size(axis)
    values = [parts[0]]
    for shift in range(1, count):
        pairs = [(at, (at + shift) % count) for at in range(count)]
        values.append(lax.ppermute(parts[shift], axis, pairs))
    return sum_all(values, False)


def halve_body(own_ref, got_ref, keep_ref, send_ref):
    for at in range(own_ref.shape[0]):
        total = own_ref[at].astype(F32) + got_ref[at].astype(F32)
        target = send_ref if at % 2 else keep_ref
        target[at // 2] = total.astype(target.dtype)


def halving_sum(keep, send, axis):
    mask = 1
    while keep.shape[0] > 1:
        got = swap(send, axis, mask)
        half = (keep.shape[0] // 2,) + keep.shape[1:]
        keep, send = local_call(
            halve_body, "halve", 6, [kept(half, F32), kept(half, BF16)], [], [keep, got]
        )
        mask *= 2
    return sum_all([keep, swap(send, axis, mask)], False)[0]


def on_device(tokens, qkv_weight, small_weight, head_param, norm_gain, out_weight, grad_out):
    rows, width = tokens.shape
    heads, key = qkv_weight.shape[2:]
    levels = small_weight.shape[2] - 2
    bits = (rows // BLOCK).bit_length() - 1
    size = lax.axis_size("ctx")
    far = size.bit_length() - 1
    count = lax.axis_size("head")
    place = jnp.stack([lax.axis_index("ctx"), lax.axis_index("head")]).astype(jnp.int32)
    flat_w = qkv_weight.reshape(width * 3 * heads, key)
    small = jnp.transpose(small_weight, (2, 1, 0))
    rates = head_param.T
    flat_out = out_weight.reshape(heads * key, width)
    gain = norm_gain.reshape(1, key)

    (wr, small_t, qkv, gate, pack, pack_t, trans, mixed_t, decay, base, lower, rates_row,
     pair) = project(
        place, tokens, flat_w, small, rates, heads, levels
    )
    first = swap(pair, "ctx", 1)
    node = join_half(place, pair, first)
    mine = [swap(node, "ctx", 2 * at) for at in range(1, size // 2)]
    (attn, attn_t, prod_t, scores, mix, mixed, local_out, hat, hat_t, grad_normed) = local_part(
        [qkv, pack, pack_t, trans, mixed_t, decay, grad_out, flat_out], levels, bits
    )
    mine, local_out, grad_normed = lax.optimization_barrier((mine, local_out, grad_normed))
    theirs = [swap(value, "ctx", 1) for value in mine]
    out_parts, (dout, found, prefix, dfar), nodes = reach(
        place, [gain, pack, local_out, hat, grad_normed, flat_out], first, (mine, theirs),
        bits, far, count
    )
    layer_out = halving_sum(*out_parts, "head")
    others = [first, *nodes]
    dhat, sends = return_states(place, pack, hat_t, dout, found, prefix, others, bits)
    got = [swap(value, "ctx", 1) for value in sends]
    arrived = [[got[0]]]
    sums = add_all(sends[1:], got[1:])
    for bit in range(1, far):
        half = 1 << (bit - 1)
        arrived.append([swap(sums[bit - 1], "ctx", 2 * at) for at in range(half, 2 * half)])
    dqkv, dgrown, dcol, drow = pull_local(
        [qkv, pack, pack_t, trans, attn, attn_t, prod_t, scores, mix, decay, base, lower, dout,
         dhat],
        levels, bits,
    )
    arrays = [qkv, gate, pack, trans, mixed, decay, base, lower, dqkv, dgrown, dcol, drow, dfar,
              rates_row, small_t]
    parts = finish(place, arrays, others, arrived, wr, levels, count)
    return layer_out, shift_sum(parts, "head")


def solution(mesh):
    placed = (
        P("ctx", None),
        P(None, None, "head", None),
        P(None, "head", None),
        P("head", None),
        P(),
        P("head", None, None),
        P("ctx", None),
    )
    return jax.shard_map(
        on_device,
        mesh=mesh,
        in_specs=placed,
        out_specs=(P("ctx", "head"), P("ctx", "head")),
        check_vma=False,
    )
```

```python
import functools

import jax
import jax.numpy as jnp
from jax import lax
from jax.experimental import pallas as pl
from jax.experimental.pallas import tpu as pltpu
from jax.sharding import PartitionSpec as P

BLOCK = 64
LANES = 128
EPS = 1e-06
MIB = 1024 * 1024
F32 = jnp.float32
BF16 = jnp.bfloat16
WHOLE = pl.BlockSpec(memory_space=pltpu.VMEM)
SCALARS = pl.BlockSpec(memory_space=pltpu.SMEM)
HBM = pl.BlockSpec(memory_space=pltpu.HBM)


def contract(left, right, dim_left, dim_right):
    return lax.dot_general(
        left.astype(BF16),
        right.astype(BF16),
        (((dim_left,), (dim_right,)), ((), ())),
        preferred_element_type=F32,
    )


def mm(left, right):
    return contract(left, right, 1, 0)


def mm_nt(left, right):
    return contract(left, right, 1, 1)


def mm_tn(left, right):
    return contract(left, right, 0, 0)


def split(values):
    high = values.astype(BF16)
    return high, (values - high.astype(F32)).astype(BF16)


def mm_nt_fine(left, right):
    left_high, left_low = split(left)
    right_high, right_low = split(right)
    return mm_nt(left_high, right_high) + (mm_nt(left_low, right_high) + mm_nt(left_high, right_low))


def mm_full(left, right):
    return jnp.dot(left, right, precision=lax.Precision.HIGHEST, preferred_element_type=F32)


def pair_ids(count):
    row_id = lax.broadcasted_iota(jnp.int32, (count, count), 0)
    col_id = lax.broadcasted_iota(jnp.int32, (count, count), 1)
    return row_id, col_id


def row_sum(values):
    return jnp.sum(values, 1, keepdims=True)


def col_sum(values):
    return jnp.sum(values, 0, keepdims=True)


def lane_of(rows):
    return lax.broadcasted_iota(jnp.int32, (rows, LANES), 1)


def decay_of(pack, pack_t, col, inclusive):
    spread = pack[:, col : col + 1] - pack_t[col : col + 1, :]
    return jnp.where(inclusive, jnp.exp(jnp.minimum(spread, 0.0)), 0.0)


def kept(shape, dtype):
    return pltpu.VMEM(shape, dtype)


def stored(shape, dtype):
    return pltpu.HBM(shape, dtype)


def pin(values, space):
    return [pltpu.with_memory_space_constraint(value, space) for value in values]


def local_call(
    body, name, limit, out_shape, scalars, arrays, scratch=(), remote=(), out_specs=None
):
    return pl.pallas_call(
        body,
        out_shape=tuple(out_shape),
        in_specs=[SCALARS] * len(scalars)
        + [WHOLE] * len(arrays)
        + [HBM] * len(remote),
        out_specs=tuple(out_specs or [WHOLE] * len(out_shape)),
        scratch_shapes=list(scratch),
        compiler_params=pltpu.CompilerParams(vmem_limit_bytes=limit * MIB),
        name=name,
    )(*scalars, *pin(arrays, pltpu.VMEM), *pin(remote, pltpu.HBM))


def column(pack, at):
    return pack[:, at : at + 1]


def level_mix(pack, head, heads, bits, apart):
    block_bit = BLOCK.bit_length() - 1
    mixed = jnp.broadcast_to(column(pack, head), apart.shape)
    for level in range(1, bits + 1):
        here = (apart >> (block_bit + level - 1)) >= 1
        mixed = jnp.where(here, column(pack, level * heads + head), mixed)
    return mixed


def head_rows(hp_ref, heads, decay_col, beta_col):
    lane_row = lane_of(1)
    rate = jnp.zeros((1, LANES), F32)
    bias = jnp.zeros((1, LANES), F32)
    for head in range(heads):
        rate = jnp.where(lane_row == decay_col + head, hp_ref[0:1, head : head + 1], rate)
        bias = jnp.where(lane_row == beta_col + head, hp_ref[1:2, head : head + 1], bias)
    return rate, bias


def merge_blocks(trans_all, edge_all, levels, first):
    if first:
        powers = [edge.astype(BF16) for edge in edge_all]
        trans_all = [trans - power for trans, power in zip(trans_all, powers)]
    else:
        powers = [mm(edge, trans).astype(BF16) for edge, trans in zip(edge_all, trans_all)]
        yield
        trans_all = [
            trans - mm(trans, power).astype(BF16) for trans, power in zip(trans_all, powers)
        ]
    for level in range(1, levels):
        powers = [mm(power, power).astype(BF16) for power in powers]
        yield
        trans_all = [
            trans + mm(trans, power).astype(BF16) for trans, power in zip(trans_all, powers)
        ]
    return trans_all


def invert(lower_all, eye, apart, rows):
    trans_all = [eye.astype(BF16) for lower in lower_all]
    bits = rows.bit_length() - 1
    start = 0
    while start < bits:
        levels = min(2 if bits - start == 2 else 3, bits - start)
        here = jnp.logical_and((apart >> start) >= 1, (apart >> (start + levels)) == 0)
        edge_all = [jnp.where(here, lower, 0.0) for lower in lower_all]
        trans_all = yield from merge_blocks(trans_all, edge_all, levels, start == 0)
        start += levels
        yield
    rest_all = []
    for trans, lower in zip(trans_all, lower_all):
        high, low = split(lower)
        rest_all.append(eye - trans.astype(F32) - mm(high, trans) - mm(low, trans))
    yield
    return [
        (trans.astype(F32) + mm(trans, rest)).astype(BF16)
        for trans, rest in zip(trans_all, rest_all)
    ]


def project_body(sizes, place_ref, hp_hbm, tokens_hbm, w_hbm, small_hbm, *refs):
    heads, levels, chunks = sizes
    (wr_hbm, small_ref, qkv_ref, gate_ref, pack_ref, pack_t_ref, trans_ref, mixed_t_ref,
     decay_ref, base_ref, lower_ref, rates_ref, pair_ref) = refs[:13]
    tokens, wide_in, wide, wr, small_in, small_wide, acc, hp_ref, sems = refs[13:]
    rows, width = tokens.shape
    depth = width // chunks
    cols = 3 * heads
    fetch_tokens = pltpu.make_async_copy(tokens_hbm, tokens, sems.at[chunks])
    fetch_small = pltpu.make_async_copy(small_hbm, small_in, sems.at[chunks + 1])
    fetch_rates = pltpu.make_async_copy(hp_hbm, hp_ref, sems.at[chunks + 2])
    half = width // 2
    keeps = []
    for at in range(6):
        span = (pl.ds(at % 2 * half, half), pl.ds(at // 2 * heads * LANES, heads * LANES))
        keeps.append(pltpu.make_async_copy(wr.at[span], wr_hbm.at[span], sems.at[chunks + 3 + at]))
    fetches = []
    for chunk in range(chunks):
        span = pl.ds(chunk * depth * cols, depth * cols)
        fetches.append(
            pltpu.make_async_copy(w_hbm.at[span, :], wide_in.at[span, :], sems.at[chunk])
        )
    fetch_small.start()
    fetch_rates.start()
    fetch_tokens.start()
    for fetch in fetches:
        fetch.start()
    decay_col = levels * heads
    beta_col = decay_col + heads
    norm_col = beta_col + heads
    lane = lane_of(rows)
    row_id, col_id = pair_ids(rows)
    inclusive = row_id >= col_id
    strict = row_id > col_id
    apart = row_id ^ col_id
    eye = (row_id == col_id).astype(F32)
    fetch_small.wait()
    small_rows = small_in.shape[0] * heads
    for level in range(small_in.shape[0]):
        small_wide[level * heads : (level + 1) * heads, :] = small_in[level].astype(F32)
    small_wide[small_rows:, :] = jnp.zeros((LANES - small_rows, width), F32)
    small_ref[...] = small_wide[...].astype(BF16)
    fetch_rates.wait()
    rate, bias = head_rows(hp_ref, heads, decay_col, beta_col)
    rates_ref[0:1, :] = rate
    rates_ref[1:2, :] = bias
    fetch_tokens.wait()
    gate = mm_nt(tokens[...], small_ref[...])
    gate_ref[...] = gate
    switch = jax.nn.sigmoid(gate + bias)
    lam = jnp.maximum(gate, 0.0) + jnp.log1p(jnp.exp(-jnp.abs(gate)))
    cum = mm_full(inclusive.astype(F32), -rate * switch)
    pack = jnp.where(lane < decay_col, lam, jnp.where(lane < beta_col, cum, switch))
    pack_t = pack.T
    pack_t_ref[...] = pack_t

    def extract(chunk, part):
        at = chunk * depth
        for col in range(part * heads, (part + 1) * heads):
            value = wide[pl.ds(at * cols + col, depth, stride=cols), :]
            wr[at : at + depth, col * LANES : (col + 1) * LANES] = value.astype(BF16)

    def multiply(part, first, last):
        span = slice((part * heads) * LANES, (part + 1) * heads * LANES)
        own = jnp.dot(
            tokens[:, first * depth : last * depth], wr[first * depth : last * depth, span],
            preferred_element_type=F32,
        )
        if first == 0:
            acc[:, span] = own
        else:
            acc[:, span] += own

    for chunk in range(chunks):
        fetches[chunk].wait()
        at = chunk * depth * cols
        wide[at : at + depth * cols, :] = wide_in[at : at + depth * cols, :].astype(F32)
        extract(chunk, 1)
        if chunk % 2 == 1:
            multiply(1, chunk - 1, chunk + 1)

    def unit_of(part, head):
        col = (part * heads + head) * LANES
        raw = acc[:, col : col + LANES]
        scale = lax.rsqrt(row_sum(raw * raw) + EPS)
        qkv_ref[part, head] = raw * scale
        return raw * scale, jnp.where(lane == norm_col + part * heads + head, scale, 0.0)

    scales = jnp.zeros((rows, LANES), F32)
    k_all, lower_all = [], []
    for head in range(heads):
        unit, scale = unit_of(1, head)
        k_all.append(unit)
        scales = scales + scale
        decay = decay_of(pack, pack_t, decay_col + head, inclusive)
        decay_ref[head] = decay.astype(BF16)
        base = jnp.where(strict, decay * mm_nt(unit, unit), 0.0)
        base_ref[head] = base.astype(BF16)
        lower = column(pack, beta_col + head) * base
        lower_ref[head] = lower.astype(BF16)
        lower_all.append(lower)

    keeps[2].start()
    keeps[3].start()

    def later():
        for part in (2, 0):
            for chunk in range(chunks):
                extract(chunk, part)
                if chunk % 4 == 3:
                    multiply(part, chunk - 3, chunk + 1)
                    keeps[2 * part + chunk // 4].start()
                if chunk % 2 == 1:
                    yield

    chain, filler = invert(lower_all, eye, apart, rows), later()
    while True:
        try:
            next(chain)
        except StopIteration as stop:
            trans_all = stop.value
            break
        next(filler, None)
    for _ in filler:
        pass
    mixed_all = []
    for head in range(heads):
        trans_ref[head] = trans_all[head]
        cum_row = pack_t[decay_col + head : decay_col + head + 1, :]
        tail_t = k_all[head].T * jnp.exp(cum_row[:, rows - 1 :] - cum_row)
        mixed_all.append(mm(tail_t, trans_all[head]).astype(BF16))
    eye_key = eye[:LANES, :LANES]
    for head in range(heads):
        mixed_t_ref[head] = mixed_all[head]
        col = (2 * heads + head) * LANES
        v_in = acc[:, col : col + LANES]
        qkv_ref[2, head] = v_in
        cum_col = column(pack, decay_col + head)
        beta = column(pack, beta_col + head)
        grown = (beta * jnp.exp(cum_col)) * k_all[head]
        both = jnp.concatenate([-grown, beta * v_in], 1)
        pair = mm(mixed_all[head], both)
        last = jnp.exp(cum_col[rows - 1 : rows, :])
        pair_ref[head, :, :LANES] = (last * eye_key + pair[:, :LANES]).astype(BF16)
        pair_ref[head, :, LANES:] = pair[:, LANES:].astype(BF16)
    for head in range(heads):
        scales = scales + unit_of(0, head)[1]
    pack_ref[...] = jnp.where(lane < norm_col, pack, scales)
    for keep in keeps:
        keep.wait()


def project(place, tokens, flat_w, small, head_param, heads, levels):
    rows, width = tokens.shape
    chunks = 8
    cols = 3 * heads
    key = flat_w.shape[1]
    square = (heads, rows, rows)
    out_shape = (
        stored((width, cols * key), BF16),
        kept((LANES, width), BF16),
        kept((3, heads, rows, key), F32),
        kept((rows, LANES), F32),
        kept((rows, LANES), F32),
        kept((LANES, rows), F32),
        kept(square, BF16),
        kept((heads, key, rows), BF16),
        kept(square, BF16),
        kept(square, BF16),
        kept(square, BF16),
        kept((2, LANES), F32),
        kept((heads, key, 2 * key), BF16),
    )
    scratch = [
        pltpu.VMEM(tokens.shape, BF16),
        pltpu.VMEM(flat_w.shape, BF16),
        pltpu.VMEM(flat_w.shape, F32),
        pltpu.VMEM((width, cols * key), BF16),
        pltpu.VMEM(small.shape, BF16),
        pltpu.VMEM((LANES, width), F32),
        pltpu.VMEM((rows, cols * key), F32),
        pltpu.VMEM(head_param.shape, F32),
        pltpu.SemaphoreType.DMA((chunks + 9,)),
    ]
    return local_call(
        functools.partial(project_body, (heads, levels, chunks)), "project", 36, out_shape,
        [place], [], scratch, [head_param, tokens, flat_w, small], [HBM] + [WHOLE] * 12,
    )


def local_body(
    sizes, qkv_ref, pack_ref, pack_t_ref, trans_ref, mixed_t_ref, decay_ref, grad_ref, weight_ref, *outs
):
    heads, levels, bits = sizes
    (attn_ref, attn_t_ref, prod_t_ref, scores_ref, mix_ref, mixed_ref, local_ref, hat_ref,
     hat_t_ref, grad_normed_ref) = outs
    grad_normed_ref[...] = mm_nt(grad_ref[...], weight_ref[...])
    rows = pack_ref.shape[0]
    decay_col = levels * heads
    beta_col = decay_col + heads
    pack = pack_ref[...]
    pack_t = pack_t_ref[...]
    row_id, col_id = pair_ids(rows)
    apart = row_id ^ col_id
    for head in range(heads):
        scores = mm_nt_fine(qkv_ref[0, head], qkv_ref[1, head]) * decay_ref[head].astype(F32)
        scores_ref[head] = scores.astype(BF16)
        mix_ref[head] = level_mix(pack, head, heads, bits, apart).astype(BF16)
        mixed_ref[head] = mixed_t_ref[head].astype(F32).T.astype(BF16)
    for head in range(heads):
        attn = mm(scores_ref[head], trans_ref[head])
        attn_ref[head] = attn.astype(BF16)
        attn_t_ref[head] = attn.T.astype(BF16)
        attn = attn * pack_t[beta_col + head : beta_col + head + 1, :]
        prod = attn * mix_ref[head].astype(F32)
        prod_t_ref[head] = prod.T.astype(BF16)
        growth = jnp.exp(column(pack, decay_col + head))
        local_ref[head] = mm(prod, qkv_ref[2, head])
        hat = growth * qkv_ref[0, head] - mm(attn, growth * qkv_ref[1, head])
        hat_ref[head] = hat.astype(BF16)
        hat_t_ref[head] = hat.T.astype(BF16)


def local_part(arrays, levels, bits):
    heads, rows, key = arrays[0].shape[1:]
    square = (heads, rows, rows)
    out_shape = (
        kept(square, BF16),
        kept(square, BF16),
        kept(square, BF16),
        kept(square, BF16),
        kept(square, BF16),
        kept((heads, rows, key), BF16),
        kept((heads, rows, key), F32),
        kept((heads, rows, key), BF16),
        kept((heads, key, rows), BF16),
        kept((rows, heads * key), F32),
    )
    return local_call(
        functools.partial(local_body, (heads, levels, bits)), "local_part", 10, out_shape,
        [], arrays,
    )


def join_pair(upper, own, other):
    key = own.shape[0]
    low = jnp.where(upper, other, own)
    high = jnp.where(upper, own, other)
    moved = mm(high[:, :key], low)
    late = jnp.concatenate([jnp.zeros((key, key), F32), high[:, key:].astype(F32)], 1)
    return (moved + late).astype(BF16)


def join_body(place_ref, own_ref, other_ref, out_ref):
    half = out_ref.shape[0]
    upper = (place_ref[0] & 1) == 1
    for slot in range(half):
        head = (place_ref[0] & 1) * half + slot
        out_ref[slot] = join_pair(upper, own_ref[head], other_ref[head])


def join_half(place, own, other):
    half = (own.shape[0] // 2,) + own.shape[1:]
    return local_call(join_body, "join_half", 6, [kept(half, BF16)], [place], [own, other])[0]


def gather_node(head, bit, first, near, uppers):
    if bit == 0:
        mine, theirs = near[first]
        half = mine.shape[0]
        here = uppers[0] if head >= half else jnp.logical_not(uppers[0])
        return jnp.where(here, mine[head % half], theirs[head % half])
    own = gather_node(head, bit - 1, first, near, uppers)
    other = gather_node(head, bit - 1, first ^ (1 << (bit - 1)), near, uppers)
    return join_pair(uppers[bit], own, other)


def reach_body(
    sizes, place_ref, gain_ref, pack_ref, local_ref, hat_ref, grad_ref, weight_ref, *refs
):
    heads, bits, far, count, near_count = sizes
    first_ref = refs[0]
    near = [None] + [(refs[1 + at], refs[1 + near_count + at]) for at in range(near_count)]
    refs = refs[2 * near_count + 1 :]
    out_refs = refs[:2]
    dout_ref, found_ref, prefix_ref, dfar_ref = refs[2:6]
    nodes = refs[6:-1]
    normed_ref = refs[-1]
    rows = pack_ref.shape[0]
    key = hat_ref.shape[2]
    pack = pack_ref[...]
    gain = gain_ref[...]
    lane = lane_of(rows)
    all_heads = range(heads)
    uppers = [((place_ref[0] >> bit) & 1) == 1 for bit in range(far)]
    others = []
    for bit in range(far):
        if bit == 0:
            others.append([first_ref[head] for head in all_heads])
        else:
            others.append(
                [gather_node(head, bit - 1, 1 << (bit - 1), near, uppers) for head in all_heads]
            )
            for head in all_heads:
                nodes[bit - 1][head] = others[bit][head]
    eye_key = jnp.where(pair_ids(key)[0] == pair_ids(key)[1], 1.0, 0.0).astype(BF16)
    prefix = [eye_key for head in all_heads]
    found = []
    for bit in range(far):
        for head in all_heads:
            prefix_ref[head, bit] = prefix[head]
        moved = [mm(prefix[head], others[bit][head]) for head in all_heads]
        found.append([jnp.where(uppers[bit], m[:, key:], 0.0).astype(BF16) for m in moved])
        prefix = [
            jnp.where(uppers[bit], moved[head][:, :key].astype(BF16), prefix[head])
            for head in all_heads
        ]
    found = [jnp.concatenate([found[bit][head] for bit in range(far)], 1) for head in all_heads]
    reached = [mm(hat_ref[head], found[head]) for head in all_heads]
    dfar = jnp.zeros((rows, LANES), F32)
    for head in all_heads:
        found_ref[head] = found[head]
        summed = local_ref[head]
        parts = []
        for bit in range(far):
            parts.append(reached[head][:, bit * key : (bit + 1) * key])
            summed = summed + column(pack, (bits + 1 + bit) * heads + head) * parts[bit]
        scale = lax.rsqrt(jnp.mean(summed * summed, -1, keepdims=True) + EPS)
        unit = summed * scale
        normed_ref[:, head * key : (head + 1) * key] = (unit * gain).astype(BF16)
        pulled = grad_ref[:, head * key : (head + 1) * key] * gain
        dout = scale * (pulled - unit * jnp.mean(pulled * unit, -1, keepdims=True))
        dout_ref[head] = dout
        for bit in range(far):
            col = (bits + 1 + bit) * heads + head
            dfar = jnp.where(lane == col, row_sum(dout * parts[bit]), dfar)
    dfar_ref[...] = dfar
    size = weight_ref.shape[1] // count
    for mask in range(count):
        dest = place_ref[1] ^ mask
        cols = pl.ds(pl.multiple_of(dest * size, size), size)
        out_refs[mask % 2][mask // 2] = jnp.dot(
            normed_ref[...], weight_ref[:, cols], preferred_element_type=F32
        ).astype(BF16)


def reach(place, arrays, first, near, bits, far, count):
    gain, pack, local_out, hat, grad_normed, weight = arrays
    heads, rows, key = hat.shape
    nodes = tuple(kept(first.shape, BF16) for bit in range(1, far))
    size = weight.shape[1] // count
    out_shape = (kept((count // 2, rows, size), BF16),) * 2 + (
        kept((heads, rows, key), F32),
        kept((heads, key, far * key), BF16),
        kept((heads, far, key, key), BF16),
        kept((rows, LANES), F32),
    ) + nodes
    mine, theirs = near
    got = local_call(
        functools.partial(reach_body, (heads, bits, far, count, len(mine))), "reach", 10, out_shape,
        [place], [*arrays, first, *mine, *theirs], [pltpu.VMEM((rows, heads * key), BF16)],
    )
    return got[:2], got[2:6], got[6:]


def return_body(sizes, place_ref, pack_ref, hat_t_ref, dout_ref, found_ref, prefix_ref, *refs):
    heads, bits, far = sizes
    others = refs[:far]
    dhat_ref = refs[far]
    sends = refs[far + 1 :]
    key = hat_t_ref.shape[1]
    pack = pack_ref[...]
    all_heads = range(heads)
    uppers = [((place_ref[0] >> bit) & 1) == 1 for bit in range(far)]
    spread = []
    for head in all_heads:
        parts = []
        for bit in range(far):
            weight = column(pack, (bits + 1 + bit) * heads + head)
            parts.append((weight * dout_ref[head]).astype(BF16))
        spread.append(jnp.concatenate(parts, 1))
    dfound = [mm(hat_t_ref[head], spread[head]) for head in all_heads]
    for head in all_heads:
        dhat_ref[head] = mm_nt(spread[head], found_ref[head])
    dprefix = [jnp.zeros((key, key), F32) for head in all_heads]
    for bit in reversed(range(far)):
        dfree = [
            jnp.where(uppers[bit], d[:, bit * key : (bit + 1) * key], 0.0) for d in dfound
        ]
        both = [
            jnp.concatenate([jnp.where(uppers[bit], dprefix[head], 0.0), dfree[head]], 1)
            for head in all_heads
        ]
        for head in all_heads:
            sent = dfree[head] if bit == far - 1 else both[head]
            sends[bit][head] = mm_tn(prefix_ref[head, bit], sent).astype(BF16)
        if bit > 0:
            moved = [mm_nt(both[head], others[bit][head]) for head in all_heads]
            dprefix = [
                jnp.where(uppers[bit], moved[head], dprefix[head]) for head in all_heads
            ]


def return_states(place, pack, hat_t, dout, found, prefix, others, bits):
    heads, rows, key = dout.shape
    far = len(others)
    sends = tuple(
        kept((heads, key, (1 if bit == far - 1 else 2) * key), BF16) for bit in range(far)
    )
    got = local_call(
        functools.partial(return_body, (heads, bits, far)), "return_states", 8,
        (kept(dout.shape, F32),) + sends, [place], [pack, hat_t, dout, found, prefix, *others],
    )
    return got[0], got[1:]


def add_body(*refs):
    count = len(refs) // 3
    for at in range(count):
        left, right = refs[at][...].astype(F32), refs[count + at][...].astype(F32)
        refs[2 * count + at][...] = (left + right).astype(BF16)


def add_all(left, right):
    out_shape = [kept(value.shape, BF16) for value in left]
    return local_call(add_body, "add_all", 6, out_shape, [], [*left, *right])


def lower_pull(dlower, base, lower, beta, decay, strict, k_in):
    dlower = jnp.where(strict, dlower, 0.0)
    dbeta = row_sum(dlower * base.astype(F32))
    dgram = dlower * (beta * decay)
    dkey = mm(dgram, k_in) + mm_tn(dgram, k_in)
    return dbeta, beta * dbeta, col_sum(dlower * lower.astype(F32)), dkey


def pull_body(sizes, *refs):
    heads, levels, bits = sizes
    (qkv_ref, pack_ref, pack_t_ref, trans_ref, attn_ref, attn_t_ref, prod_t_ref, scores_ref,
     mix_ref, decay_ref, base_ref, lower_ref, dout_ref, dhat_ref) = refs[:14]
    dqkv_ref, dgrown_ref, dcol_ref, drow_ref = refs[14:]
    rows = pack_ref.shape[0]
    decay_col = levels * heads
    beta_col = decay_col + heads
    block_bit = BLOCK.bit_length() - 1
    pack = pack_ref[...]
    pack_t = pack_t_ref[...]
    row_id, col_id = pair_ids(rows)
    strict = row_id > col_id
    apart = row_id ^ col_id
    lane = lane_of(rows)
    all_heads = range(heads)
    dcol = jnp.zeros((rows, LANES), F32)
    dbeta_rows, dcum_rows, dattn_all = [], [], []
    for head in all_heads:
        high, low = split(dout_ref[head])
        v_in = qkv_ref[2, head].astype(BF16)
        dprod = mm_nt(high, v_in) + mm_nt(low, v_in)
        dqkv_ref[2, head] = mm(prod_t_ref[head], high)
        beta_row = pack_t[beta_col + head : beta_col + head + 1, :]
        growth = jnp.exp(column(pack, decay_col + head))
        attn0 = attn_ref[head].astype(F32)
        touched = dprod * (attn0 * beta_row)
        for level in range(bits + 1):
            if level == 0:
                here = (apart >> block_bit) == 0
            else:
                here = (apart >> (block_bit + level - 1)) == 1
            dcol = jnp.where(
                lane == level * heads + head, row_sum(jnp.where(here, touched, 0.0)), dcol
            )
        dattn = dprod * mix_ref[head].astype(F32) - mm_nt(dhat_ref[head], growth * qkv_ref[1, head])
        dbeta_rows.append(col_sum(dattn * attn0))
        dattn_all.append((dattn * beta_row).astype(BF16))
    dscore_all = [mm_nt(dattn_all[head], trans_ref[head]) for head in all_heads]
    moved_all = []
    for head in all_heads:
        both = jnp.concatenate(
            [dscore_all[head].astype(BF16), dhat_ref[head].astype(BF16)], 1
        )
        moved_all.append(mm(attn_t_ref[head], both))
    for head in all_heads:
        q_in, k_in = qkv_ref[0, head], qkv_ref[1, head]
        beta = column(pack, beta_col + head)
        growth = jnp.exp(column(pack, decay_col + head))
        dscore = dscore_all[head]
        decay = decay_ref[head].astype(F32)
        dprobs = dscore * decay
        shift = dscore * scores_ref[head].astype(F32)
        dgrown_ref[head] = -beta * moved_all[head][:, rows:]
        dbeta, dcum_col, dcum_row, dk_lower = lower_pull(
            -moved_all[head][:, :rows], base_ref[head], lower_ref[head], beta, decay, strict, k_in
        )
        dhat = dhat_ref[head]
        dqkv_ref[0, head] = growth * dhat + mm(dprobs, k_in)
        dqkv_ref[1, head] = mm_tn(dprobs, q_in) + dk_lower
        dcum_col = dcum_col + row_sum(shift) + growth * row_sum(q_in * dhat)
        dcum_rows.append(-dcum_row - col_sum(shift))
        dcol = jnp.where(lane == beta_col + head, dbeta, dcol)
        dcol = jnp.where(lane == decay_col + head, dcum_col, dcol)
    dcol_ref[...] = dcol
    drow_ref[...] = jnp.concatenate(dcum_rows + dbeta_rows, 0)


def pull_local(arrays, levels, bits):
    heads, rows, key = arrays[0].shape[1:]
    out_shape = (
        kept((3, heads, rows, key), F32),
        kept((heads, rows, key), F32),
        kept((rows, LANES), F32),
        kept((2 * heads, rows), F32),
    )
    return local_call(
        functools.partial(pull_body, (heads, levels, bits)), "pull_local", 12, out_shape, [], arrays
    )


def finish_body(sizes, place_ref, *refs):
    heads, levels, far, count, arrived_counts = sizes
    (qkv_ref, gate_ref, pack_ref, trans_ref, mixed_ref, decay_ref, base_ref, lower_ref,
     dqkv_ref, dgrown_ref, dcol_ref, drow_ref, dfar_ref, rates_ref, small_ref) = refs[:15]
    others = refs[15 : 15 + far]
    refs = refs[15 + far :]
    arrived = []
    for found in arrived_counts:
        arrived.append(refs[:found])
        refs = refs[found:]
    wr_hbm = refs[0]
    keep_ref, send_ref = refs[1:3]
    direct_refs = refs[3 : 3 + count]
    dproj, wr_ref, sems = refs[3 + count :]
    size = wr_ref.shape[0] // count
    order = [*far_first(count), 0]
    spans, fetches = [], []
    for at, mask in enumerate(order):
        dest = place_ref[1] ^ mask
        spans.append(pl.ds(pl.multiple_of(dest * size, size), size))
        here, there = wr_hbm.at[spans[at], :], wr_ref.at[spans[at], :]
        fetches.append(pltpu.make_async_copy(here, there, sems.at[at]))
        fetches[at].start()
    rows = pack_ref.shape[0]
    key = qkv_ref.shape[3]
    decay_col = levels * heads
    beta_col = decay_col + heads
    norm_col = beta_col + heads
    place = place_ref[0]
    all_heads = range(heads)
    uppers = [((place >> bit) & 1) == 1 for bit in range(far)]
    pack = pack_ref[...]
    row_id, col_id = pair_ids(rows)
    strict = row_id > col_id
    lane = lane_of(rows)
    last_row = lax.broadcasted_iota(jnp.int32, (rows, 1), 0) == rows - 1
    eye_key = (pair_ids(key)[0] == pair_ids(key)[1]).astype(F32)
    dpair = [jnp.zeros((key, 2 * key), F32) for head in all_heads]
    for bit in reversed(range(far)):
        for head in all_heads:
            got = arrived[bit][0][head].astype(F32)
            for more in arrived[bit][1:]:
                got = got + more[head].astype(F32)
            other = others[bit][head]
            if bit == far - 1:
                got = jnp.concatenate([jnp.zeros((key, key), F32), got], 1)
                dpair[head] = jnp.where(uppers[bit], 0.0, got)
            else:
                as_low = mm_tn(other[:, :key], dpair[head]) + got
                as_high = mm_nt(dpair[head], other)
                as_high = jnp.concatenate([as_high, dpair[head][:, key:]], 1)
                dpair[head] = jnp.where(uppers[bit], as_high, as_low)
    moved_all, dmixed_all = [], []
    for head in all_heads:
        beta = column(pack, beta_col + head)
        growth = jnp.exp(column(pack, decay_col + head))
        both = jnp.concatenate([-growth * qkv_ref[1, head], qkv_ref[2, head]], 1)
        dmixed_all.append(mm_nt(both, dpair[head]))
        moved_all.append(mm(beta * mixed_ref[head].astype(F32), dpair[head]))
    dtail_all = [
        mm(trans_ref[head], column(pack, beta_col + head) * dmixed_all[head])
        for head in all_heads
    ]
    dlower_all = [-mm_nt(mixed_ref[head], dtail_all[head]) for head in all_heads]
    dcol = jnp.where(lane < decay_col, dcol_ref[...] + dfar_ref[...], dcol_ref[...])
    dcum_rows = []
    for head in all_heads:
        q_in, k_in = qkv_ref[0, head], qkv_ref[1, head]
        beta = column(pack, beta_col + head)
        cum_col = column(pack, decay_col + head)
        growth = jnp.exp(cum_col)
        last = cum_col[rows - 1 : rows, :]
        tail = jnp.exp(last - cum_col)
        dgrown = dgrown_ref[head] - moved_all[head][:, :key]
        dv = dqkv_ref[2, head] + moved_all[head][:, key:]
        dbeta_more = row_sum(mixed_ref[head].astype(F32) * dmixed_all[head])
        dtail = dtail_all[head]
        dbeta, dcum_col, dcum_row, dk_lower = lower_pull(
            dlower_all[head], base_ref[head], lower_ref[head], beta, decay_ref[head].astype(F32),
            strict, k_in
        )
        dcum_rows.append(-dcum_row)
        tail_pull = tail * row_sum(k_in * dtail)
        trace = col_sum(row_sum(dpair[head][:, :key] * eye_key))
        at_last = col_sum(tail_pull) + jnp.exp(last) * trace
        dcum_col = dcum_col + growth * row_sum(k_in * dgrown) - tail_pull
        dcum_col = dcum_col + jnp.where(last_row, at_last, 0.0)
        dk = dqkv_ref[1, head] + dk_lower + growth * dgrown + tail * dtail
        dq = dqkv_ref[0, head]
        dcol = dcol + jnp.where(lane == beta_col + head, dbeta + dbeta_more, 0.0)
        dcol = dcol + jnp.where(lane == decay_col + head, dcum_col, 0.0)
        for part, unit, dunit in ((0, q_in, dq), (1, k_in, dk)):
            scale = column(pack, norm_col + part * heads + head)
            back = scale * (dunit - unit * row_sum(unit * dunit))
            col = (part * heads + head) * key
            dproj[:, col : col + key] = back.astype(BF16)
        col = (2 * heads + head) * key
        dproj[:, col : col + key] = dv.astype(BF16)
    drow = drow_ref[...]
    drow = drow + jnp.concatenate(dcum_rows + [jnp.zeros((heads, rows), F32)], 0)
    drow = jnp.concatenate(
        [jnp.zeros((decay_col, rows), F32), drow,
         jnp.zeros((LANES - norm_col, rows), F32)], 0
    )
    dcol = dcol + drow.T
    rate, bias = rates_ref[0:1, :], rates_ref[1:2, :]
    switch = jax.nn.sigmoid(gate_ref[...] + bias)
    dlog = mm_full((row_id <= col_id).astype(F32), dcol)
    slope = switch * (1.0 - switch)
    dgate = jnp.where(
        lane < decay_col,
        dcol * switch,
        jnp.where(lane < beta_col, -rate * dlog * slope, dcol * slope),
    )
    dgate = jnp.where(lane < norm_col, dgate, 0.0).astype(BF16)
    half = size // 2
    for at, mask in enumerate(order):
        fetches[at].wait()
        part = mm_nt(dproj[...], wr_ref[spans[at], :]) + mm(dgate, small_ref[:, spans[at]])
        direct_refs[mask][...] = part[:, :half].astype(BF16)
        target = send_ref if mask % 2 else keep_ref
        target[mask // 2] = part[:, half:].astype(BF16)


def finish(place, arrays, others, arrived, wr, levels, count):
    rows = arrays[0].shape[2]
    width, cols = wr.shape
    far = len(others)
    counts = tuple(len(group) for group in arrived)
    heads = arrays[0].shape[1]
    flat = [value for group in arrived for value in group]
    scratch = [
        pltpu.VMEM((rows, cols), BF16), pltpu.VMEM(wr.shape, BF16),
        pltpu.SemaphoreType.DMA((count,)),
    ]
    half = width // count // 2
    out_shape = [kept((count // 2, rows, half), BF16)] * 2 + [kept((rows, half), BF16)] * count
    got = local_call(
        functools.partial(finish_body, (heads, levels, far, count, counts)), "finish", 16,
        out_shape, [place], [*arrays, *others, *flat], scratch, [wr],
    )
    return got[0], got[1], got[2:]


def swap(value, axis, mask):
    size = lax.axis_size(axis)
    return lax.ppermute(value, axis, [(at, at ^ mask) for at in range(size)])


def far_first(count):
    return sorted(range(1, count), key=lambda mask: mask < count // 2)


def halve_body(own_ref, got_ref, keep_ref, send_ref):
    for at in range(own_ref.shape[0]):
        total = own_ref[at].astype(F32) + got_ref[at].astype(F32)
        target = send_ref if at % 2 else keep_ref
        target[at // 2] = total.astype(target.dtype)


def halving(keep, send, axis, tied):
    mask = 1
    while keep.shape[0] > 1:
        got = swap(send, axis, mask)
        half = (keep.shape[0] // 2,) + keep.shape[1:]
        keep, send = local_call(
            halve_body, "halve", 6, [kept(half, F32), kept(half, BF16)], [], [keep, got]
        )
        send, tied = lax.optimization_barrier((send, tied))
        mask *= 2
    return keep, swap(send, axis, mask), tied


def sum_body(count, *refs):
    keep_ref, got_ref = refs[:2]
    out_ref = refs[-1]
    total = keep_ref[0].astype(F32) + got_ref[0].astype(F32)
    if count == 0:
        out_ref[...] = total.astype(BF16)
        return
    half = out_ref.shape[1] // 2
    out_ref[:, half:] = total.astype(BF16)
    total = refs[2][...].astype(F32)
    for ref in refs[3:-1]:
        total = total + ref[...].astype(F32)
    out_ref[:, :half] = total.astype(BF16)


def head_sum(keep, last, direct, got):
    rows, cols = keep.shape[1:]
    out = jax.ShapeDtypeStruct((rows, cols * (2 if direct else 1)), BF16)
    return local_call(
        functools.partial(sum_body, len(direct)), "head_sum", 6, [out], [],
        [keep, last, *direct[:1], *got],
    )[0]


def on_device(tokens, qkv_weight, small_weight, head_param, norm_gain, out_weight, grad_out):
    rows, width = tokens.shape
    heads, key = qkv_weight.shape[2:]
    levels = small_weight.shape[2] - 2
    bits = (rows // BLOCK).bit_length() - 1
    size = lax.axis_size("ctx")
    far = size.bit_length() - 1
    count = lax.axis_size("head")
    place = jnp.stack([lax.axis_index("ctx"), lax.axis_index("head")]).astype(jnp.int32)
    flat_w = qkv_weight.reshape(width * 3 * heads, key)
    small = jnp.transpose(small_weight, (2, 1, 0))
    rates = head_param.T
    flat_out = out_weight.reshape(heads * key, width)
    gain = norm_gain.reshape(1, key)

    (wr, small_t, qkv, gate, pack, pack_t, trans, mixed_t, decay, base, lower, rates_row,
     pair) = project(
        place, tokens, flat_w, small, rates, heads, levels
    )
    first = swap(pair, "ctx", 1)
    node = join_half(place, pair, first)
    mine = [swap(node, "ctx", 2 * at) for at in range(1, size // 2)]
    (attn, attn_t, prod_t, scores, mix, mixed, local_out, hat, hat_t, grad_normed) = local_part(
        [qkv, pack, pack_t, trans, mixed_t, decay, grad_out, flat_out], levels, bits
    )
    mine, local_out, grad_normed = lax.optimization_barrier((mine, local_out, grad_normed))
    theirs = [swap(value, "ctx", 1) for value in mine]
    out_parts, (dout, found, prefix, dfar), nodes = reach(
        place, [gain, pack, local_out, hat, grad_normed, flat_out], first, (mine, theirs),
        bits, far, count
    )
    others = [first, *nodes]
    dhat, sends = return_states(place, pack, hat_t, dout, found, prefix, others, bits)
    got = [swap(value, "ctx", 1) for value in sends]
    arrived = [[got[0]]]
    sums = add_all(sends[1:], got[1:])
    for bit in range(1, far):
        half = 1 << (bit - 1)
        arrived.append([swap(sums[bit - 1], "ctx", 2 * at) for at in range(half, 2 * half)])
    dqkv, dgrown, dcol, drow = pull_local(
        [qkv, pack, pack_t, trans, attn, attn_t, prod_t, scores, mix, decay, base, lower, dout,
         dhat],
        levels, bits,
    )
    keep_out, last_out, dcol = halving(*out_parts, "head", dcol)
    arrays = [qkv, gate, pack, trans, mixed, decay, base, lower, dqkv, dgrown, dcol, drow, dfar,
              rates_row, small_t]
    keep, send, direct = finish(place, arrays, others, arrived, wr, levels, count)
    direct, last_out = lax.optimization_barrier((direct, last_out))
    got = [swap(direct[mask], "head", mask) for mask in far_first(count)]
    keep, last, _ = halving(keep, send, "head", ())
    return head_sum(keep_out, last_out, [], []), head_sum(keep, last, direct, got)


def solution(mesh):
    placed = (
        P("ctx", None),
        P(None, None, "head", None),
        P(None, "head", None),
        P("head", None),
        P(),
        P("head", None, None),
        P("ctx", None),
    )
    return jax.shard_map(
        on_device,
        mesh=mesh,
        in_specs=placed,
        out_specs=(P("ctx", "head"), P("ctx", "head")),
        check_vma=False,
    )
```

```python
import functools

import jax
import jax.numpy as jnp
from jax import lax
from jax.experimental import pallas as pl
from jax.experimental.pallas import tpu as pltpu
from jax.sharding import PartitionSpec as P

BLOCK = 64
LANES = 128
EPS = 1e-06
MIB = 1024 * 1024
F32 = jnp.float32
BF16 = jnp.bfloat16
WHOLE = pl.BlockSpec(memory_space=pltpu.VMEM)
SCALARS = pl.BlockSpec(memory_space=pltpu.SMEM)
HBM = pl.BlockSpec(memory_space=pltpu.HBM)


def contract(left, right, dim_left, dim_right):
    return lax.dot_general(
        left.astype(BF16),
        right.astype(BF16),
        (((dim_left,), (dim_right,)), ((), ())),
        preferred_element_type=F32,
    )


def mm(left, right):
    return contract(left, right, 1, 0)


def mm_nt(left, right):
    return contract(left, right, 1, 1)


def mm_tn(left, right):
    return contract(left, right, 0, 0)


def split(values):
    high = values.astype(BF16)
    return high, (values - high.astype(F32)).astype(BF16)


def mm_nt_fine(left, right):
    left_high, left_low = split(left)
    right_high, right_low = split(right)
    return mm_nt(left_high, right_high) + (mm_nt(left_low, right_high) + mm_nt(left_high, right_low))


def mm_full(left, right):
    return jnp.dot(left, right, precision=lax.Precision.HIGHEST, preferred_element_type=F32)


def pair_ids(count):
    row_id = lax.broadcasted_iota(jnp.int32, (count, count), 0)
    col_id = lax.broadcasted_iota(jnp.int32, (count, count), 1)
    return row_id, col_id


def row_sum(values):
    return jnp.sum(values, 1, keepdims=True)


def col_sum(values):
    return jnp.sum(values, 0, keepdims=True)


def lane_of(rows):
    return lax.broadcasted_iota(jnp.int32, (rows, LANES), 1)


def decay_of(pack, pack_t, col, inclusive):
    spread = pack[:, col : col + 1] - pack_t[col : col + 1, :]
    return jnp.where(inclusive, jnp.exp(jnp.minimum(spread, 0.0)), 0.0)


def kept(shape, dtype):
    return pltpu.VMEM(shape, dtype)


def stored(shape, dtype):
    return pltpu.HBM(shape, dtype)


def pin(values, space):
    return [pltpu.with_memory_space_constraint(value, space) for value in values]


def local_call(
    body, name, limit, out_shape, scalars, arrays, scratch=(), remote=(), out_specs=None
):
    return pl.pallas_call(
        body,
        out_shape=tuple(out_shape),
        in_specs=[SCALARS] * len(scalars)
        + [WHOLE] * len(arrays)
        + [HBM] * len(remote),
        out_specs=tuple(out_specs or [WHOLE] * len(out_shape)),
        scratch_shapes=list(scratch),
        compiler_params=pltpu.CompilerParams(vmem_limit_bytes=limit * MIB),
        name=name,
    )(*scalars, *pin(arrays, pltpu.VMEM), *pin(remote, pltpu.HBM))


def column(pack, at):
    return pack[:, at : at + 1]


def level_mix(pack, head, heads, bits, apart):
    block_bit = BLOCK.bit_length() - 1
    mixed = jnp.broadcast_to(column(pack, head), apart.shape)
    for level in range(1, bits + 1):
        here = (apart >> (block_bit + level - 1)) >= 1
        mixed = jnp.where(here, column(pack, level * heads + head), mixed)
    return mixed


def head_rows(hp_ref, heads, decay_col, beta_col):
    lane_row = lane_of(1)
    rate = jnp.zeros((1, LANES), F32)
    bias = jnp.zeros((1, LANES), F32)
    for head in range(heads):
        rate = jnp.where(lane_row == decay_col + head, hp_ref[0:1, head : head + 1], rate)
        bias = jnp.where(lane_row == beta_col + head, hp_ref[1:2, head : head + 1], bias)
    return rate, bias


def merge_blocks(trans_all, edge_all, levels, first):
    if first:
        powers = [edge.astype(BF16) for edge in edge_all]
        trans_all = [trans - power for trans, power in zip(trans_all, powers)]
    else:
        powers = [mm(edge, trans).astype(BF16) for edge, trans in zip(edge_all, trans_all)]
        yield
        trans_all = [
            trans - mm(trans, power).astype(BF16) for trans, power in zip(trans_all, powers)
        ]
    for level in range(1, levels):
        powers = [mm(power, power).astype(BF16) for power in powers]
        yield
        trans_all = [
            trans + mm(trans, power).astype(BF16) for trans, power in zip(trans_all, powers)
        ]
    return trans_all


def invert(lower_all, eye, apart, rows):
    trans_all = [eye.astype(BF16) for lower in lower_all]
    bits = rows.bit_length() - 1
    start = 0
    while start < bits:
        levels = min(2 if bits - start == 2 else 3, bits - start)
        here = jnp.logical_and((apart >> start) >= 1, (apart >> (start + levels)) == 0)
        edge_all = [jnp.where(here, lower, 0.0) for lower in lower_all]
        trans_all = yield from merge_blocks(trans_all, edge_all, levels, start == 0)
        start += levels
        yield
    rest_all = []
    for trans, lower in zip(trans_all, lower_all):
        high, low = split(lower)
        rest_all.append(eye - trans.astype(F32) - mm(high, trans) - mm(low, trans))
    yield
    return [
        (trans.astype(F32) + mm(trans, rest)).astype(BF16)
        for trans, rest in zip(trans_all, rest_all)
    ]


def project_body(sizes, place_ref, hp_hbm, tokens_hbm, w_hbm, small_hbm, *refs):
    heads, levels, chunks = sizes
    (wr_hbm, small_ref, qkv_ref, gate_ref, pack_ref, pack_t_ref, trans_ref, mixed_t_ref,
     decay_ref, base_ref, lower_ref, rates_ref, pair_ref) = refs[:13]
    tokens, raw_q, raw_k, raw_v, wide_q, wide_k, wide_v, wr = refs[13:21]
    small_in, small_wide, acc, hp_ref, sems, in_sems, out_sems = refs[21:]
    raw, wide = (raw_q, raw_k, raw_v), (wide_q, wide_k, wide_v)
    rows, width = tokens.shape
    depth = width // chunks
    fetch_tokens = pltpu.make_async_copy(tokens_hbm, tokens, sems.at[0])
    fetch_small = pltpu.make_async_copy(small_hbm, small_in, sems.at[1])
    fetch_rates = pltpu.make_async_copy(hp_hbm, hp_ref, sems.at[2])
    fetches, keeps = {}, {}
    for part in range(3):
        for chunk in range(chunks):
            span = pl.ds(chunk * depth, depth)
            at = part * chunks + chunk
            fetches[part, chunk] = pltpu.make_async_copy(
                w_hbm.at[span, part], raw[part].at[span], in_sems.at[at]
            )
            block = (span, pl.ds(part * heads * LANES, heads * LANES))
            keeps[part, chunk] = pltpu.make_async_copy(
                wr.at[block], wr_hbm.at[block], out_sems.at[at]
            )
    fetch_small.start()
    fetch_rates.start()
    fetch_tokens.start(priority=1)
    for part in (1, 2, 0):
        for chunk in range(chunks):
            fetches[part, chunk].start(priority=chunk % 2)
    decay_col = levels * heads
    beta_col = decay_col + heads
    norm_col = beta_col + heads
    lane = lane_of(rows)
    row_id, col_id = pair_ids(rows)
    inclusive = row_id >= col_id
    strict = row_id > col_id
    apart = row_id ^ col_id
    eye = (row_id == col_id).astype(F32)
    fetch_small.wait()
    small_rows = small_in.shape[0] * heads
    for level in range(small_in.shape[0]):
        small_wide[level * heads : (level + 1) * heads, :] = small_in[level].astype(F32)
    small_wide[small_rows:, :] = jnp.zeros((LANES - small_rows, width), F32)
    small_ref[...] = small_wide[...].astype(BF16)
    fetch_rates.wait()
    rate, bias = head_rows(hp_ref, heads, decay_col, beta_col)
    rates_ref[0:1, :] = rate
    rates_ref[1:2, :] = bias
    fetch_tokens.wait()
    gate = mm_nt(tokens[...], small_ref[...])
    gate_ref[...] = gate
    switch = jax.nn.sigmoid(gate + bias)
    lam = jnp.maximum(gate, 0.0) + jnp.log1p(jnp.exp(-jnp.abs(gate)))
    cum = mm_full(inclusive.astype(F32), -rate * switch)
    pack = jnp.where(lane < decay_col, lam, jnp.where(lane < beta_col, cum, switch))
    pack_t = pack.T
    pack_t_ref[...] = pack_t

    def extract(part, chunk):
        fetches[part, chunk].wait()
        first, last = chunk * depth, (chunk + 1) * depth
        flat = raw[part].reshape(width * heads, LANES)
        wide[part][first * heads : last * heads, :] = (
            flat[first * heads : last * heads, :].astype(F32)
        )
        for head in range(heads):
            value = wide[part][pl.ds(first * heads + head, depth, stride=heads), :]
            col = (part * heads + head) * LANES
            wr[first:last, col : col + LANES] = value.astype(BF16)
        keeps[part, chunk].start(priority=chunk % 2)
        span = slice(part * heads * LANES, (part + 1) * heads * LANES)
        own = jnp.dot(tokens[:, first:last], wr[first:last, span], preferred_element_type=F32)
        if chunk == 0:
            acc[:, span] = own
        else:
            acc[:, span] += own

    for chunk in range(chunks):
        extract(1, chunk)

    def unit_of(part, head):
        col = (part * heads + head) * LANES
        raw = acc[:, col : col + LANES]
        scale = lax.rsqrt(row_sum(raw * raw) + EPS)
        qkv_ref[part, head] = raw * scale
        return raw * scale, jnp.where(lane == norm_col + part * heads + head, scale, 0.0)

    scales = jnp.zeros((rows, LANES), F32)
    k_all, lower_all = [], []
    for head in range(heads):
        unit, scale = unit_of(1, head)
        k_all.append(unit)
        scales = scales + scale
        decay = decay_of(pack, pack_t, decay_col + head, inclusive)
        decay_ref[head] = decay.astype(BF16)
        base = jnp.where(strict, decay * mm_nt(unit, unit), 0.0)
        base_ref[head] = base.astype(BF16)
        lower = column(pack, beta_col + head) * base
        lower_ref[head] = lower.astype(BF16)
        lower_all.append(lower)

    def later():
        for part in (2, 0):
            for chunk in range(chunks):
                yield
                extract(part, chunk)

    chain, filler = invert(lower_all, eye, apart, rows), later()
    while True:
        try:
            next(chain)
        except StopIteration as stop:
            trans_all = stop.value
            break
        next(filler, None)
    for _ in filler:
        pass
    mixed_all = []
    for head in range(heads):
        trans_ref[head] = trans_all[head]
        cum_row = pack_t[decay_col + head : decay_col + head + 1, :]
        tail_t = k_all[head].T * jnp.exp(cum_row[:, rows - 1 :] - cum_row)
        mixed_all.append(mm(tail_t, trans_all[head]).astype(BF16))
    eye_key = eye[:LANES, :LANES]
    for head in range(heads):
        mixed_t_ref[head] = mixed_all[head]
        col = (2 * heads + head) * LANES
        v_in = acc[:, col : col + LANES]
        qkv_ref[2, head] = v_in
        cum_col = column(pack, decay_col + head)
        beta = column(pack, beta_col + head)
        grown = (beta * jnp.exp(cum_col)) * k_all[head]
        both = jnp.concatenate([-grown, beta * v_in], 1)
        pair = mm(mixed_all[head], both)
        last = jnp.exp(cum_col[rows - 1 : rows, :])
        pair_ref[head, :, :LANES] = (last * eye_key + pair[:, :LANES]).astype(BF16)
        pair_ref[head, :, LANES:] = pair[:, LANES:].astype(BF16)
    for head in range(heads):
        scales = scales + unit_of(0, head)[1]
    pack_ref[...] = jnp.where(lane < norm_col, pack, scales)
    for keep in keeps.values():
        keep.wait()


def project(place, tokens, weight, small, head_param, heads, levels):
    rows, width = tokens.shape
    chunks = 4
    cols = 3 * heads
    key = weight.shape[3]
    square = (heads, rows, rows)
    out_shape = (
        stored((width, cols * key), BF16),
        kept((LANES, width), BF16),
        kept((3, heads, rows, key), F32),
        kept((rows, LANES), F32),
        kept((rows, LANES), F32),
        kept((LANES, rows), F32),
        kept(square, BF16),
        kept((heads, key, rows), BF16),
        kept(square, BF16),
        kept(square, BF16),
        kept(square, BF16),
        kept((2, LANES), F32),
        kept((heads, key, 2 * key), BF16),
    )
    scratch = [
        pltpu.VMEM(tokens.shape, BF16),
        *[pltpu.VMEM((width, heads, key), BF16) for part in range(3)],
        *[pltpu.VMEM((width * heads, key), F32) for part in range(3)],
        pltpu.VMEM((width, cols * key), BF16),
        pltpu.VMEM(small.shape, BF16),
        pltpu.VMEM((LANES, width), F32),
        pltpu.VMEM((rows, cols * key), F32),
        pltpu.VMEM(head_param.shape, F32),
        pltpu.SemaphoreType.DMA((3,)),
        pltpu.SemaphoreType.DMA((3 * chunks,)),
        pltpu.SemaphoreType.DMA((3 * chunks,)),
    ]
    return local_call(
        functools.partial(project_body, (heads, levels, chunks)), "project", 36, out_shape,
        [place], [], scratch, [head_param, tokens, weight, small], [HBM] + [WHOLE] * 12,
    )


def local_body(
    sizes, qkv_ref, pack_ref, pack_t_ref, trans_ref, mixed_t_ref, decay_ref, grad_ref, weight_ref, *outs
):
    heads, levels, bits = sizes
    (attn_ref, attn_t_ref, prod_t_ref, scores_ref, mix_ref, mixed_ref, local_ref, hat_ref,
     hat_t_ref, grad_normed_ref) = outs
    grad_normed_ref[...] = mm_nt(grad_ref[...], weight_ref[...])
    rows = pack_ref.shape[0]
    decay_col = levels * heads
    beta_col = decay_col + heads
    pack = pack_ref[...]
    pack_t = pack_t_ref[...]
    row_id, col_id = pair_ids(rows)
    apart = row_id ^ col_id
    for head in range(heads):
        scores = mm_nt_fine(qkv_ref[0, head], qkv_ref[1, head]) * decay_ref[head].astype(F32)
        scores_ref[head] = scores.astype(BF16)
        mix_ref[head] = level_mix(pack, head, heads, bits, apart).astype(BF16)
        mixed_ref[head] = mixed_t_ref[head].astype(F32).T.astype(BF16)
    for head in range(heads):
        attn = mm(scores_ref[head], trans_ref[head])
        attn_ref[head] = attn.astype(BF16)
        attn_t_ref[head] = attn.T.astype(BF16)
        attn = attn * pack_t[beta_col + head : beta_col + head + 1, :]
        prod = attn * mix_ref[head].astype(F32)
        prod_t_ref[head] = prod.T.astype(BF16)
        growth = jnp.exp(column(pack, decay_col + head))
        local_ref[head] = mm(prod, qkv_ref[2, head])
        hat = growth * qkv_ref[0, head] - mm(attn, growth * qkv_ref[1, head])
        hat_ref[head] = hat.astype(BF16)
        hat_t_ref[head] = hat.T.astype(BF16)


def local_part(arrays, levels, bits):
    heads, rows, key = arrays[0].shape[1:]
    square = (heads, rows, rows)
    out_shape = (
        kept(square, BF16),
        kept(square, BF16),
        kept(square, BF16),
        kept(square, BF16),
        kept(square, BF16),
        kept((heads, rows, key), BF16),
        kept((heads, rows, key), F32),
        kept((heads, rows, key), BF16),
        kept((heads, key, rows), BF16),
        kept((rows, heads * key), F32),
    )
    return local_call(
        functools.partial(local_body, (heads, levels, bits)), "local_part", 10, out_shape,
        [], arrays,
    )


def join_pair(upper, own, other):
    key = own.shape[0]
    low = jnp.where(upper, other, own)
    high = jnp.where(upper, own, other)
    moved = mm(high[:, :key], low)
    late = jnp.concatenate([jnp.zeros((key, key), F32), high[:, key:].astype(F32)], 1)
    return (moved + late).astype(BF16)


def join_body(place_ref, own_ref, other_ref, out_ref):
    half = out_ref.shape[0]
    upper = (place_ref[0] & 1) == 1
    for slot in range(half):
        head = (place_ref[0] & 1) * half + slot
        out_ref[slot] = join_pair(upper, own_ref[head], other_ref[head])


def join_half(place, own, other):
    half = (own.shape[0] // 2,) + own.shape[1:]
    return local_call(join_body, "join_half", 6, [kept(half, BF16)], [place], [own, other])[0]


def gather_node(head, bit, first, near, uppers):
    if bit == 0:
        mine, theirs = near[first]
        half = mine.shape[0]
        here = uppers[0] if head >= half else jnp.logical_not(uppers[0])
        return jnp.where(here, mine[head % half], theirs[head % half])
    own = gather_node(head, bit - 1, first, near, uppers)
    other = gather_node(head, bit - 1, first ^ (1 << (bit - 1)), near, uppers)
    return join_pair(uppers[bit], own, other)


def reach_body(
    sizes, place_ref, gain_ref, pack_ref, local_ref, hat_ref, grad_ref, weight_ref, *refs
):
    heads, bits, far, count, near_count = sizes
    first_ref = refs[0]
    near = [None] + [(refs[1 + at], refs[1 + near_count + at]) for at in range(near_count)]
    refs = refs[2 * near_count + 1 :]
    out_refs = refs[:2]
    dout_ref, found_ref, prefix_ref, dfar_ref = refs[2:6]
    nodes = refs[6:-1]
    normed_ref = refs[-1]
    rows = pack_ref.shape[0]
    key = hat_ref.shape[2]
    pack = pack_ref[...]
    gain = gain_ref[...]
    lane = lane_of(rows)
    all_heads = range(heads)
    uppers = [((place_ref[0] >> bit) & 1) == 1 for bit in range(far)]
    others = []
    for bit in range(far):
        if bit == 0:
            others.append([first_ref[head] for head in all_heads])
        else:
            others.append(
                [gather_node(head, bit - 1, 1 << (bit - 1), near, uppers) for head in all_heads]
            )
            for head in all_heads:
                nodes[bit - 1][head] = others[bit][head]
    eye_key = jnp.where(pair_ids(key)[0] == pair_ids(key)[1], 1.0, 0.0).astype(BF16)
    prefix = [eye_key for head in all_heads]
    found = []
    for bit in range(far):
        for head in all_heads:
            prefix_ref[head, bit] = prefix[head]
        moved = [mm(prefix[head], others[bit][head]) for head in all_heads]
        found.append([jnp.where(uppers[bit], m[:, key:], 0.0).astype(BF16) for m in moved])
        prefix = [
            jnp.where(uppers[bit], moved[head][:, :key].astype(BF16), prefix[head])
            for head in all_heads
        ]
    found = [jnp.concatenate([found[bit][head] for bit in range(far)], 1) for head in all_heads]
    reached = [mm(hat_ref[head], found[head]) for head in all_heads]
    dfar = jnp.zeros((rows, LANES), F32)
    for head in all_heads:
        found_ref[head] = found[head]
        summed = local_ref[head]
        parts = []
        for bit in range(far):
            parts.append(reached[head][:, bit * key : (bit + 1) * key])
            summed = summed + column(pack, (bits + 1 + bit) * heads + head) * parts[bit]
        scale = lax.rsqrt(jnp.mean(summed * summed, -1, keepdims=True) + EPS)
        unit = summed * scale
        normed_ref[:, head * key : (head + 1) * key] = (unit * gain).astype(BF16)
        pulled = grad_ref[:, head * key : (head + 1) * key] * gain
        dout = scale * (pulled - unit * jnp.mean(pulled * unit, -1, keepdims=True))
        dout_ref[head] = dout
        for bit in range(far):
            col = (bits + 1 + bit) * heads + head
            dfar = jnp.where(lane == col, row_sum(dout * parts[bit]), dfar)
    dfar_ref[...] = dfar
    size = weight_ref.shape[1] // count
    for mask in range(count):
        dest = place_ref[1] ^ mask
        cols = pl.ds(pl.multiple_of(dest * size, size), size)
        out_refs[mask % 2][mask // 2] = jnp.dot(
            normed_ref[...], weight_ref[:, cols], preferred_element_type=F32
        ).astype(BF16)


def reach(place, arrays, first, near, bits, far, count):
    gain, pack, local_out, hat, grad_normed, weight = arrays
    heads, rows, key = hat.shape
    nodes = tuple(kept(first.shape, BF16) for bit in range(1, far))
    size = weight.shape[1] // count
    out_shape = (kept((count // 2, rows, size), BF16),) * 2 + (
        kept((heads, rows, key), F32),
        kept((heads, key, far * key), BF16),
        kept((heads, far, key, key), BF16),
        kept((rows, LANES), F32),
    ) + nodes
    mine, theirs = near
    got = local_call(
        functools.partial(reach_body, (heads, bits, far, count, len(mine))), "reach", 10, out_shape,
        [place], [*arrays, first, *mine, *theirs], [pltpu.VMEM((rows, heads * key), BF16)],
    )
    return got[:2], got[2:6], got[6:]


def return_body(sizes, place_ref, pack_ref, hat_t_ref, dout_ref, found_ref, prefix_ref, *refs):
    heads, bits, far = sizes
    others = refs[:far]
    dhat_ref = refs[far]
    sends = refs[far + 1 :]
    key = hat_t_ref.shape[1]
    pack = pack_ref[...]
    all_heads = range(heads)
    uppers = [((place_ref[0] >> bit) & 1) == 1 for bit in range(far)]
    spread = []
    for head in all_heads:
        parts = []
        for bit in range(far):
            weight = column(pack, (bits + 1 + bit) * heads + head)
            parts.append((weight * dout_ref[head]).astype(BF16))
        spread.append(jnp.concatenate(parts, 1))
    dfound = [mm(hat_t_ref[head], spread[head]) for head in all_heads]
    for head in all_heads:
        dhat_ref[head] = mm_nt(spread[head], found_ref[head])
    dprefix = [jnp.zeros((key, key), F32) for head in all_heads]
    for bit in reversed(range(far)):
        dfree = [
            jnp.where(uppers[bit], d[:, bit * key : (bit + 1) * key], 0.0) for d in dfound
        ]
        both = [
            jnp.concatenate([jnp.where(uppers[bit], dprefix[head], 0.0), dfree[head]], 1)
            for head in all_heads
        ]
        for head in all_heads:
            sent = dfree[head] if bit == far - 1 else both[head]
            sends[bit][head] = mm_tn(prefix_ref[head, bit], sent).astype(BF16)
        if bit > 0:
            moved = [mm_nt(both[head], others[bit][head]) for head in all_heads]
            dprefix = [
                jnp.where(uppers[bit], moved[head], dprefix[head]) for head in all_heads
            ]


def return_states(place, pack, hat_t, dout, found, prefix, others, bits):
    heads, rows, key = dout.shape
    far = len(others)
    sends = tuple(
        kept((heads, key, (1 if bit == far - 1 else 2) * key), BF16) for bit in range(far)
    )
    got = local_call(
        functools.partial(return_body, (heads, bits, far)), "return_states", 8,
        (kept(dout.shape, F32),) + sends, [place], [pack, hat_t, dout, found, prefix, *others],
    )
    return got[0], got[1:]


def add_body(*refs):
    count = len(refs) // 3
    for at in range(count):
        left, right = refs[at][...].astype(F32), refs[count + at][...].astype(F32)
        refs[2 * count + at][...] = (left + right).astype(BF16)


def add_all(left, right):
    out_shape = [kept(value.shape, BF16) for value in left]
    return local_call(add_body, "add_all", 6, out_shape, [], [*left, *right])


def lower_pull(dlower, base, lower, beta, decay, strict, k_in):
    dlower = jnp.where(strict, dlower, 0.0)
    dbeta = row_sum(dlower * base.astype(F32))
    dgram = dlower * (beta * decay)
    dkey = mm(dgram, k_in) + mm_tn(dgram, k_in)
    return dbeta, beta * dbeta, col_sum(dlower * lower.astype(F32)), dkey


def pull_body(sizes, *refs):
    heads, levels, bits = sizes
    (qkv_ref, pack_ref, pack_t_ref, trans_ref, attn_ref, attn_t_ref, prod_t_ref, scores_ref,
     mix_ref, decay_ref, base_ref, lower_ref, dout_ref, dhat_ref) = refs[:14]
    dqkv_ref, dgrown_ref, dcol_ref, drow_ref = refs[14:]
    rows = pack_ref.shape[0]
    decay_col = levels * heads
    beta_col = decay_col + heads
    block_bit = BLOCK.bit_length() - 1
    pack = pack_ref[...]
    pack_t = pack_t_ref[...]
    row_id, col_id = pair_ids(rows)
    strict = row_id > col_id
    apart = row_id ^ col_id
    lane = lane_of(rows)
    all_heads = range(heads)
    dcol = jnp.zeros((rows, LANES), F32)
    dbeta_rows, dcum_rows, dattn_all = [], [], []
    for head in all_heads:
        high, low = split(dout_ref[head])
        v_in = qkv_ref[2, head].astype(BF16)
        dprod = mm_nt(high, v_in) + mm_nt(low, v_in)
        dqkv_ref[2, head] = mm(prod_t_ref[head], high)
        beta_row = pack_t[beta_col + head : beta_col + head + 1, :]
        growth = jnp.exp(column(pack, decay_col + head))
        attn0 = attn_ref[head].astype(F32)
        touched = dprod * (attn0 * beta_row)
        for level in range(bits + 1):
            if level == 0:
                here = (apart >> block_bit) == 0
            else:
                here = (apart >> (block_bit + level - 1)) == 1
            dcol = jnp.where(
                lane == level * heads + head, row_sum(jnp.where(here, touched, 0.0)), dcol
            )
        dattn = dprod * mix_ref[head].astype(F32) - mm_nt(dhat_ref[head], growth * qkv_ref[1, head])
        dbeta_rows.append(col_sum(dattn * attn0))
        dattn_all.append((dattn * beta_row).astype(BF16))
    dscore_all = [mm_nt(dattn_all[head], trans_ref[head]) for head in all_heads]
    moved_all = []
    for head in all_heads:
        both = jnp.concatenate(
            [dscore_all[head].astype(BF16), dhat_ref[head].astype(BF16)], 1
        )
        moved_all.append(mm(attn_t_ref[head], both))
    for head in all_heads:
        q_in, k_in = qkv_ref[0, head], qkv_ref[1, head]
        beta = column(pack, beta_col + head)
        growth = jnp.exp(column(pack, decay_col + head))
        dscore = dscore_all[head]
        decay = decay_ref[head].astype(F32)
        dprobs = dscore * decay
        shift = dscore * scores_ref[head].astype(F32)
        dgrown_ref[head] = -beta * moved_all[head][:, rows:]
        dbeta, dcum_col, dcum_row, dk_lower = lower_pull(
            -moved_all[head][:, :rows], base_ref[head], lower_ref[head], beta, decay, strict, k_in
        )
        dhat = dhat_ref[head]
        dqkv_ref[0, head] = growth * dhat + mm(dprobs, k_in)
        dqkv_ref[1, head] = mm_tn(dprobs, q_in) + dk_lower
        dcum_col = dcum_col + row_sum(shift) + growth * row_sum(q_in * dhat)
        dcum_rows.append(-dcum_row - col_sum(shift))
        dcol = jnp.where(lane == beta_col + head, dbeta, dcol)
        dcol = jnp.where(lane == decay_col + head, dcum_col, dcol)
    dcol_ref[...] = dcol
    drow_ref[...] = jnp.concatenate(dcum_rows + dbeta_rows, 0)


def pull_local(arrays, levels, bits):
    heads, rows, key = arrays[0].shape[1:]
    out_shape = (
        kept((3, heads, rows, key), F32),
        kept((heads, rows, key), F32),
        kept((rows, LANES), F32),
        kept((2 * heads, rows), F32),
    )
    return local_call(
        functools.partial(pull_body, (heads, levels, bits)), "pull_local", 12, out_shape, [], arrays
    )


def finish_body(sizes, place_ref, *refs):
    heads, levels, far, arrived_counts = sizes
    (qkv_ref, gate_ref, pack_ref, trans_ref, mixed_ref, decay_ref, base_ref, lower_ref,
     dqkv_ref, dgrown_ref, dcol_ref, drow_ref, dfar_ref, rates_ref) = refs[:14]
    others = refs[14 : 14 + far]
    refs = refs[14 + far :]
    arrived = []
    for found in arrived_counts:
        arrived.append(refs[:found])
        refs = refs[found:]
    dproj, dgate_ref = refs
    rows = pack_ref.shape[0]
    key = qkv_ref.shape[3]
    decay_col = levels * heads
    beta_col = decay_col + heads
    norm_col = beta_col + heads
    place = place_ref[0]
    all_heads = range(heads)
    uppers = [((place >> bit) & 1) == 1 for bit in range(far)]
    pack = pack_ref[...]
    row_id, col_id = pair_ids(rows)
    strict = row_id > col_id
    lane = lane_of(rows)
    last_row = lax.broadcasted_iota(jnp.int32, (rows, 1), 0) == rows - 1
    eye_key = (pair_ids(key)[0] == pair_ids(key)[1]).astype(F32)
    dpair = [jnp.zeros((key, 2 * key), F32) for head in all_heads]
    for bit in reversed(range(far)):
        for head in all_heads:
            got = arrived[bit][0][head].astype(F32)
            for more in arrived[bit][1:]:
                got = got + more[head].astype(F32)
            other = others[bit][head]
            if bit == far - 1:
                got = jnp.concatenate([jnp.zeros((key, key), F32), got], 1)
                dpair[head] = jnp.where(uppers[bit], 0.0, got)
            else:
                as_low = mm_tn(other[:, :key], dpair[head]) + got
                as_high = mm_nt(dpair[head], other)
                as_high = jnp.concatenate([as_high, dpair[head][:, key:]], 1)
                dpair[head] = jnp.where(uppers[bit], as_high, as_low)
    moved_all, dmixed_all = [], []
    for head in all_heads:
        beta = column(pack, beta_col + head)
        growth = jnp.exp(column(pack, decay_col + head))
        both = jnp.concatenate([-growth * qkv_ref[1, head], qkv_ref[2, head]], 1)
        dmixed_all.append(mm_nt(both, dpair[head]))
        moved_all.append(mm(beta * mixed_ref[head].astype(F32), dpair[head]))
    dtail_all = [
        mm(trans_ref[head], column(pack, beta_col + head) * dmixed_all[head])
        for head in all_heads
    ]
    dlower_all = [-mm_nt(mixed_ref[head], dtail_all[head]) for head in all_heads]
    dcol = jnp.where(lane < decay_col, dcol_ref[...] + dfar_ref[...], dcol_ref[...])
    dcum_rows = []
    for head in all_heads:
        q_in, k_in = qkv_ref[0, head], qkv_ref[1, head]
        beta = column(pack, beta_col + head)
        cum_col = column(pack, decay_col + head)
        growth = jnp.exp(cum_col)
        last = cum_col[rows - 1 : rows, :]
        tail = jnp.exp(last - cum_col)
        dgrown = dgrown_ref[head] - moved_all[head][:, :key]
        dv = dqkv_ref[2, head] + moved_all[head][:, key:]
        dbeta_more = row_sum(mixed_ref[head].astype(F32) * dmixed_all[head])
        dtail = dtail_all[head]
        dbeta, dcum_col, dcum_row, dk_lower = lower_pull(
            dlower_all[head], base_ref[head], lower_ref[head], beta, decay_ref[head].astype(F32),
            strict, k_in
        )
        dcum_rows.append(-dcum_row)
        tail_pull = tail * row_sum(k_in * dtail)
        trace = col_sum(row_sum(dpair[head][:, :key] * eye_key))
        at_last = col_sum(tail_pull) + jnp.exp(last) * trace
        dcum_col = dcum_col + growth * row_sum(k_in * dgrown) - tail_pull
        dcum_col = dcum_col + jnp.where(last_row, at_last, 0.0)
        dk = dqkv_ref[1, head] + dk_lower + growth * dgrown + tail * dtail
        dq = dqkv_ref[0, head]
        dcol = dcol + jnp.where(lane == beta_col + head, dbeta + dbeta_more, 0.0)
        dcol = dcol + jnp.where(lane == decay_col + head, dcum_col, 0.0)
        for part, unit, dunit in ((0, q_in, dq), (1, k_in, dk)):
            scale = column(pack, norm_col + part * heads + head)
            back = scale * (dunit - unit * row_sum(unit * dunit))
            col = (part * heads + head) * key
            dproj[:, col : col + key] = back.astype(BF16)
        col = (2 * heads + head) * key
        dproj[:, col : col + key] = dv.astype(BF16)
    drow = drow_ref[...]
    drow = drow + jnp.concatenate(dcum_rows + [jnp.zeros((heads, rows), F32)], 0)
    drow = jnp.concatenate(
        [jnp.zeros((decay_col, rows), F32), drow,
         jnp.zeros((LANES - norm_col, rows), F32)], 0
    )
    dcol = dcol + drow.T
    rate, bias = rates_ref[0:1, :], rates_ref[1:2, :]
    switch = jax.nn.sigmoid(gate_ref[...] + bias)
    dlog = mm_full((row_id <= col_id).astype(F32), dcol)
    slope = switch * (1.0 - switch)
    dgate = jnp.where(
        lane < decay_col,
        dcol * switch,
        jnp.where(lane < beta_col, -rate * dlog * slope, dcol * slope),
    )
    dgate_ref[...] = jnp.where(lane < norm_col, dgate, 0.0).astype(BF16)


def finish(place, arrays, others, arrived, levels):
    heads, rows, key = arrays[0].shape[1:]
    counts = tuple(len(group) for group in arrived)
    flat = [value for group in arrived for value in group]
    return local_call(
        functools.partial(finish_body, (heads, levels, len(others), counts)), "finish", 10,
        [kept((rows, 3 * heads * key), BF16), kept((rows, LANES), BF16)],
        [place], [*arrays, *others, *flat],
    )


def tokens_body(count, place_ref, dproj_ref, dgate_ref, wr_ref, small_ref, *refs):
    keep_ref, send_ref = refs[:2]
    direct_refs = refs[2:]
    size = wr_ref.shape[0] // count
    half = size // 2
    for mask in range(count):
        dest = place_ref[1] ^ mask
        span = pl.ds(pl.multiple_of(dest * size, size), size)
        part = mm_nt(dproj_ref[...], wr_ref[span, :]) + mm(dgate_ref[...], small_ref[:, span])
        direct_refs[mask][...] = part[:, :half].astype(BF16)
        target = send_ref if mask % 2 else keep_ref
        target[mask // 2] = part[:, half:].astype(BF16)


def pull_tokens(place, dproj, dgate, wr, small_t, count):
    rows = dproj.shape[0]
    half = wr.shape[0] // count // 2
    out_shape = [kept((count // 2, rows, half), BF16)] * 2 + [kept((rows, half), BF16)] * count
    got = local_call(
        functools.partial(tokens_body, count), "pull_tokens", 8, out_shape,
        [place], [dproj, dgate, wr, small_t],
    )
    return got[0], got[1], got[2:]


def swap(value, axis, mask):
    size = lax.axis_size(axis)
    return lax.ppermute(value, axis, [(at, at ^ mask) for at in range(size)])


def far_first(count):
    return sorted(range(1, count), key=lambda mask: mask < count // 2)


def halve_body(own_ref, got_ref, keep_ref, send_ref):
    for at in range(own_ref.shape[0]):
        total = own_ref[at].astype(F32) + got_ref[at].astype(F32)
        target = send_ref if at % 2 else keep_ref
        target[at // 2] = total.astype(target.dtype)


def halving(keep, send, axis, tied):
    mask = 1
    while keep.shape[0] > 1:
        got = swap(send, axis, mask)
        half = (keep.shape[0] // 2,) + keep.shape[1:]
        keep, send = local_call(
            halve_body, "halve", 6, [kept(half, F32), kept(half, BF16)], [], [keep, got]
        )
        send, tied = lax.optimization_barrier((send, tied))
        mask *= 2
    return keep, swap(send, axis, mask), tied


def sum_body(count, *refs):
    keep_ref, got_ref = refs[:2]
    out_ref = refs[-1]
    total = keep_ref[0].astype(F32) + got_ref[0].astype(F32)
    if count == 0:
        out_ref[...] = total.astype(BF16)
        return
    half = out_ref.shape[1] // 2
    out_ref[:, half:] = total.astype(BF16)
    total = refs[2][...].astype(F32)
    for ref in refs[3:-1]:
        total = total + ref[...].astype(F32)
    out_ref[:, :half] = total.astype(BF16)


def head_sum(keep, last, direct, got):
    rows, cols = keep.shape[1:]
    out = jax.ShapeDtypeStruct((rows, cols * (2 if direct else 1)), BF16)
    return local_call(
        functools.partial(sum_body, len(direct)), "head_sum", 6, [out], [],
        [keep, last, *direct[:1], *got],
    )[0]


def on_device(tokens, qkv_weight, small_weight, head_param, norm_gain, out_weight, grad_out):
    rows, width = tokens.shape
    heads, key = qkv_weight.shape[2:]
    levels = small_weight.shape[2] - 2
    bits = (rows // BLOCK).bit_length() - 1
    size = lax.axis_size("ctx")
    far = size.bit_length() - 1
    count = lax.axis_size("head")
    place = jnp.stack([lax.axis_index("ctx"), lax.axis_index("head")]).astype(jnp.int32)
    small = jnp.transpose(small_weight, (2, 1, 0))
    rates = head_param.T
    flat_out = out_weight.reshape(heads * key, width)
    gain = norm_gain.reshape(1, key)

    (wr, small_t, qkv, gate, pack, pack_t, trans, mixed_t, decay, base, lower, rates_row,
     pair) = project(
        place, tokens, qkv_weight, small, rates, heads, levels
    )
    first = swap(pair, "ctx", 1)
    node = join_half(place, pair, first)
    mine = [swap(node, "ctx", 2 * at) for at in range(1, size // 2)]
    (attn, attn_t, prod_t, scores, mix, mixed, local_out, hat, hat_t, grad_normed) = local_part(
        [qkv, pack, pack_t, trans, mixed_t, decay, grad_out, flat_out], levels, bits
    )
    mine, local_out, grad_normed = lax.optimization_barrier((mine, local_out, grad_normed))
    theirs = [swap(value, "ctx", 1) for value in mine]
    out_parts, (dout, found, prefix, dfar), nodes = reach(
        place, [gain, pack, local_out, hat, grad_normed, flat_out], first, (mine, theirs),
        bits, far, count
    )
    others = [first, *nodes]
    dhat, sends = return_states(place, pack, hat_t, dout, found, prefix, others, bits)
    got = [swap(value, "ctx", 1) for value in sends]
    arrived = [[got[0]]]
    sums = add_all(sends[1:], got[1:])
    for bit in range(1, far):
        half = 1 << (bit - 1)
        arrived.append([swap(sums[bit - 1], "ctx", 2 * at) for at in range(half, 2 * half)])
    dqkv, dgrown, dcol, drow = pull_local(
        [qkv, pack, pack_t, trans, attn, attn_t, prod_t, scores, mix, decay, base, lower, dout,
         dhat],
        levels, bits,
    )
    keep_out, last_out, dcol = halving(*out_parts, "head", dcol)
    arrays = [qkv, gate, pack, trans, mixed, decay, base, lower, dqkv, dgrown, dcol, drow, dfar,
              rates_row]
    dproj, dgate = finish(place, arrays, others, arrived, levels)
    keep, send, direct = pull_tokens(place, dproj, dgate, wr, small_t, count)
    direct, last_out = lax.optimization_barrier((direct, last_out))
    got = [swap(direct[mask], "head", mask) for mask in far_first(count)]
    keep, last, _ = halving(keep, send, "head", ())
    return head_sum(keep_out, last_out, [], []), head_sum(keep, last, direct, got)


def solution(mesh):
    placed = (
        P("ctx", None),
        P(None, None, "head", None),
        P(None, "head", None),
        P("head", None),
        P(),
        P("head", None, None),
        P("ctx", None),
    )
    return jax.shard_map(
        on_device,
        mesh=mesh,
        in_specs=placed,
        out_specs=(P("ctx", "head"), P("ctx", "head")),
        check_vma=False,
    )
```

```python
import functools

import jax
import jax.numpy as jnp
from jax import lax
from jax.experimental import pallas as pl
from jax.experimental.pallas import tpu as pltpu
from jax.sharding import PartitionSpec as P

BLOCK = 64
LANES = 128
EPS = 1e-06
MIB = 1024 * 1024
F32 = jnp.float32
BF16 = jnp.bfloat16
WHOLE = pl.BlockSpec(memory_space=pltpu.VMEM)
SCALARS = pl.BlockSpec(memory_space=pltpu.SMEM)
HBM = pl.BlockSpec(memory_space=pltpu.HBM)


def contract(left, right, dim_left, dim_right):
    return lax.dot_general(
        left.astype(BF16),
        right.astype(BF16),
        (((dim_left,), (dim_right,)), ((), ())),
        preferred_element_type=F32,
    )


def mm(left, right):
    return contract(left, right, 1, 0)


def mm_nt(left, right):
    return contract(left, right, 1, 1)


def mm_tn(left, right):
    return contract(left, right, 0, 0)


def split(values):
    high = values.astype(BF16)
    return high, (values - high.astype(F32)).astype(BF16)


def mm_nt_fine(left, right):
    left_high, left_low = split(left)
    right_high, right_low = split(right)
    return mm_nt(left_high, right_high) + (mm_nt(left_low, right_high) + mm_nt(left_high, right_low))


def mm_full(left, right):
    return jnp.dot(left, right, precision=lax.Precision.HIGHEST, preferred_element_type=F32)


def pair_ids(count):
    row_id = lax.broadcasted_iota(jnp.int32, (count, count), 0)
    col_id = lax.broadcasted_iota(jnp.int32, (count, count), 1)
    return row_id, col_id


def row_sum(values):
    return jnp.sum(values, 1, keepdims=True)


def col_sum(values):
    return jnp.sum(values, 0, keepdims=True)


def lane_of(rows):
    return lax.broadcasted_iota(jnp.int32, (rows, LANES), 1)


def decay_of(pack, pack_t, col, inclusive):
    spread = pack[:, col : col + 1] - pack_t[col : col + 1, :]
    return jnp.where(inclusive, jnp.exp(jnp.minimum(spread, 0.0)), 0.0)


def kept(shape, dtype):
    return pltpu.VMEM(shape, dtype)


def stored(shape, dtype):
    return pltpu.HBM(shape, dtype)


def pin(values, space):
    return [pltpu.with_memory_space_constraint(value, space) for value in values]


def local_call(
    body, name, limit, out_shape, scalars, arrays, scratch=(), remote=(), out_specs=None
):
    return pl.pallas_call(
        body,
        out_shape=tuple(out_shape),
        in_specs=[SCALARS] * len(scalars)
        + [WHOLE] * len(arrays)
        + [HBM] * len(remote),
        out_specs=tuple(out_specs or [WHOLE] * len(out_shape)),
        scratch_shapes=list(scratch),
        compiler_params=pltpu.CompilerParams(vmem_limit_bytes=limit * MIB),
        name=name,
    )(*scalars, *pin(arrays, pltpu.VMEM), *pin(remote, pltpu.HBM))


def column(pack, at):
    return pack[:, at : at + 1]


def level_mix(pack, head, heads, bits, apart):
    block_bit = BLOCK.bit_length() - 1
    mixed = jnp.broadcast_to(column(pack, head), apart.shape)
    for level in range(1, bits + 1):
        here = (apart >> (block_bit + level - 1)) >= 1
        mixed = jnp.where(here, column(pack, level * heads + head), mixed)
    return mixed


def head_rows(hp_ref, heads, decay_col, beta_col):
    lane_row = lane_of(1)
    rate = jnp.zeros((1, LANES), F32)
    bias = jnp.zeros((1, LANES), F32)
    for head in range(heads):
        rate = jnp.where(lane_row == decay_col + head, hp_ref[0:1, head : head + 1], rate)
        bias = jnp.where(lane_row == beta_col + head, hp_ref[1:2, head : head + 1], bias)
    return rate, bias


def merge_blocks(trans_all, edge_all, levels, first):
    if first:
        powers = [edge.astype(BF16) for edge in edge_all]
        trans_all = [trans - power for trans, power in zip(trans_all, powers)]
    else:
        powers = [mm(edge, trans).astype(BF16) for edge, trans in zip(edge_all, trans_all)]
        yield
        trans_all = [
            trans - mm(trans, power).astype(BF16) for trans, power in zip(trans_all, powers)
        ]
    for level in range(1, levels):
        powers = [mm(power, power).astype(BF16) for power in powers]
        yield
        trans_all = [
            trans + mm(trans, power).astype(BF16) for trans, power in zip(trans_all, powers)
        ]
    return trans_all


def invert(lower_all, eye, apart, rows):
    trans_all = [eye.astype(BF16) for lower in lower_all]
    bits = rows.bit_length() - 1
    start = 0
    while start < bits:
        levels = min(2 if bits - start == 2 else 3, bits - start)
        here = jnp.logical_and((apart >> start) >= 1, (apart >> (start + levels)) == 0)
        edge_all = [jnp.where(here, lower, 0.0) for lower in lower_all]
        trans_all = yield from merge_blocks(trans_all, edge_all, levels, start == 0)
        start += levels
        yield
    rest_all = []
    for trans, lower in zip(trans_all, lower_all):
        high, low = split(lower)
        rest_all.append(eye - trans.astype(F32) - mm(high, trans) - mm(low, trans))
    yield
    return [
        (trans.astype(F32) + mm(trans, rest)).astype(BF16)
        for trans, rest in zip(trans_all, rest_all)
    ]


def project_body(sizes, place_ref, hp_hbm, tokens_hbm, w_hbm, small_hbm, *refs):
    heads, levels, chunks = sizes
    (wr_hbm, small_ref, qkv_ref, gate_ref, pack_ref, pack_t_ref, trans_ref, mixed_t_ref,
     decay_ref, base_ref, lower_ref, rates_ref, pair_ref) = refs[:13]
    tokens, wide_in, wr, small_in, small_wide, acc, hp_ref, sems, in_sems, out_sems = refs[13:]
    rows, width = tokens.shape
    depth = width // chunks
    cols = 3 * heads
    fetch_tokens = pltpu.make_async_copy(tokens_hbm, tokens, sems.at[0])
    fetch_small = pltpu.make_async_copy(small_hbm, small_in, sems.at[1])
    fetch_rates = pltpu.make_async_copy(hp_hbm, hp_ref, sems.at[2])
    fetches, keeps = [], []
    for chunk in range(chunks):
        span = pl.ds(chunk * depth * cols, depth * cols)
        fetches.append(
            pltpu.make_async_copy(w_hbm.at[span, :], wide_in.at[span, :], in_sems.at[chunk])
        )
        span = pl.ds(chunk * depth, depth)
        keeps.append(
            pltpu.make_async_copy(wr.at[span, :], wr_hbm.at[span, :], out_sems.at[chunk])
        )
    fetch_small.start()
    fetch_rates.start()
    fetches[0].start()
    fetch_tokens.start()
    for fetch in fetches[1:]:
        fetch.start()
    group = 16
    size = group * cols
    turn_row, turn_col = pair_ids(size)
    turn = (turn_col == (turn_row % group) * cols + turn_row // group).astype(F32).astype(BF16)

    def relay(chunk):
        fetches[chunk].wait()
        first = chunk * depth * cols
        packs = depth // group
        side = jnp.concatenate(
            [wide_in[first + at * size : first + (at + 1) * size, :] for at in range(packs)], 1
        )
        turned = jnp.dot(turn, side, preferred_element_type=F32).astype(BF16)
        for at in range(packs):
            row = chunk * depth + at * group
            for col in range(cols):
                wr[row : row + group, col * LANES : (col + 1) * LANES] = turned[
                    col * group : (col + 1) * group, at * LANES : (at + 1) * LANES
                ]
        keeps[chunk].start()

    decay_col = levels * heads
    beta_col = decay_col + heads
    norm_col = beta_col + heads
    lane = lane_of(rows)
    row_id, col_id = pair_ids(rows)
    inclusive = row_id >= col_id
    strict = row_id > col_id
    apart = row_id ^ col_id
    eye = (row_id == col_id).astype(F32)
    fetch_small.wait()
    small_rows = small_in.shape[0] * heads
    for level in range(small_in.shape[0]):
        small_wide[level * heads : (level + 1) * heads, :] = small_in[level].astype(F32)
    small_wide[small_rows:, :] = jnp.zeros((LANES - small_rows, width), F32)
    small_ref[...] = small_wide[...].astype(BF16)
    fetch_rates.wait()
    rate, bias = head_rows(hp_ref, heads, decay_col, beta_col)
    rates_ref[0:1, :] = rate
    rates_ref[1:2, :] = bias
    fetch_tokens.wait()
    gate = mm_nt(tokens[...], small_ref[...])
    gate_ref[...] = gate
    switch = jax.nn.sigmoid(gate + bias)
    lam = jnp.maximum(gate, 0.0) + jnp.log1p(jnp.exp(-jnp.abs(gate)))
    cum = mm_full(inclusive.astype(F32), -rate * switch)
    pack = jnp.where(lane < decay_col, lam, jnp.where(lane < beta_col, cum, switch))
    pack_t = pack.T
    pack_t_ref[...] = pack_t

    def multiply(part, first, last):
        span = slice((part * heads) * LANES, (part + 1) * heads * LANES)
        own = jnp.dot(
            tokens[:, first * depth : last * depth], wr[first * depth : last * depth, span],
            preferred_element_type=F32,
        )
        if first == 0:
            acc[:, span] = own
        else:
            acc[:, span] += own

    for chunk in range(chunks):
        relay(chunk)
        if chunk % 2 == 1:
            multiply(1, chunk - 1, chunk + 1)

    def unit_of(part, head):
        col = (part * heads + head) * LANES
        raw = acc[:, col : col + LANES]
        scale = lax.rsqrt(row_sum(raw * raw) + EPS)
        qkv_ref[part, head] = raw * scale
        return raw * scale, jnp.where(lane == norm_col + part * heads + head, scale, 0.0)

    scales = jnp.zeros((rows, LANES), F32)
    k_all, lower_all = [], []
    for head in range(heads):
        unit, scale = unit_of(1, head)
        k_all.append(unit)
        scales = scales + scale
        decay = decay_of(pack, pack_t, decay_col + head, inclusive)
        decay_ref[head] = decay.astype(BF16)
        base = jnp.where(strict, decay * mm_nt(unit, unit), 0.0)
        base_ref[head] = base.astype(BF16)
        lower = column(pack, beta_col + head) * base
        lower_ref[head] = lower.astype(BF16)
        lower_all.append(lower)

    def later():
        for part in (2, 0):
            for at in range(0, chunks, chunks // 4):
                yield
                multiply(part, at, at + chunks // 4)

    chain, filler = invert(lower_all, eye, apart, rows), later()
    while True:
        try:
            next(chain)
        except StopIteration as stop:
            trans_all = stop.value
            break
        next(filler, None)
    for _ in filler:
        pass
    mixed_all = []
    for head in range(heads):
        trans_ref[head] = trans_all[head]
        cum_row = pack_t[decay_col + head : decay_col + head + 1, :]
        tail_t = k_all[head].T * jnp.exp(cum_row[:, rows - 1 :] - cum_row)
        mixed_all.append(mm(tail_t, trans_all[head]).astype(BF16))
    eye_key = eye[:LANES, :LANES]
    for head in range(heads):
        mixed_t_ref[head] = mixed_all[head]
        col = (2 * heads + head) * LANES
        v_in = acc[:, col : col + LANES]
        qkv_ref[2, head] = v_in
        cum_col = column(pack, decay_col + head)
        beta = column(pack, beta_col + head)
        grown = (beta * jnp.exp(cum_col)) * k_all[head]
        both = jnp.concatenate([-grown, beta * v_in], 1)
        pair = mm(mixed_all[head], both)
        last = jnp.exp(cum_col[rows - 1 : rows, :])
        pair_ref[head, :, :LANES] = (last * eye_key + pair[:, :LANES]).astype(BF16)
        pair_ref[head, :, LANES:] = pair[:, LANES:].astype(BF16)
    for head in range(heads):
        scales = scales + unit_of(0, head)[1]
    pack_ref[...] = jnp.where(lane < norm_col, pack, scales)
    for keep in keeps:
        keep.wait()


def project(place, tokens, flat_w, small, head_param, heads, levels):
    rows, width = tokens.shape
    chunks = 8
    cols = 3 * heads
    key = flat_w.shape[1]
    square = (heads, rows, rows)
    out_shape = (
        stored((width, cols * key), BF16),
        kept((LANES, width), BF16),
        kept((3, heads, rows, key), F32),
        kept((rows, LANES), F32),
        kept((rows, LANES), F32),
        kept((LANES, rows), F32),
        kept(square, BF16),
        kept((heads, key, rows), BF16),
        kept(square, BF16),
        kept(square, BF16),
        kept(square, BF16),
        kept((2, LANES), F32),
        kept((heads, key, 2 * key), BF16),
    )
    scratch = [
        pltpu.VMEM(tokens.shape, BF16),
        pltpu.VMEM(flat_w.shape, BF16),
        pltpu.VMEM((width, cols * key), BF16),
        pltpu.VMEM(small.shape, BF16),
        pltpu.VMEM((LANES, width), F32),
        pltpu.VMEM((rows, cols * key), F32),
        pltpu.VMEM(head_param.shape, F32),
        pltpu.SemaphoreType.DMA((3,)),
        pltpu.SemaphoreType.DMA((chunks,)),
        pltpu.SemaphoreType.DMA((chunks,)),
    ]
    return local_call(
        functools.partial(project_body, (heads, levels, chunks)), "project", 36, out_shape,
        [place], [], scratch, [head_param, tokens, flat_w, small], [HBM] + [WHOLE] * 12,
    )


def local_body(
    sizes, qkv_ref, pack_ref, pack_t_ref, trans_ref, mixed_t_ref, decay_ref, grad_ref, weight_ref, *outs
):
    heads, levels, bits = sizes
    (attn_ref, attn_t_ref, prod_t_ref, scores_ref, mix_ref, mixed_ref, local_ref, hat_ref,
     hat_t_ref, grad_normed_ref) = outs
    grad_normed_ref[...] = mm_nt(grad_ref[...], weight_ref[...])
    rows = pack_ref.shape[0]
    decay_col = levels * heads
    beta_col = decay_col + heads
    pack = pack_ref[...]
    pack_t = pack_t_ref[...]
    row_id, col_id = pair_ids(rows)
    apart = row_id ^ col_id
    for head in range(heads):
        scores = mm_nt_fine(qkv_ref[0, head], qkv_ref[1, head]) * decay_ref[head].astype(F32)
        scores_ref[head] = scores.astype(BF16)
        mix_ref[head] = level_mix(pack, head, heads, bits, apart).astype(BF16)
        mixed_ref[head] = mixed_t_ref[head].astype(F32).T.astype(BF16)
    for head in range(heads):
        attn = mm(scores_ref[head], trans_ref[head])
        attn_ref[head] = attn.astype(BF16)
        attn_t_ref[head] = attn.T.astype(BF16)
        attn = attn * pack_t[beta_col + head : beta_col + head + 1, :]
        prod = attn * mix_ref[head].astype(F32)
        prod_t_ref[head] = prod.T.astype(BF16)
        growth = jnp.exp(column(pack, decay_col + head))
        local_ref[head] = mm(prod, qkv_ref[2, head])
        hat = growth * qkv_ref[0, head] - mm(attn, growth * qkv_ref[1, head])
        hat_ref[head] = hat.astype(BF16)
        hat_t_ref[head] = hat.T.astype(BF16)


def local_part(arrays, levels, bits):
    heads, rows, key = arrays[0].shape[1:]
    square = (heads, rows, rows)
    out_shape = (
        kept(square, BF16),
        kept(square, BF16),
        kept(square, BF16),
        kept(square, BF16),
        kept(square, BF16),
        kept((heads, rows, key), BF16),
        kept((heads, rows, key), F32),
        kept((heads, rows, key), BF16),
        kept((heads, key, rows), BF16),
        kept((rows, heads * key), F32),
    )
    return local_call(
        functools.partial(local_body, (heads, levels, bits)), "local_part", 10, out_shape,
        [], arrays,
    )


def join_pair(upper, own, other):
    key = own.shape[0]
    low = jnp.where(upper, other, own)
    high = jnp.where(upper, own, other)
    moved = mm(high[:, :key], low)
    late = jnp.concatenate([jnp.zeros((key, key), F32), high[:, key:].astype(F32)], 1)
    return (moved + late).astype(BF16)


def join_body(place_ref, own_ref, other_ref, out_ref):
    half = out_ref.shape[0]
    upper = (place_ref[0] & 1) == 1
    for slot in range(half):
        head = (place_ref[0] & 1) * half + slot
        out_ref[slot] = join_pair(upper, own_ref[head], other_ref[head])


def join_half(place, own, other):
    half = (own.shape[0] // 2,) + own.shape[1:]
    return local_call(join_body, "join_half", 6, [kept(half, BF16)], [place], [own, other])[0]


def gather_node(head, bit, first, near, uppers):
    if bit == 0:
        mine, theirs = near[first]
        half = mine.shape[0]
        here = uppers[0] if head >= half else jnp.logical_not(uppers[0])
        return jnp.where(here, mine[head % half], theirs[head % half])
    own = gather_node(head, bit - 1, first, near, uppers)
    other = gather_node(head, bit - 1, first ^ (1 << (bit - 1)), near, uppers)
    return join_pair(uppers[bit], own, other)


def reach_body(
    sizes, place_ref, gain_ref, pack_ref, local_ref, hat_ref, grad_ref, weight_ref, *refs
):
    heads, bits, far, count, near_count = sizes
    first_ref = refs[0]
    near = [None] + [(refs[1 + at], refs[1 + near_count + at]) for at in range(near_count)]
    refs = refs[2 * near_count + 1 :]
    out_refs = refs[:2]
    dout_ref, found_ref, prefix_ref, dfar_ref = refs[2:6]
    nodes = refs[6:-1]
    normed_ref = refs[-1]
    rows = pack_ref.shape[0]
    key = hat_ref.shape[2]
    pack = pack_ref[...]
    gain = gain_ref[...]
    lane = lane_of(rows)
    all_heads = range(heads)
    uppers = [((place_ref[0] >> bit) & 1) == 1 for bit in range(far)]
    others = []
    for bit in range(far):
        if bit == 0:
            others.append([first_ref[head] for head in all_heads])
        else:
            others.append(
                [gather_node(head, bit - 1, 1 << (bit - 1), near, uppers) for head in all_heads]
            )
            for head in all_heads:
                nodes[bit - 1][head] = others[bit][head]
    eye_key = jnp.where(pair_ids(key)[0] == pair_ids(key)[1], 1.0, 0.0).astype(BF16)
    prefix = [eye_key for head in all_heads]
    found = []
    for bit in range(far):
        for head in all_heads:
            prefix_ref[head, bit] = prefix[head]
        moved = [mm(prefix[head], others[bit][head]) for head in all_heads]
        found.append([jnp.where(uppers[bit], m[:, key:], 0.0).astype(BF16) for m in moved])
        prefix = [
            jnp.where(uppers[bit], moved[head][:, :key].astype(BF16), prefix[head])
            for head in all_heads
        ]
    found = [jnp.concatenate([found[bit][head] for bit in range(far)], 1) for head in all_heads]
    reached = [mm(hat_ref[head], found[head]) for head in all_heads]
    dfar = jnp.zeros((rows, LANES), F32)
    for head in all_heads:
        found_ref[head] = found[head]
        summed = local_ref[head]
        parts = []
        for bit in range(far):
            parts.append(reached[head][:, bit * key : (bit + 1) * key])
            summed = summed + column(pack, (bits + 1 + bit) * heads + head) * parts[bit]
        scale = lax.rsqrt(jnp.mean(summed * summed, -1, keepdims=True) + EPS)
        unit = summed * scale
        normed_ref[:, head * key : (head + 1) * key] = (unit * gain).astype(BF16)
        pulled = grad_ref[:, head * key : (head + 1) * key] * gain
        dout = scale * (pulled - unit * jnp.mean(pulled * unit, -1, keepdims=True))
        dout_ref[head] = dout
        for bit in range(far):
            col = (bits + 1 + bit) * heads + head
            dfar = jnp.where(lane == col, row_sum(dout * parts[bit]), dfar)
    dfar_ref[...] = dfar
    size = weight_ref.shape[1] // count
    for mask in range(count):
        dest = place_ref[1] ^ mask
        cols = pl.ds(pl.multiple_of(dest * size, size), size)
        out_refs[mask % 2][mask // 2] = jnp.dot(
            normed_ref[...], weight_ref[:, cols], preferred_element_type=F32
        ).astype(BF16)


def reach(place, arrays, first, near, bits, far, count):
    gain, pack, local_out, hat, grad_normed, weight = arrays
    heads, rows, key = hat.shape
    nodes = tuple(kept(first.shape, BF16) for bit in range(1, far))
    size = weight.shape[1] // count
    out_shape = (kept((count // 2, rows, size), BF16),) * 2 + (
        kept((heads, rows, key), F32),
        kept((heads, key, far * key), BF16),
        kept((heads, far, key, key), BF16),
        kept((rows, LANES), F32),
    ) + nodes
    mine, theirs = near
    got = local_call(
        functools.partial(reach_body, (heads, bits, far, count, len(mine))), "reach", 10, out_shape,
        [place], [*arrays, first, *mine, *theirs], [pltpu.VMEM((rows, heads * key), BF16)],
    )
    return got[:2], got[2:6], got[6:]


def return_body(sizes, place_ref, pack_ref, hat_t_ref, dout_ref, found_ref, prefix_ref, *refs):
    heads, bits, far = sizes
    others = refs[:far]
    dhat_ref = refs[far]
    sends = refs[far + 1 :]
    key = hat_t_ref.shape[1]
    pack = pack_ref[...]
    all_heads = range(heads)
    uppers = [((place_ref[0] >> bit) & 1) == 1 for bit in range(far)]
    spread = []
    for head in all_heads:
        parts = []
        for bit in range(far):
            weight = column(pack, (bits + 1 + bit) * heads + head)
            parts.append((weight * dout_ref[head]).astype(BF16))
        spread.append(jnp.concatenate(parts, 1))
    dfound = [mm(hat_t_ref[head], spread[head]) for head in all_heads]
    for head in all_heads:
        dhat_ref[head] = mm_nt(spread[head], found_ref[head])
    dprefix = [jnp.zeros((key, key), F32) for head in all_heads]
    for bit in reversed(range(far)):
        dfree = [
            jnp.where(uppers[bit], d[:, bit * key : (bit + 1) * key], 0.0) for d in dfound
        ]
        both = [
            jnp.concatenate([jnp.where(uppers[bit], dprefix[head], 0.0), dfree[head]], 1)
            for head in all_heads
        ]
        for head in all_heads:
            sent = dfree[head] if bit == far - 1 else both[head]
            sends[bit][head] = mm_tn(prefix_ref[head, bit], sent).astype(BF16)
        if bit > 0:
            moved = [mm_nt(both[head], others[bit][head]) for head in all_heads]
            dprefix = [
                jnp.where(uppers[bit], moved[head], dprefix[head]) for head in all_heads
            ]


def return_states(place, pack, hat_t, dout, found, prefix, others, bits):
    heads, rows, key = dout.shape
    far = len(others)
    sends = tuple(
        kept((heads, key, (1 if bit == far - 1 else 2) * key), BF16) for bit in range(far)
    )
    got = local_call(
        functools.partial(return_body, (heads, bits, far)), "return_states", 8,
        (kept(dout.shape, F32),) + sends, [place], [pack, hat_t, dout, found, prefix, *others],
    )
    return got[0], got[1:]


def add_body(*refs):
    count = len(refs) // 3
    for at in range(count):
        left, right = refs[at][...].astype(F32), refs[count + at][...].astype(F32)
        refs[2 * count + at][...] = (left + right).astype(BF16)


def add_all(left, right):
    out_shape = [kept(value.shape, BF16) for value in left]
    return local_call(add_body, "add_all", 6, out_shape, [], [*left, *right])


def lower_pull(dlower, base, lower, beta, decay, strict, k_in):
    dlower = jnp.where(strict, dlower, 0.0)
    dbeta = row_sum(dlower * base.astype(F32))
    dgram = dlower * (beta * decay)
    dkey = mm(dgram, k_in) + mm_tn(dgram, k_in)
    return dbeta, beta * dbeta, col_sum(dlower * lower.astype(F32)), dkey


def pull_body(sizes, *refs):
    heads, levels, bits = sizes
    (qkv_ref, pack_ref, pack_t_ref, trans_ref, attn_ref, attn_t_ref, prod_t_ref, scores_ref,
     mix_ref, decay_ref, base_ref, lower_ref, dout_ref, dhat_ref) = refs[:14]
    dqkv_ref, dgrown_ref, dcol_ref, drow_ref = refs[14:]
    rows = pack_ref.shape[0]
    decay_col = levels * heads
    beta_col = decay_col + heads
    block_bit = BLOCK.bit_length() - 1
    pack = pack_ref[...]
    pack_t = pack_t_ref[...]
    row_id, col_id = pair_ids(rows)
    strict = row_id > col_id
    apart = row_id ^ col_id
    lane = lane_of(rows)
    all_heads = range(heads)
    dcol = jnp.zeros((rows, LANES), F32)
    dbeta_rows, dcum_rows, dattn_all = [], [], []
    for head in all_heads:
        high, low = split(dout_ref[head])
        v_in = qkv_ref[2, head].astype(BF16)
        dprod = mm_nt(high, v_in) + mm_nt(low, v_in)
        dqkv_ref[2, head] = mm(prod_t_ref[head], high)
        beta_row = pack_t[beta_col + head : beta_col + head + 1, :]
        growth = jnp.exp(column(pack, decay_col + head))
        attn0 = attn_ref[head].astype(F32)
        touched = dprod * (attn0 * beta_row)
        for level in range(bits + 1):
            if level == 0:
                here = (apart >> block_bit) == 0
            else:
                here = (apart >> (block_bit + level - 1)) == 1
            dcol = jnp.where(
                lane == level * heads + head, row_sum(jnp.where(here, touched, 0.0)), dcol
            )
        dattn = dprod * mix_ref[head].astype(F32) - mm_nt(dhat_ref[head], growth * qkv_ref[1, head])
        dbeta_rows.append(col_sum(dattn * attn0))
        dattn_all.append((dattn * beta_row).astype(BF16))
    dscore_all = [mm_nt(dattn_all[head], trans_ref[head]) for head in all_heads]
    moved_all = []
    for head in all_heads:
        both = jnp.concatenate(
            [dscore_all[head].astype(BF16), dhat_ref[head].astype(BF16)], 1
        )
        moved_all.append(mm(attn_t_ref[head], both))
    for head in all_heads:
        q_in, k_in = qkv_ref[0, head], qkv_ref[1, head]
        beta = column(pack, beta_col + head)
        growth = jnp.exp(column(pack, decay_col + head))
        dscore = dscore_all[head]
        decay = decay_ref[head].astype(F32)
        dprobs = dscore * decay
        shift = dscore * scores_ref[head].astype(F32)
        dgrown_ref[head] = -beta * moved_all[head][:, rows:]
        dbeta, dcum_col, dcum_row, dk_lower = lower_pull(
            -moved_all[head][:, :rows], base_ref[head], lower_ref[head], beta, decay, strict, k_in
        )
        dhat = dhat_ref[head]
        dqkv_ref[0, head] = growth * dhat + mm(dprobs, k_in)
        dqkv_ref[1, head] = mm_tn(dprobs, q_in) + dk_lower
        dcum_col = dcum_col + row_sum(shift) + growth * row_sum(q_in * dhat)
        dcum_rows.append(-dcum_row - col_sum(shift))
        dcol = jnp.where(lane == beta_col + head, dbeta, dcol)
        dcol = jnp.where(lane == decay_col + head, dcum_col, dcol)
    dcol_ref[...] = dcol
    drow_ref[...] = jnp.concatenate(dcum_rows + dbeta_rows, 0)


def pull_local(arrays, levels, bits):
    heads, rows, key = arrays[0].shape[1:]
    out_shape = (
        kept((3, heads, rows, key), F32),
        kept((heads, rows, key), F32),
        kept((rows, LANES), F32),
        kept((2 * heads, rows), F32),
    )
    return local_call(
        functools.partial(pull_body, (heads, levels, bits)), "pull_local", 12, out_shape, [], arrays
    )


def finish_body(sizes, place_ref, *refs):
    heads, levels, far, arrived_counts = sizes
    (qkv_ref, gate_ref, pack_ref, trans_ref, mixed_ref, decay_ref, base_ref, lower_ref,
     dqkv_ref, dgrown_ref, dcol_ref, drow_ref, dfar_ref, rates_ref) = refs[:14]
    others = refs[14 : 14 + far]
    refs = refs[14 + far :]
    arrived = []
    for found in arrived_counts:
        arrived.append(refs[:found])
        refs = refs[found:]
    dproj, dgate_ref = refs
    rows = pack_ref.shape[0]
    key = qkv_ref.shape[3]
    decay_col = levels * heads
    beta_col = decay_col + heads
    norm_col = beta_col + heads
    place = place_ref[0]
    all_heads = range(heads)
    uppers = [((place >> bit) & 1) == 1 for bit in range(far)]
    pack = pack_ref[...]
    row_id, col_id = pair_ids(rows)
    strict = row_id > col_id
    lane = lane_of(rows)
    last_row = lax.broadcasted_iota(jnp.int32, (rows, 1), 0) == rows - 1
    eye_key = (pair_ids(key)[0] == pair_ids(key)[1]).astype(F32)
    dpair = [jnp.zeros((key, 2 * key), F32) for head in all_heads]
    for bit in reversed(range(far)):
        for head in all_heads:
            got = arrived[bit][0][head].astype(F32)
            for more in arrived[bit][1:]:
                got = got + more[head].astype(F32)
            other = others[bit][head]
            if bit == far - 1:
                got = jnp.concatenate([jnp.zeros((key, key), F32), got], 1)
                dpair[head] = jnp.where(uppers[bit], 0.0, got)
            else:
                as_low = mm_tn(other[:, :key], dpair[head]) + got
                as_high = mm_nt(dpair[head], other)
                as_high = jnp.concatenate([as_high, dpair[head][:, key:]], 1)
                dpair[head] = jnp.where(uppers[bit], as_high, as_low)
    moved_all, dmixed_all = [], []
    for head in all_heads:
        beta = column(pack, beta_col + head)
        growth = jnp.exp(column(pack, decay_col + head))
        both = jnp.concatenate([-growth * qkv_ref[1, head], qkv_ref[2, head]], 1)
        dmixed_all.append(mm_nt(both, dpair[head]))
        moved_all.append(mm(beta * mixed_ref[head].astype(F32), dpair[head]))
    dtail_all = [
        mm(trans_ref[head], column(pack, beta_col + head) * dmixed_all[head])
        for head in all_heads
    ]
    dlower_all = [-mm_nt(mixed_ref[head], dtail_all[head]) for head in all_heads]
    dcol = jnp.where(lane < decay_col, dcol_ref[...] + dfar_ref[...], dcol_ref[...])
    dcum_rows = []
    for head in all_heads:
        q_in, k_in = qkv_ref[0, head], qkv_ref[1, head]
        beta = column(pack, beta_col + head)
        cum_col = column(pack, decay_col + head)
        growth = jnp.exp(cum_col)
        last = cum_col[rows - 1 : rows, :]
        tail = jnp.exp(last - cum_col)
        dgrown = dgrown_ref[head] - moved_all[head][:, :key]
        dv = dqkv_ref[2, head] + moved_all[head][:, key:]
        dbeta_more = row_sum(mixed_ref[head].astype(F32) * dmixed_all[head])
        dtail = dtail_all[head]
        dbeta, dcum_col, dcum_row, dk_lower = lower_pull(
            dlower_all[head], base_ref[head], lower_ref[head], beta, decay_ref[head].astype(F32),
            strict, k_in
        )
        dcum_rows.append(-dcum_row)
        tail_pull = tail * row_sum(k_in * dtail)
        trace = col_sum(row_sum(dpair[head][:, :key] * eye_key))
        at_last = col_sum(tail_pull) + jnp.exp(last) * trace
        dcum_col = dcum_col + growth * row_sum(k_in * dgrown) - tail_pull
        dcum_col = dcum_col + jnp.where(last_row, at_last, 0.0)
        dk = dqkv_ref[1, head] + dk_lower + growth * dgrown + tail * dtail
        dq = dqkv_ref[0, head]
        dcol = dcol + jnp.where(lane == beta_col + head, dbeta + dbeta_more, 0.0)
        dcol = dcol + jnp.where(lane == decay_col + head, dcum_col, 0.0)
        for part, unit, dunit in ((0, q_in, dq), (1, k_in, dk)):
            scale = column(pack, norm_col + part * heads + head)
            back = scale * (dunit - unit * row_sum(unit * dunit))
            col = (part * heads + head) * key
            dproj[:, col : col + key] = back.astype(BF16)
        col = (2 * heads + head) * key
        dproj[:, col : col + key] = dv.astype(BF16)
    drow = drow_ref[...]
    drow = drow + jnp.concatenate(dcum_rows + [jnp.zeros((heads, rows), F32)], 0)
    drow = jnp.concatenate(
        [jnp.zeros((decay_col, rows), F32), drow,
         jnp.zeros((LANES - norm_col, rows), F32)], 0
    )
    dcol = dcol + drow.T
    rate, bias = rates_ref[0:1, :], rates_ref[1:2, :]
    switch = jax.nn.sigmoid(gate_ref[...] + bias)
    dlog = mm_full((row_id <= col_id).astype(F32), dcol)
    slope = switch * (1.0 - switch)
    dgate = jnp.where(
        lane < decay_col,
        dcol * switch,
        jnp.where(lane < beta_col, -rate * dlog * slope, dcol * slope),
    )
    dgate_ref[...] = jnp.where(lane < norm_col, dgate, 0.0).astype(BF16)


def finish(place, arrays, others, arrived, levels):
    heads, rows, key = arrays[0].shape[1:]
    counts = tuple(len(group) for group in arrived)
    flat = [value for group in arrived for value in group]
    return local_call(
        functools.partial(finish_body, (heads, levels, len(others), counts)), "finish", 10,
        [kept((rows, 3 * heads * key), BF16), kept((rows, LANES), BF16)],
        [place], [*arrays, *others, *flat],
    )


def tokens_body(count, place_ref, dproj_ref, dgate_ref, wr_ref, small_ref, *refs):
    keep_ref, send_ref = refs[:2]
    direct_refs = refs[2:]
    size = wr_ref.shape[0] // count
    half = size // 2
    for mask in range(count):
        dest = place_ref[1] ^ mask
        span = pl.ds(pl.multiple_of(dest * size, size), size)
        part = mm_nt(dproj_ref[...], wr_ref[span, :]) + mm(dgate_ref[...], small_ref[:, span])
        direct_refs[mask][...] = part[:, :half].astype(BF16)
        target = send_ref if mask % 2 else keep_ref
        target[mask // 2] = part[:, half:].astype(BF16)


def pull_tokens(place, dproj, dgate, wr, small_t, count):
    rows = dproj.shape[0]
    half = wr.shape[0] // count // 2
    out_shape = [kept((count // 2, rows, half), BF16)] * 2 + [kept((rows, half), BF16)] * count
    got = local_call(
        functools.partial(tokens_body, count), "pull_tokens", 8, out_shape,
        [place], [dproj, dgate, wr, small_t],
    )
    return got[0], got[1], got[2:]


def swap(value, axis, mask):
    size = lax.axis_size(axis)
    return lax.ppermute(value, axis, [(at, at ^ mask) for at in range(size)])


def far_first(count):
    return sorted(range(1, count), key=lambda mask: mask < count // 2)


def halve_body(own_ref, got_ref, keep_ref, send_ref):
    for at in range(own_ref.shape[0]):
        total = own_ref[at].astype(F32) + got_ref[at].astype(F32)
        target = send_ref if at % 2 else keep_ref
        target[at // 2] = total.astype(target.dtype)


def halving(keep, send, axis, tied):
    mask = 1
    while keep.shape[0] > 1:
        got = swap(send, axis, mask)
        half = (keep.shape[0] // 2,) + keep.shape[1:]
        keep, send = local_call(
            halve_body, "halve", 6, [kept(half, F32), kept(half, BF16)], [], [keep, got]
        )
        send, tied = lax.optimization_barrier((send, tied))
        mask *= 2
    return keep, swap(send, axis, mask), tied


def sum_body(count, *refs):
    keep_ref, got_ref = refs[:2]
    out_ref = refs[-1]
    total = keep_ref[0].astype(F32) + got_ref[0].astype(F32)
    if count == 0:
        out_ref[...] = total.astype(BF16)
        return
    half = out_ref.shape[1] // 2
    out_ref[:, half:] = total.astype(BF16)
    total = refs[2][...].astype(F32)
    for ref in refs[3:-1]:
        total = total + ref[...].astype(F32)
    out_ref[:, :half] = total.astype(BF16)


def head_sum(keep, last, direct, got):
    rows, cols = keep.shape[1:]
    out = jax.ShapeDtypeStruct((rows, cols * (2 if direct else 1)), BF16)
    return local_call(
        functools.partial(sum_body, len(direct)), "head_sum", 6, [out], [],
        [keep, last, *direct[:1], *got],
    )[0]


def on_device(tokens, qkv_weight, small_weight, head_param, norm_gain, out_weight, grad_out):
    rows, width = tokens.shape
    heads, key = qkv_weight.shape[2:]
    levels = small_weight.shape[2] - 2
    bits = (rows // BLOCK).bit_length() - 1
    size = lax.axis_size("ctx")
    far = size.bit_length() - 1
    count = lax.axis_size("head")
    place = jnp.stack([lax.axis_index("ctx"), lax.axis_index("head")]).astype(jnp.int32)
    flat_w = qkv_weight.reshape(width * 3 * heads, key)
    small = jnp.transpose(small_weight, (2, 1, 0))
    rates = head_param.T
    flat_out = out_weight.reshape(heads * key, width)
    gain = norm_gain.reshape(1, key)

    (wr, small_t, qkv, gate, pack, pack_t, trans, mixed_t, decay, base, lower, rates_row,
     pair) = project(
        place, tokens, flat_w, small, rates, heads, levels
    )
    first = swap(pair, "ctx", 1)
    node = join_half(place, pair, first)
    mine = [swap(node, "ctx", 2 * at) for at in range(1, size // 2)]
    (attn, attn_t, prod_t, scores, mix, mixed, local_out, hat, hat_t, grad_normed) = local_part(
        [qkv, pack, pack_t, trans, mixed_t, decay, grad_out, flat_out], levels, bits
    )
    mine, local_out, grad_normed = lax.optimization_barrier((mine, local_out, grad_normed))
    theirs = [swap(value, "ctx", 1) for value in mine]
    out_parts, (dout, found, prefix, dfar), nodes = reach(
        place, [gain, pack, local_out, hat, grad_normed, flat_out], first, (mine, theirs),
        bits, far, count
    )
    others = [first, *nodes]
    dhat, sends = return_states(place, pack, hat_t, dout, found, prefix, others, bits)
    got = [swap(value, "ctx", 1) for value in sends]
    arrived = [[got[0]]]
    sums = add_all(sends[1:], got[1:])
    for bit in range(1, far):
        half = 1 << (bit - 1)
        arrived.append([swap(sums[bit - 1], "ctx", 2 * at) for at in range(half, 2 * half)])
    dqkv, dgrown, dcol, drow = pull_local(
        [qkv, pack, pack_t, trans, attn, attn_t, prod_t, scores, mix, decay, base, lower, dout,
         dhat],
        levels, bits,
    )
    keep_out, last_out, dcol = halving(*out_parts, "head", dcol)
    arrays = [qkv, gate, pack, trans, mixed, decay, base, lower, dqkv, dgrown, dcol, drow, dfar,
              rates_row]
    dproj, dgate = finish(place, arrays, others, arrived, levels)
    keep, send, direct = pull_tokens(place, dproj, dgate, wr, small_t, count)
    direct, last_out = lax.optimization_barrier((direct, last_out))
    got = [swap(direct[mask], "head", mask) for mask in far_first(count)]
    keep, last, _ = halving(keep, send, "head", ())
    return head_sum(keep_out, last_out, [], []), head_sum(keep, last, direct, got)


def solution(mesh):
    placed = (
        P("ctx", None),
        P(None, None, "head", None),
        P(None, "head", None),
        P("head", None),
        P(),
        P("head", None, None),
        P("ctx", None),
    )
    return jax.shard_map(
        on_device,
        mesh=mesh,
        in_specs=placed,
        out_specs=(P("ctx", "head"), P("ctx", "head")),
        check_vma=False,
    )
```

```python
import functools

import jax
import jax.numpy as jnp
from jax import lax
from jax.experimental import pallas as pl
from jax.experimental.pallas import tpu as pltpu
from jax.sharding import PartitionSpec as P

BLOCK = 64
LANES = 128
EPS = 1e-06
MIB = 1024 * 1024
F32 = jnp.float32
BF16 = jnp.bfloat16
WHOLE = pl.BlockSpec(memory_space=pltpu.VMEM)
SCALARS = pl.BlockSpec(memory_space=pltpu.SMEM)
HBM = pl.BlockSpec(memory_space=pltpu.HBM)


def contract(left, right, dim_left, dim_right):
    return lax.dot_general(
        left.astype(BF16),
        right.astype(BF16),
        (((dim_left,), (dim_right,)), ((), ())),
        preferred_element_type=F32,
    )


def mm(left, right):
    return contract(left, right, 1, 0)


def mm_nt(left, right):
    return contract(left, right, 1, 1)


def mm_tn(left, right):
    return contract(left, right, 0, 0)


def split(values):
    high = values.astype(BF16)
    return high, (values - high.astype(F32)).astype(BF16)


def mm_nt_fine(left, right):
    left_high, left_low = split(left)
    right_high, right_low = split(right)
    return mm_nt(left_high, right_high) + (mm_nt(left_low, right_high) + mm_nt(left_high, right_low))


def mm_ones(ones, values):
    high = values.astype(BF16)
    rest = values - high.astype(F32)
    middle = rest.astype(BF16)
    low = (rest - middle.astype(F32)).astype(BF16)
    return mm(ones, high) + (mm(ones, middle) + mm(ones, low))


def pair_ids(count):
    row_id = lax.broadcasted_iota(jnp.int32, (count, count), 0)
    col_id = lax.broadcasted_iota(jnp.int32, (count, count), 1)
    return row_id, col_id


def row_sum(values):
    return jnp.sum(values, 1, keepdims=True)


def col_sum(values):
    return jnp.sum(values, 0, keepdims=True)


def lane_of(rows):
    return lax.broadcasted_iota(jnp.int32, (rows, LANES), 1)


def decay_of(pack, pack_t, col, inclusive):
    spread = pack[:, col : col + 1] - pack_t[col : col + 1, :]
    return jnp.where(inclusive, jnp.exp(jnp.minimum(spread, 0.0)), 0.0)


def kept(shape, dtype):
    return pltpu.VMEM(shape, dtype)


def stored(shape, dtype):
    return pltpu.HBM(shape, dtype)


def pin(values, space):
    return [pltpu.with_memory_space_constraint(value, space) for value in values]


def local_call(
    body, name, limit, out_shape, scalars, arrays, scratch=(), remote=(), out_specs=None
):
    return pl.pallas_call(
        body,
        out_shape=tuple(out_shape),
        in_specs=[SCALARS] * len(scalars)
        + [WHOLE] * len(arrays)
        + [HBM] * len(remote),
        out_specs=tuple(out_specs or [WHOLE] * len(out_shape)),
        scratch_shapes=list(scratch),
        compiler_params=pltpu.CompilerParams(vmem_limit_bytes=limit * MIB),
        name=name,
    )(*scalars, *pin(arrays, pltpu.VMEM), *pin(remote, pltpu.HBM))


def column(pack, at):
    return pack[:, at : at + 1]


def level_mix(pack, head, heads, bits, apart):
    block_bit = BLOCK.bit_length() - 1
    mixed = jnp.broadcast_to(column(pack, head), apart.shape)
    for level in range(1, bits + 1):
        here = (apart >> (block_bit + level - 1)) >= 1
        mixed = jnp.where(here, column(pack, level * heads + head), mixed)
    return mixed


def head_rows(hp_ref, heads, decay_col, beta_col):
    lane_row = lane_of(1)
    rate = jnp.zeros((1, LANES), F32)
    bias = jnp.zeros((1, LANES), F32)
    for head in range(heads):
        rate = jnp.where(lane_row == decay_col + head, hp_ref[0:1, head : head + 1], rate)
        bias = jnp.where(lane_row == beta_col + head, hp_ref[1:2, head : head + 1], bias)
    return rate, bias


def merge_blocks(trans_all, edge_all, levels, first):
    if first:
        powers = [edge.astype(BF16) for edge in edge_all]
        trans_all = [trans - power for trans, power in zip(trans_all, powers)]
    else:
        powers = [mm(edge, trans).astype(BF16) for edge, trans in zip(edge_all, trans_all)]
        yield
        trans_all = [
            trans - mm(trans, power).astype(BF16) for trans, power in zip(trans_all, powers)
        ]
    for level in range(1, levels):
        powers = [mm(power, power).astype(BF16) for power in powers]
        yield
        trans_all = [
            trans + mm(trans, power).astype(BF16) for trans, power in zip(trans_all, powers)
        ]
    return trans_all


def invert(lower_all, eye, apart, rows):
    trans_all = [eye.astype(BF16) for lower in lower_all]
    bits = rows.bit_length() - 1
    start = 0
    while start < bits:
        levels = min(2 if bits - start == 2 else 3, bits - start)
        here = jnp.logical_and((apart >> start) >= 1, (apart >> (start + levels)) == 0)
        edge_all = [jnp.where(here, lower, 0.0) for lower in lower_all]
        trans_all = yield from merge_blocks(trans_all, edge_all, levels, start == 0)
        start += levels
        yield
    rest_all = []
    for trans, lower in zip(trans_all, lower_all):
        high, low = split(lower)
        rest_all.append(eye - trans.astype(F32) - mm(high, trans) - mm(low, trans))
    yield
    return [
        (trans.astype(F32) + mm(trans, rest)).astype(BF16)
        for trans, rest in zip(trans_all, rest_all)
    ]


def project_body(sizes, place_ref, hp_hbm, tokens_hbm, w_hbm, small_hbm, *refs):
    heads, levels, chunks = sizes
    (wr_hbm, small_ref, qkv_ref, gate_ref, pack_ref, pack_t_ref, trans_ref, mixed_t_ref,
     decay_ref, base_ref, lower_ref, rates_ref, pair_ref) = refs[:13]
    tokens, wide_in, wide_even, wide_odd, wr, small_in, small_wide, acc, hp_ref = refs[13:22]
    sems, in_sems, out_sems = refs[22:]
    rows, width = tokens.shape
    depth = width // chunks
    cols = 3 * heads
    fetch_tokens = pltpu.make_async_copy(tokens_hbm, tokens, sems.at[0])
    fetch_small = pltpu.make_async_copy(small_hbm, small_in, sems.at[1])
    fetch_rates = pltpu.make_async_copy(hp_hbm, hp_ref, sems.at[2])
    fetches, keeps = [], []
    for chunk in range(chunks):
        span = pl.ds(chunk * depth * cols, depth * cols)
        fetches.append(
            pltpu.make_async_copy(w_hbm.at[span, :], wide_in.at[span, :], in_sems.at[chunk])
        )
        span = pl.ds(chunk * depth, depth)
        keeps.append(
            pltpu.make_async_copy(wr.at[span, :], wr_hbm.at[span, :], out_sems.at[chunk])
        )
    fetch_small.start()
    fetch_rates.start()
    fetches[0].start()
    fetch_tokens.start()
    for fetch in fetches[1:]:
        fetch.start()

    def relay(chunk):
        fetches[chunk].wait()
        wide = wide_odd if chunk % 2 else wide_even
        at = chunk * depth
        wide[...] = wide_in[at * cols : (at + depth) * cols, :].astype(F32)
        for col in range(cols):
            value = wide[pl.ds(col, depth, stride=cols), :]
            wr[at : at + depth, col * LANES : (col + 1) * LANES] = value.astype(BF16)
        keeps[chunk].start()

    decay_col = levels * heads
    beta_col = decay_col + heads
    norm_col = beta_col + heads
    lane = lane_of(rows)
    row_id, col_id = pair_ids(rows)
    inclusive = row_id >= col_id
    strict = row_id > col_id
    apart = row_id ^ col_id
    eye = (row_id == col_id).astype(F32)
    fetch_small.wait()
    small_rows = small_in.shape[0] * heads
    for level in range(small_in.shape[0]):
        small_wide[level * heads : (level + 1) * heads, :] = small_in[level].astype(F32)
    small_wide[small_rows:, :] = jnp.zeros((LANES - small_rows, width), F32)
    small_ref[...] = small_wide[...].astype(BF16)
    fetch_rates.wait()
    rate, bias = head_rows(hp_ref, heads, decay_col, beta_col)
    rates_ref[0:1, :] = rate
    rates_ref[1:2, :] = bias
    fetch_tokens.wait()
    gate = mm_nt(tokens[...], small_ref[...])
    gate_ref[...] = gate
    switch = jax.nn.sigmoid(gate + bias)
    lam = jnp.maximum(gate, 0.0) + jnp.log1p(jnp.exp(-jnp.abs(gate)))
    cum = mm_ones(inclusive.astype(F32), -rate * switch)
    pack = jnp.where(lane < decay_col, lam, jnp.where(lane < beta_col, cum, switch))
    pack_t = pack.T
    pack_t_ref[...] = pack_t

    def multiply(part, first, last):
        span = slice((part * heads) * LANES, (part + 1) * heads * LANES)
        own = jnp.dot(
            tokens[:, first * depth : last * depth], wr[first * depth : last * depth, span],
            preferred_element_type=F32,
        )
        if first == 0:
            acc[:, span] = own
        else:
            acc[:, span] += own

    for chunk in range(chunks):
        relay(chunk)
        if chunk % 2 == 1:
            multiply(1, chunk - 1, chunk + 1)

    def unit_of(part, head):
        col = (part * heads + head) * LANES
        raw = acc[:, col : col + LANES]
        scale = lax.rsqrt(row_sum(raw * raw) + EPS)
        qkv_ref[part, head] = raw * scale
        return raw * scale, jnp.where(lane == norm_col + part * heads + head, scale, 0.0)

    scales = jnp.zeros((rows, LANES), F32)
    k_all, lower_all = [], []
    for head in range(heads):
        unit, scale = unit_of(1, head)
        k_all.append(unit)
        scales = scales + scale
        decay = decay_of(pack, pack_t, decay_col + head, inclusive)
        decay_ref[head] = decay.astype(BF16)
        base = jnp.where(strict, decay * mm_nt(unit, unit), 0.0)
        base_ref[head] = base.astype(BF16)
        lower = column(pack, beta_col + head) * base
        lower_ref[head] = lower.astype(BF16)
        lower_all.append(lower)

    def later():
        for part in (2, 0):
            for at in range(0, chunks, chunks // 2):
                yield
                multiply(part, at, at + chunks // 2)

    chain, filler = invert(lower_all, eye, apart, rows), later()
    while True:
        try:
            next(chain)
        except StopIteration as stop:
            trans_all = stop.value
            break
        next(filler, None)
    for _ in filler:
        pass
    mixed_all = []
    for head in range(heads):
        trans_ref[head] = trans_all[head]
        cum_row = pack_t[decay_col + head : decay_col + head + 1, :]
        tail_t = k_all[head].T * jnp.exp(cum_row[:, rows - 1 :] - cum_row)
        mixed_all.append(mm(tail_t, trans_all[head]).astype(BF16))
    eye_key = eye[:LANES, :LANES]
    for head in range(heads):
        mixed_t_ref[head] = mixed_all[head]
        col = (2 * heads + head) * LANES
        v_in = acc[:, col : col + LANES]
        qkv_ref[2, head] = v_in
        cum_col = column(pack, decay_col + head)
        beta = column(pack, beta_col + head)
        grown = (beta * jnp.exp(cum_col)) * k_all[head]
        both = jnp.concatenate([-grown, beta * v_in], 1)
        pair = mm(mixed_all[head], both)
        last = jnp.exp(cum_col[rows - 1 : rows, :])
        pair_ref[head, :, :LANES] = (last * eye_key + pair[:, :LANES]).astype(BF16)
        pair_ref[head, :, LANES:] = pair[:, LANES:].astype(BF16)
    for head in range(heads):
        scales = scales + unit_of(0, head)[1]
    pack_ref[...] = jnp.where(lane < norm_col, pack, scales)
    for keep in keeps:
        keep.wait()


def project(place, tokens, flat_w, small, head_param, heads, levels):
    rows, width = tokens.shape
    chunks = 8
    cols = 3 * heads
    key = flat_w.shape[1]
    square = (heads, rows, rows)
    out_shape = (
        stored((width, cols * key), BF16),
        kept((LANES, width), BF16),
        kept((3, heads, rows, key), F32),
        kept((rows, LANES), F32),
        kept((rows, LANES), F32),
        kept((LANES, rows), F32),
        kept(square, BF16),
        kept((heads, key, rows), BF16),
        kept(square, BF16),
        kept(square, BF16),
        kept(square, BF16),
        kept((2, LANES), F32),
        kept((heads, key, 2 * key), BF16),
    )
    scratch = [
        pltpu.VMEM(tokens.shape, BF16),
        pltpu.VMEM(flat_w.shape, BF16),
        pltpu.VMEM((width // chunks * cols, key), F32),
        pltpu.VMEM((width // chunks * cols, key), F32),
        pltpu.VMEM((width, cols * key), BF16),
        pltpu.VMEM(small.shape, BF16),
        pltpu.VMEM((LANES, width), F32),
        pltpu.VMEM((rows, cols * key), F32),
        pltpu.VMEM(head_param.shape, F32),
        pltpu.SemaphoreType.DMA((3,)),
        pltpu.SemaphoreType.DMA((chunks,)),
        pltpu.SemaphoreType.DMA((chunks,)),
    ]
    return local_call(
        functools.partial(project_body, (heads, levels, chunks)), "project", 36, out_shape,
        [place], [], scratch, [head_param, tokens, flat_w, small], [HBM] + [WHOLE] * 12,
    )


def local_body(
    sizes, qkv_ref, pack_ref, pack_t_ref, trans_ref, mixed_t_ref, decay_ref, grad_ref, weight_ref, *outs
):
    heads, levels, bits = sizes
    (attn_ref, attn_t_ref, prod_t_ref, scores_ref, mix_ref, mixed_ref, local_ref, hat_ref,
     hat_t_ref, grad_normed_ref) = outs
    grad_normed_ref[...] = mm_nt(grad_ref[...], weight_ref[...])
    rows = pack_ref.shape[0]
    decay_col = levels * heads
    beta_col = decay_col + heads
    pack = pack_ref[...]
    pack_t = pack_t_ref[...]
    row_id, col_id = pair_ids(rows)
    apart = row_id ^ col_id
    for head in range(heads):
        scores = mm_nt_fine(qkv_ref[0, head], qkv_ref[1, head]) * decay_ref[head].astype(F32)
        scores_ref[head] = scores.astype(BF16)
        mix_ref[head] = level_mix(pack, head, heads, bits, apart).astype(BF16)
        mixed_ref[head] = mixed_t_ref[head].astype(F32).T.astype(BF16)
    for head in range(heads):
        attn = mm(scores_ref[head], trans_ref[head])
        attn_ref[head] = attn.astype(BF16)
        attn_t_ref[head] = attn.T.astype(BF16)
        attn = attn * pack_t[beta_col + head : beta_col + head + 1, :]
        prod = attn * mix_ref[head].astype(F32)
        prod_t_ref[head] = prod.T.astype(BF16)
        growth = jnp.exp(column(pack, decay_col + head))
        local_ref[head] = mm(prod, qkv_ref[2, head])
        hat = growth * qkv_ref[0, head] - mm(attn, growth * qkv_ref[1, head])
        hat_ref[head] = hat.astype(BF16)
        hat_t_ref[head] = hat.T.astype(BF16)


def local_part(arrays, levels, bits):
    heads, rows, key = arrays[0].shape[1:]
    square = (heads, rows, rows)
    out_shape = (
        kept(square, BF16),
        kept(square, BF16),
        kept(square, BF16),
        kept(square, BF16),
        kept(square, BF16),
        kept((heads, rows, key), BF16),
        kept((heads, rows, key), F32),
        kept((heads, rows, key), BF16),
        kept((heads, key, rows), BF16),
        kept((rows, heads * key), F32),
    )
    return local_call(
        functools.partial(local_body, (heads, levels, bits)), "local_part", 10, out_shape,
        [], arrays,
    )


def join_pair(upper, own, other):
    key = own.shape[0]
    low = jnp.where(upper, other, own)
    high = jnp.where(upper, own, other)
    moved = mm(high[:, :key], low)
    late = jnp.concatenate([jnp.zeros((key, key), F32), high[:, key:].astype(F32)], 1)
    return (moved + late).astype(BF16)


def join_body(place_ref, own_ref, other_ref, out_ref):
    half = out_ref.shape[0]
    upper = (place_ref[0] & 1) == 1
    for slot in range(half):
        head = (place_ref[0] & 1) * half + slot
        out_ref[slot] = join_pair(upper, own_ref[head], other_ref[head])


def join_half(place, own, other):
    half = (own.shape[0] // 2,) + own.shape[1:]
    return local_call(join_body, "join_half", 6, [kept(half, BF16)], [place], [own, other])[0]


def gather_node(head, bit, first, near, uppers):
    if bit == 0:
        mine, theirs = near[first]
        half = mine.shape[0]
        here = uppers[0] if head >= half else jnp.logical_not(uppers[0])
        return jnp.where(here, mine[head % half], theirs[head % half])
    own = gather_node(head, bit - 1, first, near, uppers)
    other = gather_node(head, bit - 1, first ^ (1 << (bit - 1)), near, uppers)
    return join_pair(uppers[bit], own, other)


def reach_body(
    sizes, place_ref, gain_ref, pack_ref, local_ref, hat_ref, grad_ref, weight_ref, *refs
):
    heads, bits, far, count, near_count = sizes
    first_ref = refs[0]
    near = [None] + [(refs[1 + at], refs[1 + near_count + at]) for at in range(near_count)]
    refs = refs[2 * near_count + 1 :]
    out_refs = refs[:2]
    dout_ref, found_ref, prefix_ref, dfar_ref = refs[2:6]
    nodes = refs[6:-1]
    normed_ref = refs[-1]
    rows = pack_ref.shape[0]
    key = hat_ref.shape[2]
    pack = pack_ref[...]
    gain = gain_ref[...]
    lane = lane_of(rows)
    all_heads = range(heads)
    uppers = [((place_ref[0] >> bit) & 1) == 1 for bit in range(far)]
    others = []
    for bit in range(far):
        if bit == 0:
            others.append([first_ref[head] for head in all_heads])
        else:
            others.append(
                [gather_node(head, bit - 1, 1 << (bit - 1), near, uppers) for head in all_heads]
            )
            for head in all_heads:
                nodes[bit - 1][head] = others[bit][head]
    eye_key = jnp.where(pair_ids(key)[0] == pair_ids(key)[1], 1.0, 0.0).astype(BF16)
    prefix = [eye_key for head in all_heads]
    found = []
    for bit in range(far):
        for head in all_heads:
            prefix_ref[head, bit] = prefix[head]
        moved = [mm(prefix[head], others[bit][head]) for head in all_heads]
        found.append([jnp.where(uppers[bit], m[:, key:], 0.0).astype(BF16) for m in moved])
        prefix = [
            jnp.where(uppers[bit], moved[head][:, :key].astype(BF16), prefix[head])
            for head in all_heads
        ]
    found = [jnp.concatenate([found[bit][head] for bit in range(far)], 1) for head in all_heads]
    reached = [mm(hat_ref[head], found[head]) for head in all_heads]
    dfar = jnp.zeros((rows, LANES), F32)
    for head in all_heads:
        found_ref[head] = found[head]
        summed = local_ref[head]
        parts = []
        for bit in range(far):
            parts.append(reached[head][:, bit * key : (bit + 1) * key])
            summed = summed + column(pack, (bits + 1 + bit) * heads + head) * parts[bit]
        scale = lax.rsqrt(jnp.mean(summed * summed, -1, keepdims=True) + EPS)
        unit = summed * scale
        normed_ref[:, head * key : (head + 1) * key] = (unit * gain).astype(BF16)
        pulled = grad_ref[:, head * key : (head + 1) * key] * gain
        dout = scale * (pulled - unit * jnp.mean(pulled * unit, -1, keepdims=True))
        dout_ref[head] = dout
        for bit in range(far):
            col = (bits + 1 + bit) * heads + head
            dfar = jnp.where(lane == col, row_sum(dout * parts[bit]), dfar)
    dfar_ref[...] = dfar
    size = weight_ref.shape[1] // count
    for mask in range(count):
        dest = place_ref[1] ^ mask
        cols = pl.ds(pl.multiple_of(dest * size, size), size)
        out_refs[mask % 2][mask // 2] = jnp.dot(
            normed_ref[...], weight_ref[:, cols], preferred_element_type=F32
        ).astype(BF16)


def reach(place, arrays, first, near, bits, far, count):
    gain, pack, local_out, hat, grad_normed, weight = arrays
    heads, rows, key = hat.shape
    nodes = tuple(kept(first.shape, BF16) for bit in range(1, far))
    size = weight.shape[1] // count
    out_shape = (kept((count // 2, rows, size), BF16),) * 2 + (
        kept((heads, rows, key), F32),
        kept((heads, key, far * key), BF16),
        kept((heads, far, key, key), BF16),
        kept((rows, LANES), F32),
    ) + nodes
    mine, theirs = near
    got = local_call(
        functools.partial(reach_body, (heads, bits, far, count, len(mine))), "reach", 10, out_shape,
        [place], [*arrays, first, *mine, *theirs], [pltpu.VMEM((rows, heads * key), BF16)],
    )
    return got[:2], got[2:6], got[6:]


def return_body(sizes, place_ref, pack_ref, hat_t_ref, dout_ref, found_ref, prefix_ref, *refs):
    heads, bits, far = sizes
    others = refs[:far]
    dhat_ref = refs[far]
    sends = refs[far + 1 :]
    key = hat_t_ref.shape[1]
    pack = pack_ref[...]
    all_heads = range(heads)
    uppers = [((place_ref[0] >> bit) & 1) == 1 for bit in range(far)]
    spread = []
    for head in all_heads:
        parts = []
        for bit in range(far):
            weight = column(pack, (bits + 1 + bit) * heads + head)
            parts.append((weight * dout_ref[head]).astype(BF16))
        spread.append(jnp.concatenate(parts, 1))
    dfound = [mm(hat_t_ref[head], spread[head]) for head in all_heads]
    for head in all_heads:
        dhat_ref[head] = mm_nt(spread[head], found_ref[head])
    dprefix = [jnp.zeros((key, key), F32) for head in all_heads]
    for bit in reversed(range(far)):
        dfree = [
            jnp.where(uppers[bit], d[:, bit * key : (bit + 1) * key], 0.0) for d in dfound
        ]
        both = [
            jnp.concatenate([jnp.where(uppers[bit], dprefix[head], 0.0), dfree[head]], 1)
            for head in all_heads
        ]
        for head in all_heads:
            sent = dfree[head] if bit == far - 1 else both[head]
            sends[bit][head] = mm_tn(prefix_ref[head, bit], sent).astype(BF16)
        if bit > 0:
            moved = [mm_nt(both[head], others[bit][head]) for head in all_heads]
            dprefix = [
                jnp.where(uppers[bit], moved[head], dprefix[head]) for head in all_heads
            ]


def return_states(place, pack, hat_t, dout, found, prefix, others, bits):
    heads, rows, key = dout.shape
    far = len(others)
    sends = tuple(
        kept((heads, key, (1 if bit == far - 1 else 2) * key), BF16) for bit in range(far)
    )
    got = local_call(
        functools.partial(return_body, (heads, bits, far)), "return_states", 8,
        (kept(dout.shape, F32),) + sends, [place], [pack, hat_t, dout, found, prefix, *others],
    )
    return got[0], got[1:]


def add_body(*refs):
    count = len(refs) // 3
    for at in range(count):
        left, right = refs[at][...].astype(F32), refs[count + at][...].astype(F32)
        refs[2 * count + at][...] = (left + right).astype(BF16)


def add_all(left, right):
    out_shape = [kept(value.shape, BF16) for value in left]
    return local_call(add_body, "add_all", 6, out_shape, [], [*left, *right])


def lower_pull(dlower, base, lower, beta, decay, strict, k_in):
    dlower = jnp.where(strict, dlower, 0.0)
    dbeta = row_sum(dlower * base.astype(F32))
    dgram = dlower * (beta * decay)
    dkey = mm(dgram, k_in) + mm_tn(dgram, k_in)
    return dbeta, beta * dbeta, col_sum(dlower * lower.astype(F32)), dkey


def pull_body(sizes, *refs):
    heads, levels, bits = sizes
    (qkv_ref, pack_ref, pack_t_ref, trans_ref, attn_ref, attn_t_ref, prod_t_ref, scores_ref,
     mix_ref, decay_ref, base_ref, lower_ref, dout_ref, dhat_ref) = refs[:14]
    dqkv_ref, dgrown_ref, dcol_ref, drow_ref = refs[14:]
    rows = pack_ref.shape[0]
    decay_col = levels * heads
    beta_col = decay_col + heads
    block_bit = BLOCK.bit_length() - 1
    pack = pack_ref[...]
    pack_t = pack_t_ref[...]
    row_id, col_id = pair_ids(rows)
    strict = row_id > col_id
    apart = row_id ^ col_id
    lane = lane_of(rows)
    all_heads = range(heads)
    dcol = jnp.zeros((rows, LANES), F32)
    dbeta_rows, dcum_rows, dattn_all = [], [], []
    for head in all_heads:
        high, low = split(dout_ref[head])
        v_in = qkv_ref[2, head].astype(BF16)
        dprod = mm_nt(high, v_in) + mm_nt(low, v_in)
        dqkv_ref[2, head] = mm(prod_t_ref[head], high)
        beta_row = pack_t[beta_col + head : beta_col + head + 1, :]
        growth = jnp.exp(column(pack, decay_col + head))
        attn0 = attn_ref[head].astype(F32)
        touched = dprod * (attn0 * beta_row)
        for level in range(bits + 1):
            if level == 0:
                here = (apart >> block_bit) == 0
            else:
                here = (apart >> (block_bit + level - 1)) == 1
            dcol = jnp.where(
                lane == level * heads + head, row_sum(jnp.where(here, touched, 0.0)), dcol
            )
        dattn = dprod * mix_ref[head].astype(F32) - mm_nt(dhat_ref[head], growth * qkv_ref[1, head])
        dbeta_rows.append(col_sum(dattn * attn0))
        dattn_all.append((dattn * beta_row).astype(BF16))
    dscore_all = [mm_nt(dattn_all[head], trans_ref[head]) for head in all_heads]
    moved_all = []
    for head in all_heads:
        both = jnp.concatenate(
            [dscore_all[head].astype(BF16), dhat_ref[head].astype(BF16)], 1
        )
        moved_all.append(mm(attn_t_ref[head], both))
    for head in all_heads:
        q_in, k_in = qkv_ref[0, head], qkv_ref[1, head]
        beta = column(pack, beta_col + head)
        growth = jnp.exp(column(pack, decay_col + head))
        dscore = dscore_all[head]
        decay = decay_ref[head].astype(F32)
        dprobs = dscore * decay
        shift = dscore * scores_ref[head].astype(F32)
        dgrown_ref[head] = -beta * moved_all[head][:, rows:]
        dbeta, dcum_col, dcum_row, dk_lower = lower_pull(
            -moved_all[head][:, :rows], base_ref[head], lower_ref[head], beta, decay, strict, k_in
        )
        dhat = dhat_ref[head]
        dqkv_ref[0, head] = growth * dhat + mm(dprobs, k_in)
        dqkv_ref[1, head] = mm_tn(dprobs, q_in) + dk_lower
        dcum_col = dcum_col + row_sum(shift) + growth * row_sum(q_in * dhat)
        dcum_rows.append(-dcum_row - col_sum(shift))
        dcol = jnp.where(lane == beta_col + head, dbeta, dcol)
        dcol = jnp.where(lane == decay_col + head, dcum_col, dcol)
    dcol_ref[...] = dcol
    drow_ref[...] = jnp.concatenate(dcum_rows + dbeta_rows, 0)


def pull_local(arrays, levels, bits):
    heads, rows, key = arrays[0].shape[1:]
    out_shape = (
        kept((3, heads, rows, key), F32),
        kept((heads, rows, key), F32),
        kept((rows, LANES), F32),
        kept((2 * heads, rows), F32),
    )
    return local_call(
        functools.partial(pull_body, (heads, levels, bits)), "pull_local", 12, out_shape, [], arrays
    )


def finish_body(sizes, place_ref, *refs):
    heads, levels, far, arrived_counts = sizes
    (qkv_ref, gate_ref, pack_ref, trans_ref, mixed_ref, decay_ref, base_ref, lower_ref,
     dqkv_ref, dgrown_ref, dcol_ref, drow_ref, dfar_ref, rates_ref) = refs[:14]
    others = refs[14 : 14 + far]
    refs = refs[14 + far :]
    arrived = []
    for found in arrived_counts:
        arrived.append(refs[:found])
        refs = refs[found:]
    dproj, dgate_ref = refs
    rows = pack_ref.shape[0]
    key = qkv_ref.shape[3]
    decay_col = levels * heads
    beta_col = decay_col + heads
    norm_col = beta_col + heads
    place = place_ref[0]
    all_heads = range(heads)
    uppers = [((place >> bit) & 1) == 1 for bit in range(far)]
    pack = pack_ref[...]
    row_id, col_id = pair_ids(rows)
    strict = row_id > col_id
    lane = lane_of(rows)
    last_row = lax.broadcasted_iota(jnp.int32, (rows, 1), 0) == rows - 1
    eye_key = (pair_ids(key)[0] == pair_ids(key)[1]).astype(F32)
    dpair = [jnp.zeros((key, 2 * key), F32) for head in all_heads]
    for bit in reversed(range(far)):
        for head in all_heads:
            got = arrived[bit][0][head].astype(F32)
            for more in arrived[bit][1:]:
                got = got + more[head].astype(F32)
            other = others[bit][head]
            if bit == far - 1:
                got = jnp.concatenate([jnp.zeros((key, key), F32), got], 1)
                dpair[head] = jnp.where(uppers[bit], 0.0, got)
            else:
                as_low = mm_tn(other[:, :key], dpair[head]) + got
                as_high = mm_nt(dpair[head], other)
                as_high = jnp.concatenate([as_high, dpair[head][:, key:]], 1)
                dpair[head] = jnp.where(uppers[bit], as_high, as_low)
    moved_all, dmixed_all = [], []
    for head in all_heads:
        beta = column(pack, beta_col + head)
        growth = jnp.exp(column(pack, decay_col + head))
        both = jnp.concatenate([-growth * qkv_ref[1, head], qkv_ref[2, head]], 1)
        dmixed_all.append(mm_nt(both, dpair[head]))
        moved_all.append(mm(beta * mixed_ref[head].astype(F32), dpair[head]))
    dtail_all = [
        mm(trans_ref[head], column(pack, beta_col + head) * dmixed_all[head])
        for head in all_heads
    ]
    dlower_all = [-mm_nt(mixed_ref[head], dtail_all[head]) for head in all_heads]
    dcol = jnp.where(lane < decay_col, dcol_ref[...] + dfar_ref[...], dcol_ref[...])
    dcum_rows = []
    for head in all_heads:
        q_in, k_in = qkv_ref[0, head], qkv_ref[1, head]
        beta = column(pack, beta_col + head)
        cum_col = column(pack, decay_col + head)
        growth = jnp.exp(cum_col)
        last = cum_col[rows - 1 : rows, :]
        tail = jnp.exp(last - cum_col)
        dgrown = dgrown_ref[head] - moved_all[head][:, :key]
        dv = dqkv_ref[2, head] + moved_all[head][:, key:]
        dbeta_more = row_sum(mixed_ref[head].astype(F32) * dmixed_all[head])
        dtail = dtail_all[head]
        dbeta, dcum_col, dcum_row, dk_lower = lower_pull(
            dlower_all[head], base_ref[head], lower_ref[head], beta, decay_ref[head].astype(F32),
            strict, k_in
        )
        dcum_rows.append(-dcum_row)
        tail_pull = tail * row_sum(k_in * dtail)
        trace = col_sum(row_sum(dpair[head][:, :key] * eye_key))
        at_last = col_sum(tail_pull) + jnp.exp(last) * trace
        dcum_col = dcum_col + growth * row_sum(k_in * dgrown) - tail_pull
        dcum_col = dcum_col + jnp.where(last_row, at_last, 0.0)
        dk = dqkv_ref[1, head] + dk_lower + growth * dgrown + tail * dtail
        dq = dqkv_ref[0, head]
        dcol = dcol + jnp.where(lane == beta_col + head, dbeta + dbeta_more, 0.0)
        dcol = dcol + jnp.where(lane == decay_col + head, dcum_col, 0.0)
        for part, unit, dunit in ((0, q_in, dq), (1, k_in, dk)):
            scale = column(pack, norm_col + part * heads + head)
            back = scale * (dunit - unit * row_sum(unit * dunit))
            col = (part * heads + head) * key
            dproj[:, col : col + key] = back.astype(BF16)
        col = (2 * heads + head) * key
        dproj[:, col : col + key] = dv.astype(BF16)
    drow = drow_ref[...]
    drow = drow + jnp.concatenate(dcum_rows + [jnp.zeros((heads, rows), F32)], 0)
    drow = jnp.concatenate(
        [jnp.zeros((decay_col, rows), F32), drow,
         jnp.zeros((LANES - norm_col, rows), F32)], 0
    )
    dcol = dcol + drow.T
    rate, bias = rates_ref[0:1, :], rates_ref[1:2, :]
    switch = jax.nn.sigmoid(gate_ref[...] + bias)
    dlog = mm_ones((row_id <= col_id).astype(F32), dcol)
    slope = switch * (1.0 - switch)
    dgate = jnp.where(
        lane < decay_col,
        dcol * switch,
        jnp.where(lane < beta_col, -rate * dlog * slope, dcol * slope),
    )
    dgate_ref[...] = jnp.where(lane < norm_col, dgate, 0.0).astype(BF16)


def finish(place, arrays, others, arrived, levels):
    heads, rows, key = arrays[0].shape[1:]
    counts = tuple(len(group) for group in arrived)
    flat = [value for group in arrived for value in group]
    return local_call(
        functools.partial(finish_body, (heads, levels, len(others), counts)), "finish", 10,
        [kept((rows, 3 * heads * key), BF16), kept((rows, LANES), BF16)],
        [place], [*arrays, *others, *flat],
    )


def tokens_body(count, place_ref, dproj_ref, dgate_ref, wr_ref, small_ref, *refs):
    keep_ref, send_ref = refs[:2]
    direct_refs = refs[2:]
    size = wr_ref.shape[0] // count
    half = size // 2
    for mask in range(count):
        dest = place_ref[1] ^ mask
        span = pl.ds(pl.multiple_of(dest * size, size), size)
        part = mm_nt(dproj_ref[...], wr_ref[span, :]) + mm(dgate_ref[...], small_ref[:, span])
        direct_refs[mask][...] = part[:, :half].astype(BF16)
        target = send_ref if mask % 2 else keep_ref
        target[mask // 2] = part[:, half:].astype(BF16)


def pull_tokens(place, dproj, dgate, wr, small_t, count):
    rows = dproj.shape[0]
    half = wr.shape[0] // count // 2
    out_shape = [kept((count // 2, rows, half), BF16)] * 2 + [kept((rows, half), BF16)] * count
    got = local_call(
        functools.partial(tokens_body, count), "pull_tokens", 8, out_shape,
        [place], [dproj, dgate, wr, small_t],
    )
    return got[0], got[1], got[2:]


def swap(value, axis, mask):
    size = lax.axis_size(axis)
    return lax.ppermute(value, axis, [(at, at ^ mask) for at in range(size)])


def far_first(count):
    return sorted(range(1, count), key=lambda mask: mask < count // 2)


def halve_body(own_ref, got_ref, keep_ref, send_ref):
    for at in range(own_ref.shape[0]):
        total = own_ref[at].astype(F32) + got_ref[at].astype(F32)
        target = send_ref if at % 2 else keep_ref
        target[at // 2] = total.astype(target.dtype)


def halving(keep, send, axis, tied):
    mask = 1
    while keep.shape[0] > 1:
        got = swap(send, axis, mask)
        half = (keep.shape[0] // 2,) + keep.shape[1:]
        keep, send = local_call(
            halve_body, "halve", 6, [kept(half, F32), kept(half, BF16)], [], [keep, got]
        )
        send, tied = lax.optimization_barrier((send, tied))
        mask *= 2
    return keep, swap(send, axis, mask), tied


def sum_body(count, *refs):
    keep_ref, got_ref = refs[:2]
    out_ref = refs[-1]
    total = keep_ref[0].astype(F32) + got_ref[0].astype(F32)
    if count == 0:
        out_ref[...] = total.astype(BF16)
        return
    half = out_ref.shape[1] // 2
    out_ref[:, half:] = total.astype(BF16)
    total = refs[2][...].astype(F32)
    for ref in refs[3:-1]:
        total = total + ref[...].astype(F32)
    out_ref[:, :half] = total.astype(BF16)


def head_sum(keep, last, direct, got):
    rows, cols = keep.shape[1:]
    out = jax.ShapeDtypeStruct((rows, cols * (2 if direct else 1)), BF16)
    return local_call(
        functools.partial(sum_body, len(direct)), "head_sum", 6, [out], [],
        [keep, last, *direct[:1], *got],
    )[0]


def on_device(tokens, qkv_weight, small_weight, head_param, norm_gain, out_weight, grad_out):
    rows, width = tokens.shape
    heads, key = qkv_weight.shape[2:]
    levels = small_weight.shape[2] - 2
    bits = (rows // BLOCK).bit_length() - 1
    size = lax.axis_size("ctx")
    far = size.bit_length() - 1
    count = lax.axis_size("head")
    place = jnp.stack([lax.axis_index("ctx"), lax.axis_index("head")]).astype(jnp.int32)
    flat_w = qkv_weight.reshape(width * 3 * heads, key)
    small = jnp.transpose(small_weight, (2, 1, 0))
    rates = head_param.T
    flat_out = out_weight.reshape(heads * key, width)
    gain = norm_gain.reshape(1, key)

    (wr, small_t, qkv, gate, pack, pack_t, trans, mixed_t, decay, base, lower, rates_row,
     pair) = project(
        place, tokens, flat_w, small, rates, heads, levels
    )
    first = swap(pair, "ctx", 1)
    node = join_half(place, pair, first)
    mine = [swap(node, "ctx", 2 * at) for at in range(1, size // 2)]
    (attn, attn_t, prod_t, scores, mix, mixed, local_out, hat, hat_t, grad_normed) = local_part(
        [qkv, pack, pack_t, trans, mixed_t, decay, grad_out, flat_out], levels, bits
    )
    mine, local_out, grad_normed = lax.optimization_barrier((mine, local_out, grad_normed))
    theirs = [swap(value, "ctx", 1) for value in mine]
    out_parts, (dout, found, prefix, dfar), nodes = reach(
        place, [gain, pack, local_out, hat, grad_normed, flat_out], first, (mine, theirs),
        bits, far, count
    )
    others = [first, *nodes]
    dhat, sends = return_states(place, pack, hat_t, dout, found, prefix, others, bits)
    got = [swap(value, "ctx", 1) for value in sends]
    arrived = [[got[0]]]
    sums = add_all(sends[1:], got[1:])
    for bit in range(1, far):
        half = 1 << (bit - 1)
        arrived.append([swap(sums[bit - 1], "ctx", 2 * at) for at in range(half, 2 * half)])
    dqkv, dgrown, dcol, drow = pull_local(
        [qkv, pack, pack_t, trans, attn, attn_t, prod_t, scores, mix, decay, base, lower, dout,
         dhat],
        levels, bits,
    )
    keep_out, last_out, dcol = halving(*out_parts, "head", dcol)
    arrays = [qkv, gate, pack, trans, mixed, decay, base, lower, dqkv, dgrown, dcol, drow, dfar,
              rates_row]
    dproj, dgate = finish(place, arrays, others, arrived, levels)
    keep, send, direct = pull_tokens(place, dproj, dgate, wr, small_t, count)
    direct, last_out = lax.optimization_barrier((direct, last_out))
    got = [swap(direct[mask], "head", mask) for mask in far_first(count)]
    keep, last, _ = halving(keep, send, "head", ())
    return head_sum(keep_out, last_out, [], []), head_sum(keep, last, direct, got)


def solution(mesh):
    placed = (
        P("ctx", None),
        P(None, None, "head", None),
        P(None, "head", None),
        P("head", None),
        P(),
        P("head", None, None),
        P("ctx", None),
    )
    return jax.shard_map(
        on_device,
        mesh=mesh,
        in_specs=placed,
        out_specs=(P("ctx", "head"), P("ctx", "head")),
        check_vma=False,
    )
```

```python
import functools

import jax
import jax.numpy as jnp
from jax import lax
from jax.experimental import pallas as pl
from jax.experimental.pallas import tpu as pltpu
from jax.sharding import PartitionSpec as P

BLOCK = 64
LANES = 128
EPS = 1e-06
MIB = 1024 * 1024
F32 = jnp.float32
BF16 = jnp.bfloat16
WHOLE = pl.BlockSpec(memory_space=pltpu.VMEM)
SCALARS = pl.BlockSpec(memory_space=pltpu.SMEM)
HBM = pl.BlockSpec(memory_space=pltpu.HBM)


def contract(left, right, dim_left, dim_right):
    return lax.dot_general(
        left.astype(BF16),
        right.astype(BF16),
        (((dim_left,), (dim_right,)), ((), ())),
        preferred_element_type=F32,
    )


def mm(left, right):
    return contract(left, right, 1, 0)


def mm_nt(left, right):
    return contract(left, right, 1, 1)


def mm_tn(left, right):
    return contract(left, right, 0, 0)


def split(values):
    high = values.astype(BF16)
    return high, (values - high.astype(F32)).astype(BF16)


def mm_nt_fine(left, right):
    left_high, left_low = split(left)
    right_high, right_low = split(right)
    return mm_nt(left_high, right_high) + (mm_nt(left_low, right_high) + mm_nt(left_high, right_low))


def mm_ones(ones, values):
    high = values.astype(BF16)
    rest = values - high.astype(F32)
    middle = rest.astype(BF16)
    low = (rest - middle.astype(F32)).astype(BF16)
    return mm(ones, high) + (mm(ones, middle) + mm(ones, low))


def pair_ids(count):
    row_id = lax.broadcasted_iota(jnp.int32, (count, count), 0)
    col_id = lax.broadcasted_iota(jnp.int32, (count, count), 1)
    return row_id, col_id


def row_sum(values):
    return jnp.sum(values, 1, keepdims=True)


def col_sum(values):
    return jnp.sum(values, 0, keepdims=True)


def lane_of(rows):
    return lax.broadcasted_iota(jnp.int32, (rows, LANES), 1)


def decay_of(pack, pack_t, col, inclusive):
    spread = pack[:, col : col + 1] - pack_t[col : col + 1, :]
    return jnp.where(inclusive, jnp.exp(jnp.minimum(spread, 0.0)), 0.0)


def kept(shape, dtype):
    return pltpu.VMEM(shape, dtype)


def stored(shape, dtype):
    return pltpu.HBM(shape, dtype)


def pin(values, space):
    return [pltpu.with_memory_space_constraint(value, space) for value in values]


def local_call(
    body, name, limit, out_shape, scalars, arrays, scratch=(), remote=(), out_specs=None, alias=None
):
    return pl.pallas_call(
        body,
        out_shape=tuple(out_shape),
        in_specs=[SCALARS] * len(scalars)
        + [WHOLE] * len(arrays)
        + [HBM] * len(remote),
        out_specs=tuple(out_specs or [WHOLE] * len(out_shape)),
        scratch_shapes=list(scratch),
        input_output_aliases=alias or {},
        compiler_params=pltpu.CompilerParams(vmem_limit_bytes=limit * MIB),
        name=name,
    )(*scalars, *pin(arrays, pltpu.VMEM), *pin(remote, pltpu.HBM))


def column(pack, at):
    return pack[:, at : at + 1]


def level_mix(pack, head, heads, bits, apart):
    block_bit = BLOCK.bit_length() - 1
    mixed = jnp.broadcast_to(column(pack, head), apart.shape)
    for level in range(1, bits + 1):
        here = (apart >> (block_bit + level - 1)) >= 1
        mixed = jnp.where(here, column(pack, level * heads + head), mixed)
    return mixed


def head_rows(hp_ref, heads, decay_col, beta_col):
    lane_row = lane_of(1)
    rate = jnp.zeros((1, LANES), F32)
    bias = jnp.zeros((1, LANES), F32)
    for head in range(heads):
        rate = jnp.where(lane_row == decay_col + head, hp_ref[0:1, head : head + 1], rate)
        bias = jnp.where(lane_row == beta_col + head, hp_ref[1:2, head : head + 1], bias)
    return rate, bias


def merge_blocks(trans_all, edge_all, levels, first):
    if first:
        powers = [edge.astype(BF16) for edge in edge_all]
        trans_all = [trans - power for trans, power in zip(trans_all, powers)]
    else:
        powers = [mm(edge, trans).astype(BF16) for edge, trans in zip(edge_all, trans_all)]
        yield
        trans_all = [
            trans - mm(trans, power).astype(BF16) for trans, power in zip(trans_all, powers)
        ]
    for level in range(1, levels):
        powers = [mm(power, power).astype(BF16) for power in powers]
        yield
        trans_all = [
            trans + mm(trans, power).astype(BF16) for trans, power in zip(trans_all, powers)
        ]
    return trans_all


def invert(lower_all, eye, apart, rows):
    trans_all = [eye.astype(BF16) for lower in lower_all]
    bits = rows.bit_length() - 1
    start = 0
    while start < bits:
        levels = min(2 if bits - start == 2 else 3, bits - start)
        here = jnp.logical_and((apart >> start) >= 1, (apart >> (start + levels)) == 0)
        edge_all = [jnp.where(here, lower, 0.0) for lower in lower_all]
        trans_all = yield from merge_blocks(trans_all, edge_all, levels, start == 0)
        start += levels
        yield
    rest_all = []
    for trans, lower in zip(trans_all, lower_all):
        high, low = split(lower)
        rest_all.append(eye - trans.astype(F32) - mm(high, trans) - mm(low, trans))
    yield
    return [
        (trans.astype(F32) + mm(trans, rest)).astype(BF16)
        for trans, rest in zip(trans_all, rest_all)
    ]


def project_body(sizes, place_ref, hp_hbm, tokens_hbm, w_hbm, small_hbm, *refs):
    heads, levels, chunks = sizes
    (wr_hbm, query_ref, value_ref, small_ref, qkv_ref, gate_ref, pack_ref, pack_t_ref, trans_ref, mixed_t_ref,
     decay_ref, base_ref, lower_ref, rates_ref, pair_ref) = refs[:15]
    tokens, wide_in, wide, key_ref, small_in, small_wide, acc, hp_ref = refs[15:23]
    sems, in_sems, out_sems = refs[23:]
    laid = (query_ref, key_ref, value_ref)
    rows, width = tokens.shape
    depth = width // chunks
    cols = 3 * heads
    fetch_tokens = pltpu.make_async_copy(tokens_hbm, tokens, sems.at[0])
    fetch_small = pltpu.make_async_copy(small_hbm, small_in, sems.at[1])
    fetch_rates = pltpu.make_async_copy(hp_hbm, hp_ref, sems.at[2])
    fetches, keeps = [], []
    for chunk in range(chunks):
        span = pl.ds(chunk * depth * cols, depth * cols)
        fetches.append(
            pltpu.make_async_copy(w_hbm.at[span, :], wide_in.at[span, :], in_sems.at[chunk])
        )
        span = pl.ds(chunk * depth, depth)
        block = wr_hbm.at[span, pl.ds(heads * LANES, heads * LANES)]
        keeps.append(pltpu.make_async_copy(key_ref.at[span, :], block, out_sems.at[chunk]))
    fetch_small.start()
    fetch_rates.start()
    fetches[0].start()
    fetch_tokens.start()
    for fetch in fetches[1:]:
        fetch.start()

    def extract(part, chunk):
        at = chunk * depth
        for head in range(heads):
            first = at * cols + part * heads + head
            value = wide[pl.ds(first, depth, stride=cols), :]
            laid[part][at : at + depth, head * LANES : (head + 1) * LANES] = value.astype(BF16)

    def relay(chunk):
        fetches[chunk].wait()
        span = slice(chunk * depth * cols, (chunk + 1) * depth * cols)
        wide[span, :] = wide_in[span, :].astype(F32)
        extract(1, chunk)
        keeps[chunk].start()

    decay_col = levels * heads
    beta_col = decay_col + heads
    norm_col = beta_col + heads
    lane = lane_of(rows)
    row_id, col_id = pair_ids(rows)
    inclusive = row_id >= col_id
    strict = row_id > col_id
    apart = row_id ^ col_id
    eye = (row_id == col_id).astype(F32)
    fetch_small.wait()
    small_rows = small_in.shape[0] * heads
    for level in range(small_in.shape[0]):
        small_wide[level * heads : (level + 1) * heads, :] = small_in[level].astype(F32)
    small_wide[small_rows:, :] = jnp.zeros((LANES - small_rows, width), F32)
    small_ref[...] = small_wide[...].astype(BF16)
    fetch_rates.wait()
    rate, bias = head_rows(hp_ref, heads, decay_col, beta_col)
    rates_ref[0:1, :] = rate
    rates_ref[1:2, :] = bias
    fetch_tokens.wait()
    gate = mm_nt(tokens[...], small_ref[...])
    gate_ref[...] = gate
    switch = jax.nn.sigmoid(gate + bias)
    lam = jnp.maximum(gate, 0.0) + jnp.log1p(jnp.exp(-jnp.abs(gate)))
    cum = mm_ones(inclusive.astype(F32), -rate * switch)
    pack = jnp.where(lane < decay_col, lam, jnp.where(lane < beta_col, cum, switch))
    pack_t = pack.T
    pack_t_ref[...] = pack_t

    def multiply(part, first, last):
        span = slice((part * heads) * LANES, (part + 1) * heads * LANES)
        own = jnp.dot(
            tokens[:, first * depth : last * depth],
            laid[part][first * depth : last * depth, :],
            preferred_element_type=F32,
        )
        if first == 0:
            acc[:, span] = own
        else:
            acc[:, span] += own

    for chunk in range(chunks):
        relay(chunk)
        if chunk % 2 == 1:
            multiply(1, chunk - 1, chunk + 1)

    def unit_of(part, head):
        col = (part * heads + head) * LANES
        raw = acc[:, col : col + LANES]
        scale = lax.rsqrt(row_sum(raw * raw) + EPS)
        qkv_ref[part, head] = raw * scale
        return raw * scale, jnp.where(lane == norm_col + part * heads + head, scale, 0.0)

    scales = jnp.zeros((rows, LANES), F32)
    k_all, lower_all = [], []
    for head in range(heads):
        unit, scale = unit_of(1, head)
        k_all.append(unit)
        scales = scales + scale
        decay = decay_of(pack, pack_t, decay_col + head, inclusive)
        decay_ref[head] = decay.astype(BF16)
        base = jnp.where(strict, decay * mm_nt(unit, unit), 0.0)
        base_ref[head] = base.astype(BF16)
        lower = column(pack, beta_col + head) * base
        lower_ref[head] = lower.astype(BF16)
        lower_all.append(lower)

    def later():
        for part in (2, 0):
            for chunk in range(chunks):
                extract(part, chunk)
                if chunk % 4 == 3:
                    multiply(part, chunk - 3, chunk + 1)
                if chunk % 2 == 1:
                    yield

    chain, filler = invert(lower_all, eye, apart, rows), later()
    while True:
        try:
            next(chain)
        except StopIteration as stop:
            trans_all = stop.value
            break
        next(filler, None)
    for _ in filler:
        pass
    mixed_all = []
    for head in range(heads):
        trans_ref[head] = trans_all[head]
        cum_row = pack_t[decay_col + head : decay_col + head + 1, :]
        tail_t = k_all[head].T * jnp.exp(cum_row[:, rows - 1 :] - cum_row)
        mixed_all.append(mm(tail_t, trans_all[head]).astype(BF16))
    eye_key = eye[:LANES, :LANES]
    for head in range(heads):
        mixed_t_ref[head] = mixed_all[head]
        col = (2 * heads + head) * LANES
        v_in = acc[:, col : col + LANES]
        qkv_ref[2, head] = v_in
        cum_col = column(pack, decay_col + head)
        beta = column(pack, beta_col + head)
        grown = (beta * jnp.exp(cum_col)) * k_all[head]
        both = jnp.concatenate([-grown, beta * v_in], 1)
        pair = mm(mixed_all[head], both)
        last = jnp.exp(cum_col[rows - 1 : rows, :])
        pair_ref[head, :, :LANES] = (last * eye_key + pair[:, :LANES]).astype(BF16)
        pair_ref[head, :, LANES:] = pair[:, LANES:].astype(BF16)
    for head in range(heads):
        scales = scales + unit_of(0, head)[1]
    pack_ref[...] = jnp.where(lane < norm_col, pack, scales)
    for keep in keeps:
        keep.wait()


def project(place, tokens, flat_w, small, head_param, heads, levels):
    rows, width = tokens.shape
    chunks = 8
    cols = 3 * heads
    key = flat_w.shape[1]
    square = (heads, rows, rows)
    out_shape = (
        stored((width, cols * key), BF16),
        kept((width, heads * key), BF16),
        kept((width, heads * key), BF16),
        kept((LANES, width), BF16),
        kept((3, heads, rows, key), F32),
        kept((rows, LANES), F32),
        kept((rows, LANES), F32),
        kept((LANES, rows), F32),
        kept(square, BF16),
        kept((heads, key, rows), BF16),
        kept(square, BF16),
        kept(square, BF16),
        kept(square, BF16),
        kept((2, LANES), F32),
        kept((heads, key, 2 * key), BF16),
    )
    scratch = [
        pltpu.VMEM(tokens.shape, BF16),
        pltpu.VMEM(flat_w.shape, BF16),
        pltpu.VMEM(flat_w.shape, F32),
        pltpu.VMEM((width, heads * key), BF16),
        pltpu.VMEM(small.shape, BF16),
        pltpu.VMEM((LANES, width), F32),
        pltpu.VMEM((rows, cols * key), F32),
        pltpu.VMEM(head_param.shape, F32),
        pltpu.SemaphoreType.DMA((3,)),
        pltpu.SemaphoreType.DMA((chunks,)),
        pltpu.SemaphoreType.DMA((chunks,)),
    ]
    return local_call(
        functools.partial(project_body, (heads, levels, chunks)), "project", 36, out_shape,
        [place], [], scratch, [head_param, tokens, flat_w, small], [HBM] + [WHOLE] * 14,
    )


def local_body(
    sizes, qkv_ref, pack_ref, pack_t_ref, trans_ref, mixed_t_ref, decay_ref, grad_ref, weight_ref,
    query_ref, value_ref, wr_in, *outs
):
    heads, levels, bits = sizes
    (attn_ref, attn_t_ref, prod_t_ref, scores_ref, mix_ref, mixed_ref, local_ref, hat_ref,
     hat_t_ref, grad_normed_ref, wr_hbm, sems) = outs
    del wr_in
    half, size = query_ref.shape[0] // 2, query_ref.shape[1]
    keeps = []
    for at in range(4):
        span = pl.ds(at % 2 * half, half)
        here, col = ((query_ref, 0), (value_ref, 2 * size))[at // 2]
        there = wr_hbm.at[span, pl.ds(col, size)]
        keeps.append(pltpu.make_async_copy(here.at[span, :], there, sems.at[at]))
        keeps[at].start()
    grad_normed_ref[...] = mm_nt(grad_ref[...], weight_ref[...])
    rows = pack_ref.shape[0]
    decay_col = levels * heads
    beta_col = decay_col + heads
    pack = pack_ref[...]
    pack_t = pack_t_ref[...]
    row_id, col_id = pair_ids(rows)
    apart = row_id ^ col_id
    for head in range(heads):
        scores = mm_nt_fine(qkv_ref[0, head], qkv_ref[1, head]) * decay_ref[head].astype(F32)
        scores_ref[head] = scores.astype(BF16)
        mix_ref[head] = level_mix(pack, head, heads, bits, apart).astype(BF16)
        mixed_ref[head] = mixed_t_ref[head].astype(F32).T.astype(BF16)
    for head in range(heads):
        attn = mm(scores_ref[head], trans_ref[head])
        attn_ref[head] = attn.astype(BF16)
        attn_t_ref[head] = attn.T.astype(BF16)
        attn = attn * pack_t[beta_col + head : beta_col + head + 1, :]
        prod = attn * mix_ref[head].astype(F32)
        prod_t_ref[head] = prod.T.astype(BF16)
        growth = jnp.exp(column(pack, decay_col + head))
        local_ref[head] = mm(prod, qkv_ref[2, head])
        hat = growth * qkv_ref[0, head] - mm(attn, growth * qkv_ref[1, head])
        hat_ref[head] = hat.astype(BF16)
        hat_t_ref[head] = hat.T.astype(BF16)
    for keep in keeps:
        keep.wait()


def local_part(arrays, wr, levels, bits):
    heads, rows, key = arrays[0].shape[1:]
    square = (heads, rows, rows)
    out_shape = (
        kept(square, BF16),
        kept(square, BF16),
        kept(square, BF16),
        kept(square, BF16),
        kept(square, BF16),
        kept((heads, rows, key), BF16),
        kept((heads, rows, key), F32),
        kept((heads, rows, key), BF16),
        kept((heads, key, rows), BF16),
        kept((rows, heads * key), F32),
        stored(wr.shape, BF16),
    )
    return local_call(
        functools.partial(local_body, (heads, levels, bits)), "local_part", 10, out_shape,
        [], arrays, [pltpu.SemaphoreType.DMA((4,))], [wr], [WHOLE] * 10 + [HBM],
        {len(arrays): 10},
    )


def join_pair(upper, own, other):
    key = own.shape[0]
    low = jnp.where(upper, other, own)
    high = jnp.where(upper, own, other)
    moved = mm(high[:, :key], low)
    late = jnp.concatenate([jnp.zeros((key, key), F32), high[:, key:].astype(F32)], 1)
    return (moved + late).astype(BF16)


def join_body(place_ref, own_ref, other_ref, out_ref):
    half = out_ref.shape[0]
    upper = (place_ref[0] & 1) == 1
    for slot in range(half):
        head = (place_ref[0] & 1) * half + slot
        out_ref[slot] = join_pair(upper, own_ref[head], other_ref[head])


def join_half(place, own, other):
    half = (own.shape[0] // 2,) + own.shape[1:]
    return local_call(join_body, "join_half", 6, [kept(half, BF16)], [place], [own, other])[0]


def gather_node(head, bit, first, near, uppers):
    if bit == 0:
        mine, theirs = near[first]
        half = mine.shape[0]
        here = uppers[0] if head >= half else jnp.logical_not(uppers[0])
        return jnp.where(here, mine[head % half], theirs[head % half])
    own = gather_node(head, bit - 1, first, near, uppers)
    other = gather_node(head, bit - 1, first ^ (1 << (bit - 1)), near, uppers)
    return join_pair(uppers[bit], own, other)


def reach_body(
    sizes, place_ref, gain_ref, pack_ref, local_ref, hat_ref, grad_ref, weight_ref, *refs
):
    heads, bits, far, count, near_count = sizes
    first_ref = refs[0]
    near = [None] + [(refs[1 + at], refs[1 + near_count + at]) for at in range(near_count)]
    refs = refs[2 * near_count + 1 :]
    out_refs = refs[:2]
    dout_ref, found_ref, prefix_ref, dfar_ref = refs[2:6]
    nodes = refs[6:-1]
    normed_ref = refs[-1]
    rows = pack_ref.shape[0]
    key = hat_ref.shape[2]
    pack = pack_ref[...]
    gain = gain_ref[...]
    lane = lane_of(rows)
    all_heads = range(heads)
    uppers = [((place_ref[0] >> bit) & 1) == 1 for bit in range(far)]
    others = []
    for bit in range(far):
        if bit == 0:
            others.append([first_ref[head] for head in all_heads])
        else:
            others.append(
                [gather_node(head, bit - 1, 1 << (bit - 1), near, uppers) for head in all_heads]
            )
            for head in all_heads:
                nodes[bit - 1][head] = others[bit][head]
    eye_key = jnp.where(pair_ids(key)[0] == pair_ids(key)[1], 1.0, 0.0).astype(BF16)
    prefix = [eye_key for head in all_heads]
    found = []
    for bit in range(far):
        for head in all_heads:
            prefix_ref[head, bit] = prefix[head]
        moved = [mm(prefix[head], others[bit][head]) for head in all_heads]
        found.append([jnp.where(uppers[bit], m[:, key:], 0.0).astype(BF16) for m in moved])
        prefix = [
            jnp.where(uppers[bit], moved[head][:, :key].astype(BF16), prefix[head])
            for head in all_heads
        ]
    found = [jnp.concatenate([found[bit][head] for bit in range(far)], 1) for head in all_heads]
    reached = [mm(hat_ref[head], found[head]) for head in all_heads]
    dfar = jnp.zeros((rows, LANES), F32)
    for head in all_heads:
        found_ref[head] = found[head]
        summed = local_ref[head]
        parts = []
        for bit in range(far):
            parts.append(reached[head][:, bit * key : (bit + 1) * key])
            summed = summed + column(pack, (bits + 1 + bit) * heads + head) * parts[bit]
        scale = lax.rsqrt(jnp.mean(summed * summed, -1, keepdims=True) + EPS)
        unit = summed * scale
        normed_ref[:, head * key : (head + 1) * key] = (unit * gain).astype(BF16)
        pulled = grad_ref[:, head * key : (head + 1) * key] * gain
        dout = scale * (pulled - unit * jnp.mean(pulled * unit, -1, keepdims=True))
        dout_ref[head] = dout
        for bit in range(far):
            col = (bits + 1 + bit) * heads + head
            dfar = jnp.where(lane == col, row_sum(dout * parts[bit]), dfar)
    dfar_ref[...] = dfar
    size = weight_ref.shape[1] // count
    for mask in range(count):
        dest = place_ref[1] ^ mask
        cols = pl.ds(pl.multiple_of(dest * size, size), size)
        out_refs[mask % 2][mask // 2] = jnp.dot(
            normed_ref[...], weight_ref[:, cols], preferred_element_type=F32
        ).astype(BF16)


def reach(place, arrays, first, near, bits, far, count):
    gain, pack, local_out, hat, grad_normed, weight = arrays
    heads, rows, key = hat.shape
    nodes = tuple(kept(first.shape, BF16) for bit in range(1, far))
    size = weight.shape[1] // count
    out_shape = (kept((count // 2, rows, size), BF16),) * 2 + (
        kept((heads, rows, key), F32),
        kept((heads, key, far * key), BF16),
        kept((heads, far, key, key), BF16),
        kept((rows, LANES), F32),
    ) + nodes
    mine, theirs = near
    got = local_call(
        functools.partial(reach_body, (heads, bits, far, count, len(mine))), "reach", 10, out_shape,
        [place], [*arrays, first, *mine, *theirs], [pltpu.VMEM((rows, heads * key), BF16)],
    )
    return got[:2], got[2:6], got[6:]


def return_body(sizes, place_ref, pack_ref, hat_t_ref, dout_ref, found_ref, prefix_ref, *refs):
    heads, bits, far = sizes
    others = refs[:far]
    dhat_ref = refs[far]
    sends = refs[far + 1 :]
    key = hat_t_ref.shape[1]
    pack = pack_ref[...]
    all_heads = range(heads)
    uppers = [((place_ref[0] >> bit) & 1) == 1 for bit in range(far)]
    spread = []
    for head in all_heads:
        parts = []
        for bit in range(far):
            weight = column(pack, (bits + 1 + bit) * heads + head)
            parts.append((weight * dout_ref[head]).astype(BF16))
        spread.append(jnp.concatenate(parts, 1))
    dfound = [mm(hat_t_ref[head], spread[head]) for head in all_heads]
    for head in all_heads:
        dhat_ref[head] = mm_nt(spread[head], found_ref[head])
    dprefix = [jnp.zeros((key, key), F32) for head in all_heads]
    for bit in reversed(range(far)):
        dfree = [
            jnp.where(uppers[bit], d[:, bit * key : (bit + 1) * key], 0.0) for d in dfound
        ]
        both = [
            jnp.concatenate([jnp.where(uppers[bit], dprefix[head], 0.0), dfree[head]], 1)
            for head in all_heads
        ]
        for head in all_heads:
            sent = dfree[head] if bit == far - 1 else both[head]
            sends[bit][head] = mm_tn(prefix_ref[head, bit], sent).astype(BF16)
        if bit > 0:
            moved = [mm_nt(both[head], others[bit][head]) for head in all_heads]
            dprefix = [
                jnp.where(uppers[bit], moved[head], dprefix[head]) for head in all_heads
            ]


def return_states(place, pack, hat_t, dout, found, prefix, others, bits):
    heads, rows, key = dout.shape
    far = len(others)
    sends = tuple(
        kept((heads, key, (1 if bit == far - 1 else 2) * key), BF16) for bit in range(far)
    )
    got = local_call(
        functools.partial(return_body, (heads, bits, far)), "return_states", 8,
        (kept(dout.shape, F32),) + sends, [place], [pack, hat_t, dout, found, prefix, *others],
    )
    return got[0], got[1:]


def add_body(*refs):
    count = len(refs) // 3
    for at in range(count):
        left, right = refs[at][...].astype(F32), refs[count + at][...].astype(F32)
        refs[2 * count + at][...] = (left + right).astype(BF16)


def add_all(left, right):
    out_shape = [kept(value.shape, BF16) for value in left]
    return local_call(add_body, "add_all", 6, out_shape, [], [*left, *right])


def lower_pull(dlower, base, lower, beta, decay, strict, k_in):
    dlower = jnp.where(strict, dlower, 0.0)
    dbeta = row_sum(dlower * base.astype(F32))
    dgram = dlower * (beta * decay)
    dkey = mm(dgram, k_in) + mm_tn(dgram, k_in)
    return dbeta, beta * dbeta, col_sum(dlower * lower.astype(F32)), dkey


def pull_body(sizes, *refs):
    heads, levels, bits = sizes
    (qkv_ref, pack_ref, pack_t_ref, trans_ref, attn_ref, attn_t_ref, prod_t_ref, scores_ref,
     mix_ref, decay_ref, base_ref, lower_ref, dout_ref, dhat_ref) = refs[:14]
    dqkv_ref, dgrown_ref, dcol_ref, drow_ref = refs[14:]
    rows = pack_ref.shape[0]
    decay_col = levels * heads
    beta_col = decay_col + heads
    block_bit = BLOCK.bit_length() - 1
    pack = pack_ref[...]
    pack_t = pack_t_ref[...]
    row_id, col_id = pair_ids(rows)
    strict = row_id > col_id
    apart = row_id ^ col_id
    lane = lane_of(rows)
    all_heads = range(heads)
    dcol = jnp.zeros((rows, LANES), F32)
    dbeta_rows, dcum_rows, dattn_all = [], [], []
    for head in all_heads:
        high, low = split(dout_ref[head])
        v_in = qkv_ref[2, head].astype(BF16)
        dprod = mm_nt(high, v_in) + mm_nt(low, v_in)
        dqkv_ref[2, head] = mm(prod_t_ref[head], high)
        beta_row = pack_t[beta_col + head : beta_col + head + 1, :]
        growth = jnp.exp(column(pack, decay_col + head))
        attn0 = attn_ref[head].astype(F32)
        touched = dprod * (attn0 * beta_row)
        for level in range(bits + 1):
            if level == 0:
                here = (apart >> block_bit) == 0
            else:
                here = (apart >> (block_bit + level - 1)) == 1
            dcol = jnp.where(
                lane == level * heads + head, row_sum(jnp.where(here, touched, 0.0)), dcol
            )
        dattn = dprod * mix_ref[head].astype(F32) - mm_nt(dhat_ref[head], growth * qkv_ref[1, head])
        dbeta_rows.append(col_sum(dattn * attn0))
        dattn_all.append((dattn * beta_row).astype(BF16))
    dscore_all = [mm_nt(dattn_all[head], trans_ref[head]) for head in all_heads]
    moved_all = []
    for head in all_heads:
        both = jnp.concatenate(
            [dscore_all[head].astype(BF16), dhat_ref[head].astype(BF16)], 1
        )
        moved_all.append(mm(attn_t_ref[head], both))
    for head in all_heads:
        q_in, k_in = qkv_ref[0, head], qkv_ref[1, head]
        beta = column(pack, beta_col + head)
        growth = jnp.exp(column(pack, decay_col + head))
        dscore = dscore_all[head]
        decay = decay_ref[head].astype(F32)
        dprobs = dscore * decay
        shift = dscore * scores_ref[head].astype(F32)
        dgrown_ref[head] = -beta * moved_all[head][:, rows:]
        dbeta, dcum_col, dcum_row, dk_lower = lower_pull(
            -moved_all[head][:, :rows], base_ref[head], lower_ref[head], beta, decay, strict, k_in
        )
        dhat = dhat_ref[head]
        dqkv_ref[0, head] = growth * dhat + mm(dprobs, k_in)
        dqkv_ref[1, head] = mm_tn(dprobs, q_in) + dk_lower
        dcum_col = dcum_col + row_sum(shift) + growth * row_sum(q_in * dhat)
        dcum_rows.append(-dcum_row - col_sum(shift))
        dcol = jnp.where(lane == beta_col + head, dbeta, dcol)
        dcol = jnp.where(lane == decay_col + head, dcum_col, dcol)
    dcol_ref[...] = dcol
    drow_ref[...] = jnp.concatenate(dcum_rows + dbeta_rows, 0)


def pull_local(arrays, levels, bits):
    heads, rows, key = arrays[0].shape[1:]
    out_shape = (
        kept((3, heads, rows, key), F32),
        kept((heads, rows, key), F32),
        kept((rows, LANES), F32),
        kept((2 * heads, rows), F32),
    )
    return local_call(
        functools.partial(pull_body, (heads, levels, bits)), "pull_local", 12, out_shape, [], arrays
    )


def finish_body(sizes, place_ref, *refs):
    heads, levels, far, arrived_counts = sizes
    (qkv_ref, gate_ref, pack_ref, trans_ref, mixed_ref, decay_ref, base_ref, lower_ref,
     dqkv_ref, dgrown_ref, dcol_ref, drow_ref, dfar_ref, rates_ref) = refs[:14]
    others = refs[14 : 14 + far]
    refs = refs[14 + far :]
    arrived = []
    for found in arrived_counts:
        arrived.append(refs[:found])
        refs = refs[found:]
    dproj, dgate_ref = refs
    rows = pack_ref.shape[0]
    key = qkv_ref.shape[3]
    decay_col = levels * heads
    beta_col = decay_col + heads
    norm_col = beta_col + heads
    place = place_ref[0]
    all_heads = range(heads)
    uppers = [((place >> bit) & 1) == 1 for bit in range(far)]
    pack = pack_ref[...]
    row_id, col_id = pair_ids(rows)
    strict = row_id > col_id
    lane = lane_of(rows)
    last_row = lax.broadcasted_iota(jnp.int32, (rows, 1), 0) == rows - 1
    eye_key = (pair_ids(key)[0] == pair_ids(key)[1]).astype(F32)
    dpair = [jnp.zeros((key, 2 * key), F32) for head in all_heads]
    for bit in reversed(range(far)):
        for head in all_heads:
            got = arrived[bit][0][head].astype(F32)
            for more in arrived[bit][1:]:
                got = got + more[head].astype(F32)
            other = others[bit][head]
            if bit == far - 1:
                got = jnp.concatenate([jnp.zeros((key, key), F32), got], 1)
                dpair[head] = jnp.where(uppers[bit], 0.0, got)
            else:
                as_low = mm_tn(other[:, :key], dpair[head]) + got
                as_high = mm_nt(dpair[head], other)
                as_high = jnp.concatenate([as_high, dpair[head][:, key:]], 1)
                dpair[head] = jnp.where(uppers[bit], as_high, as_low)
    moved_all, dmixed_all = [], []
    for head in all_heads:
        beta = column(pack, beta_col + head)
        growth = jnp.exp(column(pack, decay_col + head))
        both = jnp.concatenate([-growth * qkv_ref[1, head], qkv_ref[2, head]], 1)
        dmixed_all.append(mm_nt(both, dpair[head]))
        moved_all.append(mm(beta * mixed_ref[head].astype(F32), dpair[head]))
    dtail_all = [
        mm(trans_ref[head], column(pack, beta_col + head) * dmixed_all[head])
        for head in all_heads
    ]
    dlower_all = [-mm_nt(mixed_ref[head], dtail_all[head]) for head in all_heads]
    dcol = jnp.where(lane < decay_col, dcol_ref[...] + dfar_ref[...], dcol_ref[...])
    dcum_rows = []
    for head in all_heads:
        q_in, k_in = qkv_ref[0, head], qkv_ref[1, head]
        beta = column(pack, beta_col + head)
        cum_col = column(pack, decay_col + head)
        growth = jnp.exp(cum_col)
        last = cum_col[rows - 1 : rows, :]
        tail = jnp.exp(last - cum_col)
        dgrown = dgrown_ref[head] - moved_all[head][:, :key]
        dv = dqkv_ref[2, head] + moved_all[head][:, key:]
        dbeta_more = row_sum(mixed_ref[head].astype(F32) * dmixed_all[head])
        dtail = dtail_all[head]
        dbeta, dcum_col, dcum_row, dk_lower = lower_pull(
            dlower_all[head], base_ref[head], lower_ref[head], beta, decay_ref[head].astype(F32),
            strict, k_in
        )
        dcum_rows.append(-dcum_row)
        tail_pull = tail * row_sum(k_in * dtail)
        trace = col_sum(row_sum(dpair[head][:, :key] * eye_key))
        at_last = col_sum(tail_pull) + jnp.exp(last) * trace
        dcum_col = dcum_col + growth * row_sum(k_in * dgrown) - tail_pull
        dcum_col = dcum_col + jnp.where(last_row, at_last, 0.0)
        dk = dqkv_ref[1, head] + dk_lower + growth * dgrown + tail * dtail
        dq = dqkv_ref[0, head]
        dcol = dcol + jnp.where(lane == beta_col + head, dbeta + dbeta_more, 0.0)
        dcol = dcol + jnp.where(lane == decay_col + head, dcum_col, 0.0)
        for part, unit, dunit in ((0, q_in, dq), (1, k_in, dk)):
            scale = column(pack, norm_col + part * heads + head)
            back = scale * (dunit - unit * row_sum(unit * dunit))
            col = (part * heads + head) * key
            dproj[:, col : col + key] = back.astype(BF16)
        col = (2 * heads + head) * key
        dproj[:, col : col + key] = dv.astype(BF16)
    drow = drow_ref[...]
    drow = drow + jnp.concatenate(dcum_rows + [jnp.zeros((heads, rows), F32)], 0)
    drow = jnp.concatenate(
        [jnp.zeros((decay_col, rows), F32), drow,
         jnp.zeros((LANES - norm_col, rows), F32)], 0
    )
    dcol = dcol + drow.T
    rate, bias = rates_ref[0:1, :], rates_ref[1:2, :]
    switch = jax.nn.sigmoid(gate_ref[...] + bias)
    dlog = mm_ones((row_id <= col_id).astype(F32), dcol)
    slope = switch * (1.0 - switch)
    dgate = jnp.where(
        lane < decay_col,
        dcol * switch,
        jnp.where(lane < beta_col, -rate * dlog * slope, dcol * slope),
    )
    dgate_ref[...] = jnp.where(lane < norm_col, dgate, 0.0).astype(BF16)


def finish(place, arrays, others, arrived, levels):
    heads, rows, key = arrays[0].shape[1:]
    counts = tuple(len(group) for group in arrived)
    flat = [value for group in arrived for value in group]
    return local_call(
        functools.partial(finish_body, (heads, levels, len(others), counts)), "finish", 10,
        [kept((rows, 3 * heads * key), BF16), kept((rows, LANES), BF16)],
        [place], [*arrays, *others, *flat],
    )


def tokens_body(count, place_ref, dproj_ref, dgate_ref, wr_ref, small_ref, *refs):
    keep_ref, send_ref = refs[:2]
    direct_refs = refs[2:]
    size = wr_ref.shape[0] // count
    half = size // 2
    for mask in range(count):
        dest = place_ref[1] ^ mask
        span = pl.ds(pl.multiple_of(dest * size, size), size)
        part = mm_nt(dproj_ref[...], wr_ref[span, :]) + mm(dgate_ref[...], small_ref[:, span])
        direct_refs[mask][...] = part[:, :half].astype(BF16)
        target = send_ref if mask % 2 else keep_ref
        target[mask // 2] = part[:, half:].astype(BF16)


def pull_tokens(place, dproj, dgate, wr, small_t, count):
    rows = dproj.shape[0]
    half = wr.shape[0] // count // 2
    out_shape = [kept((count // 2, rows, half), BF16)] * 2 + [kept((rows, half), BF16)] * count
    got = local_call(
        functools.partial(tokens_body, count), "pull_tokens", 8, out_shape,
        [place], [dproj, dgate, wr, small_t],
    )
    return got[0], got[1], got[2:]


def swap(value, axis, mask):
    size = lax.axis_size(axis)
    return lax.ppermute(value, axis, [(at, at ^ mask) for at in range(size)])


def far_first(count):
    return sorted(range(1, count), key=lambda mask: mask < count // 2)


def halve_body(own_ref, got_ref, keep_ref, send_ref):
    for at in range(own_ref.shape[0]):
        total = own_ref[at].astype(F32) + got_ref[at].astype(F32)
        target = send_ref if at % 2 else keep_ref
        target[at // 2] = total.astype(target.dtype)


def halving(keep, send, axis, tied):
    mask = 1
    while keep.shape[0] > 1:
        got = swap(send, axis, mask)
        half = (keep.shape[0] // 2,) + keep.shape[1:]
        keep, send = local_call(
            halve_body, "halve", 6, [kept(half, F32), kept(half, BF16)], [], [keep, got]
        )
        send, tied = lax.optimization_barrier((send, tied))
        mask *= 2
    return keep, swap(send, axis, mask), tied


def sum_body(count, *refs):
    keep_ref, got_ref = refs[:2]
    out_ref = refs[-1]
    total = keep_ref[0].astype(F32) + got_ref[0].astype(F32)
    if count == 0:
        out_ref[...] = total.astype(BF16)
        return
    half = out_ref.shape[1] // 2
    out_ref[:, half:] = total.astype(BF16)
    total = refs[2][...].astype(F32)
    for ref in refs[3:-1]:
        total = total + ref[...].astype(F32)
    out_ref[:, :half] = total.astype(BF16)


def head_sum(keep, last, direct, got):
    rows, cols = keep.shape[1:]
    out = jax.ShapeDtypeStruct((rows, cols * (2 if direct else 1)), BF16)
    return local_call(
        functools.partial(sum_body, len(direct)), "head_sum", 6, [out], [],
        [keep, last, *direct[:1], *got],
    )[0]


def on_device(tokens, qkv_weight, small_weight, head_param, norm_gain, out_weight, grad_out):
    rows, width = tokens.shape
    heads, key = qkv_weight.shape[2:]
    levels = small_weight.shape[2] - 2
    bits = (rows // BLOCK).bit_length() - 1
    size = lax.axis_size("ctx")
    far = size.bit_length() - 1
    count = lax.axis_size("head")
    place = jnp.stack([lax.axis_index("ctx"), lax.axis_index("head")]).astype(jnp.int32)
    flat_w = qkv_weight.reshape(width * 3 * heads, key)
    small = jnp.transpose(small_weight, (2, 1, 0))
    rates = head_param.T
    flat_out = out_weight.reshape(heads * key, width)
    gain = norm_gain.reshape(1, key)

    (wr, query_w, value_w, small_t, qkv, gate, pack, pack_t, trans, mixed_t, decay, base, lower, rates_row,
     pair) = project(
        place, tokens, flat_w, small, rates, heads, levels
    )
    first = swap(pair, "ctx", 1)
    node = join_half(place, pair, first)
    mine = [swap(node, "ctx", 2 * at) for at in range(1, size // 2)]
    (attn, attn_t, prod_t, scores, mix, mixed, local_out, hat, hat_t, grad_normed, wr) = local_part(
        [qkv, pack, pack_t, trans, mixed_t, decay, grad_out, flat_out, query_w, value_w],
        wr, levels, bits,
    )
    mine, local_out, grad_normed = lax.optimization_barrier((mine, local_out, grad_normed))
    theirs = [swap(value, "ctx", 1) for value in mine]
    out_parts, (dout, found, prefix, dfar), nodes = reach(
        place, [gain, pack, local_out, hat, grad_normed, flat_out], first, (mine, theirs),
        bits, far, count
    )
    others = [first, *nodes]
    dhat, sends = return_states(place, pack, hat_t, dout, found, prefix, others, bits)
    got = [swap(value, "ctx", 1) for value in sends]
    arrived = [[got[0]]]
    sums = add_all(sends[1:], got[1:])
    for bit in range(1, far):
        half = 1 << (bit - 1)
        arrived.append([swap(sums[bit - 1], "ctx", 2 * at) for at in range(half, 2 * half)])
    dqkv, dgrown, dcol, drow = pull_local(
        [qkv, pack, pack_t, trans, attn, attn_t, prod_t, scores, mix, decay, base, lower, dout,
         dhat],
        levels, bits,
    )
    keep_out, last_out, dcol = halving(*out_parts, "head", dcol)
    arrays = [qkv, gate, pack, trans, mixed, decay, base, lower, dqkv, dgrown, dcol, drow, dfar,
              rates_row]
    dproj, dgate = finish(place, arrays, others, arrived, levels)
    keep, send, direct = pull_tokens(place, dproj, dgate, wr, small_t, count)
    direct, last_out = lax.optimization_barrier((direct, last_out))
    got = [swap(direct[mask], "head", mask) for mask in far_first(count)]
    keep, last, _ = halving(keep, send, "head", ())
    return head_sum(keep_out, last_out, [], []), head_sum(keep, last, direct, got)


def solution(mesh):
    placed = (
        P("ctx", None),
        P(None, None, "head", None),
        P(None, "head", None),
        P("head", None),
        P(),
        P("head", None, None),
        P("ctx", None),
    )
    return jax.shard_map(
        on_device,
        mesh=mesh,
        in_specs=placed,
        out_specs=(P("ctx", "head"), P("ctx", "head")),
        check_vma=False,
    )
```

```python
import functools

import jax
import jax.numpy as jnp
from jax import lax
from jax.experimental import pallas as pl
from jax.experimental.pallas import tpu as pltpu
from jax.sharding import PartitionSpec as P

BLOCK = 64
LANES = 128
EPS = 1e-06
MIB = 1024 * 1024
F32 = jnp.float32
BF16 = jnp.bfloat16
WHOLE = pl.BlockSpec(memory_space=pltpu.VMEM)
SCALARS = pl.BlockSpec(memory_space=pltpu.SMEM)
HBM = pl.BlockSpec(memory_space=pltpu.HBM)


def contract(left, right, dim_left, dim_right):
    return lax.dot_general(
        left.astype(BF16),
        right.astype(BF16),
        (((dim_left,), (dim_right,)), ((), ())),
        preferred_element_type=F32,
    )


def mm(left, right):
    return contract(left, right, 1, 0)


def mm_nt(left, right):
    return contract(left, right, 1, 1)


def mm_tn(left, right):
    return contract(left, right, 0, 0)


def split(values):
    high = values.astype(BF16)
    return high, (values - high.astype(F32)).astype(BF16)


def mm_nt_fine(left, right):
    left_high, left_low = split(left)
    right_high, right_low = split(right)
    return mm_nt(left_high, right_high) + (mm_nt(left_low, right_high) + mm_nt(left_high, right_low))


def mm_ones(ones, values):
    high = values.astype(BF16)
    rest = values - high.astype(F32)
    middle = rest.astype(BF16)
    low = (rest - middle.astype(F32)).astype(BF16)
    return mm(ones, high) + (mm(ones, middle) + mm(ones, low))


def pair_ids(count):
    row_id = lax.broadcasted_iota(jnp.int32, (count, count), 0)
    col_id = lax.broadcasted_iota(jnp.int32, (count, count), 1)
    return row_id, col_id


def row_sum(values):
    return jnp.sum(values, 1, keepdims=True)


def col_sum(values):
    return jnp.sum(values, 0, keepdims=True)


def lane_of(rows):
    return lax.broadcasted_iota(jnp.int32, (rows, LANES), 1)


def decay_of(pack, pack_t, col, inclusive):
    spread = pack[:, col : col + 1] - pack_t[col : col + 1, :]
    return jnp.where(inclusive, jnp.exp(jnp.minimum(spread, 0.0)), 0.0)


def kept(shape, dtype):
    return pltpu.VMEM(shape, dtype)


def stored(shape, dtype):
    return pltpu.HBM(shape, dtype)


def pin(values, space):
    return [pltpu.with_memory_space_constraint(value, space) for value in values]


def local_call(
    body, name, limit, out_shape, scalars, arrays, scratch=(), remote=(), out_specs=None, alias=None
):
    return pl.pallas_call(
        body,
        out_shape=tuple(out_shape),
        in_specs=[SCALARS] * len(scalars)
        + [WHOLE] * len(arrays)
        + [HBM] * len(remote),
        out_specs=tuple(out_specs or [WHOLE] * len(out_shape)),
        scratch_shapes=list(scratch),
        input_output_aliases=alias or {},
        compiler_params=pltpu.CompilerParams(vmem_limit_bytes=limit * MIB),
        name=name,
    )(*scalars, *pin(arrays, pltpu.VMEM), *pin(remote, pltpu.HBM))


def column(pack, at):
    return pack[:, at : at + 1]


def level_mix(pack, head, heads, bits, apart):
    block_bit = BLOCK.bit_length() - 1
    mixed = jnp.broadcast_to(column(pack, head), apart.shape)
    for level in range(1, bits + 1):
        here = (apart >> (block_bit + level - 1)) >= 1
        mixed = jnp.where(here, column(pack, level * heads + head), mixed)
    return mixed


def head_rows(hp_ref, heads, decay_col, beta_col):
    lane_row = lane_of(1)
    rate = jnp.zeros((1, LANES), F32)
    bias = jnp.zeros((1, LANES), F32)
    for head in range(heads):
        rate = jnp.where(lane_row == decay_col + head, hp_ref[0:1, head : head + 1], rate)
        bias = jnp.where(lane_row == beta_col + head, hp_ref[1:2, head : head + 1], bias)
    return rate, bias


def merge_blocks(trans_all, edge_all, levels, first):
    if first:
        powers = [edge.astype(BF16) for edge in edge_all]
        trans_all = [trans - power for trans, power in zip(trans_all, powers)]
    else:
        powers = [mm(edge, trans).astype(BF16) for edge, trans in zip(edge_all, trans_all)]
        trans_all = [
            trans - mm(trans, power).astype(BF16) for trans, power in zip(trans_all, powers)
        ]
    for level in range(1, levels):
        powers = [mm(power, power).astype(BF16) for power in powers]
        trans_all = [
            trans + mm(trans, power).astype(BF16) for trans, power in zip(trans_all, powers)
        ]
    return trans_all


def invert(lower_all, eye, apart, rows):
    trans_all = [eye.astype(BF16) for lower in lower_all]
    bits = rows.bit_length() - 1
    start = 0
    while start < bits:
        levels = min(2 if bits - start == 2 else 3, bits - start)
        here = jnp.logical_and((apart >> start) >= 1, (apart >> (start + levels)) == 0)
        edge_all = [jnp.where(here, lower, 0.0) for lower in lower_all]
        trans_all = merge_blocks(trans_all, edge_all, levels, start == 0)
        start += levels
    rest_all = []
    for trans, lower in zip(trans_all, lower_all):
        high, low = split(lower)
        rest_all.append(eye - trans.astype(F32) - mm(high, trans) - mm(low, trans))
    return [
        (trans.astype(F32) + mm(trans, rest)).astype(BF16)
        for trans, rest in zip(trans_all, rest_all)
    ]


def project_body(sizes, place_ref, hp_hbm, tokens_hbm, w_hbm, small_hbm, *refs):
    heads, levels, chunks = sizes
    (wr_hbm, query_ref, value_ref, small_ref, qkv_ref, gate_ref, pack_ref, pack_t_ref, trans_ref, mixed_t_ref,
     decay_ref, base_ref, lower_ref, rates_ref, pair_ref) = refs[:15]
    tokens, wide_in, wide_even, wide_odd, key_ref, small_in, small_wide, acc, hp_ref = refs[15:24]
    sems, in_sems, out_sems = refs[24:]
    laid = (query_ref, key_ref, value_ref)
    rows, width = tokens.shape
    depth = width // chunks
    cols = 3 * heads
    fetch_tokens = pltpu.make_async_copy(tokens_hbm, tokens, sems.at[0])
    fetch_small = pltpu.make_async_copy(small_hbm, small_in, sems.at[1])
    fetch_rates = pltpu.make_async_copy(hp_hbm, hp_ref, sems.at[2])
    fetches, keeps = [], []
    for chunk in range(chunks):
        span = pl.ds(chunk * depth * cols, depth * cols)
        fetches.append(
            pltpu.make_async_copy(w_hbm.at[span, :], wide_in.at[span, :], in_sems.at[chunk])
        )
        span = pl.ds(chunk * depth, depth)
        block = wr_hbm.at[span, pl.ds(heads * LANES, heads * LANES)]
        keeps.append(pltpu.make_async_copy(key_ref.at[span, :], block, out_sems.at[chunk]))
    fetches[0].start()
    fetch_tokens.start()
    fetches[1].start()
    fetch_small.start()
    fetch_rates.start()
    for fetch in fetches[2:]:
        fetch.start()

    def relay(chunk):
        fetches[chunk].wait()
        wide = wide_odd if chunk % 2 else wide_even
        at = chunk * depth
        wide[...] = wide_in[at * cols : (at + depth) * cols, :].astype(F32)
        for col in range(cols):
            value = wide[pl.ds(col, depth, stride=cols), :].astype(BF16)
            lanes = slice(col % heads * LANES, (col % heads + 1) * LANES)
            laid[col // heads][at : at + depth, lanes] = value
        keeps[chunk].start()

    def multiply(first, last):
        for part in (1, 2, 0):
            span = slice((part * heads) * LANES, (part + 1) * heads * LANES)
            own = jnp.dot(
                tokens[:, first * depth : last * depth],
                laid[part][first * depth : last * depth, :],
                preferred_element_type=F32,
            )
            if first == 0:
                acc[:, span] = own
            else:
                acc[:, span] += own

    def lay(first, last):
        for chunk in range(first, last, 2):
            relay(chunk)
            relay(chunk + 1)
            if chunk == 0:
                fetch_tokens.wait()
            multiply(chunk, chunk + 2)

    decay_col = levels * heads
    beta_col = decay_col + heads
    norm_col = beta_col + heads
    lane = lane_of(rows)
    row_id, col_id = pair_ids(rows)
    inclusive = row_id >= col_id
    strict = row_id > col_id
    apart = row_id ^ col_id
    eye = (row_id == col_id).astype(F32)
    lay(0, chunks // 2)
    fetch_small.wait()
    small_rows = small_in.shape[0] * heads
    for level in range(small_in.shape[0]):
        small_wide[level * heads : (level + 1) * heads, :] = small_in[level].astype(F32)
    small_wide[small_rows:, :] = jnp.zeros((LANES - small_rows, width), F32)
    small_ref[...] = small_wide[...].astype(BF16)
    fetch_rates.wait()
    rate, bias = head_rows(hp_ref, heads, decay_col, beta_col)
    rates_ref[0:1, :] = rate
    rates_ref[1:2, :] = bias
    gate = mm_nt(tokens[...], small_ref[...])
    gate_ref[...] = gate
    switch = jax.nn.sigmoid(gate + bias)
    lam = jnp.maximum(gate, 0.0) + jnp.log1p(jnp.exp(-jnp.abs(gate)))
    cum = mm_ones(inclusive.astype(F32), -rate * switch)
    pack = jnp.where(lane < decay_col, lam, jnp.where(lane < beta_col, cum, switch))
    pack_t = pack.T
    pack_t_ref[...] = pack_t

    lay(chunks // 2, chunks)

    def unit_of(part, head):
        col = (part * heads + head) * LANES
        raw = acc[:, col : col + LANES]
        scale = lax.rsqrt(row_sum(raw * raw) + EPS)
        qkv_ref[part, head] = raw * scale
        return raw * scale, jnp.where(lane == norm_col + part * heads + head, scale, 0.0)

    scales = jnp.zeros((rows, LANES), F32)
    k_all, lower_all = [], []
    for head in range(heads):
        unit, scale = unit_of(1, head)
        k_all.append(unit)
        scales = scales + scale
        decay = decay_of(pack, pack_t, decay_col + head, inclusive)
        decay_ref[head] = decay.astype(BF16)
        base = jnp.where(strict, decay * mm_nt(unit, unit), 0.0)
        base_ref[head] = base.astype(BF16)
        lower = column(pack, beta_col + head) * base
        lower_ref[head] = lower.astype(BF16)
        lower_all.append(lower)

    trans_all = invert(lower_all, eye, apart, rows)
    mixed_all = []
    for head in range(heads):
        trans_ref[head] = trans_all[head]
        cum_row = pack_t[decay_col + head : decay_col + head + 1, :]
        tail_t = k_all[head].T * jnp.exp(cum_row[:, rows - 1 :] - cum_row)
        mixed_all.append(mm(tail_t, trans_all[head]).astype(BF16))
    eye_key = eye[:LANES, :LANES]
    for head in range(heads):
        mixed_t_ref[head] = mixed_all[head]
        col = (2 * heads + head) * LANES
        v_in = acc[:, col : col + LANES]
        qkv_ref[2, head] = v_in
        cum_col = column(pack, decay_col + head)
        beta = column(pack, beta_col + head)
        grown = (beta * jnp.exp(cum_col)) * k_all[head]
        both = jnp.concatenate([-grown, beta * v_in], 1)
        pair = mm(mixed_all[head], both)
        last = jnp.exp(cum_col[rows - 1 : rows, :])
        pair_ref[head, :, :LANES] = (last * eye_key + pair[:, :LANES]).astype(BF16)
        pair_ref[head, :, LANES:] = pair[:, LANES:].astype(BF16)
    for head in range(heads):
        scales = scales + unit_of(0, head)[1]
    pack_ref[...] = jnp.where(lane < norm_col, pack, scales)
    for keep in keeps:
        keep.wait()


def project(place, tokens, flat_w, small, head_param, heads, levels):
    rows, width = tokens.shape
    chunks = 8
    cols = 3 * heads
    key = flat_w.shape[1]
    square = (heads, rows, rows)
    out_shape = (
        stored((width, cols * key), BF16),
        kept((width, heads * key), BF16),
        kept((width, heads * key), BF16),
        kept((LANES, width), BF16),
        kept((3, heads, rows, key), F32),
        kept((rows, LANES), F32),
        kept((rows, LANES), F32),
        kept((LANES, rows), F32),
        kept(square, BF16),
        kept((heads, key, rows), BF16),
        kept(square, BF16),
        kept(square, BF16),
        kept(square, BF16),
        kept((2, LANES), F32),
        kept((heads, key, 2 * key), BF16),
    )
    scratch = [
        pltpu.VMEM(tokens.shape, BF16),
        pltpu.VMEM(flat_w.shape, BF16),
        pltpu.VMEM((width // chunks * cols, key), F32),
        pltpu.VMEM((width // chunks * cols, key), F32),
        pltpu.VMEM((width, heads * key), BF16),
        pltpu.VMEM(small.shape, BF16),
        pltpu.VMEM((LANES, width), F32),
        pltpu.VMEM((rows, cols * key), F32),
        pltpu.VMEM(head_param.shape, F32),
        pltpu.SemaphoreType.DMA((3,)),
        pltpu.SemaphoreType.DMA((chunks,)),
        pltpu.SemaphoreType.DMA((chunks,)),
    ]
    return local_call(
        functools.partial(project_body, (heads, levels, chunks)), "project", 36, out_shape,
        [place], [], scratch, [head_param, tokens, flat_w, small], [HBM] + [WHOLE] * 14,
    )


def local_body(
    sizes, qkv_ref, pack_ref, pack_t_ref, trans_ref, mixed_t_ref, decay_ref, grad_ref, weight_ref,
    query_ref, value_ref, wr_in, *outs
):
    heads, levels, bits = sizes
    (attn_ref, attn_t_ref, prod_t_ref, scores_ref, mix_ref, mixed_ref, local_ref, hat_ref,
     hat_t_ref, grad_normed_ref, wr_hbm, sems) = outs
    del wr_in
    half, size = query_ref.shape[0] // 2, query_ref.shape[1]
    keeps = []
    for at in range(4):
        span = pl.ds(at % 2 * half, half)
        here, col = ((query_ref, 0), (value_ref, 2 * size))[at // 2]
        there = wr_hbm.at[span, pl.ds(col, size)]
        keeps.append(pltpu.make_async_copy(here.at[span, :], there, sems.at[at]))
        keeps[at].start()
    grad_normed_ref[...] = mm_nt(grad_ref[...], weight_ref[...])
    rows = pack_ref.shape[0]
    decay_col = levels * heads
    beta_col = decay_col + heads
    pack = pack_ref[...]
    pack_t = pack_t_ref[...]
    row_id, col_id = pair_ids(rows)
    apart = row_id ^ col_id
    for head in range(heads):
        scores = mm_nt_fine(qkv_ref[0, head], qkv_ref[1, head]) * decay_ref[head].astype(F32)
        scores_ref[head] = scores.astype(BF16)
        mix_ref[head] = level_mix(pack, head, heads, bits, apart).astype(BF16)
        mixed_ref[head] = mixed_t_ref[head].astype(F32).T.astype(BF16)
    for head in range(heads):
        attn = mm(scores_ref[head], trans_ref[head])
        attn_ref[head] = attn.astype(BF16)
        attn_t_ref[head] = attn.T.astype(BF16)
        attn = attn * pack_t[beta_col + head : beta_col + head + 1, :]
        prod = attn * mix_ref[head].astype(F32)
        prod_t_ref[head] = prod.T.astype(BF16)
        growth = jnp.exp(column(pack, decay_col + head))
        local_ref[head] = mm(prod, qkv_ref[2, head])
        hat = growth * qkv_ref[0, head] - mm(attn, growth * qkv_ref[1, head])
        hat_ref[head] = hat.astype(BF16)
        hat_t_ref[head] = hat.T.astype(BF16)
    for keep in keeps:
        keep.wait()


def local_part(arrays, wr, levels, bits):
    heads, rows, key = arrays[0].shape[1:]
    square = (heads, rows, rows)
    out_shape = (
        kept(square, BF16),
        kept(square, BF16),
        kept(square, BF16),
        kept(square, BF16),
        kept(square, BF16),
        kept((heads, rows, key), BF16),
        kept((heads, rows, key), F32),
        kept((heads, rows, key), BF16),
        kept((heads, key, rows), BF16),
        kept((rows, heads * key), F32),
        stored(wr.shape, BF16),
    )
    return local_call(
        functools.partial(local_body, (heads, levels, bits)), "local_part", 10, out_shape,
        [], arrays, [pltpu.SemaphoreType.DMA((4,))], [wr], [WHOLE] * 10 + [HBM],
        {len(arrays): 10},
    )


def join_pair(upper, own, other):
    key = own.shape[0]
    low = jnp.where(upper, other, own)
    high = jnp.where(upper, own, other)
    moved = mm(high[:, :key], low)
    late = jnp.concatenate([jnp.zeros((key, key), F32), high[:, key:].astype(F32)], 1)
    return (moved + late).astype(BF16)


def join_body(place_ref, own_ref, other_ref, out_ref):
    half = out_ref.shape[0]
    upper = (place_ref[0] & 1) == 1
    for slot in range(half):
        head = (place_ref[0] & 1) * half + slot
        out_ref[slot] = join_pair(upper, own_ref[head], other_ref[head])


def join_half(place, own, other):
    half = (own.shape[0] // 2,) + own.shape[1:]
    return local_call(join_body, "join_half", 6, [kept(half, BF16)], [place], [own, other])[0]


def gather_node(head, bit, first, near, uppers):
    if bit == 0:
        mine, theirs = near[first]
        half = mine.shape[0]
        here = uppers[0] if head >= half else jnp.logical_not(uppers[0])
        return jnp.where(here, mine[head % half], theirs[head % half])
    own = gather_node(head, bit - 1, first, near, uppers)
    other = gather_node(head, bit - 1, first ^ (1 << (bit - 1)), near, uppers)
    return join_pair(uppers[bit], own, other)


def reach_body(
    sizes, place_ref, gain_ref, pack_ref, local_ref, hat_ref, grad_ref, weight_ref, *refs
):
    heads, bits, far, count, near_count = sizes
    first_ref = refs[0]
    near = [None] + [(refs[1 + at], refs[1 + near_count + at]) for at in range(near_count)]
    refs = refs[2 * near_count + 1 :]
    out_refs = refs[:2]
    dout_ref, found_ref, prefix_ref, dfar_ref = refs[2:6]
    nodes = refs[6:-1]
    normed_ref = refs[-1]
    rows = pack_ref.shape[0]
    key = hat_ref.shape[2]
    pack = pack_ref[...]
    gain = gain_ref[...]
    lane = lane_of(rows)
    all_heads = range(heads)
    uppers = [((place_ref[0] >> bit) & 1) == 1 for bit in range(far)]
    others = []
    for bit in range(far):
        if bit == 0:
            others.append([first_ref[head] for head in all_heads])
        else:
            others.append(
                [gather_node(head, bit - 1, 1 << (bit - 1), near, uppers) for head in all_heads]
            )
            for head in all_heads:
                nodes[bit - 1][head] = others[bit][head]
    eye_key = jnp.where(pair_ids(key)[0] == pair_ids(key)[1], 1.0, 0.0).astype(BF16)
    prefix = [eye_key for head in all_heads]
    found = []
    for bit in range(far):
        for head in all_heads:
            prefix_ref[head, bit] = prefix[head]
        moved = [mm(prefix[head], others[bit][head]) for head in all_heads]
        found.append([jnp.where(uppers[bit], m[:, key:], 0.0).astype(BF16) for m in moved])
        prefix = [
            jnp.where(uppers[bit], moved[head][:, :key].astype(BF16), prefix[head])
            for head in all_heads
        ]
    found = [jnp.concatenate([found[bit][head] for bit in range(far)], 1) for head in all_heads]
    reached = [mm(hat_ref[head], found[head]) for head in all_heads]
    dfar = jnp.zeros((rows, LANES), F32)
    for head in all_heads:
        found_ref[head] = found[head]
        summed = local_ref[head]
        parts = []
        for bit in range(far):
            parts.append(reached[head][:, bit * key : (bit + 1) * key])
            summed = summed + column(pack, (bits + 1 + bit) * heads + head) * parts[bit]
        scale = lax.rsqrt(jnp.mean(summed * summed, -1, keepdims=True) + EPS)
        unit = summed * scale
        normed_ref[:, head * key : (head + 1) * key] = (unit * gain).astype(BF16)
        pulled = grad_ref[:, head * key : (head + 1) * key] * gain
        dout = scale * (pulled - unit * jnp.mean(pulled * unit, -1, keepdims=True))
        dout_ref[head] = dout
        for bit in range(far):
            col = (bits + 1 + bit) * heads + head
            dfar = jnp.where(lane == col, row_sum(dout * parts[bit]), dfar)
    dfar_ref[...] = dfar
    size = weight_ref.shape[1] // count
    for mask in range(count):
        dest = place_ref[1] ^ mask
        cols = pl.ds(pl.multiple_of(dest * size, size), size)
        out_refs[mask % 2][mask // 2] = jnp.dot(
            normed_ref[...], weight_ref[:, cols], preferred_element_type=F32
        ).astype(BF16)


def reach(place, arrays, first, near, bits, far, count):
    gain, pack, local_out, hat, grad_normed, weight = arrays
    heads, rows, key = hat.shape
    nodes = tuple(kept(first.shape, BF16) for bit in range(1, far))
    size = weight.shape[1] // count
    out_shape = (kept((count // 2, rows, size), BF16),) * 2 + (
        kept((heads, rows, key), F32),
        kept((heads, key, far * key), BF16),
        kept((heads, far, key, key), BF16),
        kept((rows, LANES), F32),
    ) + nodes
    mine, theirs = near
    got = local_call(
        functools.partial(reach_body, (heads, bits, far, count, len(mine))), "reach", 10, out_shape,
        [place], [*arrays, first, *mine, *theirs], [pltpu.VMEM((rows, heads * key), BF16)],
    )
    return got[:2], got[2:6], got[6:]


def return_body(sizes, place_ref, pack_ref, hat_t_ref, dout_ref, found_ref, prefix_ref, *refs):
    heads, bits, far = sizes
    others = refs[:far]
    dhat_ref = refs[far]
    sends = refs[far + 1 :]
    key = hat_t_ref.shape[1]
    pack = pack_ref[...]
    all_heads = range(heads)
    uppers = [((place_ref[0] >> bit) & 1) == 1 for bit in range(far)]
    spread = []
    for head in all_heads:
        parts = []
        for bit in range(far):
            weight = column(pack, (bits + 1 + bit) * heads + head)
            parts.append((weight * dout_ref[head]).astype(BF16))
        spread.append(jnp.concatenate(parts, 1))
    dfound = [mm(hat_t_ref[head], spread[head]) for head in all_heads]
    for head in all_heads:
        dhat_ref[head] = mm_nt(spread[head], found_ref[head])
    dprefix = [jnp.zeros((key, key), F32) for head in all_heads]
    for bit in reversed(range(far)):
        dfree = [
            jnp.where(uppers[bit], d[:, bit * key : (bit + 1) * key], 0.0) for d in dfound
        ]
        both = [
            jnp.concatenate([jnp.where(uppers[bit], dprefix[head], 0.0), dfree[head]], 1)
            for head in all_heads
        ]
        for head in all_heads:
            sent = dfree[head] if bit == far - 1 else both[head]
            sends[bit][head] = mm_tn(prefix_ref[head, bit], sent).astype(BF16)
        if bit > 0:
            moved = [mm_nt(both[head], others[bit][head]) for head in all_heads]
            dprefix = [
                jnp.where(uppers[bit], moved[head], dprefix[head]) for head in all_heads
            ]


def return_states(place, pack, hat_t, dout, found, prefix, others, bits):
    heads, rows, key = dout.shape
    far = len(others)
    sends = tuple(
        kept((heads, key, (1 if bit == far - 1 else 2) * key), BF16) for bit in range(far)
    )
    got = local_call(
        functools.partial(return_body, (heads, bits, far)), "return_states", 8,
        (kept(dout.shape, F32),) + sends, [place], [pack, hat_t, dout, found, prefix, *others],
    )
    return got[0], got[1:]


def add_body(*refs):
    count = len(refs) // 3
    for at in range(count):
        left, right = refs[at][...].astype(F32), refs[count + at][...].astype(F32)
        refs[2 * count + at][...] = (left + right).astype(BF16)


def add_all(left, right):
    out_shape = [kept(value.shape, BF16) for value in left]
    return local_call(add_body, "add_all", 6, out_shape, [], [*left, *right])


def lower_pull(dlower, base, lower, beta, decay, strict, k_in):
    dlower = jnp.where(strict, dlower, 0.0)
    dbeta = row_sum(dlower * base.astype(F32))
    dgram = dlower * (beta * decay)
    dkey = mm(dgram, k_in) + mm_tn(dgram, k_in)
    return dbeta, beta * dbeta, col_sum(dlower * lower.astype(F32)), dkey


def pull_body(sizes, *refs):
    heads, levels, bits = sizes
    (qkv_ref, pack_ref, pack_t_ref, trans_ref, attn_ref, attn_t_ref, prod_t_ref, scores_ref,
     mix_ref, decay_ref, base_ref, lower_ref, dout_ref, dhat_ref) = refs[:14]
    dqkv_ref, dgrown_ref, dcol_ref, drow_ref = refs[14:]
    rows = pack_ref.shape[0]
    decay_col = levels * heads
    beta_col = decay_col + heads
    block_bit = BLOCK.bit_length() - 1
    pack = pack_ref[...]
    pack_t = pack_t_ref[...]
    row_id, col_id = pair_ids(rows)
    strict = row_id > col_id
    apart = row_id ^ col_id
    lane = lane_of(rows)
    all_heads = range(heads)
    dcol = jnp.zeros((rows, LANES), F32)
    dbeta_rows, dcum_rows, dattn_all = [], [], []
    for head in all_heads:
        high, low = split(dout_ref[head])
        v_in = qkv_ref[2, head].astype(BF16)
        dprod = mm_nt(high, v_in) + mm_nt(low, v_in)
        dqkv_ref[2, head] = mm(prod_t_ref[head], high)
        beta_row = pack_t[beta_col + head : beta_col + head + 1, :]
        growth = jnp.exp(column(pack, decay_col + head))
        attn0 = attn_ref[head].astype(F32)
        touched = dprod * (attn0 * beta_row)
        for level in range(bits + 1):
            if level == 0:
                here = (apart >> block_bit) == 0
            else:
                here = (apart >> (block_bit + level - 1)) == 1
            dcol = jnp.where(
                lane == level * heads + head, row_sum(jnp.where(here, touched, 0.0)), dcol
            )
        dattn = dprod * mix_ref[head].astype(F32) - mm_nt(dhat_ref[head], growth * qkv_ref[1, head])
        dbeta_rows.append(col_sum(dattn * attn0))
        dattn_all.append((dattn * beta_row).astype(BF16))
    dscore_all = [mm_nt(dattn_all[head], trans_ref[head]) for head in all_heads]
    moved_all = []
    for head in all_heads:
        both = jnp.concatenate(
            [dscore_all[head].astype(BF16), dhat_ref[head].astype(BF16)], 1
        )
        moved_all.append(mm(attn_t_ref[head], both))
    for head in all_heads:
        q_in, k_in = qkv_ref[0, head], qkv_ref[1, head]
        beta = column(pack, beta_col + head)
        growth = jnp.exp(column(pack, decay_col + head))
        dscore = dscore_all[head]
        decay = decay_ref[head].astype(F32)
        dprobs = dscore * decay
        shift = dscore * scores_ref[head].astype(F32)
        dgrown_ref[head] = -beta * moved_all[head][:, rows:]
        dbeta, dcum_col, dcum_row, dk_lower = lower_pull(
            -moved_all[head][:, :rows], base_ref[head], lower_ref[head], beta, decay, strict, k_in
        )
        dhat = dhat_ref[head]
        dqkv_ref[0, head] = growth * dhat + mm(dprobs, k_in)
        dqkv_ref[1, head] = mm_tn(dprobs, q_in) + dk_lower
        dcum_col = dcum_col + row_sum(shift) + growth * row_sum(q_in * dhat)
        dcum_rows.append(-dcum_row - col_sum(shift))
        dcol = jnp.where(lane == beta_col + head, dbeta, dcol)
        dcol = jnp.where(lane == decay_col + head, dcum_col, dcol)
    dcol_ref[...] = dcol
    drow_ref[...] = jnp.concatenate(dcum_rows + dbeta_rows, 0)


def pull_local(arrays, levels, bits):
    heads, rows, key = arrays[0].shape[1:]
    out_shape = (
        kept((3, heads, rows, key), F32),
        kept((heads, rows, key), F32),
        kept((rows, LANES), F32),
        kept((2 * heads, rows), F32),
    )
    return local_call(
        functools.partial(pull_body, (heads, levels, bits)), "pull_local", 12, out_shape, [], arrays
    )


def finish_body(sizes, place_ref, *refs):
    heads, levels, far, arrived_counts = sizes
    (qkv_ref, gate_ref, pack_ref, trans_ref, mixed_ref, decay_ref, base_ref, lower_ref,
     dqkv_ref, dgrown_ref, dcol_ref, drow_ref, dfar_ref, rates_ref) = refs[:14]
    others = refs[14 : 14 + far]
    refs = refs[14 + far :]
    arrived = []
    for found in arrived_counts:
        arrived.append(refs[:found])
        refs = refs[found:]
    dproj, dgate_ref = refs
    rows = pack_ref.shape[0]
    key = qkv_ref.shape[3]
    decay_col = levels * heads
    beta_col = decay_col + heads
    norm_col = beta_col + heads
    place = place_ref[0]
    all_heads = range(heads)
    uppers = [((place >> bit) & 1) == 1 for bit in range(far)]
    pack = pack_ref[...]
    row_id, col_id = pair_ids(rows)
    strict = row_id > col_id
    lane = lane_of(rows)
    last_row = lax.broadcasted_iota(jnp.int32, (rows, 1), 0) == rows - 1
    eye_key = (pair_ids(key)[0] == pair_ids(key)[1]).astype(F32)
    dpair = [jnp.zeros((key, 2 * key), F32) for head in all_heads]
    for bit in reversed(range(far)):
        for head in all_heads:
            got = arrived[bit][0][head].astype(F32)
            for more in arrived[bit][1:]:
                got = got + more[head].astype(F32)
            other = others[bit][head]
            if bit == far - 1:
                got = jnp.concatenate([jnp.zeros((key, key), F32), got], 1)
                dpair[head] = jnp.where(uppers[bit], 0.0, got)
            else:
                as_low = mm_tn(other[:, :key], dpair[head]) + got
                as_high = mm_nt(dpair[head], other)
                as_high = jnp.concatenate([as_high, dpair[head][:, key:]], 1)
                dpair[head] = jnp.where(uppers[bit], as_high, as_low)
    moved_all, dmixed_all = [], []
    for head in all_heads:
        beta = column(pack, beta_col + head)
        growth = jnp.exp(column(pack, decay_col + head))
        both = jnp.concatenate([-growth * qkv_ref[1, head], qkv_ref[2, head]], 1)
        dmixed_all.append(mm_nt(both, dpair[head]))
        moved_all.append(mm(beta * mixed_ref[head].astype(F32), dpair[head]))
    dtail_all = [
        mm(trans_ref[head], column(pack, beta_col + head) * dmixed_all[head])
        for head in all_heads
    ]
    dlower_all = [-mm_nt(mixed_ref[head], dtail_all[head]) for head in all_heads]
    dcol = jnp.where(lane < decay_col, dcol_ref[...] + dfar_ref[...], dcol_ref[...])
    dcum_rows = []
    for head in all_heads:
        q_in, k_in = qkv_ref[0, head], qkv_ref[1, head]
        beta = column(pack, beta_col + head)
        cum_col = column(pack, decay_col + head)
        growth = jnp.exp(cum_col)
        last = cum_col[rows - 1 : rows, :]
        tail = jnp.exp(last - cum_col)
        dgrown = dgrown_ref[head] - moved_all[head][:, :key]
        dv = dqkv_ref[2, head] + moved_all[head][:, key:]
        dbeta_more = row_sum(mixed_ref[head].astype(F32) * dmixed_all[head])
        dtail = dtail_all[head]
        dbeta, dcum_col, dcum_row, dk_lower = lower_pull(
            dlower_all[head], base_ref[head], lower_ref[head], beta, decay_ref[head].astype(F32),
            strict, k_in
        )
        dcum_rows.append(-dcum_row)
        tail_pull = tail * row_sum(k_in * dtail)
        trace = col_sum(row_sum(dpair[head][:, :key] * eye_key))
        at_last = col_sum(tail_pull) + jnp.exp(last) * trace
        dcum_col = dcum_col + growth * row_sum(k_in * dgrown) - tail_pull
        dcum_col = dcum_col + jnp.where(last_row, at_last, 0.0)
        dk = dqkv_ref[1, head] + dk_lower + growth * dgrown + tail * dtail
        dq = dqkv_ref[0, head]
        dcol = dcol + jnp.where(lane == beta_col + head, dbeta + dbeta_more, 0.0)
        dcol = dcol + jnp.where(lane == decay_col + head, dcum_col, 0.0)
        for part, unit, dunit in ((0, q_in, dq), (1, k_in, dk)):
            scale = column(pack, norm_col + part * heads + head)
            back = scale * (dunit - unit * row_sum(unit * dunit))
            col = (part * heads + head) * key
            dproj[:, col : col + key] = back.astype(BF16)
        col = (2 * heads + head) * key
        dproj[:, col : col + key] = dv.astype(BF16)
    drow = drow_ref[...]
    drow = drow + jnp.concatenate(dcum_rows + [jnp.zeros((heads, rows), F32)], 0)
    drow = jnp.concatenate(
        [jnp.zeros((decay_col, rows), F32), drow,
         jnp.zeros((LANES - norm_col, rows), F32)], 0
    )
    dcol = dcol + drow.T
    rate, bias = rates_ref[0:1, :], rates_ref[1:2, :]
    switch = jax.nn.sigmoid(gate_ref[...] + bias)
    dlog = mm_ones((row_id <= col_id).astype(F32), dcol)
    slope = switch * (1.0 - switch)
    dgate = jnp.where(
        lane < decay_col,
        dcol * switch,
        jnp.where(lane < beta_col, -rate * dlog * slope, dcol * slope),
    )
    dgate_ref[...] = jnp.where(lane < norm_col, dgate, 0.0).astype(BF16)


def finish(place, arrays, others, arrived, levels):
    heads, rows, key = arrays[0].shape[1:]
    counts = tuple(len(group) for group in arrived)
    flat = [value for group in arrived for value in group]
    return local_call(
        functools.partial(finish_body, (heads, levels, len(others), counts)), "finish", 10,
        [kept((rows, 3 * heads * key), BF16), kept((rows, LANES), BF16)],
        [place], [*arrays, *others, *flat],
    )


def tokens_body(count, place_ref, dproj_ref, dgate_ref, wr_ref, small_ref, *refs):
    keep_ref, send_ref = refs[:2]
    direct_refs = refs[2:]
    size = wr_ref.shape[0] // count
    half = size // 2
    for mask in range(count):
        dest = place_ref[1] ^ mask
        span = pl.ds(pl.multiple_of(dest * size, size), size)
        part = mm_nt(dproj_ref[...], wr_ref[span, :]) + mm(dgate_ref[...], small_ref[:, span])
        direct_refs[mask][...] = part[:, :half].astype(BF16)
        target = send_ref if mask % 2 else keep_ref
        target[mask // 2] = part[:, half:].astype(BF16)


def pull_tokens(place, dproj, dgate, wr, small_t, count):
    rows = dproj.shape[0]
    half = wr.shape[0] // count // 2
    out_shape = [kept((count // 2, rows, half), BF16)] * 2 + [kept((rows, half), BF16)] * count
    got = local_call(
        functools.partial(tokens_body, count), "pull_tokens", 8, out_shape,
        [place], [dproj, dgate, wr, small_t],
    )
    return got[0], got[1], got[2:]


def swap(value, axis, mask):
    size = lax.axis_size(axis)
    return lax.ppermute(value, axis, [(at, at ^ mask) for at in range(size)])


def far_first(count):
    return sorted(range(1, count), key=lambda mask: mask < count // 2)


def halve_body(own_ref, got_ref, keep_ref, send_ref):
    for at in range(own_ref.shape[0]):
        total = own_ref[at].astype(F32) + got_ref[at].astype(F32)
        target = send_ref if at % 2 else keep_ref
        target[at // 2] = total.astype(target.dtype)


def halving(keep, send, axis, tied):
    mask = 1
    while keep.shape[0] > 1:
        got = swap(send, axis, mask)
        half = (keep.shape[0] // 2,) + keep.shape[1:]
        keep, send = local_call(
            halve_body, "halve", 6, [kept(half, F32), kept(half, BF16)], [], [keep, got]
        )
        send, tied = lax.optimization_barrier((send, tied))
        mask *= 2
    return keep, swap(send, axis, mask), tied


def sum_body(count, *refs):
    keep_ref, got_ref = refs[:2]
    out_ref = refs[-1]
    total = keep_ref[0].astype(F32) + got_ref[0].astype(F32)
    if count == 0:
        out_ref[...] = total.astype(BF16)
        return
    half = out_ref.shape[1] // 2
    out_ref[:, half:] = total.astype(BF16)
    total = refs[2][...].astype(F32)
    for ref in refs[3:-1]:
        total = total + ref[...].astype(F32)
    out_ref[:, :half] = total.astype(BF16)


def head_sum(keep, last, direct, got):
    rows, cols = keep.shape[1:]
    out = jax.ShapeDtypeStruct((rows, cols * (2 if direct else 1)), BF16)
    return local_call(
        functools.partial(sum_body, len(direct)), "head_sum", 6, [out], [],
        [keep, last, *direct[:1], *got],
    )[0]


def on_device(tokens, qkv_weight, small_weight, head_param, norm_gain, out_weight, grad_out):
    rows, width = tokens.shape
    heads, key = qkv_weight.shape[2:]
    levels = small_weight.shape[2] - 2
    bits = (rows // BLOCK).bit_length() - 1
    size = lax.axis_size("ctx")
    far = size.bit_length() - 1
    count = lax.axis_size("head")
    place = jnp.stack([lax.axis_index("ctx"), lax.axis_index("head")]).astype(jnp.int32)
    flat_w = qkv_weight.reshape(width * 3 * heads, key)
    small = jnp.transpose(small_weight, (2, 1, 0))
    rates = head_param.T
    flat_out = out_weight.reshape(heads * key, width)
    gain = norm_gain.reshape(1, key)

    (wr, query_w, value_w, small_t, qkv, gate, pack, pack_t, trans, mixed_t, decay, base, lower, rates_row,
     pair) = project(
        place, tokens, flat_w, small, rates, heads, levels
    )
    first = swap(pair, "ctx", 1)
    node = join_half(place, pair, first)
    mine = [swap(node, "ctx", 2 * at) for at in range(1, size // 2)]
    (attn, attn_t, prod_t, scores, mix, mixed, local_out, hat, hat_t, grad_normed, wr) = local_part(
        [qkv, pack, pack_t, trans, mixed_t, decay, grad_out, flat_out, query_w, value_w],
        wr, levels, bits,
    )
    mine, local_out, grad_normed = lax.optimization_barrier((mine, local_out, grad_normed))
    theirs = [swap(value, "ctx", 1) for value in mine]
    out_parts, (dout, found, prefix, dfar), nodes = reach(
        place, [gain, pack, local_out, hat, grad_normed, flat_out], first, (mine, theirs),
        bits, far, count
    )
    others = [first, *nodes]
    dhat, sends = return_states(place, pack, hat_t, dout, found, prefix, others, bits)
    got = [swap(value, "ctx", 1) for value in sends]
    arrived = [[got[0]]]
    sums = add_all(sends[1:], got[1:])
    for bit in range(1, far):
        half = 1 << (bit - 1)
        arrived.append([swap(sums[bit - 1], "ctx", 2 * at) for at in range(half, 2 * half)])
    dqkv, dgrown, dcol, drow = pull_local(
        [qkv, pack, pack_t, trans, attn, attn_t, prod_t, scores, mix, decay, base, lower, dout,
         dhat],
        levels, bits,
    )
    keep_out, last_out, dcol = halving(*out_parts, "head", dcol)
    arrays = [qkv, gate, pack, trans, mixed, decay, base, lower, dqkv, dgrown, dcol, drow, dfar,
              rates_row]
    dproj, dgate = finish(place, arrays, others, arrived, levels)
    keep, send, direct = pull_tokens(place, dproj, dgate, wr, small_t, count)
    direct, last_out = lax.optimization_barrier((direct, last_out))
    got = [swap(direct[mask], "head", mask) for mask in far_first(count)]
    keep, last, _ = halving(keep, send, "head", ())
    return head_sum(keep_out, last_out, [], []), head_sum(keep, last, direct, got)


def solution(mesh):
    placed = (
        P("ctx", None),
        P(None, None, "head", None),
        P(None, "head", None),
        P("head", None),
        P(),
        P("head", None, None),
        P("ctx", None),
    )
    return jax.shard_map(
        on_device,
        mesh=mesh,
        in_specs=placed,
        out_specs=(P("ctx", "head"), P("ctx", "head")),
        check_vma=False,
    )
```

```python
import functools

import jax
import jax.numpy as jnp
from jax import lax
from jax.experimental import pallas as pl
from jax.experimental.pallas import tpu as pltpu
from jax.sharding import PartitionSpec as P

BLOCK = 64
LANES = 128
EPS = 1e-06
MIB = 1024 * 1024
F32 = jnp.float32
BF16 = jnp.bfloat16
WHOLE = pl.BlockSpec(memory_space=pltpu.VMEM)
SCALARS = pl.BlockSpec(memory_space=pltpu.SMEM)
HBM = pl.BlockSpec(memory_space=pltpu.HBM)


def contract(left, right, dim_left, dim_right):
    return lax.dot_general(
        left.astype(BF16),
        right.astype(BF16),
        (((dim_left,), (dim_right,)), ((), ())),
        preferred_element_type=F32,
    )


def mm(left, right):
    return contract(left, right, 1, 0)


def mm_nt(left, right):
    return contract(left, right, 1, 1)


def mm_tn(left, right):
    return contract(left, right, 0, 0)


def split(values):
    high = values.astype(BF16)
    return high, (values - high.astype(F32)).astype(BF16)


def mm_nt_fine(left, right):
    left_high, left_low = split(left)
    right_high, right_low = split(right)
    return mm_nt(left_high, right_high) + (mm_nt(left_low, right_high) + mm_nt(left_high, right_low))


def mm_full(left, right):
    return jnp.dot(left, right, precision=lax.Precision.HIGHEST, preferred_element_type=F32)


def mm_ones(ones, values):
    high = values.astype(BF16)
    rest = values - high.astype(F32)
    middle = rest.astype(BF16)
    low = (rest - middle.astype(F32)).astype(BF16)
    return mm(ones, high) + (mm(ones, middle) + mm(ones, low))


def pair_ids(count):
    row_id = lax.broadcasted_iota(jnp.int32, (count, count), 0)
    col_id = lax.broadcasted_iota(jnp.int32, (count, count), 1)
    return row_id, col_id


def row_sum(values):
    return jnp.sum(values, 1, keepdims=True)


def col_sum(values):
    return jnp.sum(values, 0, keepdims=True)


def lane_of(rows):
    return lax.broadcasted_iota(jnp.int32, (rows, LANES), 1)


def decay_of(pack, pack_t, col, inclusive):
    spread = pack[:, col : col + 1] - pack_t[col : col + 1, :]
    return jnp.where(inclusive, jnp.exp(jnp.minimum(spread, 0.0)), 0.0)


def kept(shape, dtype):
    return pltpu.VMEM(shape, dtype)


def stored(shape, dtype):
    return pltpu.HBM(shape, dtype)


def pin(values, space):
    return [pltpu.with_memory_space_constraint(value, space) for value in values]


def local_call(
    body, name, limit, out_shape, scalars, arrays, scratch=(), remote=(), out_specs=None, alias=None
):
    return pl.pallas_call(
        body,
        out_shape=tuple(out_shape),
        in_specs=[SCALARS] * len(scalars)
        + [WHOLE] * len(arrays)
        + [HBM] * len(remote),
        out_specs=tuple(out_specs or [WHOLE] * len(out_shape)),
        scratch_shapes=list(scratch),
        input_output_aliases=alias or {},
        compiler_params=pltpu.CompilerParams(vmem_limit_bytes=limit * MIB),
        name=name,
    )(*scalars, *pin(arrays, pltpu.VMEM), *pin(remote, pltpu.HBM))


def column(pack, at):
    return pack[:, at : at + 1]


def level_mix(pack, head, heads, bits, apart):
    block_bit = BLOCK.bit_length() - 1
    mixed = jnp.broadcast_to(column(pack, head), apart.shape)
    for level in range(1, bits + 1):
        here = (apart >> (block_bit + level - 1)) >= 1
        mixed = jnp.where(here, column(pack, level * heads + head), mixed)
    return mixed


def head_rows(hp_ref, heads, decay_col, beta_col):
    lane_row = lane_of(1)
    rate = jnp.zeros((1, LANES), F32)
    bias = jnp.zeros((1, LANES), F32)
    for head in range(heads):
        rate = jnp.where(lane_row == decay_col + head, hp_ref[0:1, head : head + 1], rate)
        bias = jnp.where(lane_row == beta_col + head, hp_ref[1:2, head : head + 1], bias)
    return rate, bias


def invert(lower_all, eye, apart, rows):
    trans_all = [(eye - jnp.where(apart == 1, lower, 0.0)).astype(BF16) for lower in lower_all]
    for bit in range(1, rows.bit_length() - 1):
        here = (apart >> bit) == 1
        edge = [jnp.where(here, lower, 0.0) for lower in lower_all]
        half = [mm(trans, part) for trans, part in zip(trans_all, edge)]
        trans_all = [
            trans - mm(part, trans).astype(BF16) for trans, part in zip(trans_all, half)
        ]
    rest_all = []
    for trans, lower in zip(trans_all, lower_all):
        high, low = split(lower)
        rest_all.append(eye - trans.astype(F32) - mm(high, trans) - mm(low, trans))
    return [
        (trans.astype(F32) + mm(trans, rest)).astype(BF16)
        for trans, rest in zip(trans_all, rest_all)
    ]


def project_body(sizes, place_ref, hp_hbm, tokens_hbm, w_hbm, small_hbm, *refs):
    heads, levels, chunks = sizes
    (wr_hbm, query_ref, value_ref, small_ref, qkv_ref, gate_ref, pack_ref, pack_t_ref, trans_ref, mixed_t_ref,
     decay_ref, base_ref, lower_ref, rates_ref, pair_ref) = refs[:15]
    tokens, wide_in, wide_even, wide_odd, key_ref, small_in, small_wide, acc, hp_ref = refs[15:24]
    sems, in_sems, out_sems = refs[24:]
    laid = (query_ref, key_ref, value_ref)
    rows, width = tokens.shape
    depth = width // chunks
    cols = 3 * heads
    fetch_tokens = pltpu.make_async_copy(tokens_hbm, tokens, sems.at[0])
    fetch_small = pltpu.make_async_copy(small_hbm, small_in, sems.at[1])
    fetch_rates = pltpu.make_async_copy(hp_hbm, hp_ref, sems.at[2])
    fetches, keeps = [], []
    for chunk in range(chunks):
        span = pl.ds(chunk * depth * cols, depth * cols)
        fetches.append(
            pltpu.make_async_copy(w_hbm.at[span, :], wide_in.at[span, :], in_sems.at[chunk])
        )
        span = pl.ds(chunk * depth, depth)
        block = wr_hbm.at[span, pl.ds(heads * LANES, heads * LANES)]
        keeps.append(pltpu.make_async_copy(key_ref.at[span, :], block, out_sems.at[chunk]))
    fetches[0].start()
    fetch_tokens.start()
    fetch_small.start()
    fetch_rates.start()
    for fetch in fetches[1:]:
        fetch.start()

    def relay(chunk):
        fetches[chunk].wait()
        wide = wide_odd if chunk % 2 else wide_even
        at = chunk * depth
        wide[...] = wide_in[at * cols : (at + depth) * cols, :].astype(F32)
        for col in range(cols):
            value = wide[pl.ds(col, depth, stride=cols), :].astype(BF16)
            lanes = slice(col % heads * LANES, (col % heads + 1) * LANES)
            laid[col // heads][at : at + depth, lanes] = value

    def multiply(first, last):
        for part in (1, 2, 0):
            span = slice((part * heads) * LANES, (part + 1) * heads * LANES)
            own = jnp.dot(
                tokens[:, first * depth : last * depth],
                laid[part][first * depth : last * depth, :],
                preferred_element_type=F32,
            )
            if first == 0:
                acc[:, span] = own
            else:
                acc[:, span] += own

    def lay(first, last):
        for chunk in range(first, last):
            relay(chunk)
            if chunk == 0:
                fetch_tokens.wait()
            multiply(chunk, chunk + 1)

    decay_col = levels * heads
    beta_col = decay_col + heads
    norm_col = beta_col + heads
    lane = lane_of(rows)
    row_id, col_id = pair_ids(rows)
    inclusive = row_id >= col_id
    strict = row_id > col_id
    apart = row_id ^ col_id
    eye = (row_id == col_id).astype(F32)
    lay(0, chunks)
    for keep in keeps:
        keep.start()
    fetch_small.wait()
    small_rows = small_in.shape[0] * heads
    for level in range(small_in.shape[0]):
        small_wide[level * heads : (level + 1) * heads, :] = small_in[level].astype(F32)
    small_wide[small_rows:, :] = jnp.zeros((LANES - small_rows, width), F32)
    small_ref[...] = small_wide[...].astype(BF16)
    fetch_rates.wait()
    rate, bias = head_rows(hp_ref, heads, decay_col, beta_col)
    rates_ref[0:1, :] = rate
    rates_ref[1:2, :] = bias
    gate = mm_nt(tokens[...], small_ref[...])
    gate_ref[...] = gate
    switch = jax.nn.sigmoid(gate + bias)
    lam = jnp.maximum(gate, 0.0) + jnp.log1p(jnp.exp(-jnp.abs(gate)))
    cum = mm_full(inclusive.astype(F32), -rate * switch)
    pack = jnp.where(lane < decay_col, lam, jnp.where(lane < beta_col, cum, switch))
    pack_t = pack.T
    pack_t_ref[...] = pack_t

    def unit_of(part, head):
        col = (part * heads + head) * LANES
        raw = acc[:, col : col + LANES]
        scale = lax.rsqrt(row_sum(raw * raw) + EPS)
        qkv_ref[part, head] = raw * scale
        return raw * scale, jnp.where(lane == norm_col + part * heads + head, scale, 0.0)

    scales = jnp.zeros((rows, LANES), F32)
    k_all, lower_all = [], []
    for head in range(heads):
        unit, scale = unit_of(1, head)
        k_all.append(unit)
        scales = scales + scale
        decay = decay_of(pack, pack_t, decay_col + head, inclusive)
        decay_ref[head] = decay.astype(BF16)
        base = jnp.where(strict, decay * mm_nt(unit, unit), 0.0)
        base_ref[head] = base.astype(BF16)
        lower = column(pack, beta_col + head) * base
        lower_ref[head] = lower.astype(BF16)
        lower_all.append(lower)

    trans_all = invert(lower_all, eye, apart, rows)
    mixed_all = []
    for head in range(heads):
        trans_ref[head] = trans_all[head]
        cum_row = pack_t[decay_col + head : decay_col + head + 1, :]
        tail_t = k_all[head].T * jnp.exp(cum_row[:, rows - 1 :] - cum_row)
        mixed_all.append(mm(tail_t, trans_all[head]).astype(BF16))
    eye_key = eye[:LANES, :LANES]
    for head in range(heads):
        mixed_t_ref[head] = mixed_all[head]
        col = (2 * heads + head) * LANES
        v_in = acc[:, col : col + LANES]
        qkv_ref[2, head] = v_in
        cum_col = column(pack, decay_col + head)
        beta = column(pack, beta_col + head)
        grown = (beta * jnp.exp(cum_col)) * k_all[head]
        both = jnp.concatenate([-grown, beta * v_in], 1)
        pair = mm(mixed_all[head], both)
        last = jnp.exp(cum_col[rows - 1 : rows, :])
        pair_ref[head, :, :LANES] = (last * eye_key + pair[:, :LANES]).astype(BF16)
        pair_ref[head, :, LANES:] = pair[:, LANES:].astype(BF16)
    for head in range(heads):
        scales = scales + unit_of(0, head)[1]
    pack_ref[...] = jnp.where(lane < norm_col, pack, scales)
    for keep in keeps:
        keep.wait()


def project(place, tokens, flat_w, small, head_param, heads, levels):
    rows, width = tokens.shape
    chunks = 8
    cols = 3 * heads
    key = flat_w.shape[1]
    square = (heads, rows, rows)
    out_shape = (
        stored((width, cols * key), BF16),
        kept((width, heads * key), BF16),
        kept((width, heads * key), BF16),
        kept((LANES, width), BF16),
        kept((3, heads, rows, key), F32),
        kept((rows, LANES), F32),
        kept((rows, LANES), F32),
        kept((LANES, rows), F32),
        kept(square, BF16),
        kept((heads, key, rows), BF16),
        kept(square, BF16),
        kept(square, BF16),
        kept(square, BF16),
        kept((2, LANES), F32),
        kept((heads, key, 2 * key), BF16),
    )
    scratch = [
        pltpu.VMEM(tokens.shape, BF16),
        pltpu.VMEM(flat_w.shape, BF16),
        pltpu.VMEM((width // chunks * cols, key), F32),
        pltpu.VMEM((width // chunks * cols, key), F32),
        pltpu.VMEM((width, heads * key), BF16),
        pltpu.VMEM(small.shape, BF16),
        pltpu.VMEM((LANES, width), F32),
        pltpu.VMEM((rows, cols * key), F32),
        pltpu.VMEM(head_param.shape, F32),
        pltpu.SemaphoreType.DMA((3,)),
        pltpu.SemaphoreType.DMA((chunks,)),
        pltpu.SemaphoreType.DMA((chunks,)),
    ]
    return local_call(
        functools.partial(project_body, (heads, levels, chunks)), "project", 36, out_shape,
        [place], [], scratch, [head_param, tokens, flat_w, small], [HBM] + [WHOLE] * 14,
    )


def local_body(
    sizes, qkv_ref, pack_ref, pack_t_ref, trans_ref, mixed_t_ref, decay_ref, grad_ref, weight_ref,
    query_ref, value_ref, wr_in, *outs
):
    heads, levels, bits = sizes
    (attn_ref, attn_t_ref, prod_t_ref, scores_ref, mix_ref, mixed_ref, local_ref, hat_ref,
     hat_t_ref, grad_normed_ref, wr_hbm, sems) = outs
    del wr_in
    half, size = query_ref.shape[0] // 2, query_ref.shape[1]
    keeps = []
    for at in range(4):
        span = pl.ds(at % 2 * half, half)
        here, col = ((query_ref, 0), (value_ref, 2 * size))[at // 2]
        there = wr_hbm.at[span, pl.ds(col, size)]
        keeps.append(pltpu.make_async_copy(here.at[span, :], there, sems.at[at]))
        keeps[at].start()
    grad_normed_ref[...] = mm_nt(grad_ref[...], weight_ref[...])
    rows = pack_ref.shape[0]
    decay_col = levels * heads
    beta_col = decay_col + heads
    pack = pack_ref[...]
    pack_t = pack_t_ref[...]
    row_id, col_id = pair_ids(rows)
    apart = row_id ^ col_id
    for head in range(heads):
        scores = mm_nt_fine(qkv_ref[0, head], qkv_ref[1, head]) * decay_ref[head].astype(F32)
        scores_ref[head] = scores.astype(BF16)
        mix_ref[head] = level_mix(pack, head, heads, bits, apart).astype(BF16)
        mixed_ref[head] = mixed_t_ref[head].astype(F32).T.astype(BF16)
    for head in range(heads):
        attn = mm(scores_ref[head], trans_ref[head])
        attn_ref[head] = attn.astype(BF16)
        attn_t_ref[head] = attn.T.astype(BF16)
        attn = attn * pack_t[beta_col + head : beta_col + head + 1, :]
        prod = attn * mix_ref[head].astype(F32)
        prod_t_ref[head] = prod.T.astype(BF16)
        growth = jnp.exp(column(pack, decay_col + head))
        local_ref[head] = mm(prod, qkv_ref[2, head])
        hat = growth * qkv_ref[0, head] - mm(attn, growth * qkv_ref[1, head])
        hat_ref[head] = hat.astype(BF16)
        hat_t_ref[head] = hat.T.astype(BF16)
    for keep in keeps:
        keep.wait()


def local_part(arrays, wr, levels, bits):
    heads, rows, key = arrays[0].shape[1:]
    square = (heads, rows, rows)
    out_shape = (
        kept(square, BF16),
        kept(square, BF16),
        kept(square, BF16),
        kept(square, BF16),
        kept(square, BF16),
        kept((heads, rows, key), BF16),
        kept((heads, rows, key), F32),
        kept((heads, rows, key), BF16),
        kept((heads, key, rows), BF16),
        kept((rows, heads * key), F32),
        stored(wr.shape, BF16),
    )
    return local_call(
        functools.partial(local_body, (heads, levels, bits)), "local_part", 10, out_shape,
        [], arrays, [pltpu.SemaphoreType.DMA((4,))], [wr], [WHOLE] * 10 + [HBM],
        {len(arrays): 10},
    )


def join_pair(upper, own, other):
    key = own.shape[0]
    low = jnp.where(upper, other, own)
    high = jnp.where(upper, own, other)
    moved = mm(high[:, :key], low)
    late = jnp.concatenate([jnp.zeros((key, key), F32), high[:, key:].astype(F32)], 1)
    return (moved + late).astype(BF16)


def join_body(place_ref, own_ref, other_ref, out_ref):
    half = out_ref.shape[0]
    upper = (place_ref[0] & 1) == 1
    for slot in range(half):
        head = (place_ref[0] & 1) * half + slot
        out_ref[slot] = join_pair(upper, own_ref[head], other_ref[head])


def join_half(place, own, other):
    half = (own.shape[0] // 2,) + own.shape[1:]
    return local_call(join_body, "join_half", 6, [kept(half, BF16)], [place], [own, other])[0]


def gather_node(head, bit, first, near, uppers):
    if bit == 0:
        mine, theirs = near[first]
        half = mine.shape[0]
        here = uppers[0] if head >= half else jnp.logical_not(uppers[0])
        return jnp.where(here, mine[head % half], theirs[head % half])
    own = gather_node(head, bit - 1, first, near, uppers)
    other = gather_node(head, bit - 1, first ^ (1 << (bit - 1)), near, uppers)
    return join_pair(uppers[bit], own, other)


def reach_body(
    sizes, place_ref, gain_ref, pack_ref, local_ref, hat_ref, grad_ref, weight_ref, *refs
):
    heads, bits, far, count, near_count = sizes
    first_ref = refs[0]
    near = [None] + [(refs[1 + at], refs[1 + near_count + at]) for at in range(near_count)]
    refs = refs[2 * near_count + 1 :]
    out_refs = refs[:2]
    dout_ref, found_ref, prefix_ref, dfar_ref = refs[2:6]
    nodes = refs[6:-1]
    normed_ref = refs[-1]
    rows = pack_ref.shape[0]
    key = hat_ref.shape[2]
    pack = pack_ref[...]
    gain = gain_ref[...]
    lane = lane_of(rows)
    all_heads = range(heads)
    uppers = [((place_ref[0] >> bit) & 1) == 1 for bit in range(far)]
    others = []
    for bit in range(far):
        if bit == 0:
            others.append([first_ref[head] for head in all_heads])
        else:
            others.append(
                [gather_node(head, bit - 1, 1 << (bit - 1), near, uppers) for head in all_heads]
            )
            for head in all_heads:
                nodes[bit - 1][head] = others[bit][head]
    eye_key = jnp.where(pair_ids(key)[0] == pair_ids(key)[1], 1.0, 0.0).astype(BF16)
    prefix = [eye_key for head in all_heads]
    found = []
    for bit in range(far):
        for head in all_heads:
            prefix_ref[head, bit] = prefix[head]
        moved = [mm(prefix[head], others[bit][head]) for head in all_heads]
        found.append([jnp.where(uppers[bit], m[:, key:], 0.0).astype(BF16) for m in moved])
        prefix = [
            jnp.where(uppers[bit], moved[head][:, :key].astype(BF16), prefix[head])
            for head in all_heads
        ]
    found = [jnp.concatenate([found[bit][head] for bit in range(far)], 1) for head in all_heads]
    reached = [mm(hat_ref[head], found[head]) for head in all_heads]
    dfar = jnp.zeros((rows, LANES), F32)
    for head in all_heads:
        found_ref[head] = found[head]
        summed = local_ref[head]
        parts = []
        for bit in range(far):
            parts.append(reached[head][:, bit * key : (bit + 1) * key])
            summed = summed + column(pack, (bits + 1 + bit) * heads + head) * parts[bit]
        scale = lax.rsqrt(jnp.mean(summed * summed, -1, keepdims=True) + EPS)
        unit = summed * scale
        normed_ref[:, head * key : (head + 1) * key] = (unit * gain).astype(BF16)
        pulled = grad_ref[:, head * key : (head + 1) * key] * gain
        dout = scale * (pulled - unit * jnp.mean(pulled * unit, -1, keepdims=True))
        dout_ref[head] = dout
        for bit in range(far):
            col = (bits + 1 + bit) * heads + head
            dfar = jnp.where(lane == col, row_sum(dout * parts[bit]), dfar)
    dfar_ref[...] = dfar
    size = weight_ref.shape[1] // count
    for mask in range(count):
        dest = place_ref[1] ^ mask
        cols = pl.ds(pl.multiple_of(dest * size, size), size)
        out_refs[mask % 2][mask // 2] = jnp.dot(
            normed_ref[...], weight_ref[:, cols], preferred_element_type=F32
        ).astype(BF16)


def reach(place, arrays, first, near, bits, far, count):
    gain, pack, local_out, hat, grad_normed, weight = arrays
    heads, rows, key = hat.shape
    nodes = tuple(kept(first.shape, BF16) for bit in range(1, far))
    size = weight.shape[1] // count
    out_shape = (kept((count // 2, rows, size), BF16),) * 2 + (
        kept((heads, rows, key), F32),
        kept((heads, key, far * key), BF16),
        kept((heads, far, key, key), BF16),
        kept((rows, LANES), F32),
    ) + nodes
    mine, theirs = near
    got = local_call(
        functools.partial(reach_body, (heads, bits, far, count, len(mine))), "reach", 10, out_shape,
        [place], [*arrays, first, *mine, *theirs], [pltpu.VMEM((rows, heads * key), BF16)],
    )
    return got[:2], got[2:6], got[6:]


def return_body(sizes, place_ref, pack_ref, hat_t_ref, dout_ref, found_ref, prefix_ref, *refs):
    heads, bits, far = sizes
    others = refs[:far]
    dhat_ref = refs[far]
    sends = refs[far + 1 :]
    key = hat_t_ref.shape[1]
    pack = pack_ref[...]
    all_heads = range(heads)
    uppers = [((place_ref[0] >> bit) & 1) == 1 for bit in range(far)]
    spread = []
    for head in all_heads:
        parts = []
        for bit in range(far):
            weight = column(pack, (bits + 1 + bit) * heads + head)
            parts.append((weight * dout_ref[head]).astype(BF16))
        spread.append(jnp.concatenate(parts, 1))
    dfound = [mm(hat_t_ref[head], spread[head]) for head in all_heads]
    for head in all_heads:
        dhat_ref[head] = mm_nt(spread[head], found_ref[head])
    dprefix = [jnp.zeros((key, key), F32) for head in all_heads]
    for bit in reversed(range(far)):
        dfree = [
            jnp.where(uppers[bit], d[:, bit * key : (bit + 1) * key], 0.0) for d in dfound
        ]
        both = [
            jnp.concatenate([jnp.where(uppers[bit], dprefix[head], 0.0), dfree[head]], 1)
            for head in all_heads
        ]
        for head in all_heads:
            sent = dfree[head] if bit == far - 1 else both[head]
            sends[bit][head] = mm_tn(prefix_ref[head, bit], sent).astype(BF16)
        if bit > 0:
            moved = [mm_nt(both[head], others[bit][head]) for head in all_heads]
            dprefix = [
                jnp.where(uppers[bit], moved[head], dprefix[head]) for head in all_heads
            ]


def return_states(place, pack, hat_t, dout, found, prefix, others, bits):
    heads, rows, key = dout.shape
    far = len(others)
    sends = tuple(
        kept((heads, key, (1 if bit == far - 1 else 2) * key), BF16) for bit in range(far)
    )
    got = local_call(
        functools.partial(return_body, (heads, bits, far)), "return_states", 8,
        (kept(dout.shape, F32),) + sends, [place], [pack, hat_t, dout, found, prefix, *others],
    )
    return got[0], got[1:]


def add_body(*refs):
    count = len(refs) // 3
    for at in range(count):
        left, right = refs[at][...].astype(F32), refs[count + at][...].astype(F32)
        refs[2 * count + at][...] = (left + right).astype(BF16)


def add_all(left, right):
    out_shape = [kept(value.shape, BF16) for value in left]
    return local_call(add_body, "add_all", 6, out_shape, [], [*left, *right])


def lower_pull(dlower, base, lower, beta, decay, strict, k_in):
    dlower = jnp.where(strict, dlower, 0.0)
    dbeta = row_sum(dlower * base.astype(F32))
    dgram = dlower * (beta * decay)
    dkey = mm(dgram, k_in) + mm_tn(dgram, k_in)
    return dbeta, beta * dbeta, col_sum(dlower * lower.astype(F32)), dkey


def pull_body(sizes, *refs):
    heads, levels, bits = sizes
    (qkv_ref, pack_ref, pack_t_ref, trans_ref, attn_ref, attn_t_ref, prod_t_ref, scores_ref,
     mix_ref, decay_ref, base_ref, lower_ref, dout_ref, dhat_ref) = refs[:14]
    dqkv_ref, dgrown_ref, dcol_ref, drow_ref = refs[14:]
    rows = pack_ref.shape[0]
    decay_col = levels * heads
    beta_col = decay_col + heads
    block_bit = BLOCK.bit_length() - 1
    pack = pack_ref[...]
    pack_t = pack_t_ref[...]
    row_id, col_id = pair_ids(rows)
    strict = row_id > col_id
    apart = row_id ^ col_id
    lane = lane_of(rows)
    all_heads = range(heads)
    dcol = jnp.zeros((rows, LANES), F32)
    dbeta_rows, dcum_rows, dattn_all = [], [], []
    for head in all_heads:
        high, low = split(dout_ref[head])
        v_in = qkv_ref[2, head].astype(BF16)
        dprod = mm_nt(high, v_in) + mm_nt(low, v_in)
        dqkv_ref[2, head] = mm(prod_t_ref[head], high)
        beta_row = pack_t[beta_col + head : beta_col + head + 1, :]
        growth = jnp.exp(column(pack, decay_col + head))
        attn0 = attn_ref[head].astype(F32)
        touched = dprod * (attn0 * beta_row)
        for level in range(bits + 1):
            if level == 0:
                here = (apart >> block_bit) == 0
            else:
                here = (apart >> (block_bit + level - 1)) == 1
            dcol = jnp.where(
                lane == level * heads + head, row_sum(jnp.where(here, touched, 0.0)), dcol
            )
        dattn = dprod * mix_ref[head].astype(F32) - mm_nt(dhat_ref[head], growth * qkv_ref[1, head])
        dbeta_rows.append(col_sum(dattn * attn0))
        dattn_all.append((dattn * beta_row).astype(BF16))
    dscore_all = [mm_nt(dattn_all[head], trans_ref[head]) for head in all_heads]
    moved_all = []
    for head in all_heads:
        both = jnp.concatenate(
            [dscore_all[head].astype(BF16), dhat_ref[head].astype(BF16)], 1
        )
        moved_all.append(mm(attn_t_ref[head], both))
    for head in all_heads:
        q_in, k_in = qkv_ref[0, head], qkv_ref[1, head]
        beta = column(pack, beta_col + head)
        growth = jnp.exp(column(pack, decay_col + head))
        dscore = dscore_all[head]
        decay = decay_ref[head].astype(F32)
        dprobs = dscore * decay
        shift = dscore * scores_ref[head].astype(F32)
        dgrown_ref[head] = -beta * moved_all[head][:, rows:]
        dbeta, dcum_col, dcum_row, dk_lower = lower_pull(
            -moved_all[head][:, :rows], base_ref[head], lower_ref[head], beta, decay, strict, k_in
        )
        dhat = dhat_ref[head]
        dqkv_ref[0, head] = growth * dhat + mm(dprobs, k_in)
        dqkv_ref[1, head] = mm_tn(dprobs, q_in) + dk_lower
        dcum_col = dcum_col + row_sum(shift) + growth * row_sum(q_in * dhat)
        dcum_rows.append(-dcum_row - col_sum(shift))
        dcol = jnp.where(lane == beta_col + head, dbeta, dcol)
        dcol = jnp.where(lane == decay_col + head, dcum_col, dcol)
    dcol_ref[...] = dcol
    drow_ref[...] = jnp.concatenate(dcum_rows + dbeta_rows, 0)


def pull_local(arrays, levels, bits):
    heads, rows, key = arrays[0].shape[1:]
    out_shape = (
        kept((3, heads, rows, key), F32),
        kept((heads, rows, key), F32),
        kept((rows, LANES), F32),
        kept((2 * heads, rows), F32),
    )
    return local_call(
        functools.partial(pull_body, (heads, levels, bits)), "pull_local", 12, out_shape, [], arrays
    )


def finish_body(sizes, place_ref, *refs):
    heads, levels, far, arrived_counts = sizes
    (qkv_ref, gate_ref, pack_ref, trans_ref, mixed_ref, decay_ref, base_ref, lower_ref,
     dqkv_ref, dgrown_ref, dcol_ref, drow_ref, dfar_ref, rates_ref) = refs[:14]
    others = refs[14 : 14 + far]
    refs = refs[14 + far :]
    arrived = []
    for found in arrived_counts:
        arrived.append(refs[:found])
        refs = refs[found:]
    dproj, dgate_ref = refs
    rows = pack_ref.shape[0]
    key = qkv_ref.shape[3]
    decay_col = levels * heads
    beta_col = decay_col + heads
    norm_col = beta_col + heads
    place = place_ref[0]
    all_heads = range(heads)
    uppers = [((place >> bit) & 1) == 1 for bit in range(far)]
    pack = pack_ref[...]
    row_id, col_id = pair_ids(rows)
    strict = row_id > col_id
    lane = lane_of(rows)
    last_row = lax.broadcasted_iota(jnp.int32, (rows, 1), 0) == rows - 1
    eye_key = (pair_ids(key)[0] == pair_ids(key)[1]).astype(F32)
    dpair = [jnp.zeros((key, 2 * key), F32) for head in all_heads]
    for bit in reversed(range(far)):
        for head in all_heads:
            got = arrived[bit][0][head].astype(F32)
            for more in arrived[bit][1:]:
                got = got + more[head].astype(F32)
            other = others[bit][head]
            if bit == far - 1:
                got = jnp.concatenate([jnp.zeros((key, key), F32), got], 1)
                dpair[head] = jnp.where(uppers[bit], 0.0, got)
            else:
                as_low = mm_tn(other[:, :key], dpair[head]) + got
                as_high = mm_nt(dpair[head], other)
                as_high = jnp.concatenate([as_high, dpair[head][:, key:]], 1)
                dpair[head] = jnp.where(uppers[bit], as_high, as_low)
    moved_all, dmixed_all = [], []
    for head in all_heads:
        beta = column(pack, beta_col + head)
        growth = jnp.exp(column(pack, decay_col + head))
        both = jnp.concatenate([-growth * qkv_ref[1, head], qkv_ref[2, head]], 1)
        dmixed_all.append(mm_nt(both, dpair[head]))
        moved_all.append(mm(beta * mixed_ref[head].astype(F32), dpair[head]))
    dtail_all = [
        mm(trans_ref[head], column(pack, beta_col + head) * dmixed_all[head])
        for head in all_heads
    ]
    dlower_all = [-mm_nt(mixed_ref[head], dtail_all[head]) for head in all_heads]
    dcol = jnp.where(lane < decay_col, dcol_ref[...] + dfar_ref[...], dcol_ref[...])
    dcum_rows = []
    for head in all_heads:
        q_in, k_in = qkv_ref[0, head], qkv_ref[1, head]
        beta = column(pack, beta_col + head)
        cum_col = column(pack, decay_col + head)
        growth = jnp.exp(cum_col)
        last = cum_col[rows - 1 : rows, :]
        tail = jnp.exp(last - cum_col)
        dgrown = dgrown_ref[head] - moved_all[head][:, :key]
        dv = dqkv_ref[2, head] + moved_all[head][:, key:]
        dbeta_more = row_sum(mixed_ref[head].astype(F32) * dmixed_all[head])
        dtail = dtail_all[head]
        dbeta, dcum_col, dcum_row, dk_lower = lower_pull(
            dlower_all[head], base_ref[head], lower_ref[head], beta, decay_ref[head].astype(F32),
            strict, k_in
        )
        dcum_rows.append(-dcum_row)
        tail_pull = tail * row_sum(k_in * dtail)
        trace = col_sum(row_sum(dpair[head][:, :key] * eye_key))
        at_last = col_sum(tail_pull) + jnp.exp(last) * trace
        dcum_col = dcum_col + growth * row_sum(k_in * dgrown) - tail_pull
        dcum_col = dcum_col + jnp.where(last_row, at_last, 0.0)
        dk = dqkv_ref[1, head] + dk_lower + growth * dgrown + tail * dtail
        dq = dqkv_ref[0, head]
        dcol = dcol + jnp.where(lane == beta_col + head, dbeta + dbeta_more, 0.0)
        dcol = dcol + jnp.where(lane == decay_col + head, dcum_col, 0.0)
        for part, unit, dunit in ((0, q_in, dq), (1, k_in, dk)):
            scale = column(pack, norm_col + part * heads + head)
            back = scale * (dunit - unit * row_sum(unit * dunit))
            col = (part * heads + head) * key
            dproj[:, col : col + key] = back.astype(BF16)
        col = (2 * heads + head) * key
        dproj[:, col : col + key] = dv.astype(BF16)
    drow = drow_ref[...]
    drow = drow + jnp.concatenate(dcum_rows + [jnp.zeros((heads, rows), F32)], 0)
    drow = jnp.concatenate(
        [jnp.zeros((decay_col, rows), F32), drow,
         jnp.zeros((LANES - norm_col, rows), F32)], 0
    )
    dcol = dcol + drow.T
    rate, bias = rates_ref[0:1, :], rates_ref[1:2, :]
    switch = jax.nn.sigmoid(gate_ref[...] + bias)
    dlog = mm_ones((row_id <= col_id).astype(F32), dcol)
    slope = switch * (1.0 - switch)
    dgate = jnp.where(
        lane < decay_col,
        dcol * switch,
        jnp.where(lane < beta_col, -rate * dlog * slope, dcol * slope),
    )
    dgate_ref[...] = jnp.where(lane < norm_col, dgate, 0.0).astype(BF16)


def finish(place, arrays, others, arrived, levels):
    heads, rows, key = arrays[0].shape[1:]
    counts = tuple(len(group) for group in arrived)
    flat = [value for group in arrived for value in group]
    return local_call(
        functools.partial(finish_body, (heads, levels, len(others), counts)), "finish", 10,
        [kept((rows, 3 * heads * key), BF16), kept((rows, LANES), BF16)],
        [place], [*arrays, *others, *flat],
    )


def tokens_body(count, place_ref, dproj_ref, dgate_ref, wr_ref, small_ref, *refs):
    keep_ref, send_ref = refs[:2]
    direct_refs = refs[2:]
    size = wr_ref.shape[0] // count
    half = size // 2
    for mask in range(count):
        dest = place_ref[1] ^ mask
        span = pl.ds(pl.multiple_of(dest * size, size), size)
        part = mm_nt(dproj_ref[...], wr_ref[span, :]) + mm(dgate_ref[...], small_ref[:, span])
        direct_refs[mask][...] = part[:, :half].astype(BF16)
        target = send_ref if mask % 2 else keep_ref
        target[mask // 2] = part[:, half:].astype(BF16)


def pull_tokens(place, dproj, dgate, wr, small_t, count):
    rows = dproj.shape[0]
    half = wr.shape[0] // count // 2
    out_shape = [kept((count // 2, rows, half), BF16)] * 2 + [kept((rows, half), BF16)] * count
    got = local_call(
        functools.partial(tokens_body, count), "pull_tokens", 8, out_shape,
        [place], [dproj, dgate, wr, small_t],
    )
    return got[0], got[1], got[2:]


def swap(value, axis, mask):
    size = lax.axis_size(axis)
    return lax.ppermute(value, axis, [(at, at ^ mask) for at in range(size)])


def far_first(count):
    return sorted(range(1, count), key=lambda mask: mask < count // 2)


def halve_body(own_ref, got_ref, keep_ref, send_ref):
    for at in range(own_ref.shape[0]):
        total = own_ref[at].astype(F32) + got_ref[at].astype(F32)
        target = send_ref if at % 2 else keep_ref
        target[at // 2] = total.astype(target.dtype)


def halving(keep, send, axis, tied):
    mask = 1
    while keep.shape[0] > 1:
        got = swap(send, axis, mask)
        half = (keep.shape[0] // 2,) + keep.shape[1:]
        keep, send = local_call(
            halve_body, "halve", 6, [kept(half, F32), kept(half, BF16)], [], [keep, got]
        )
        send, tied = lax.optimization_barrier((send, tied))
        mask *= 2
    return keep, swap(send, axis, mask), tied


def sum_body(count, *refs):
    keep_ref, got_ref = refs[:2]
    out_ref = refs[-1]
    total = keep_ref[0].astype(F32) + got_ref[0].astype(F32)
    if count == 0:
        out_ref[...] = total.astype(BF16)
        return
    half = out_ref.shape[1] // 2
    out_ref[:, half:] = total.astype(BF16)
    total = refs[2][...].astype(F32)
    for ref in refs[3:-1]:
        total = total + ref[...].astype(F32)
    out_ref[:, :half] = total.astype(BF16)


def head_sum(keep, last, direct, got):
    rows, cols = keep.shape[1:]
    out = jax.ShapeDtypeStruct((rows, cols * (2 if direct else 1)), BF16)
    return local_call(
        functools.partial(sum_body, len(direct)), "head_sum", 6, [out], [],
        [keep, last, *direct[:1], *got],
    )[0]


def on_device(tokens, qkv_weight, small_weight, head_param, norm_gain, out_weight, grad_out):
    rows, width = tokens.shape
    heads, key = qkv_weight.shape[2:]
    levels = small_weight.shape[2] - 2
    bits = (rows // BLOCK).bit_length() - 1
    size = lax.axis_size("ctx")
    far = size.bit_length() - 1
    count = lax.axis_size("head")
    place = jnp.stack([lax.axis_index("ctx"), lax.axis_index("head")]).astype(jnp.int32)
    flat_w = qkv_weight.reshape(width * 3 * heads, key)
    small = jnp.transpose(small_weight, (2, 1, 0))
    rates = head_param.T
    flat_out = out_weight.reshape(heads * key, width)
    gain = norm_gain.reshape(1, key)

    (wr, query_w, value_w, small_t, qkv, gate, pack, pack_t, trans, mixed_t, decay, base, lower, rates_row,
     pair) = project(
        place, tokens, flat_w, small, rates, heads, levels
    )
    first = swap(pair, "ctx", 1)
    node = join_half(place, pair, first)
    mine = [swap(node, "ctx", 2 * at) for at in range(1, size // 2)]
    (attn, attn_t, prod_t, scores, mix, mixed, local_out, hat, hat_t, grad_normed, wr) = local_part(
        [qkv, pack, pack_t, trans, mixed_t, decay, grad_out, flat_out, query_w, value_w],
        wr, levels, bits,
    )
    mine, local_out, grad_normed = lax.optimization_barrier((mine, local_out, grad_normed))
    theirs = [swap(value, "ctx", 1) for value in mine]
    out_parts, (dout, found, prefix, dfar), nodes = reach(
        place, [gain, pack, local_out, hat, grad_normed, flat_out], first, (mine, theirs),
        bits, far, count
    )
    others = [first, *nodes]
    dhat, sends = return_states(place, pack, hat_t, dout, found, prefix, others, bits)
    got = [swap(value, "ctx", 1) for value in sends]
    arrived = [[got[0]]]
    sums = add_all(sends[1:], got[1:])
    for bit in range(1, far):
        half = 1 << (bit - 1)
        arrived.append([swap(sums[bit - 1], "ctx", 2 * at) for at in range(half, 2 * half)])
    dqkv, dgrown, dcol, drow = pull_local(
        [qkv, pack, pack_t, trans, attn, attn_t, prod_t, scores, mix, decay, base, lower, dout,
         dhat],
        levels, bits,
    )
    keep_out, last_out, dcol = halving(*out_parts, "head", dcol)
    arrays = [qkv, gate, pack, trans, mixed, decay, base, lower, dqkv, dgrown, dcol, drow, dfar,
              rates_row]
    dproj, dgate = finish(place, arrays, others, arrived, levels)
    keep, send, direct = pull_tokens(place, dproj, dgate, wr, small_t, count)
    direct, last_out = lax.optimization_barrier((direct, last_out))
    keep, last, late = halving(keep, send, "head", direct[1])
    direct = [direct[0], late, *direct[2:]]
    got = [swap(direct[mask], "head", mask) for mask in far_first(count)]
    return head_sum(keep_out, last_out, [], []), head_sum(keep, last, direct, got)


def solution(mesh):
    placed = (
        P("ctx", None),
        P(None, None, "head", None),
        P(None, "head", None),
        P("head", None),
        P(),
        P("head", None, None),
        P("ctx", None),
    )
    return jax.shard_map(
        on_device,
        mesh=mesh,
        in_specs=placed,
        out_specs=(P("ctx", "head"), P("ctx", "head")),
        check_vma=False,
    )
```

```python
import functools

import jax
import jax.numpy as jnp
from jax import lax
from jax.experimental import pallas as pl
from jax.experimental.pallas import tpu as pltpu
from jax.sharding import PartitionSpec as P

BLOCK = 64
LANES = 128
EPS = 1e-06
MIB = 1024 * 1024
F32 = jnp.float32
BF16 = jnp.bfloat16
WHOLE = pl.BlockSpec(memory_space=pltpu.VMEM)
SCALARS = pl.BlockSpec(memory_space=pltpu.SMEM)
HBM = pl.BlockSpec(memory_space=pltpu.HBM)


def contract(left, right, dim_left, dim_right):
    return lax.dot_general(
        left.astype(BF16),
        right.astype(BF16),
        (((dim_left,), (dim_right,)), ((), ())),
        preferred_element_type=F32,
    )


def mm(left, right):
    return contract(left, right, 1, 0)


def mm_nt(left, right):
    return contract(left, right, 1, 1)


def mm_tn(left, right):
    return contract(left, right, 0, 0)


def split(values):
    high = values.astype(BF16)
    return high, (values - high.astype(F32)).astype(BF16)


def mm_nt_fine(left, right):
    left_high, left_low = split(left)
    right_high, right_low = split(right)
    return mm_nt(left_high, right_high) + (mm_nt(left_low, right_high) + mm_nt(left_high, right_low))


def mm_full(left, right):
    return jnp.dot(left, right, precision=lax.Precision.HIGHEST, preferred_element_type=F32)


def mm_ones(ones, values):
    high = values.astype(BF16)
    rest = values - high.astype(F32)
    middle = rest.astype(BF16)
    low = (rest - middle.astype(F32)).astype(BF16)
    return mm(ones, high) + (mm(ones, middle) + mm(ones, low))


def pair_ids(count):
    row_id = lax.broadcasted_iota(jnp.int32, (count, count), 0)
    col_id = lax.broadcasted_iota(jnp.int32, (count, count), 1)
    return row_id, col_id


def row_sum(values):
    return jnp.sum(values, 1, keepdims=True)


def col_sum(values):
    return jnp.sum(values, 0, keepdims=True)


def lane_of(rows):
    return lax.broadcasted_iota(jnp.int32, (rows, LANES), 1)


def decay_of(pack, pack_t, col, inclusive):
    spread = pack[:, col : col + 1] - pack_t[col : col + 1, :]
    return jnp.where(inclusive, jnp.exp(jnp.minimum(spread, 0.0)), 0.0)


def kept(shape, dtype):
    return pltpu.VMEM(shape, dtype)


def stored(shape, dtype):
    return pltpu.HBM(shape, dtype)


def pin(values, space):
    return [pltpu.with_memory_space_constraint(value, space) for value in values]


def local_call(
    body, name, limit, out_shape, scalars, arrays, scratch=(), remote=(), out_specs=None, alias=None
):
    return pl.pallas_call(
        body,
        out_shape=tuple(out_shape),
        in_specs=[SCALARS] * len(scalars)
        + [WHOLE] * len(arrays)
        + [HBM] * len(remote),
        out_specs=tuple(out_specs or [WHOLE] * len(out_shape)),
        scratch_shapes=list(scratch),
        input_output_aliases=alias or {},
        compiler_params=pltpu.CompilerParams(vmem_limit_bytes=limit * MIB),
        name=name,
    )(*scalars, *pin(arrays, pltpu.VMEM), *pin(remote, pltpu.HBM))


def column(pack, at):
    return pack[:, at : at + 1]


def level_mix(pack, head, heads, bits, apart):
    block_bit = BLOCK.bit_length() - 1
    mixed = jnp.broadcast_to(column(pack, head), apart.shape)
    for level in range(1, bits + 1):
        here = (apart >> (block_bit + level - 1)) >= 1
        mixed = jnp.where(here, column(pack, level * heads + head), mixed)
    return mixed


def head_rows(hp_ref, heads, decay_col, beta_col):
    lane_row = lane_of(1)
    rate = jnp.zeros((1, LANES), F32)
    bias = jnp.zeros((1, LANES), F32)
    for head in range(heads):
        rate = jnp.where(lane_row == decay_col + head, hp_ref[0:1, head : head + 1], rate)
        bias = jnp.where(lane_row == beta_col + head, hp_ref[1:2, head : head + 1], bias)
    return rate, bias


def invert(lower_all, eye, apart, rows):
    trans_all = [(eye - jnp.where(apart == 1, lower, 0.0)).astype(BF16) for lower in lower_all]
    for bit in range(1, rows.bit_length() - 1):
        here = (apart >> bit) == 1
        edge = [jnp.where(here, lower, 0.0) for lower in lower_all]
        half = [mm(trans, part) for trans, part in zip(trans_all, edge)]
        trans_all = [
            trans - mm(part, trans).astype(BF16) for trans, part in zip(trans_all, half)
        ]
    rest_all = []
    for trans, lower in zip(trans_all, lower_all):
        high, low = split(lower)
        rest_all.append(eye - trans.astype(F32) - mm(high, trans) - mm(low, trans))
    return [
        (trans.astype(F32) + mm(trans, rest)).astype(BF16)
        for trans, rest in zip(trans_all, rest_all)
    ]


def project_body(sizes, place_ref, hp_hbm, tokens_hbm, w_hbm, small_hbm, *refs):
    heads, levels, chunks = sizes
    (wr_hbm, query_ref, value_ref, small_ref, qkv_ref, gate_ref, pack_ref, pack_t_ref, trans_ref, mixed_t_ref,
     decay_ref, base_ref, lower_ref, rates_ref, pair_ref) = refs[:15]
    tokens, wide_in, wide_even, wide_odd, key_ref, small_in, small_wide, acc, hp_ref = refs[15:24]
    sems, in_sems, out_sems = refs[24:]
    laid = (query_ref, key_ref, value_ref)
    rows, width = tokens.shape
    depth = width // chunks
    cols = 3 * heads
    fetch_tokens = pltpu.make_async_copy(tokens_hbm, tokens, sems.at[0])
    fetch_small = pltpu.make_async_copy(small_hbm, small_in, sems.at[1])
    fetch_rates = pltpu.make_async_copy(hp_hbm, hp_ref, sems.at[2])
    fetches, keeps = [], []
    for chunk in range(chunks):
        span = pl.ds(chunk * depth * cols, depth * cols)
        fetches.append(
            pltpu.make_async_copy(w_hbm.at[span, :], wide_in.at[span, :], in_sems.at[chunk])
        )
        span = pl.ds(chunk * depth, depth)
        block = wr_hbm.at[span, pl.ds(heads * LANES, heads * LANES)]
        keeps.append(pltpu.make_async_copy(key_ref.at[span, :], block, out_sems.at[chunk]))
    fetches[0].start()
    fetch_tokens.start()
    fetch_small.start()
    fetch_rates.start()
    for fetch in fetches[1:]:
        fetch.start()

    def relay(chunk):
        fetches[chunk].wait()
        wide = wide_odd if chunk % 2 else wide_even
        at = chunk * depth
        wide[...] = wide_in[at * cols : (at + depth) * cols, :].astype(F32)
        for col in range(cols):
            value = wide[pl.ds(col, depth, stride=cols), :].astype(BF16)
            lanes = slice(col % heads * LANES, (col % heads + 1) * LANES)
            laid[col // heads][at : at + depth, lanes] = value

    def multiply(first, last):
        for part in (1, 2):
            span = slice((part * heads) * LANES, (part + 1) * heads * LANES)
            own = jnp.dot(
                tokens[:, first * depth : last * depth],
                laid[part][first * depth : last * depth, :],
                preferred_element_type=F32,
            )
            if first == 0:
                acc[:, span] = own
            else:
                acc[:, span] += own

    def lay(first, last):
        for chunk in range(first, last):
            relay(chunk)
            if chunk == 0:
                fetch_tokens.wait()
            multiply(chunk, chunk + 1)

    decay_col = levels * heads
    beta_col = decay_col + heads
    norm_col = beta_col + heads
    lane = lane_of(rows)
    row_id, col_id = pair_ids(rows)
    inclusive = row_id >= col_id
    strict = row_id > col_id
    apart = row_id ^ col_id
    eye = (row_id == col_id).astype(F32)
    lay(0, chunks)
    for keep in keeps:
        keep.start()
    fetch_small.wait()
    small_rows = small_in.shape[0] * heads
    for level in range(small_in.shape[0]):
        small_wide[level * heads : (level + 1) * heads, :] = small_in[level].astype(F32)
    small_wide[small_rows:, :] = jnp.zeros((LANES - small_rows, width), F32)
    small_ref[...] = small_wide[...].astype(BF16)
    fetch_rates.wait()
    rate, bias = head_rows(hp_ref, heads, decay_col, beta_col)
    rates_ref[0:1, :] = rate
    rates_ref[1:2, :] = bias
    gate = mm_nt(tokens[...], small_ref[...])
    gate_ref[...] = gate
    switch = jax.nn.sigmoid(gate + bias)
    lam = jnp.maximum(gate, 0.0) + jnp.log1p(jnp.exp(-jnp.abs(gate)))
    cum = mm_full(inclusive.astype(F32), -rate * switch)
    pack = jnp.where(lane < decay_col, lam, jnp.where(lane < beta_col, cum, switch))
    pack_t = pack.T
    pack_t_ref[...] = pack_t

    def unit_of(part, head):
        col = (part * heads + head) * LANES
        raw = acc[:, col : col + LANES]
        scale = lax.rsqrt(row_sum(raw * raw) + EPS)
        qkv_ref[part, head] = raw * scale
        return raw * scale, jnp.where(lane == norm_col + part * heads + head, scale, 0.0)

    scales = jnp.zeros((rows, LANES), F32)
    k_all, lower_all = [], []
    for head in range(heads):
        unit, scale = unit_of(1, head)
        k_all.append(unit)
        scales = scales + scale
        decay = decay_of(pack, pack_t, decay_col + head, inclusive)
        decay_ref[head] = decay.astype(BF16)
        base = jnp.where(strict, decay * mm_nt(unit, unit), 0.0)
        base_ref[head] = base.astype(BF16)
        lower = column(pack, beta_col + head) * base
        lower_ref[head] = lower.astype(BF16)
        lower_all.append(lower)

    trans_all = invert(lower_all, eye, apart, rows)
    mixed_all = []
    for head in range(heads):
        trans_ref[head] = trans_all[head]
        cum_row = pack_t[decay_col + head : decay_col + head + 1, :]
        tail_t = k_all[head].T * jnp.exp(cum_row[:, rows - 1 :] - cum_row)
        mixed_all.append(mm(tail_t, trans_all[head]).astype(BF16))
    eye_key = eye[:LANES, :LANES]
    for head in range(heads):
        mixed_t_ref[head] = mixed_all[head]
        col = (2 * heads + head) * LANES
        v_in = acc[:, col : col + LANES]
        qkv_ref[2, head] = v_in
        cum_col = column(pack, decay_col + head)
        beta = column(pack, beta_col + head)
        grown = (beta * jnp.exp(cum_col)) * k_all[head]
        both = jnp.concatenate([-grown, beta * v_in], 1)
        pair = mm(mixed_all[head], both)
        last = jnp.exp(cum_col[rows - 1 : rows, :])
        pair_ref[head, :, :LANES] = (last * eye_key + pair[:, :LANES]).astype(BF16)
        pair_ref[head, :, LANES:] = pair[:, LANES:].astype(BF16)
    pack_ref[...] = jnp.where(lane < norm_col, pack, scales)
    for keep in keeps:
        keep.wait()


def project(place, tokens, flat_w, small, head_param, heads, levels):
    rows, width = tokens.shape
    chunks = 8
    cols = 3 * heads
    key = flat_w.shape[1]
    square = (heads, rows, rows)
    out_shape = (
        stored((width, cols * key), BF16),
        kept((width, heads * key), BF16),
        kept((width, heads * key), BF16),
        kept((LANES, width), BF16),
        kept((3, heads, rows, key), F32),
        kept((rows, LANES), F32),
        kept((rows, LANES), F32),
        kept((LANES, rows), F32),
        kept(square, BF16),
        kept((heads, key, rows), BF16),
        kept(square, BF16),
        kept(square, BF16),
        kept(square, BF16),
        kept((2, LANES), F32),
        kept((heads, key, 2 * key), BF16),
    )
    scratch = [
        pltpu.VMEM(tokens.shape, BF16),
        pltpu.VMEM(flat_w.shape, BF16),
        pltpu.VMEM((width // chunks * cols, key), F32),
        pltpu.VMEM((width // chunks * cols, key), F32),
        pltpu.VMEM((width, heads * key), BF16),
        pltpu.VMEM(small.shape, BF16),
        pltpu.VMEM((LANES, width), F32),
        pltpu.VMEM((rows, cols * key), F32),
        pltpu.VMEM(head_param.shape, F32),
        pltpu.SemaphoreType.DMA((3,)),
        pltpu.SemaphoreType.DMA((chunks,)),
        pltpu.SemaphoreType.DMA((chunks,)),
    ]
    return local_call(
        functools.partial(project_body, (heads, levels, chunks)), "project", 36, out_shape,
        [place], [], scratch, [head_param, tokens, flat_w, small], [HBM] + [WHOLE] * 14,
    )


def local_body(
    sizes, qkv_ref, pack_ref, pack_t_ref, trans_ref, mixed_t_ref, decay_ref, grad_ref, weight_ref,
    query_ref, value_ref, tokens_ref, wr_in, *outs
):
    heads, levels, bits = sizes
    (attn_ref, attn_t_ref, prod_t_ref, scores_ref, mix_ref, mixed_ref, local_ref, hat_ref,
     hat_t_ref, grad_normed_ref, qkv_out, pack_out, wr_hbm, sems) = outs
    del wr_in
    half, size = query_ref.shape[0] // 2, query_ref.shape[1]
    keeps = []
    for at in range(4):
        span = pl.ds(at % 2 * half, half)
        here, col = ((query_ref, 0), (value_ref, 2 * size))[at // 2]
        there = wr_hbm.at[span, pl.ds(col, size)]
        keeps.append(pltpu.make_async_copy(here.at[span, :], there, sems.at[at]))
        keeps[at].start()
    rows = pack_ref.shape[0]
    decay_col = levels * heads
    beta_col = decay_col + heads
    norm_col = beta_col + heads
    lane = lane_of(rows)
    raw_all = jnp.dot(tokens_ref[...], query_ref[...], preferred_element_type=F32)
    pack = pack_ref[...]
    q_all = []
    for head in range(heads):
        raw = raw_all[:, head * LANES : (head + 1) * LANES]
        scale = lax.rsqrt(row_sum(raw * raw) + EPS)
        q_all.append(raw * scale)
        qkv_out[0, head] = q_all[head]
        pack = jnp.where(lane == norm_col + head, scale, pack)
    pack_out[...] = pack
    grad_normed_ref[...] = mm_nt(grad_ref[...], weight_ref[...])
    pack_t = pack_t_ref[...]
    row_id, col_id = pair_ids(rows)
    apart = row_id ^ col_id
    for head in range(heads):
        scores = mm_nt_fine(q_all[head], qkv_ref[1, head]) * decay_ref[head].astype(F32)
        scores_ref[head] = scores.astype(BF16)
        mix_ref[head] = level_mix(pack, head, heads, bits, apart).astype(BF16)
        mixed_ref[head] = mixed_t_ref[head].astype(F32).T.astype(BF16)
    for head in range(heads):
        attn = mm(scores_ref[head], trans_ref[head])
        attn_ref[head] = attn.astype(BF16)
        attn_t_ref[head] = attn.T.astype(BF16)
        attn = attn * pack_t[beta_col + head : beta_col + head + 1, :]
        prod = attn * mix_ref[head].astype(F32)
        prod_t_ref[head] = prod.T.astype(BF16)
        growth = jnp.exp(column(pack, decay_col + head))
        local_ref[head] = mm(prod, qkv_ref[2, head])
        hat = growth * q_all[head] - mm(attn, growth * qkv_ref[1, head])
        hat_ref[head] = hat.astype(BF16)
        hat_t_ref[head] = hat.T.astype(BF16)
    for keep in keeps:
        keep.wait()


def local_part(arrays, wr, levels, bits):
    heads, rows, key = arrays[0].shape[1:]
    square = (heads, rows, rows)
    out_shape = (
        kept(square, BF16),
        kept(square, BF16),
        kept(square, BF16),
        kept(square, BF16),
        kept(square, BF16),
        kept((heads, rows, key), BF16),
        kept((heads, rows, key), F32),
        kept((heads, rows, key), BF16),
        kept((heads, key, rows), BF16),
        kept((rows, heads * key), F32),
        kept(arrays[0].shape, F32),
        kept(arrays[1].shape, F32),
        stored(wr.shape, BF16),
    )
    return local_call(
        functools.partial(local_body, (heads, levels, bits)), "local_part", 10, out_shape,
        [], arrays, [pltpu.SemaphoreType.DMA((4,))], [wr], [WHOLE] * 12 + [HBM],
        {0: 10, 1: 11, len(arrays): 12},
    )


def join_pair(upper, own, other):
    key = own.shape[0]
    low = jnp.where(upper, other, own)
    high = jnp.where(upper, own, other)
    moved = mm(high[:, :key], low)
    late = jnp.concatenate([jnp.zeros((key, key), F32), high[:, key:].astype(F32)], 1)
    return (moved + late).astype(BF16)


def join_body(place_ref, own_ref, other_ref, out_ref):
    half = out_ref.shape[0]
    upper = (place_ref[0] & 1) == 1
    for slot in range(half):
        head = (place_ref[0] & 1) * half + slot
        out_ref[slot] = join_pair(upper, own_ref[head], other_ref[head])


def join_half(place, own, other):
    half = (own.shape[0] // 2,) + own.shape[1:]
    return local_call(join_body, "join_half", 6, [kept(half, BF16)], [place], [own, other])[0]


def gather_node(head, bit, first, near, uppers):
    if bit == 0:
        mine, theirs = near[first]
        half = mine.shape[0]
        here = uppers[0] if head >= half else jnp.logical_not(uppers[0])
        return jnp.where(here, mine[head % half], theirs[head % half])
    own = gather_node(head, bit - 1, first, near, uppers)
    other = gather_node(head, bit - 1, first ^ (1 << (bit - 1)), near, uppers)
    return join_pair(uppers[bit], own, other)


def reach_body(
    sizes, place_ref, gain_ref, pack_ref, local_ref, hat_ref, weight_ref, *refs
):
    heads, bits, far, count, near_count = sizes
    first_ref = refs[0]
    near = [None] + [(refs[1 + at], refs[1 + near_count + at]) for at in range(near_count)]
    refs = refs[2 * near_count + 1 :]
    out_refs = refs[:2]
    summed_ref, scale_ref, found_ref, prefix_ref = refs[2:6]
    nodes = refs[6:-1]
    normed_ref = refs[-1]
    rows = pack_ref.shape[0]
    key = hat_ref.shape[2]
    pack = pack_ref[...]
    gain = gain_ref[...]
    lane = lane_of(rows)
    all_heads = range(heads)
    uppers = [((place_ref[0] >> bit) & 1) == 1 for bit in range(far)]
    others = []
    for bit in range(far):
        if bit == 0:
            others.append([first_ref[head] for head in all_heads])
        else:
            others.append(
                [gather_node(head, bit - 1, 1 << (bit - 1), near, uppers) for head in all_heads]
            )
            for head in all_heads:
                nodes[bit - 1][head] = others[bit][head]
    eye_key = jnp.where(pair_ids(key)[0] == pair_ids(key)[1], 1.0, 0.0).astype(BF16)
    prefix = [eye_key for head in all_heads]
    found = []
    for bit in range(far):
        for head in all_heads:
            prefix_ref[head, bit] = prefix[head]
        moved = [mm(prefix[head], others[bit][head]) for head in all_heads]
        found.append([jnp.where(uppers[bit], m[:, key:], 0.0).astype(BF16) for m in moved])
        prefix = [
            jnp.where(uppers[bit], moved[head][:, :key].astype(BF16), prefix[head])
            for head in all_heads
        ]
    found = [jnp.concatenate([found[bit][head] for bit in range(far)], 1) for head in all_heads]
    reached = [mm(hat_ref[head], found[head]) for head in all_heads]
    scales = jnp.zeros((rows, LANES), F32)
    for head in all_heads:
        found_ref[head] = found[head]
        summed = local_ref[head]
        for bit in range(far):
            part = reached[head][:, bit * key : (bit + 1) * key]
            summed = summed + column(pack, (bits + 1 + bit) * heads + head) * part
        scale = lax.rsqrt(jnp.mean(summed * summed, -1, keepdims=True) + EPS)
        unit = summed * scale
        normed_ref[:, head * key : (head + 1) * key] = (unit * gain).astype(BF16)
        summed_ref[head] = unit
        scales = jnp.where(lane == head, scale, scales)
    scale_ref[...] = scales
    size = weight_ref.shape[1] // count
    for mask in range(count):
        dest = place_ref[1] ^ mask
        cols = pl.ds(pl.multiple_of(dest * size, size), size)
        out_refs[mask % 2][mask // 2] = jnp.dot(
            normed_ref[...], weight_ref[:, cols], preferred_element_type=F32
        ).astype(BF16)


def reach(place, arrays, first, near, bits, far, count):
    gain, pack, local_out, hat, weight = arrays
    heads, rows, key = hat.shape
    nodes = tuple(kept(first.shape, BF16) for bit in range(1, far))
    size = weight.shape[1] // count
    out_shape = (kept((count // 2, rows, size), BF16),) * 2 + (
        kept((heads, rows, key), F32),
        kept((rows, LANES), F32),
        kept((heads, key, far * key), BF16),
        kept((heads, far, key, key), BF16),
    ) + nodes
    mine, theirs = near
    got = local_call(
        functools.partial(reach_body, (heads, bits, far, count, len(mine))), "reach", 10, out_shape,
        [place], [*arrays, first, *mine, *theirs], [pltpu.VMEM((rows, heads * key), BF16)],
    )
    return got[:2], got[2:6], got[6:]


def return_body(
    sizes, place_ref, gain_ref, pack_ref, hat_ref, hat_t_ref, grad_ref, unit_ref, scale_ref,
    found_ref, prefix_ref, *refs
):
    heads, bits, far = sizes
    others = refs[:far]
    dhat_ref, dout_ref, dfar_ref = refs[far : far + 3]
    sends = refs[far + 3 :]
    rows = pack_ref.shape[0]
    lane = lane_of(rows)
    gain, scales = gain_ref[...], scale_ref[...]
    key = hat_t_ref.shape[1]
    pack = pack_ref[...]
    all_heads = range(heads)
    uppers = [((place_ref[0] >> bit) & 1) == 1 for bit in range(far)]
    reached = [mm(hat_ref[head], found_ref[head]) for head in all_heads]
    dfar = jnp.zeros((rows, LANES), F32)
    spread = []
    for head in all_heads:
        unit = unit_ref[head]
        pulled = grad_ref[:, head * key : (head + 1) * key] * gain
        mean = jnp.mean(pulled * unit, -1, keepdims=True)
        dout = column(scales, head) * (pulled - unit * mean)
        dout_ref[head] = dout
        parts = []
        for bit in range(far):
            col = (bits + 1 + bit) * heads + head
            parts.append((column(pack, col) * dout).astype(BF16))
            here = reached[head][:, bit * key : (bit + 1) * key]
            dfar = jnp.where(lane == col, row_sum(dout * here), dfar)
        spread.append(jnp.concatenate(parts, 1))
    dfar_ref[...] = dfar
    dfound = [mm(hat_t_ref[head], spread[head]) for head in all_heads]
    for head in all_heads:
        dhat_ref[head] = mm_nt(spread[head], found_ref[head])
    dprefix = [jnp.zeros((key, key), F32) for head in all_heads]
    for bit in reversed(range(far)):
        dfree = [
            jnp.where(uppers[bit], d[:, bit * key : (bit + 1) * key], 0.0) for d in dfound
        ]
        both = [
            jnp.concatenate([jnp.where(uppers[bit], dprefix[head], 0.0), dfree[head]], 1)
            for head in all_heads
        ]
        for head in all_heads:
            sent = dfree[head] if bit == far - 1 else both[head]
            sends[bit][head] = mm_tn(prefix_ref[head, bit], sent).astype(BF16)
        if bit > 0:
            moved = [mm_nt(both[head], others[bit][head]) for head in all_heads]
            dprefix = [
                jnp.where(uppers[bit], moved[head], dprefix[head]) for head in all_heads
            ]


def return_states(place, arrays, others, bits):
    heads, rows, key = arrays[2].shape
    far = len(others)
    sends = tuple(
        kept((heads, key, (1 if bit == far - 1 else 2) * key), BF16) for bit in range(far)
    )
    wide = kept((heads, rows, key), F32)
    got = local_call(
        functools.partial(return_body, (heads, bits, far)), "return_states", 8,
        (wide, wide, kept((rows, LANES), F32)) + sends, [place], [*arrays, *others],
    )
    return got[:3], got[3:]


def add_body(*refs):
    count = len(refs) // 3
    for at in range(count):
        left, right = refs[at][...].astype(F32), refs[count + at][...].astype(F32)
        refs[2 * count + at][...] = (left + right).astype(BF16)


def add_all(left, right):
    out_shape = [kept(value.shape, BF16) for value in left]
    return local_call(add_body, "add_all", 6, out_shape, [], [*left, *right])


def lower_pull(dlower, base, lower, beta, decay, strict, k_in):
    dlower = jnp.where(strict, dlower, 0.0)
    dbeta = row_sum(dlower * base.astype(F32))
    dgram = dlower * (beta * decay)
    dkey = mm(dgram, k_in) + mm_tn(dgram, k_in)
    return dbeta, beta * dbeta, col_sum(dlower * lower.astype(F32)), dkey


def pull_body(sizes, *refs):
    heads, levels, bits = sizes
    (qkv_ref, pack_ref, pack_t_ref, trans_ref, attn_ref, attn_t_ref, prod_t_ref, scores_ref,
     mix_ref, decay_ref, base_ref, lower_ref, dout_ref, dhat_ref) = refs[:14]
    dqkv_ref, dgrown_ref, dcol_ref, drow_ref = refs[14:]
    rows = pack_ref.shape[0]
    decay_col = levels * heads
    beta_col = decay_col + heads
    block_bit = BLOCK.bit_length() - 1
    pack = pack_ref[...]
    pack_t = pack_t_ref[...]
    row_id, col_id = pair_ids(rows)
    strict = row_id > col_id
    apart = row_id ^ col_id
    lane = lane_of(rows)
    all_heads = range(heads)
    dcol = jnp.zeros((rows, LANES), F32)
    dbeta_rows, dcum_rows, dattn_all = [], [], []
    for head in all_heads:
        high, low = split(dout_ref[head])
        v_in = qkv_ref[2, head].astype(BF16)
        dprod = mm_nt(high, v_in) + mm_nt(low, v_in)
        dqkv_ref[2, head] = mm(prod_t_ref[head], high)
        beta_row = pack_t[beta_col + head : beta_col + head + 1, :]
        growth = jnp.exp(column(pack, decay_col + head))
        attn0 = attn_ref[head].astype(F32)
        touched = dprod * (attn0 * beta_row)
        for level in range(bits + 1):
            if level == 0:
                here = (apart >> block_bit) == 0
            else:
                here = (apart >> (block_bit + level - 1)) == 1
            dcol = jnp.where(
                lane == level * heads + head, row_sum(jnp.where(here, touched, 0.0)), dcol
            )
        dattn = dprod * mix_ref[head].astype(F32) - mm_nt(dhat_ref[head], growth * qkv_ref[1, head])
        dbeta_rows.append(col_sum(dattn * attn0))
        dattn_all.append((dattn * beta_row).astype(BF16))
    dscore_all = [mm_nt(dattn_all[head], trans_ref[head]) for head in all_heads]
    moved_all = []
    for head in all_heads:
        both = jnp.concatenate(
            [dscore_all[head].astype(BF16), dhat_ref[head].astype(BF16)], 1
        )
        moved_all.append(mm(attn_t_ref[head], both))
    for head in all_heads:
        q_in, k_in = qkv_ref[0, head], qkv_ref[1, head]
        beta = column(pack, beta_col + head)
        growth = jnp.exp(column(pack, decay_col + head))
        dscore = dscore_all[head]
        decay = decay_ref[head].astype(F32)
        dprobs = dscore * decay
        shift = dscore * scores_ref[head].astype(F32)
        dgrown_ref[head] = -beta * moved_all[head][:, rows:]
        dbeta, dcum_col, dcum_row, dk_lower = lower_pull(
            -moved_all[head][:, :rows], base_ref[head], lower_ref[head], beta, decay, strict, k_in
        )
        dhat = dhat_ref[head]
        dqkv_ref[0, head] = growth * dhat + mm(dprobs, k_in)
        dqkv_ref[1, head] = mm_tn(dprobs, q_in) + dk_lower
        dcum_col = dcum_col + row_sum(shift) + growth * row_sum(q_in * dhat)
        dcum_rows.append(-dcum_row - col_sum(shift))
        dcol = jnp.where(lane == beta_col + head, dbeta, dcol)
        dcol = jnp.where(lane == decay_col + head, dcum_col, dcol)
    dcol_ref[...] = dcol
    drow_ref[...] = jnp.concatenate(dcum_rows + dbeta_rows, 0)


def pull_local(arrays, levels, bits):
    heads, rows, key = arrays[0].shape[1:]
    out_shape = (
        kept((3, heads, rows, key), F32),
        kept((heads, rows, key), F32),
        kept((rows, LANES), F32),
        kept((2 * heads, rows), F32),
    )
    return local_call(
        functools.partial(pull_body, (heads, levels, bits)), "pull_local", 12, out_shape, [], arrays
    )


def finish_body(sizes, place_ref, *refs):
    heads, levels, far, arrived_counts = sizes
    (qkv_ref, gate_ref, pack_ref, trans_ref, mixed_ref, decay_ref, base_ref, lower_ref,
     dqkv_ref, dgrown_ref, dcol_ref, drow_ref, dfar_ref, rates_ref) = refs[:14]
    others = refs[14 : 14 + far]
    refs = refs[14 + far :]
    arrived = []
    for found in arrived_counts:
        arrived.append(refs[:found])
        refs = refs[found:]
    dproj, dgate_ref = refs
    rows = pack_ref.shape[0]
    key = qkv_ref.shape[3]
    decay_col = levels * heads
    beta_col = decay_col + heads
    norm_col = beta_col + heads
    place = place_ref[0]
    all_heads = range(heads)
    uppers = [((place >> bit) & 1) == 1 for bit in range(far)]
    pack = pack_ref[...]
    row_id, col_id = pair_ids(rows)
    strict = row_id > col_id
    lane = lane_of(rows)
    last_row = lax.broadcasted_iota(jnp.int32, (rows, 1), 0) == rows - 1
    eye_key = (pair_ids(key)[0] == pair_ids(key)[1]).astype(F32)
    dpair = [jnp.zeros((key, 2 * key), F32) for head in all_heads]
    for bit in reversed(range(far)):
        for head in all_heads:
            got = arrived[bit][0][head].astype(F32)
            for more in arrived[bit][1:]:
                got = got + more[head].astype(F32)
            other = others[bit][head]
            if bit == far - 1:
                got = jnp.concatenate([jnp.zeros((key, key), F32), got], 1)
                dpair[head] = jnp.where(uppers[bit], 0.0, got)
            else:
                as_low = mm_tn(other[:, :key], dpair[head]) + got
                as_high = mm_nt(dpair[head], other)
                as_high = jnp.concatenate([as_high, dpair[head][:, key:]], 1)
                dpair[head] = jnp.where(uppers[bit], as_high, as_low)
    moved_all, dmixed_all = [], []
    for head in all_heads:
        beta = column(pack, beta_col + head)
        growth = jnp.exp(column(pack, decay_col + head))
        both = jnp.concatenate([-growth * qkv_ref[1, head], qkv_ref[2, head]], 1)
        dmixed_all.append(mm_nt(both, dpair[head]))
        moved_all.append(mm(beta * mixed_ref[head].astype(F32), dpair[head]))
    dtail_all = [
        mm(trans_ref[head], column(pack, beta_col + head) * dmixed_all[head])
        for head in all_heads
    ]
    dlower_all = [-mm_nt(mixed_ref[head], dtail_all[head]) for head in all_heads]
    dcol = jnp.where(lane < decay_col, dcol_ref[...] + dfar_ref[...], dcol_ref[...])
    dcum_rows = []
    for head in all_heads:
        q_in, k_in = qkv_ref[0, head], qkv_ref[1, head]
        beta = column(pack, beta_col + head)
        cum_col = column(pack, decay_col + head)
        growth = jnp.exp(cum_col)
        last = cum_col[rows - 1 : rows, :]
        tail = jnp.exp(last - cum_col)
        dgrown = dgrown_ref[head] - moved_all[head][:, :key]
        dv = dqkv_ref[2, head] + moved_all[head][:, key:]
        dbeta_more = row_sum(mixed_ref[head].astype(F32) * dmixed_all[head])
        dtail = dtail_all[head]
        dbeta, dcum_col, dcum_row, dk_lower = lower_pull(
            dlower_all[head], base_ref[head], lower_ref[head], beta, decay_ref[head].astype(F32),
            strict, k_in
        )
        dcum_rows.append(-dcum_row)
        tail_pull = tail * row_sum(k_in * dtail)
        trace = col_sum(row_sum(dpair[head][:, :key] * eye_key))
        at_last = col_sum(tail_pull) + jnp.exp(last) * trace
        dcum_col = dcum_col + growth * row_sum(k_in * dgrown) - tail_pull
        dcum_col = dcum_col + jnp.where(last_row, at_last, 0.0)
        dk = dqkv_ref[1, head] + dk_lower + growth * dgrown + tail * dtail
        dq = dqkv_ref[0, head]
        dcol = dcol + jnp.where(lane == beta_col + head, dbeta + dbeta_more, 0.0)
        dcol = dcol + jnp.where(lane == decay_col + head, dcum_col, 0.0)
        for part, unit, dunit in ((0, q_in, dq), (1, k_in, dk)):
            scale = column(pack, norm_col + part * heads + head)
            back = scale * (dunit - unit * row_sum(unit * dunit))
            col = (part * heads + head) * key
            dproj[:, col : col + key] = back.astype(BF16)
        col = (2 * heads + head) * key
        dproj[:, col : col + key] = dv.astype(BF16)
    drow = drow_ref[...]
    drow = drow + jnp.concatenate(dcum_rows + [jnp.zeros((heads, rows), F32)], 0)
    drow = jnp.concatenate(
        [jnp.zeros((decay_col, rows), F32), drow,
         jnp.zeros((LANES - norm_col, rows), F32)], 0
    )
    dcol = dcol + drow.T
    rate, bias = rates_ref[0:1, :], rates_ref[1:2, :]
    switch = jax.nn.sigmoid(gate_ref[...] + bias)
    dlog = mm_ones((row_id <= col_id).astype(F32), dcol)
    slope = switch * (1.0 - switch)
    dgate = jnp.where(
        lane < decay_col,
        dcol * switch,
        jnp.where(lane < beta_col, -rate * dlog * slope, dcol * slope),
    )
    dgate_ref[...] = jnp.where(lane < norm_col, dgate, 0.0).astype(BF16)


def finish(place, arrays, others, arrived, levels):
    heads, rows, key = arrays[0].shape[1:]
    counts = tuple(len(group) for group in arrived)
    flat = [value for group in arrived for value in group]
    return local_call(
        functools.partial(finish_body, (heads, levels, len(others), counts)), "finish", 10,
        [kept((rows, 3 * heads * key), BF16), kept((rows, LANES), BF16)],
        [place], [*arrays, *others, *flat],
    )


def tokens_body(count, place_ref, dproj_ref, dgate_ref, wr_ref, small_ref, *refs):
    keep_ref, send_ref = refs[:2]
    direct_refs = refs[2:]
    size = wr_ref.shape[0] // count
    half = size // 2
    for mask in range(count):
        dest = place_ref[1] ^ mask
        span = pl.ds(pl.multiple_of(dest * size, size), size)
        part = mm_nt(dproj_ref[...], wr_ref[span, :]) + mm(dgate_ref[...], small_ref[:, span])
        direct_refs[mask][...] = part[:, :half].astype(BF16)
        target = send_ref if mask % 2 else keep_ref
        target[mask // 2] = part[:, half:].astype(BF16)


def pull_tokens(place, dproj, dgate, wr, small_t, count):
    rows = dproj.shape[0]
    half = wr.shape[0] // count // 2
    out_shape = [kept((count // 2, rows, half), BF16)] * 2 + [kept((rows, half), BF16)] * count
    got = local_call(
        functools.partial(tokens_body, count), "pull_tokens", 8, out_shape,
        [place], [dproj, dgate, wr, small_t],
    )
    return got[0], got[1], got[2:]


def swap(value, axis, mask):
    size = lax.axis_size(axis)
    return lax.ppermute(value, axis, [(at, at ^ mask) for at in range(size)])


def far_first(count):
    return sorted(range(1, count), key=lambda mask: mask < count // 2)


def halve_body(own_ref, got_ref, keep_ref, send_ref):
    for at in range(own_ref.shape[0]):
        total = own_ref[at].astype(F32) + got_ref[at].astype(F32)
        target = send_ref if at % 2 else keep_ref
        target[at // 2] = total.astype(target.dtype)


def halving(keep, send, axis, tied):
    mask = 1
    while keep.shape[0] > 1:
        got = swap(send, axis, mask)
        half = (keep.shape[0] // 2,) + keep.shape[1:]
        keep, send = local_call(
            halve_body, "halve", 6, [kept(half, F32), kept(half, BF16)], [], [keep, got]
        )
        send, tied = lax.optimization_barrier((send, tied))
        mask *= 2
    return keep, swap(send, axis, mask), tied


def sum_body(count, *refs):
    keep_ref, got_ref = refs[:2]
    out_ref = refs[-1]
    total = keep_ref[0].astype(F32) + got_ref[0].astype(F32)
    if count == 0:
        out_ref[...] = total.astype(BF16)
        return
    half = out_ref.shape[1] // 2
    out_ref[:, half:] = total.astype(BF16)
    total = refs[2][...].astype(F32)
    for ref in refs[3:-1]:
        total = total + ref[...].astype(F32)
    out_ref[:, :half] = total.astype(BF16)


def head_sum(keep, last, direct, got):
    rows, cols = keep.shape[1:]
    out = jax.ShapeDtypeStruct((rows, cols * (2 if direct else 1)), BF16)
    return local_call(
        functools.partial(sum_body, len(direct)), "head_sum", 6, [out], [],
        [keep, last, *direct[:1], *got],
    )[0]


def on_device(tokens, qkv_weight, small_weight, head_param, norm_gain, out_weight, grad_out):
    rows, width = tokens.shape
    heads, key = qkv_weight.shape[2:]
    levels = small_weight.shape[2] - 2
    bits = (rows // BLOCK).bit_length() - 1
    size = lax.axis_size("ctx")
    far = size.bit_length() - 1
    count = lax.axis_size("head")
    place = jnp.stack([lax.axis_index("ctx"), lax.axis_index("head")]).astype(jnp.int32)
    flat_w = qkv_weight.reshape(width * 3 * heads, key)
    small = jnp.transpose(small_weight, (2, 1, 0))
    rates = head_param.T
    flat_out = out_weight.reshape(heads * key, width)
    gain = norm_gain.reshape(1, key)

    (wr, query_w, value_w, small_t, qkv, gate, pack, pack_t, trans, mixed_t, decay, base, lower, rates_row,
     pair) = project(
        place, tokens, flat_w, small, rates, heads, levels
    )
    first = swap(pair, "ctx", 1)
    node = join_half(place, pair, first)
    mine = [swap(node, "ctx", 2 * at) for at in range(1, size // 2)]
    (attn, attn_t, prod_t, scores, mix, mixed, local_out, hat, hat_t, grad_normed, qkv, pack,
     wr) = local_part(
        [qkv, pack, pack_t, trans, mixed_t, decay, grad_out, flat_out, query_w, value_w, tokens],
        wr, levels, bits,
    )
    mine, local_out, grad_normed = lax.optimization_barrier((mine, local_out, grad_normed))
    theirs = [swap(value, "ctx", 1) for value in mine]
    out_parts, (unit, scale, found, prefix), nodes = reach(
        place, [gain, pack, local_out, hat, flat_out], first, (mine, theirs), bits, far, count
    )
    others = [first, *nodes]
    (dhat, dout, dfar), sends = return_states(
        place, [gain, pack, hat, hat_t, grad_normed, unit, scale, found, prefix], others, bits
    )
    got = [swap(value, "ctx", 1) for value in sends]
    arrived = [[got[0]]]
    sums = add_all(sends[1:], got[1:])
    for bit in range(1, far):
        half = 1 << (bit - 1)
        arrived.append([swap(sums[bit - 1], "ctx", 2 * at) for at in range(half, 2 * half)])
    dqkv, dgrown, dcol, drow = pull_local(
        [qkv, pack, pack_t, trans, attn, attn_t, prod_t, scores, mix, decay, base, lower, dout,
         dhat],
        levels, bits,
    )
    keep_out, last_out, dcol = halving(*out_parts, "head", dcol)
    arrays = [qkv, gate, pack, trans, mixed, decay, base, lower, dqkv, dgrown, dcol, drow, dfar,
              rates_row]
    dproj, dgate = finish(place, arrays, others, arrived, levels)
    keep, send, direct = pull_tokens(place, dproj, dgate, wr, small_t, count)
    direct, last_out = lax.optimization_barrier((direct, last_out))
    keep, last, late = halving(keep, send, "head", direct[1])
    direct = [direct[0], late, *direct[2:]]
    got = [swap(direct[mask], "head", mask) for mask in far_first(count)]
    return head_sum(keep_out, last_out, [], []), head_sum(keep, last, direct, got)


def solution(mesh):
    placed = (
        P("ctx", None),
        P(None, None, "head", None),
        P(None, "head", None),
        P("head", None),
        P(),
        P("head", None, None),
        P("ctx", None),
    )
    return jax.shard_map(
        on_device,
        mesh=mesh,
        in_specs=placed,
        out_specs=(P("ctx", "head"), P("ctx", "head")),
        check_vma=False,
    )
```

```python
import functools

import jax
import jax.numpy as jnp
from jax import lax
from jax.experimental import pallas as pl
from jax.experimental.pallas import tpu as pltpu
from jax.sharding import PartitionSpec as P

BLOCK = 64
LANES = 128
EPS = 1e-06
MIB = 1024 * 1024
F32 = jnp.float32
BF16 = jnp.bfloat16
WHOLE = pl.BlockSpec(memory_space=pltpu.VMEM)
SCALARS = pl.BlockSpec(memory_space=pltpu.SMEM)
HBM = pl.BlockSpec(memory_space=pltpu.HBM)


def contract(left, right, dim_left, dim_right):
    return lax.dot_general(
        left.astype(BF16),
        right.astype(BF16),
        (((dim_left,), (dim_right,)), ((), ())),
        preferred_element_type=F32,
    )


def mm(left, right):
    return contract(left, right, 1, 0)


def mm_nt(left, right):
    return contract(left, right, 1, 1)


def mm_tn(left, right):
    return contract(left, right, 0, 0)


def split(values):
    high = values.astype(BF16)
    return high, (values - high.astype(F32)).astype(BF16)


def mm_nt_fine(left, right):
    left_high, left_low = split(left)
    right_high, right_low = split(right)
    return mm_nt(left_high, right_high) + (mm_nt(left_low, right_high) + mm_nt(left_high, right_low))


def mm_full(left, right):
    return jnp.dot(left, right, precision=lax.Precision.HIGHEST, preferred_element_type=F32)


def mm_ones(ones, values):
    high = values.astype(BF16)
    rest = values - high.astype(F32)
    middle = rest.astype(BF16)
    low = (rest - middle.astype(F32)).astype(BF16)
    return mm(ones, high) + (mm(ones, middle) + mm(ones, low))


def pair_ids(count):
    row_id = lax.broadcasted_iota(jnp.int32, (count, count), 0)
    col_id = lax.broadcasted_iota(jnp.int32, (count, count), 1)
    return row_id, col_id


def row_sum(values):
    return jnp.sum(values, 1, keepdims=True)


def col_sum(values):
    return jnp.sum(values, 0, keepdims=True)


def lane_of(rows):
    return lax.broadcasted_iota(jnp.int32, (rows, LANES), 1)


def decay_of(pack, pack_t, col, inclusive):
    spread = pack[:, col : col + 1] - pack_t[col : col + 1, :]
    return jnp.where(inclusive, jnp.exp(jnp.minimum(spread, 0.0)), 0.0)


def kept(shape, dtype):
    return pltpu.VMEM(shape, dtype)


def stored(shape, dtype):
    return pltpu.HBM(shape, dtype)


def pin(values, space):
    return [pltpu.with_memory_space_constraint(value, space) for value in values]


def local_call(
    body, name, limit, out_shape, scalars, arrays, scratch=(), remote=(), out_specs=None, alias=None
):
    return pl.pallas_call(
        body,
        out_shape=tuple(out_shape),
        in_specs=[SCALARS] * len(scalars)
        + [WHOLE] * len(arrays)
        + [HBM] * len(remote),
        out_specs=tuple(out_specs or [WHOLE] * len(out_shape)),
        scratch_shapes=list(scratch),
        input_output_aliases=alias or {},
        compiler_params=pltpu.CompilerParams(vmem_limit_bytes=limit * MIB),
        name=name,
    )(*scalars, *pin(arrays, pltpu.VMEM), *pin(remote, pltpu.HBM))


def column(pack, at):
    return pack[:, at : at + 1]


def level_mix(pack, head, heads, bits, apart):
    block_bit = BLOCK.bit_length() - 1
    mixed = jnp.broadcast_to(column(pack, head), apart.shape)
    for level in range(1, bits + 1):
        here = (apart >> (block_bit + level - 1)) >= 1
        mixed = jnp.where(here, column(pack, level * heads + head), mixed)
    return mixed


def head_rows(hp_ref, heads, decay_col, beta_col):
    lane_row = lane_of(1)
    rate = jnp.zeros((1, LANES), F32)
    bias = jnp.zeros((1, LANES), F32)
    for head in range(heads):
        rate = jnp.where(lane_row == decay_col + head, hp_ref[0:1, head : head + 1], rate)
        bias = jnp.where(lane_row == beta_col + head, hp_ref[1:2, head : head + 1], bias)
    return rate, bias


def invert(lower_all, eye, apart, rows):
    trans_all = [(eye - jnp.where(apart == 1, lower, 0.0)).astype(BF16) for lower in lower_all]
    for bit in range(1, rows.bit_length() - 1):
        here = (apart >> bit) == 1
        edge = [jnp.where(here, lower, 0.0) for lower in lower_all]
        half = [mm(trans, part) for trans, part in zip(trans_all, edge)]
        trans_all = [
            trans - mm(part, trans).astype(BF16) for trans, part in zip(trans_all, half)
        ]
    rest_all = []
    for trans, lower in zip(trans_all, lower_all):
        high, low = split(lower)
        rest_all.append(eye - trans.astype(F32) - mm(high, trans) - mm(low, trans))
    return [
        (trans.astype(F32) + mm(trans, rest)).astype(BF16)
        for trans, rest in zip(trans_all, rest_all)
    ]


def project_body(sizes, place_ref, hp_hbm, tokens_hbm, w_hbm, small_hbm, *refs):
    heads, levels, chunks = sizes
    (wr_hbm, query_ref, value_ref, small_ref, qkv_ref, gate_ref, pack_ref, pack_t_ref, trans_ref, mixed_t_ref,
     decay_ref, base_ref, lower_ref, rates_ref, pair_ref) = refs[:15]
    tokens, wide_in, wide_even, wide_odd, key_ref, small_in, small_wide, acc, hp_ref = refs[15:24]
    sems, in_sems, out_sems = refs[24:]
    laid = (query_ref, key_ref, value_ref)
    rows, width = tokens.shape
    depth = width // chunks
    cols = 3 * heads
    fetch_tokens = pltpu.make_async_copy(tokens_hbm, tokens, sems.at[0])
    fetch_small = pltpu.make_async_copy(small_hbm, small_in, sems.at[1])
    fetch_rates = pltpu.make_async_copy(hp_hbm, hp_ref, sems.at[2])
    fetches, keeps = [], []
    for chunk in range(chunks):
        span = pl.ds(chunk * depth * cols, depth * cols)
        fetches.append(
            pltpu.make_async_copy(w_hbm.at[span, :], wide_in.at[span, :], in_sems.at[chunk])
        )
        span = pl.ds(chunk * depth, depth)
        block = wr_hbm.at[span, pl.ds(heads * LANES, heads * LANES)]
        keeps.append(pltpu.make_async_copy(key_ref.at[span, :], block, out_sems.at[chunk]))
    fetches[0].start()
    fetches[1].start(priority=1)
    fetch_tokens.start()
    fetch_small.start(priority=1)
    fetch_rates.start(priority=1)
    for chunk in range(2, chunks):
        fetches[chunk].start(priority=chunk % 2)

    def relay(chunk):
        fetches[chunk].wait()
        wide = wide_odd if chunk % 2 else wide_even
        at = chunk * depth
        wide[...] = wide_in[at * cols : (at + depth) * cols, :].astype(F32)
        for col in range(cols):
            value = wide[pl.ds(col, depth, stride=cols), :].astype(BF16)
            lanes = slice(col % heads * LANES, (col % heads + 1) * LANES)
            laid[col // heads][at : at + depth, lanes] = value

    def multiply(first, last):
        for part in (1, 2):
            span = slice((part * heads) * LANES, (part + 1) * heads * LANES)
            own = jnp.dot(
                tokens[:, first * depth : last * depth],
                laid[part][first * depth : last * depth, :],
                preferred_element_type=F32,
            )
            if first == 0:
                acc[:, span] = own
            else:
                acc[:, span] += own

    def lay(first, last):
        for chunk in range(first, last, 2):
            relay(chunk)
            relay(chunk + 1)
            if chunk == 0:
                fetch_tokens.wait()
            multiply(chunk, chunk + 2)

    decay_col = levels * heads
    beta_col = decay_col + heads
    norm_col = beta_col + heads
    lane = lane_of(rows)
    row_id, col_id = pair_ids(rows)
    inclusive = row_id >= col_id
    strict = row_id > col_id
    apart = row_id ^ col_id
    eye = (row_id == col_id).astype(F32)
    lay(0, chunks)
    for chunk, keep in enumerate(keeps):
        keep.start(priority=chunk % 2)
    fetch_small.wait()
    small_rows = small_in.shape[0] * heads
    for level in range(small_in.shape[0]):
        small_wide[level * heads : (level + 1) * heads, :] = small_in[level].astype(F32)
    small_wide[small_rows:, :] = jnp.zeros((LANES - small_rows, width), F32)
    small_ref[...] = small_wide[...].astype(BF16)
    fetch_rates.wait()
    rate, bias = head_rows(hp_ref, heads, decay_col, beta_col)
    rates_ref[0:1, :] = rate
    rates_ref[1:2, :] = bias
    gate = mm_nt(tokens[...], small_ref[...])
    gate_ref[...] = gate
    switch = jax.nn.sigmoid(gate + bias)
    lam = jnp.maximum(gate, 0.0) + jnp.log1p(jnp.exp(-jnp.abs(gate)))
    cum = mm_full(inclusive.astype(F32), -rate * switch)
    pack = jnp.where(lane < decay_col, lam, jnp.where(lane < beta_col, cum, switch))
    pack_t = pack.T
    pack_t_ref[...] = pack_t

    def unit_of(part, head):
        col = (part * heads + head) * LANES
        raw = acc[:, col : col + LANES]
        scale = lax.rsqrt(row_sum(raw * raw) + EPS)
        qkv_ref[part, head] = raw * scale
        return raw * scale, jnp.where(lane == norm_col + part * heads + head, scale, 0.0)

    scales = jnp.zeros((rows, LANES), F32)
    k_all, lower_all = [], []
    for head in range(heads):
        unit, scale = unit_of(1, head)
        k_all.append(unit)
        scales = scales + scale
        decay = decay_of(pack, pack_t, decay_col + head, inclusive)
        decay_ref[head] = decay.astype(BF16)
        base = jnp.where(strict, decay * mm_nt(unit, unit), 0.0)
        base_ref[head] = base.astype(BF16)
        lower = column(pack, beta_col + head) * base
        lower_ref[head] = lower.astype(BF16)
        lower_all.append(lower)

    trans_all = invert(lower_all, eye, apart, rows)
    mixed_all = []
    for head in range(heads):
        trans_ref[head] = trans_all[head]
        cum_row = pack_t[decay_col + head : decay_col + head + 1, :]
        tail_t = k_all[head].T * jnp.exp(cum_row[:, rows - 1 :] - cum_row)
        mixed_all.append(mm(tail_t, trans_all[head]).astype(BF16))
    eye_key = eye[:LANES, :LANES]
    for head in range(heads):
        mixed_t_ref[head] = mixed_all[head]
        col = (2 * heads + head) * LANES
        v_in = acc[:, col : col + LANES]
        qkv_ref[2, head] = v_in
        cum_col = column(pack, decay_col + head)
        beta = column(pack, beta_col + head)
        grown = (beta * jnp.exp(cum_col)) * k_all[head]
        both = jnp.concatenate([-grown, beta * v_in], 1)
        pair = mm(mixed_all[head], both)
        last = jnp.exp(cum_col[rows - 1 : rows, :])
        pair_ref[head, :, :LANES] = (last * eye_key + pair[:, :LANES]).astype(BF16)
        pair_ref[head, :, LANES:] = pair[:, LANES:].astype(BF16)
    pack_ref[...] = jnp.where(lane < norm_col, pack, scales)
    for keep in keeps:
        keep.wait()


def project(place, tokens, flat_w, small, head_param, heads, levels):
    rows, width = tokens.shape
    chunks = 16
    cols = 3 * heads
    key = flat_w.shape[1]
    square = (heads, rows, rows)
    out_shape = (
        stored((width, cols * key), BF16),
        kept((width, heads * key), BF16),
        kept((width, heads * key), BF16),
        kept((LANES, width), BF16),
        kept((3, heads, rows, key), F32),
        kept((rows, LANES), F32),
        kept((rows, LANES), F32),
        kept((LANES, rows), F32),
        kept(square, BF16),
        kept((heads, key, rows), BF16),
        kept(square, BF16),
        kept(square, BF16),
        kept(square, BF16),
        kept((2, LANES), F32),
        kept((heads, key, 2 * key), BF16),
    )
    scratch = [
        pltpu.VMEM(tokens.shape, BF16),
        pltpu.VMEM(flat_w.shape, BF16),
        pltpu.VMEM((width // chunks * cols, key), F32),
        pltpu.VMEM((width // chunks * cols, key), F32),
        pltpu.VMEM((width, heads * key), BF16),
        pltpu.VMEM(small.shape, BF16),
        pltpu.VMEM((LANES, width), F32),
        pltpu.VMEM((rows, cols * key), F32),
        pltpu.VMEM(head_param.shape, F32),
        pltpu.SemaphoreType.DMA((3,)),
        pltpu.SemaphoreType.DMA((chunks,)),
        pltpu.SemaphoreType.DMA((chunks,)),
    ]
    return local_call(
        functools.partial(project_body, (heads, levels, chunks)), "project", 36, out_shape,
        [place], [], scratch, [head_param, tokens, flat_w, small], [HBM] + [WHOLE] * 14,
    )


def local_body(
    sizes, qkv_ref, pack_ref, pack_t_ref, trans_ref, mixed_t_ref, decay_ref, grad_ref, weight_ref,
    query_ref, value_ref, tokens_ref, wr_in, *outs
):
    heads, levels, bits = sizes
    (attn_ref, attn_t_ref, prod_t_ref, scores_ref, mix_ref, mixed_ref, local_ref, hat_ref,
     hat_t_ref, grad_normed_ref, qkv_out, pack_out, wr_hbm, sems) = outs
    del wr_in
    half, size = query_ref.shape[0] // 2, query_ref.shape[1]
    keeps = []
    for at in range(4):
        span = pl.ds(at % 2 * half, half)
        here, col = ((query_ref, 0), (value_ref, 2 * size))[at // 2]
        there = wr_hbm.at[span, pl.ds(col, size)]
        keeps.append(pltpu.make_async_copy(here.at[span, :], there, sems.at[at]))
        keeps[at].start()
    rows = pack_ref.shape[0]
    decay_col = levels * heads
    beta_col = decay_col + heads
    norm_col = beta_col + heads
    lane = lane_of(rows)
    raw_all = jnp.dot(tokens_ref[...], query_ref[...], preferred_element_type=F32)
    pack = pack_ref[...]
    q_all = []
    for head in range(heads):
        raw = raw_all[:, head * LANES : (head + 1) * LANES]
        scale = lax.rsqrt(row_sum(raw * raw) + EPS)
        q_all.append(raw * scale)
        qkv_out[0, head] = q_all[head]
        pack = jnp.where(lane == norm_col + head, scale, pack)
    pack_out[...] = pack
    grad_normed_ref[...] = mm_nt(grad_ref[...], weight_ref[...])
    pack_t = pack_t_ref[...]
    row_id, col_id = pair_ids(rows)
    apart = row_id ^ col_id
    for head in range(heads):
        scores = mm_nt_fine(q_all[head], qkv_ref[1, head]) * decay_ref[head].astype(F32)
        scores_ref[head] = scores.astype(BF16)
        mix_ref[head] = level_mix(pack, head, heads, bits, apart).astype(BF16)
        mixed_ref[head] = mixed_t_ref[head].astype(F32).T.astype(BF16)
    for head in range(heads):
        attn = mm(scores_ref[head], trans_ref[head])
        attn_ref[head] = attn.astype(BF16)
        attn_t_ref[head] = attn.T.astype(BF16)
        attn = attn * pack_t[beta_col + head : beta_col + head + 1, :]
        prod = attn * mix_ref[head].astype(F32)
        prod_t_ref[head] = prod.T.astype(BF16)
        growth = jnp.exp(column(pack, decay_col + head))
        local_ref[head] = mm(prod, qkv_ref[2, head])
        hat = growth * q_all[head] - mm(attn, growth * qkv_ref[1, head])
        hat_ref[head] = hat.astype(BF16)
        hat_t_ref[head] = hat.T.astype(BF16)
    for keep in keeps:
        keep.wait()


def local_part(arrays, wr, levels, bits):
    heads, rows, key = arrays[0].shape[1:]
    square = (heads, rows, rows)
    out_shape = (
        kept(square, BF16),
        kept(square, BF16),
        kept(square, BF16),
        kept(square, BF16),
        kept(square, BF16),
        kept((heads, rows, key), BF16),
        kept((heads, rows, key), F32),
        kept((heads, rows, key), BF16),
        kept((heads, key, rows), BF16),
        kept((rows, heads * key), F32),
        kept(arrays[0].shape, F32),
        kept(arrays[1].shape, F32),
        stored(wr.shape, BF16),
    )
    return local_call(
        functools.partial(local_body, (heads, levels, bits)), "local_part", 10, out_shape,
        [], arrays, [pltpu.SemaphoreType.DMA((4,))], [wr], [WHOLE] * 12 + [HBM],
        {0: 10, 1: 11, len(arrays): 12},
    )


def join_pair(upper, own, other):
    key = own.shape[0]
    low = jnp.where(upper, other, own)
    high = jnp.where(upper, own, other)
    moved = mm(high[:, :key], low)
    late = jnp.concatenate([jnp.zeros((key, key), F32), high[:, key:].astype(F32)], 1)
    return (moved + late).astype(BF16)


def join_body(place_ref, own_ref, other_ref, out_ref):
    half = out_ref.shape[0]
    upper = (place_ref[0] & 1) == 1
    for slot in range(half):
        head = (place_ref[0] & 1) * half + slot
        out_ref[slot] = join_pair(upper, own_ref[head], other_ref[head])


def join_half(place, own, other):
    half = (own.shape[0] // 2,) + own.shape[1:]
    return local_call(join_body, "join_half", 6, [kept(half, BF16)], [place], [own, other])[0]


def gather_node(head, bit, first, near, uppers):
    if bit == 0:
        mine, theirs = near[first]
        half = mine.shape[0]
        here = uppers[0] if head >= half else jnp.logical_not(uppers[0])
        return jnp.where(here, mine[head % half], theirs[head % half])
    own = gather_node(head, bit - 1, first, near, uppers)
    other = gather_node(head, bit - 1, first ^ (1 << (bit - 1)), near, uppers)
    return join_pair(uppers[bit], own, other)


def reach_body(
    sizes, place_ref, gain_ref, pack_ref, local_ref, hat_ref, weight_ref, *refs
):
    heads, bits, far, count, near_count = sizes
    first_ref = refs[0]
    near = [None] + [(refs[1 + at], refs[1 + near_count + at]) for at in range(near_count)]
    refs = refs[2 * near_count + 1 :]
    out_refs = refs[:2]
    summed_ref, scale_ref, found_ref, prefix_ref = refs[2:6]
    nodes = refs[6:-1]
    normed_ref = refs[-1]
    rows = pack_ref.shape[0]
    key = hat_ref.shape[2]
    pack = pack_ref[...]
    gain = gain_ref[...]
    lane = lane_of(rows)
    all_heads = range(heads)
    uppers = [((place_ref[0] >> bit) & 1) == 1 for bit in range(far)]
    others = []
    for bit in range(far):
        if bit == 0:
            others.append([first_ref[head] for head in all_heads])
        else:
            others.append(
                [gather_node(head, bit - 1, 1 << (bit - 1), near, uppers) for head in all_heads]
            )
            for head in all_heads:
                nodes[bit - 1][head] = others[bit][head]
    eye_key = jnp.where(pair_ids(key)[0] == pair_ids(key)[1], 1.0, 0.0).astype(BF16)
    prefix = [eye_key for head in all_heads]
    found = []
    for bit in range(far):
        for head in all_heads:
            prefix_ref[head, bit] = prefix[head]
        moved = [mm(prefix[head], others[bit][head]) for head in all_heads]
        found.append([jnp.where(uppers[bit], m[:, key:], 0.0).astype(BF16) for m in moved])
        prefix = [
            jnp.where(uppers[bit], moved[head][:, :key].astype(BF16), prefix[head])
            for head in all_heads
        ]
    found = [jnp.concatenate([found[bit][head] for bit in range(far)], 1) for head in all_heads]
    reached = [mm(hat_ref[head], found[head]) for head in all_heads]
    scales = jnp.zeros((rows, LANES), F32)
    for head in all_heads:
        found_ref[head] = found[head]
        summed = local_ref[head]
        for bit in range(far):
            part = reached[head][:, bit * key : (bit + 1) * key]
            summed = summed + column(pack, (bits + 1 + bit) * heads + head) * part
        scale = lax.rsqrt(jnp.mean(summed * summed, -1, keepdims=True) + EPS)
        unit = summed * scale
        normed_ref[:, head * key : (head + 1) * key] = (unit * gain).astype(BF16)
        summed_ref[head] = unit
        scales = jnp.where(lane == head, scale, scales)
    scale_ref[...] = scales
    size = weight_ref.shape[1] // count
    for mask in range(count):
        dest = place_ref[1] ^ mask
        cols = pl.ds(pl.multiple_of(dest * size, size), size)
        out_refs[mask % 2][mask // 2] = jnp.dot(
            normed_ref[...], weight_ref[:, cols], preferred_element_type=F32
        ).astype(BF16)


def reach(place, arrays, first, near, bits, far, count):
    gain, pack, local_out, hat, weight = arrays
    heads, rows, key = hat.shape
    nodes = tuple(kept(first.shape, BF16) for bit in range(1, far))
    size = weight.shape[1] // count
    out_shape = (kept((count // 2, rows, size), BF16),) * 2 + (
        kept((heads, rows, key), F32),
        kept((rows, LANES), F32),
        kept((heads, key, far * key), BF16),
        kept((heads, far, key, key), BF16),
    ) + nodes
    mine, theirs = near
    got = local_call(
        functools.partial(reach_body, (heads, bits, far, count, len(mine))), "reach", 10, out_shape,
        [place], [*arrays, first, *mine, *theirs], [pltpu.VMEM((rows, heads * key), BF16)],
    )
    return got[:2], got[2:6], got[6:]


def return_body(
    sizes, place_ref, gain_ref, pack_ref, hat_ref, hat_t_ref, grad_ref, unit_ref, scale_ref,
    found_ref, prefix_ref, *refs
):
    heads, bits, far = sizes
    others = refs[:far]
    dhat_ref, dout_ref, dfar_ref = refs[far : far + 3]
    sends = refs[far + 3 :]
    rows = pack_ref.shape[0]
    lane = lane_of(rows)
    gain, scales = gain_ref[...], scale_ref[...]
    key = hat_t_ref.shape[1]
    pack = pack_ref[...]
    all_heads = range(heads)
    uppers = [((place_ref[0] >> bit) & 1) == 1 for bit in range(far)]
    reached = [mm(hat_ref[head], found_ref[head]) for head in all_heads]
    dfar = jnp.zeros((rows, LANES), F32)
    spread = []
    for head in all_heads:
        unit = unit_ref[head]
        pulled = grad_ref[:, head * key : (head + 1) * key] * gain
        mean = jnp.mean(pulled * unit, -1, keepdims=True)
        dout = column(scales, head) * (pulled - unit * mean)
        dout_ref[head] = dout
        parts = []
        for bit in range(far):
            col = (bits + 1 + bit) * heads + head
            parts.append((column(pack, col) * dout).astype(BF16))
            here = reached[head][:, bit * key : (bit + 1) * key]
            dfar = jnp.where(lane == col, row_sum(dout * here), dfar)
        spread.append(jnp.concatenate(parts, 1))
    dfar_ref[...] = dfar
    dfound = [mm(hat_t_ref[head], spread[head]) for head in all_heads]
    for head in all_heads:
        dhat_ref[head] = mm_nt(spread[head], found_ref[head])
    dprefix = [jnp.zeros((key, key), F32) for head in all_heads]
    for bit in reversed(range(far)):
        dfree = [
            jnp.where(uppers[bit], d[:, bit * key : (bit + 1) * key], 0.0) for d in dfound
        ]
        both = [
            jnp.concatenate([jnp.where(uppers[bit], dprefix[head], 0.0), dfree[head]], 1)
            for head in all_heads
        ]
        for head in all_heads:
            sent = dfree[head] if bit == far - 1 else both[head]
            sends[bit][head] = mm_tn(prefix_ref[head, bit], sent).astype(BF16)
        if bit > 0:
            moved = [mm_nt(both[head], others[bit][head]) for head in all_heads]
            dprefix = [
                jnp.where(uppers[bit], moved[head], dprefix[head]) for head in all_heads
            ]


def return_states(place, arrays, others, bits):
    heads, rows, key = arrays[2].shape
    far = len(others)
    sends = tuple(
        kept((heads, key, (1 if bit == far - 1 else 2) * key), BF16) for bit in range(far)
    )
    wide = kept((heads, rows, key), F32)
    got = local_call(
        functools.partial(return_body, (heads, bits, far)), "return_states", 8,
        (wide, wide, kept((rows, LANES), F32)) + sends, [place], [*arrays, *others],
    )
    return got[:3], got[3:]


def add_body(*refs):
    count = len(refs) // 3
    for at in range(count):
        left, right = refs[at][...].astype(F32), refs[count + at][...].astype(F32)
        refs[2 * count + at][...] = (left + right).astype(BF16)


def add_all(left, right):
    out_shape = [kept(value.shape, BF16) for value in left]
    return local_call(add_body, "add_all", 6, out_shape, [], [*left, *right])


def lower_pull(dlower, base, lower, beta, decay, strict, k_in):
    dlower = jnp.where(strict, dlower, 0.0)
    dbeta = row_sum(dlower * base.astype(F32))
    dgram = dlower * (beta * decay)
    dkey = mm(dgram, k_in) + mm_tn(dgram, k_in)
    return dbeta, beta * dbeta, col_sum(dlower * lower.astype(F32)), dkey


def pull_body(sizes, *refs):
    heads, levels, bits = sizes
    (qkv_ref, pack_ref, pack_t_ref, trans_ref, attn_ref, attn_t_ref, prod_t_ref, scores_ref,
     mix_ref, decay_ref, base_ref, lower_ref, dout_ref, dhat_ref) = refs[:14]
    dqkv_ref, dgrown_ref, dcol_ref, drow_ref = refs[14:]
    rows = pack_ref.shape[0]
    decay_col = levels * heads
    beta_col = decay_col + heads
    block_bit = BLOCK.bit_length() - 1
    pack = pack_ref[...]
    pack_t = pack_t_ref[...]
    row_id, col_id = pair_ids(rows)
    strict = row_id > col_id
    apart = row_id ^ col_id
    lane = lane_of(rows)
    all_heads = range(heads)
    dcol = jnp.zeros((rows, LANES), F32)
    dbeta_rows, dcum_rows, dattn_all = [], [], []
    for head in all_heads:
        high, low = split(dout_ref[head])
        v_in = qkv_ref[2, head].astype(BF16)
        dprod = mm_nt(high, v_in) + mm_nt(low, v_in)
        dqkv_ref[2, head] = mm(prod_t_ref[head], high)
        beta_row = pack_t[beta_col + head : beta_col + head + 1, :]
        growth = jnp.exp(column(pack, decay_col + head))
        attn0 = attn_ref[head].astype(F32)
        touched = dprod * (attn0 * beta_row)
        for level in range(bits + 1):
            if level == 0:
                here = (apart >> block_bit) == 0
            else:
                here = (apart >> (block_bit + level - 1)) == 1
            dcol = jnp.where(
                lane == level * heads + head, row_sum(jnp.where(here, touched, 0.0)), dcol
            )
        dattn = dprod * mix_ref[head].astype(F32) - mm_nt(dhat_ref[head], growth * qkv_ref[1, head])
        dbeta_rows.append(col_sum(dattn * attn0))
        dattn_all.append((dattn * beta_row).astype(BF16))
    dscore_all = [mm_nt(dattn_all[head], trans_ref[head]) for head in all_heads]
    moved_all = []
    for head in all_heads:
        both = jnp.concatenate(
            [dscore_all[head].astype(BF16), dhat_ref[head].astype(BF16)], 1
        )
        moved_all.append(mm(attn_t_ref[head], both))
    for head in all_heads:
        q_in, k_in = qkv_ref[0, head], qkv_ref[1, head]
        beta = column(pack, beta_col + head)
        growth = jnp.exp(column(pack, decay_col + head))
        dscore = dscore_all[head]
        decay = decay_ref[head].astype(F32)
        dprobs = dscore * decay
        shift = dscore * scores_ref[head].astype(F32)
        dgrown_ref[head] = -beta * moved_all[head][:, rows:]
        dbeta, dcum_col, dcum_row, dk_lower = lower_pull(
            -moved_all[head][:, :rows], base_ref[head], lower_ref[head], beta, decay, strict, k_in
        )
        dhat = dhat_ref[head]
        dqkv_ref[0, head] = growth * dhat + mm(dprobs, k_in)
        dqkv_ref[1, head] = mm_tn(dprobs, q_in) + dk_lower
        dcum_col = dcum_col + row_sum(shift) + growth * row_sum(q_in * dhat)
        dcum_rows.append(-dcum_row - col_sum(shift))
        dcol = jnp.where(lane == beta_col + head, dbeta, dcol)
        dcol = jnp.where(lane == decay_col + head, dcum_col, dcol)
    dcol_ref[...] = dcol
    drow_ref[...] = jnp.concatenate(dcum_rows + dbeta_rows, 0)


def pull_local(arrays, levels, bits):
    heads, rows, key = arrays[0].shape[1:]
    out_shape = (
        kept((3, heads, rows, key), F32),
        kept((heads, rows, key), F32),
        kept((rows, LANES), F32),
        kept((2 * heads, rows), F32),
    )
    return local_call(
        functools.partial(pull_body, (heads, levels, bits)), "pull_local", 12, out_shape, [], arrays
    )


def finish_body(sizes, place_ref, *refs):
    heads, levels, far, arrived_counts = sizes
    (qkv_ref, gate_ref, pack_ref, trans_ref, mixed_ref, decay_ref, base_ref, lower_ref,
     dqkv_ref, dgrown_ref, dcol_ref, drow_ref, dfar_ref, rates_ref) = refs[:14]
    others = refs[14 : 14 + far]
    refs = refs[14 + far :]
    arrived = []
    for found in arrived_counts:
        arrived.append(refs[:found])
        refs = refs[found:]
    dproj, dgate_ref = refs
    rows = pack_ref.shape[0]
    key = qkv_ref.shape[3]
    decay_col = levels * heads
    beta_col = decay_col + heads
    norm_col = beta_col + heads
    place = place_ref[0]
    all_heads = range(heads)
    uppers = [((place >> bit) & 1) == 1 for bit in range(far)]
    pack = pack_ref[...]
    row_id, col_id = pair_ids(rows)
    strict = row_id > col_id
    lane = lane_of(rows)
    last_row = lax.broadcasted_iota(jnp.int32, (rows, 1), 0) == rows - 1
    eye_key = (pair_ids(key)[0] == pair_ids(key)[1]).astype(F32)
    dpair = [jnp.zeros((key, 2 * key), F32) for head in all_heads]
    for bit in reversed(range(far)):
        for head in all_heads:
            got = arrived[bit][0][head].astype(F32)
            for more in arrived[bit][1:]:
                got = got + more[head].astype(F32)
            other = others[bit][head]
            if bit == far - 1:
                got = jnp.concatenate([jnp.zeros((key, key), F32), got], 1)
                dpair[head] = jnp.where(uppers[bit], 0.0, got)
            else:
                as_low = mm_tn(other[:, :key], dpair[head]) + got
                as_high = mm_nt(dpair[head], other)
                as_high = jnp.concatenate([as_high, dpair[head][:, key:]], 1)
                dpair[head] = jnp.where(uppers[bit], as_high, as_low)
    moved_all, dmixed_all = [], []
    for head in all_heads:
        beta = column(pack, beta_col + head)
        growth = jnp.exp(column(pack, decay_col + head))
        both = jnp.concatenate([-growth * qkv_ref[1, head], qkv_ref[2, head]], 1)
        dmixed_all.append(mm_nt(both, dpair[head]))
        moved_all.append(mm(beta * mixed_ref[head].astype(F32), dpair[head]))
    dtail_all = [
        mm(trans_ref[head], column(pack, beta_col + head) * dmixed_all[head])
        for head in all_heads
    ]
    dlower_all = [-mm_nt(mixed_ref[head], dtail_all[head]) for head in all_heads]
    dcol = jnp.where(lane < decay_col, dcol_ref[...] + dfar_ref[...], dcol_ref[...])
    dcum_rows = []
    for head in all_heads:
        q_in, k_in = qkv_ref[0, head], qkv_ref[1, head]
        beta = column(pack, beta_col + head)
        cum_col = column(pack, decay_col + head)
        growth = jnp.exp(cum_col)
        last = cum_col[rows - 1 : rows, :]
        tail = jnp.exp(last - cum_col)
        dgrown = dgrown_ref[head] - moved_all[head][:, :key]
        dv = dqkv_ref[2, head] + moved_all[head][:, key:]
        dbeta_more = row_sum(mixed_ref[head].astype(F32) * dmixed_all[head])
        dtail = dtail_all[head]
        dbeta, dcum_col, dcum_row, dk_lower = lower_pull(
            dlower_all[head], base_ref[head], lower_ref[head], beta, decay_ref[head].astype(F32),
            strict, k_in
        )
        dcum_rows.append(-dcum_row)
        tail_pull = tail * row_sum(k_in * dtail)
        trace = col_sum(row_sum(dpair[head][:, :key] * eye_key))
        at_last = col_sum(tail_pull) + jnp.exp(last) * trace
        dcum_col = dcum_col + growth * row_sum(k_in * dgrown) - tail_pull
        dcum_col = dcum_col + jnp.where(last_row, at_last, 0.0)
        dk = dqkv_ref[1, head] + dk_lower + growth * dgrown + tail * dtail
        dq = dqkv_ref[0, head]
        dcol = dcol + jnp.where(lane == beta_col + head, dbeta + dbeta_more, 0.0)
        dcol = dcol + jnp.where(lane == decay_col + head, dcum_col, 0.0)
        for part, unit, dunit in ((0, q_in, dq), (1, k_in, dk)):
            scale = column(pack, norm_col + part * heads + head)
            back = scale * (dunit - unit * row_sum(unit * dunit))
            col = (part * heads + head) * key
            dproj[:, col : col + key] = back.astype(BF16)
        col = (2 * heads + head) * key
        dproj[:, col : col + key] = dv.astype(BF16)
    drow = drow_ref[...]
    drow = drow + jnp.concatenate(dcum_rows + [jnp.zeros((heads, rows), F32)], 0)
    drow = jnp.concatenate(
        [jnp.zeros((decay_col, rows), F32), drow,
         jnp.zeros((LANES - norm_col, rows), F32)], 0
    )
    dcol = dcol + drow.T
    rate, bias = rates_ref[0:1, :], rates_ref[1:2, :]
    switch = jax.nn.sigmoid(gate_ref[...] + bias)
    dlog = mm_ones((row_id <= col_id).astype(F32), dcol)
    slope = switch * (1.0 - switch)
    dgate = jnp.where(
        lane < decay_col,
        dcol * switch,
        jnp.where(lane < beta_col, -rate * dlog * slope, dcol * slope),
    )
    dgate_ref[...] = jnp.where(lane < norm_col, dgate, 0.0).astype(BF16)


def finish(place, arrays, others, arrived, levels):
    heads, rows, key = arrays[0].shape[1:]
    counts = tuple(len(group) for group in arrived)
    flat = [value for group in arrived for value in group]
    return local_call(
        functools.partial(finish_body, (heads, levels, len(others), counts)), "finish", 10,
        [kept((rows, 3 * heads * key), BF16), kept((rows, LANES), BF16)],
        [place], [*arrays, *others, *flat],
    )


def tokens_body(count, place_ref, dproj_ref, dgate_ref, wr_ref, small_ref, *refs):
    keep_ref, send_ref = refs[:2]
    direct_refs = refs[2:]
    size = wr_ref.shape[0] // count
    half = size // 2
    for mask in range(count):
        dest = place_ref[1] ^ mask
        span = pl.ds(pl.multiple_of(dest * size, size), size)
        part = mm_nt(dproj_ref[...], wr_ref[span, :]) + mm(dgate_ref[...], small_ref[:, span])
        direct_refs[mask][...] = part[:, :half].astype(BF16)
        target = send_ref if mask % 2 else keep_ref
        target[mask // 2] = part[:, half:].astype(BF16)


def pull_tokens(place, dproj, dgate, wr, small_t, count):
    rows = dproj.shape[0]
    half = wr.shape[0] // count // 2
    out_shape = [kept((count // 2, rows, half), BF16)] * 2 + [kept((rows, half), BF16)] * count
    got = local_call(
        functools.partial(tokens_body, count), "pull_tokens", 8, out_shape,
        [place], [dproj, dgate, wr, small_t],
    )
    return got[0], got[1], got[2:]


def swap(value, axis, mask):
    size = lax.axis_size(axis)
    return lax.ppermute(value, axis, [(at, at ^ mask) for at in range(size)])


def far_first(count):
    return sorted(range(1, count), key=lambda mask: mask < count // 2)


def halve_body(own_ref, got_ref, keep_ref, send_ref):
    for at in range(own_ref.shape[0]):
        total = own_ref[at].astype(F32) + got_ref[at].astype(F32)
        target = send_ref if at % 2 else keep_ref
        target[at // 2] = total.astype(target.dtype)


def halving(keep, send, axis, tied):
    mask = 1
    while keep.shape[0] > 1:
        got = swap(send, axis, mask)
        half = (keep.shape[0] // 2,) + keep.shape[1:]
        keep, send = local_call(
            halve_body, "halve", 6, [kept(half, F32), kept(half, BF16)], [], [keep, got]
        )
        send, tied = lax.optimization_barrier((send, tied))
        mask *= 2
    return keep, swap(send, axis, mask), tied


def sum_body(count, *refs):
    keep_ref, got_ref = refs[:2]
    out_ref = refs[-1]
    total = keep_ref[0].astype(F32) + got_ref[0].astype(F32)
    if count == 0:
        out_ref[...] = total.astype(BF16)
        return
    half = out_ref.shape[1] // 2
    out_ref[:, half:] = total.astype(BF16)
    total = refs[2][...].astype(F32)
    for ref in refs[3:-1]:
        total = total + ref[...].astype(F32)
    out_ref[:, :half] = total.astype(BF16)


def head_sum(keep, last, direct, got):
    rows, cols = keep.shape[1:]
    out = jax.ShapeDtypeStruct((rows, cols * (2 if direct else 1)), BF16)
    return local_call(
        functools.partial(sum_body, len(direct)), "head_sum", 6, [out], [],
        [keep, last, *direct[:1], *got],
    )[0]


def on_device(tokens, qkv_weight, small_weight, head_param, norm_gain, out_weight, grad_out):
    rows, width = tokens.shape
    heads, key = qkv_weight.shape[2:]
    levels = small_weight.shape[2] - 2
    bits = (rows // BLOCK).bit_length() - 1
    size = lax.axis_size("ctx")
    far = size.bit_length() - 1
    count = lax.axis_size("head")
    place = jnp.stack([lax.axis_index("ctx"), lax.axis_index("head")]).astype(jnp.int32)
    flat_w = qkv_weight.reshape(width * 3 * heads, key)
    small = jnp.transpose(small_weight, (2, 1, 0))
    rates = head_param.T
    flat_out = out_weight.reshape(heads * key, width)
    gain = norm_gain.reshape(1, key)

    (wr, query_w, value_w, small_t, qkv, gate, pack, pack_t, trans, mixed_t, decay, base, lower, rates_row,
     pair) = project(
        place, tokens, flat_w, small, rates, heads, levels
    )
    first = swap(pair, "ctx", 1)
    node = join_half(place, pair, first)
    mine = [swap(node, "ctx", 2 * at) for at in range(1, size // 2)]
    (attn, attn_t, prod_t, scores, mix, mixed, local_out, hat, hat_t, grad_normed, qkv, pack,
     wr) = local_part(
        [qkv, pack, pack_t, trans, mixed_t, decay, grad_out, flat_out, query_w, value_w, tokens],
        wr, levels, bits,
    )
    mine, local_out, grad_normed = lax.optimization_barrier((mine, local_out, grad_normed))
    theirs = [swap(value, "ctx", 1) for value in mine]
    out_parts, (unit, scale, found, prefix), nodes = reach(
        place, [gain, pack, local_out, hat, flat_out], first, (mine, theirs), bits, far, count
    )
    others = [first, *nodes]
    (dhat, dout, dfar), sends = return_states(
        place, [gain, pack, hat, hat_t, grad_normed, unit, scale, found, prefix], others, bits
    )
    got = [swap(value, "ctx", 1) for value in sends]
    arrived = [[got[0]]]
    sums = add_all(sends[1:], got[1:])
    for bit in range(1, far):
        half = 1 << (bit - 1)
        arrived.append([swap(sums[bit - 1], "ctx", 2 * at) for at in range(half, 2 * half)])
    dqkv, dgrown, dcol, drow = pull_local(
        [qkv, pack, pack_t, trans, attn, attn_t, prod_t, scores, mix, decay, base, lower, dout,
         dhat],
        levels, bits,
    )
    keep_out, last_out, dcol = halving(*out_parts, "head", dcol)
    arrays = [qkv, gate, pack, trans, mixed, decay, base, lower, dqkv, dgrown, dcol, drow, dfar,
              rates_row]
    dproj, dgate = finish(place, arrays, others, arrived, levels)
    keep, send, direct = pull_tokens(place, dproj, dgate, wr, small_t, count)
    direct, last_out = lax.optimization_barrier((direct, last_out))
    keep, last, late = halving(keep, send, "head", direct[1])
    direct = [direct[0], late, *direct[2:]]
    got = [swap(direct[mask], "head", mask) for mask in far_first(count)]
    return head_sum(keep_out, last_out, [], []), head_sum(keep, last, direct, got)


def solution(mesh):
    placed = (
        P("ctx", None),
        P(None, None, "head", None),
        P(None, "head", None),
        P("head", None),
        P(),
        P("head", None, None),
        P("ctx", None),
    )
    return jax.shard_map(
        on_device,
        mesh=mesh,
        in_specs=placed,
        out_specs=(P("ctx", "head"), P("ctx", "head")),
        check_vma=False,
    )
```

```python
import functools

import jax
import jax.numpy as jnp
from jax import lax
from jax.experimental import pallas as pl
from jax.experimental.pallas import tpu as pltpu
from jax.sharding import PartitionSpec as P

BLOCK = 64
LANES = 128
EPS = 1e-06
MIB = 1024 * 1024
F32 = jnp.float32
BF16 = jnp.bfloat16
WHOLE = pl.BlockSpec(memory_space=pltpu.VMEM)
SCALARS = pl.BlockSpec(memory_space=pltpu.SMEM)
HBM = pl.BlockSpec(memory_space=pltpu.HBM)


def contract(left, right, dim_left, dim_right):
    return lax.dot_general(
        left.astype(BF16),
        right.astype(BF16),
        (((dim_left,), (dim_right,)), ((), ())),
        preferred_element_type=F32,
    )


def mm(left, right):
    return contract(left, right, 1, 0)


def mm_nt(left, right):
    return contract(left, right, 1, 1)


def mm_tn(left, right):
    return contract(left, right, 0, 0)


def split(values):
    high = values.astype(BF16)
    return high, (values - high.astype(F32)).astype(BF16)


def mm_nt_fine(left, right):
    left_high, left_low = split(left)
    right_high, right_low = split(right)
    return mm_nt(left_high, right_high) + (mm_nt(left_low, right_high) + mm_nt(left_high, right_low))


def mm_full(left, right):
    return jnp.dot(left, right, precision=lax.Precision.HIGHEST, preferred_element_type=F32)


def mm_ones(ones, values):
    high = values.astype(BF16)
    rest = values - high.astype(F32)
    middle = rest.astype(BF16)
    low = (rest - middle.astype(F32)).astype(BF16)
    return mm(ones, high) + (mm(ones, middle) + mm(ones, low))


def pair_ids(count):
    row_id = lax.broadcasted_iota(jnp.int32, (count, count), 0)
    col_id = lax.broadcasted_iota(jnp.int32, (count, count), 1)
    return row_id, col_id


def row_sum(values):
    return jnp.sum(values, 1, keepdims=True)


def col_sum(values):
    return jnp.sum(values, 0, keepdims=True)


def lane_of(rows):
    return lax.broadcasted_iota(jnp.int32, (rows, LANES), 1)


def decay_of(pack, pack_t, col, inclusive):
    spread = pack[:, col : col + 1] - pack_t[col : col + 1, :]
    return jnp.where(inclusive, jnp.exp(jnp.minimum(spread, 0.0)), 0.0)


def kept(shape, dtype):
    return pltpu.VMEM(shape, dtype)


def stored(shape, dtype):
    return pltpu.HBM(shape, dtype)


def pin(values, space):
    return [pltpu.with_memory_space_constraint(value, space) for value in values]


def local_call(
    body, name, limit, out_shape, scalars, arrays, scratch=(), remote=(), out_specs=None, alias=None
):
    return pl.pallas_call(
        body,
        out_shape=tuple(out_shape),
        in_specs=[SCALARS] * len(scalars)
        + [WHOLE] * len(arrays)
        + [HBM] * len(remote),
        out_specs=tuple(out_specs or [WHOLE] * len(out_shape)),
        scratch_shapes=list(scratch),
        input_output_aliases=alias or {},
        compiler_params=pltpu.CompilerParams(vmem_limit_bytes=limit * MIB),
        name=name,
    )(*scalars, *pin(arrays, pltpu.VMEM), *pin(remote, pltpu.HBM))


def column(pack, at):
    return pack[:, at : at + 1]


def level_mix(pack, head, heads, bits, apart):
    block_bit = BLOCK.bit_length() - 1
    mixed = jnp.broadcast_to(column(pack, head), apart.shape)
    for level in range(1, bits + 1):
        here = (apart >> (block_bit + level - 1)) >= 1
        mixed = jnp.where(here, column(pack, level * heads + head), mixed)
    return mixed


def head_rows(hp_ref, heads, decay_col, beta_col):
    lane_row = lane_of(1)
    rate = jnp.zeros((1, LANES), F32)
    bias = jnp.zeros((1, LANES), F32)
    for head in range(heads):
        rate = jnp.where(lane_row == decay_col + head, hp_ref[0:1, head : head + 1], rate)
        bias = jnp.where(lane_row == beta_col + head, hp_ref[1:2, head : head + 1], bias)
    return rate, bias


def invert(lower_all, eye, apart, rows):
    trans_all = [(eye - jnp.where(apart == 1, lower, 0.0)).astype(BF16) for lower in lower_all]
    for bit in range(1, rows.bit_length() - 1):
        here = (apart >> bit) == 1
        edge = [jnp.where(here, lower, 0.0) for lower in lower_all]
        half = [mm(trans, part) for trans, part in zip(trans_all, edge)]
        trans_all = [
            trans - mm(part, trans).astype(BF16) for trans, part in zip(trans_all, half)
        ]
    rest_all = []
    for trans, lower in zip(trans_all, lower_all):
        high, low = split(lower)
        rest_all.append(eye - trans.astype(F32) - mm(high, trans) - mm(low, trans))
    return [
        (trans.astype(F32) + mm(trans, rest)).astype(BF16)
        for trans, rest in zip(trans_all, rest_all)
    ]


def project_body(sizes, place_ref, hp_hbm, tokens_hbm, w_hbm, small_hbm, *refs):
    heads, levels, chunks = sizes
    (wr_hbm, query_ref, value_ref, small_ref, qkv_ref, gate_ref, pack_ref, pack_t_ref, trans_ref, mixed_t_ref,
     decay_ref, base_ref, lower_ref, rates_ref, pair_ref) = refs[:15]
    tokens, wide_in, wide_even, wide_odd, key_ref, small_in, small_wide, acc, hp_ref = refs[15:24]
    sems, in_sems, out_sems = refs[24:]
    laid = (query_ref, key_ref, value_ref)
    rows, width = tokens.shape
    depth = width // chunks
    cols = 3 * heads
    fetch_tokens = pltpu.make_async_copy(tokens_hbm, tokens, sems.at[0])
    fetch_small = pltpu.make_async_copy(small_hbm, small_in, sems.at[1])
    fetch_rates = pltpu.make_async_copy(hp_hbm, hp_ref, sems.at[2])
    fetches, keeps = [], []
    for chunk in range(chunks):
        span = pl.ds(chunk * depth * cols, depth * cols)
        fetches.append(
            pltpu.make_async_copy(w_hbm.at[span, :], wide_in.at[span, :], in_sems.at[chunk])
        )
        span = pl.ds(chunk * depth, depth)
        block = wr_hbm.at[span, pl.ds(heads * LANES, heads * LANES)]
        keeps.append(pltpu.make_async_copy(key_ref.at[span, :], block, out_sems.at[chunk]))
    fetches[0].start()
    fetches[1].start(priority=1)
    fetch_tokens.start()
    fetch_small.start(priority=1)
    fetch_rates.start(priority=1)
    for chunk in range(2, chunks):
        fetches[chunk].start(priority=chunk % 2)

    def relay(chunk):
        fetches[chunk].wait()
        wide = wide_odd if chunk % 2 else wide_even
        at = chunk * depth
        wide[...] = wide_in[at * cols : (at + depth) * cols, :].astype(F32)
        for col in range(cols):
            value = wide[pl.ds(col, depth, stride=cols), :].astype(BF16)
            lanes = slice(col % heads * LANES, (col % heads + 1) * LANES)
            laid[col // heads][at : at + depth, lanes] = value

    def multiply(first, last):
        for part in (1, 2):
            span = slice((part * heads) * LANES, (part + 1) * heads * LANES)
            own = jnp.dot(
                tokens[:, first * depth : last * depth],
                laid[part][first * depth : last * depth, :],
                preferred_element_type=F32,
            )
            if first == 0:
                acc[:, span] = own
            else:
                acc[:, span] += own

    def lay(first, last):
        for chunk in range(first, last, 2):
            relay(chunk)
            relay(chunk + 1)
            if chunk == 0:
                fetch_tokens.wait()
            multiply(chunk, chunk + 2)

    decay_col = levels * heads
    beta_col = decay_col + heads
    norm_col = beta_col + heads
    lane = lane_of(rows)
    row_id, col_id = pair_ids(rows)
    inclusive = row_id >= col_id
    strict = row_id > col_id
    apart = row_id ^ col_id
    eye = (row_id == col_id).astype(F32)
    lay(0, chunks)
    for chunk, keep in enumerate(keeps):
        keep.start(priority=chunk % 2)
    fetch_small.wait()
    small_rows = small_in.shape[0] * heads
    for level in range(small_in.shape[0]):
        small_wide[level * heads : (level + 1) * heads, :] = small_in[level].astype(F32)
    small_wide[small_rows:, :] = jnp.zeros((LANES - small_rows, width), F32)
    small_ref[...] = small_wide[...].astype(BF16)
    fetch_rates.wait()
    rate, bias = head_rows(hp_ref, heads, decay_col, beta_col)
    rates_ref[0:1, :] = rate
    rates_ref[1:2, :] = bias
    gate = mm_nt(tokens[...], small_ref[...])
    gate_ref[...] = gate
    switch = jax.nn.sigmoid(gate + bias)
    lam = jnp.maximum(gate, 0.0) + jnp.log1p(jnp.exp(-jnp.abs(gate)))
    cum = mm_full(inclusive.astype(F32), -rate * switch)
    pack = jnp.where(lane < decay_col, lam, jnp.where(lane < beta_col, cum, switch))
    pack_t = pack.T
    pack_t_ref[...] = pack_t

    def unit_of(part, head):
        col = (part * heads + head) * LANES
        raw = acc[:, col : col + LANES]
        scale = lax.rsqrt(row_sum(raw * raw) + EPS)
        qkv_ref[part, head] = raw * scale
        return raw * scale, jnp.where(lane == norm_col + part * heads + head, scale, 0.0)

    scales = jnp.zeros((rows, LANES), F32)
    k_all, lower_all = [], []
    for head in range(heads):
        unit, scale = unit_of(1, head)
        k_all.append(unit)
        scales = scales + scale
        decay = decay_of(pack, pack_t, decay_col + head, inclusive)
        decay_ref[head] = decay.astype(BF16)
        base = jnp.where(strict, decay * mm_nt(unit, unit), 0.0)
        base_ref[head] = base.astype(BF16)
        lower = column(pack, beta_col + head) * base
        lower_ref[head] = lower.astype(BF16)
        lower_all.append(lower)

    trans_all = invert(lower_all, eye, apart, rows)
    mixed_all = []
    for head in range(heads):
        trans_ref[head] = trans_all[head]
        cum_row = pack_t[decay_col + head : decay_col + head + 1, :]
        tail_t = k_all[head].T * jnp.exp(cum_row[:, rows - 1 :] - cum_row)
        mixed_all.append(mm(tail_t, trans_all[head]).astype(BF16))
    eye_key = eye[:LANES, :LANES]
    for head in range(heads):
        mixed_t_ref[head] = mixed_all[head]
        col = (2 * heads + head) * LANES
        v_in = acc[:, col : col + LANES]
        qkv_ref[2, head] = v_in
        cum_col = column(pack, decay_col + head)
        beta = column(pack, beta_col + head)
        grown = (beta * jnp.exp(cum_col)) * k_all[head]
        both = jnp.concatenate([-grown, beta * v_in], 1)
        pair = mm(mixed_all[head], both)
        last = jnp.exp(cum_col[rows - 1 : rows, :])
        pair_ref[head, :, :LANES] = (last * eye_key + pair[:, :LANES]).astype(BF16)
        pair_ref[head, :, LANES:] = pair[:, LANES:].astype(BF16)
    pack_ref[...] = jnp.where(lane < norm_col, pack, scales)
    for keep in keeps:
        keep.wait()


def project(place, tokens, flat_w, small, head_param, heads, levels):
    rows, width = tokens.shape
    chunks = 16
    cols = 3 * heads
    key = flat_w.shape[1]
    square = (heads, rows, rows)
    out_shape = (
        stored((width, cols * key), BF16),
        kept((width, heads * key), BF16),
        kept((width, heads * key), BF16),
        kept((LANES, width), BF16),
        kept((3, heads, rows, key), F32),
        kept((rows, LANES), F32),
        kept((rows, LANES), F32),
        kept((LANES, rows), F32),
        kept(square, BF16),
        kept((heads, key, rows), BF16),
        kept(square, BF16),
        kept(square, BF16),
        kept(square, BF16),
        kept((2, LANES), F32),
        kept((heads, key, 2 * key), BF16),
    )
    scratch = [
        pltpu.VMEM(tokens.shape, BF16),
        pltpu.VMEM(flat_w.shape, BF16),
        pltpu.VMEM((width // chunks * cols, key), F32),
        pltpu.VMEM((width // chunks * cols, key), F32),
        pltpu.VMEM((width, heads * key), BF16),
        pltpu.VMEM(small.shape, BF16),
        pltpu.VMEM((LANES, width), F32),
        pltpu.VMEM((rows, cols * key), F32),
        pltpu.VMEM(head_param.shape, F32),
        pltpu.SemaphoreType.DMA((3,)),
        pltpu.SemaphoreType.DMA((chunks,)),
        pltpu.SemaphoreType.DMA((chunks,)),
    ]
    return local_call(
        functools.partial(project_body, (heads, levels, chunks)), "project", 36, out_shape,
        [place], [], scratch, [head_param, tokens, flat_w, small], [HBM] + [WHOLE] * 14,
    )


def local_body(
    sizes, qkv_ref, pack_ref, pack_t_ref, trans_ref, mixed_t_ref, decay_ref, grad_ref, weight_ref,
    query_ref, value_ref, tokens_ref, wr_in, *outs
):
    heads, levels, bits = sizes
    (attn_ref, attn_t_ref, prod_t_ref, scores_ref, mix_ref, mixed_ref, local_ref, hat_ref,
     hat_t_ref, grad_normed_ref, qkv_out, pack_out, wr_hbm, sems) = outs
    del wr_in
    half, size = query_ref.shape[0] // 2, query_ref.shape[1]
    keeps = []
    for at in range(4):
        span = pl.ds(at % 2 * half, half)
        here, col = ((query_ref, 0), (value_ref, 2 * size))[at // 2]
        there = wr_hbm.at[span, pl.ds(col, size)]
        keeps.append(pltpu.make_async_copy(here.at[span, :], there, sems.at[at]))
        keeps[at].start()
    rows = pack_ref.shape[0]
    decay_col = levels * heads
    beta_col = decay_col + heads
    norm_col = beta_col + heads
    lane = lane_of(rows)
    raw_all = jnp.dot(tokens_ref[...], query_ref[...], preferred_element_type=F32)
    pack = pack_ref[...]
    q_all = []
    for head in range(heads):
        raw = raw_all[:, head * LANES : (head + 1) * LANES]
        scale = lax.rsqrt(row_sum(raw * raw) + EPS)
        q_all.append(raw * scale)
        qkv_out[0, head] = q_all[head]
        pack = jnp.where(lane == norm_col + head, scale, pack)
    pack_out[...] = pack
    grad_normed_ref[...] = mm_nt(grad_ref[...], weight_ref[...])
    pack_t = pack_t_ref[...]
    row_id, col_id = pair_ids(rows)
    apart = row_id ^ col_id
    for head in range(heads):
        scores = mm_nt_fine(q_all[head], qkv_ref[1, head]) * decay_ref[head].astype(F32)
        scores_ref[head] = scores.astype(BF16)
        mix_ref[head] = level_mix(pack, head, heads, bits, apart).astype(BF16)
        mixed_ref[head] = mixed_t_ref[head].astype(F32).T.astype(BF16)
    for head in range(heads):
        attn = mm(scores_ref[head], trans_ref[head])
        attn_ref[head] = attn.astype(BF16)
        attn_t_ref[head] = attn.T.astype(BF16)
        attn = attn * pack_t[beta_col + head : beta_col + head + 1, :]
        prod = attn * mix_ref[head].astype(F32)
        prod_t_ref[head] = prod.T.astype(BF16)
        growth = jnp.exp(column(pack, decay_col + head))
        local_ref[head] = mm(prod, qkv_ref[2, head])
        hat = growth * q_all[head] - mm(attn, growth * qkv_ref[1, head])
        hat_ref[head] = hat.astype(BF16)
        hat_t_ref[head] = hat.T.astype(BF16)
    for keep in keeps:
        keep.wait()


def local_part(arrays, wr, levels, bits):
    heads, rows, key = arrays[0].shape[1:]
    square = (heads, rows, rows)
    out_shape = (
        kept(square, BF16),
        kept(square, BF16),
        kept(square, BF16),
        kept(square, BF16),
        kept(square, BF16),
        kept((heads, rows, key), BF16),
        kept((heads, rows, key), F32),
        kept((heads, rows, key), BF16),
        kept((heads, key, rows), BF16),
        kept((rows, heads * key), F32),
        kept(arrays[0].shape, F32),
        kept(arrays[1].shape, F32),
        stored(wr.shape, BF16),
    )
    return local_call(
        functools.partial(local_body, (heads, levels, bits)), "local_part", 10, out_shape,
        [], arrays, [pltpu.SemaphoreType.DMA((4,))], [wr], [WHOLE] * 12 + [HBM],
        {0: 10, 1: 11, len(arrays): 12},
    )


def join_pair(upper, own, other):
    key = own.shape[0]
    low = jnp.where(upper, other, own)
    high = jnp.where(upper, own, other)
    moved = mm(high[:, :key], low)
    late = jnp.concatenate([jnp.zeros((key, key), F32), high[:, key:].astype(F32)], 1)
    return (moved + late).astype(BF16)


def join_body(place_ref, own_ref, other_ref, out_ref):
    half = out_ref.shape[0]
    upper = (place_ref[0] & 1) == 1
    for slot in range(half):
        head = (place_ref[0] & 1) * half + slot
        out_ref[slot] = join_pair(upper, own_ref[head], other_ref[head])


def join_half(place, own, other):
    half = (own.shape[0] // 2,) + own.shape[1:]
    return local_call(join_body, "join_half", 6, [kept(half, BF16)], [place], [own, other])[0]


def gather_node(head, bit, first, near, uppers):
    if bit == 0:
        mine, theirs = near[first]
        half = mine.shape[0]
        here = uppers[0] if head >= half else jnp.logical_not(uppers[0])
        return jnp.where(here, mine[head % half], theirs[head % half])
    own = gather_node(head, bit - 1, first, near, uppers)
    other = gather_node(head, bit - 1, first ^ (1 << (bit - 1)), near, uppers)
    return join_pair(uppers[bit], own, other)


def reach_body(
    sizes, place_ref, gain_ref, pack_ref, local_ref, hat_ref, weight_ref, *refs
):
    heads, bits, far, count, near_count = sizes
    first_ref = refs[0]
    near = [None] + [(refs[1 + at], refs[1 + near_count + at]) for at in range(near_count)]
    refs = refs[2 * near_count + 1 :]
    out_refs = refs[:2]
    summed_ref, scale_ref, found_ref, prefix_ref = refs[2:6]
    nodes = refs[6:-1]
    normed_ref = refs[-1]
    rows = pack_ref.shape[0]
    key = hat_ref.shape[2]
    pack = pack_ref[...]
    gain = gain_ref[...]
    lane = lane_of(rows)
    all_heads = range(heads)
    uppers = [((place_ref[0] >> bit) & 1) == 1 for bit in range(far)]
    others = []
    for bit in range(far):
        if bit == 0:
            others.append([first_ref[head] for head in all_heads])
        else:
            others.append(
                [gather_node(head, bit - 1, 1 << (bit - 1), near, uppers) for head in all_heads]
            )
            for head in all_heads:
                nodes[bit - 1][head] = others[bit][head]
    eye_key = jnp.where(pair_ids(key)[0] == pair_ids(key)[1], 1.0, 0.0).astype(BF16)
    prefix = [eye_key for head in all_heads]
    found = []
    for bit in range(far):
        for head in all_heads:
            prefix_ref[head, bit] = prefix[head]
        moved = [mm(prefix[head], others[bit][head]) for head in all_heads]
        found.append([jnp.where(uppers[bit], m[:, key:], 0.0).astype(BF16) for m in moved])
        prefix = [
            jnp.where(uppers[bit], moved[head][:, :key].astype(BF16), prefix[head])
            for head in all_heads
        ]
    found = [jnp.concatenate([found[bit][head] for bit in range(far)], 1) for head in all_heads]
    reached = [mm(hat_ref[head], found[head]) for head in all_heads]
    scales = jnp.zeros((rows, LANES), F32)
    for head in all_heads:
        found_ref[head] = found[head]
        summed = local_ref[head]
        for bit in range(far):
            part = reached[head][:, bit * key : (bit + 1) * key]
            summed = summed + column(pack, (bits + 1 + bit) * heads + head) * part
        scale = lax.rsqrt(jnp.mean(summed * summed, -1, keepdims=True) + EPS)
        unit = summed * scale
        normed_ref[:, head * key : (head + 1) * key] = (unit * gain).astype(BF16)
        summed_ref[head] = unit
        scales = jnp.where(lane == head, scale, scales)
    scale_ref[...] = scales
    size = weight_ref.shape[1] // count
    for mask in range(count):
        dest = place_ref[1] ^ mask
        cols = pl.ds(pl.multiple_of(dest * size, size), size)
        out_refs[mask % 2][mask // 2] = jnp.dot(
            normed_ref[...], weight_ref[:, cols], preferred_element_type=F32
        ).astype(BF16)


def reach(place, arrays, first, near, bits, far, count):
    gain, pack, local_out, hat, weight = arrays
    heads, rows, key = hat.shape
    nodes = tuple(kept(first.shape, BF16) for bit in range(1, far))
    size = weight.shape[1] // count
    out_shape = (kept((count // 2, rows, size), BF16),) * 2 + (
        kept((heads, rows, key), F32),
        kept((rows, LANES), F32),
        kept((heads, key, far * key), BF16),
        kept((heads, far, key, key), BF16),
    ) + nodes
    mine, theirs = near
    got = local_call(
        functools.partial(reach_body, (heads, bits, far, count, len(mine))), "reach", 10, out_shape,
        [place], [*arrays, first, *mine, *theirs], [pltpu.VMEM((rows, heads * key), BF16)],
    )
    return got[:2], got[2:6], got[6:]


def return_body(
    sizes, place_ref, gain_ref, pack_ref, hat_t_ref, grad_ref, unit_ref, scale_ref,
    found_ref, prefix_ref, *refs
):
    heads, bits, far = sizes
    others = refs[:far]
    dhat_ref, dout_ref = refs[far : far + 2]
    sends = refs[far + 2 :]
    gain, scales = gain_ref[...], scale_ref[...]
    key = hat_t_ref.shape[1]
    pack = pack_ref[...]
    all_heads = range(heads)
    uppers = [((place_ref[0] >> bit) & 1) == 1 for bit in range(far)]
    spread = []
    for head in all_heads:
        unit = unit_ref[head]
        pulled = grad_ref[:, head * key : (head + 1) * key] * gain
        mean = jnp.mean(pulled * unit, -1, keepdims=True)
        dout = column(scales, head) * (pulled - unit * mean)
        dout_ref[head] = dout
        parts = []
        for bit in range(far):
            col = (bits + 1 + bit) * heads + head
            parts.append((column(pack, col) * dout).astype(BF16))
        spread.append(jnp.concatenate(parts, 1))
    dfound = [mm(hat_t_ref[head], spread[head]) for head in all_heads]
    for head in all_heads:
        dhat_ref[head] = mm_nt(spread[head], found_ref[head])
    dprefix = [jnp.zeros((key, key), F32) for head in all_heads]
    for bit in reversed(range(far)):
        dfree = [
            jnp.where(uppers[bit], d[:, bit * key : (bit + 1) * key], 0.0) for d in dfound
        ]
        both = [
            jnp.concatenate([jnp.where(uppers[bit], dprefix[head], 0.0), dfree[head]], 1)
            for head in all_heads
        ]
        for head in all_heads:
            sent = dfree[head] if bit == far - 1 else both[head]
            sends[bit][head] = mm_tn(prefix_ref[head, bit], sent).astype(BF16)
        if bit > 0:
            moved = [mm_nt(both[head], others[bit][head]) for head in all_heads]
            dprefix = [
                jnp.where(uppers[bit], moved[head], dprefix[head]) for head in all_heads
            ]


def return_states(place, arrays, others, bits):
    heads, key, rows = arrays[2].shape
    far = len(others)
    sends = tuple(
        kept((heads, key, (1 if bit == far - 1 else 2) * key), BF16) for bit in range(far)
    )
    wide = kept((heads, rows, key), F32)
    got = local_call(
        functools.partial(return_body, (heads, bits, far)), "return_states", 8,
        (wide, wide) + sends, [place], [*arrays, *others],
    )
    return got[:2], got[2:]


def add_body(*refs):
    count = len(refs) // 3
    for at in range(count):
        left, right = refs[at][...].astype(F32), refs[count + at][...].astype(F32)
        refs[2 * count + at][...] = (left + right).astype(BF16)


def add_all(left, right):
    out_shape = [kept(value.shape, BF16) for value in left]
    return local_call(add_body, "add_all", 6, out_shape, [], [*left, *right])


def lower_pull(dlower, base, lower, beta, decay, strict, k_in):
    dlower = jnp.where(strict, dlower, 0.0)
    dbeta = row_sum(dlower * base.astype(F32))
    dgram = dlower * (beta * decay)
    dkey = mm(dgram, k_in) + mm_tn(dgram, k_in)
    return dbeta, beta * dbeta, col_sum(dlower * lower.astype(F32)), dkey


def pull_body(sizes, *refs):
    heads, levels, bits = sizes
    (qkv_ref, pack_ref, pack_t_ref, trans_ref, attn_ref, attn_t_ref, prod_t_ref, scores_ref,
     mix_ref, decay_ref, base_ref, lower_ref, dout_ref, dhat_ref, hat_ref, found_ref) = refs[:16]
    dqkv_ref, dgrown_ref, dcol_ref, drow_ref, dfar_ref = refs[16:]
    rows = pack_ref.shape[0]
    decay_col = levels * heads
    beta_col = decay_col + heads
    block_bit = BLOCK.bit_length() - 1
    pack = pack_ref[...]
    pack_t = pack_t_ref[...]
    row_id, col_id = pair_ids(rows)
    strict = row_id > col_id
    apart = row_id ^ col_id
    lane = lane_of(rows)
    all_heads = range(heads)
    dcol = jnp.zeros((rows, LANES), F32)
    dbeta_rows, dcum_rows, dattn_all = [], [], []
    key = hat_ref.shape[2]
    dfar = jnp.zeros((rows, LANES), F32)
    for head in all_heads:
        reached = mm(hat_ref[head], found_ref[head])
        for bit in range(reached.shape[1] // key):
            here = row_sum(dout_ref[head] * reached[:, bit * key : (bit + 1) * key])
            dfar = jnp.where(lane == (bits + 1 + bit) * heads + head, here, dfar)
    dfar_ref[...] = dfar
    for head in all_heads:
        high, low = split(dout_ref[head])
        v_in = qkv_ref[2, head].astype(BF16)
        dprod = mm_nt(high, v_in) + mm_nt(low, v_in)
        dqkv_ref[2, head] = mm(prod_t_ref[head], high)
        beta_row = pack_t[beta_col + head : beta_col + head + 1, :]
        growth = jnp.exp(column(pack, decay_col + head))
        attn0 = attn_ref[head].astype(F32)
        touched = dprod * (attn0 * beta_row)
        for level in range(bits + 1):
            if level == 0:
                here = (apart >> block_bit) == 0
            else:
                here = (apart >> (block_bit + level - 1)) == 1
            dcol = jnp.where(
                lane == level * heads + head, row_sum(jnp.where(here, touched, 0.0)), dcol
            )
        dattn = dprod * mix_ref[head].astype(F32) - mm_nt(dhat_ref[head], growth * qkv_ref[1, head])
        dbeta_rows.append(col_sum(dattn * attn0))
        dattn_all.append((dattn * beta_row).astype(BF16))
    dscore_all = [mm_nt(dattn_all[head], trans_ref[head]) for head in all_heads]
    moved_all = []
    for head in all_heads:
        both = jnp.concatenate(
            [dscore_all[head].astype(BF16), dhat_ref[head].astype(BF16)], 1
        )
        moved_all.append(mm(attn_t_ref[head], both))
    for head in all_heads:
        q_in, k_in = qkv_ref[0, head], qkv_ref[1, head]
        beta = column(pack, beta_col + head)
        growth = jnp.exp(column(pack, decay_col + head))
        dscore = dscore_all[head]
        decay = decay_ref[head].astype(F32)
        dprobs = dscore * decay
        shift = dscore * scores_ref[head].astype(F32)
        dgrown_ref[head] = -beta * moved_all[head][:, rows:]
        dbeta, dcum_col, dcum_row, dk_lower = lower_pull(
            -moved_all[head][:, :rows], base_ref[head], lower_ref[head], beta, decay, strict, k_in
        )
        dhat = dhat_ref[head]
        dqkv_ref[0, head] = growth * dhat + mm(dprobs, k_in)
        dqkv_ref[1, head] = mm_tn(dprobs, q_in) + dk_lower
        dcum_col = dcum_col + row_sum(shift) + growth * row_sum(q_in * dhat)
        dcum_rows.append(-dcum_row - col_sum(shift))
        dcol = jnp.where(lane == beta_col + head, dbeta, dcol)
        dcol = jnp.where(lane == decay_col + head, dcum_col, dcol)
    dcol_ref[...] = dcol
    drow_ref[...] = jnp.concatenate(dcum_rows + dbeta_rows, 0)


def pull_local(arrays, levels, bits):
    heads, rows, key = arrays[0].shape[1:]
    out_shape = (
        kept((3, heads, rows, key), F32),
        kept((heads, rows, key), F32),
        kept((rows, LANES), F32),
        kept((2 * heads, rows), F32),
        kept((rows, LANES), F32),
    )
    return local_call(
        functools.partial(pull_body, (heads, levels, bits)), "pull_local", 12, out_shape, [], arrays
    )


def finish_body(sizes, place_ref, *refs):
    heads, levels, far, arrived_counts = sizes
    (qkv_ref, gate_ref, pack_ref, trans_ref, mixed_ref, decay_ref, base_ref, lower_ref,
     dqkv_ref, dgrown_ref, dcol_ref, drow_ref, dfar_ref, rates_ref) = refs[:14]
    others = refs[14 : 14 + far]
    refs = refs[14 + far :]
    arrived = []
    for found in arrived_counts:
        arrived.append(refs[:found])
        refs = refs[found:]
    dproj, dgate_ref = refs
    rows = pack_ref.shape[0]
    key = qkv_ref.shape[3]
    decay_col = levels * heads
    beta_col = decay_col + heads
    norm_col = beta_col + heads
    place = place_ref[0]
    all_heads = range(heads)
    uppers = [((place >> bit) & 1) == 1 for bit in range(far)]
    pack = pack_ref[...]
    row_id, col_id = pair_ids(rows)
    strict = row_id > col_id
    lane = lane_of(rows)
    last_row = lax.broadcasted_iota(jnp.int32, (rows, 1), 0) == rows - 1
    eye_key = (pair_ids(key)[0] == pair_ids(key)[1]).astype(F32)
    dpair = [jnp.zeros((key, 2 * key), F32) for head in all_heads]
    for bit in reversed(range(far)):
        for head in all_heads:
            got = arrived[bit][0][head].astype(F32)
            for more in arrived[bit][1:]:
                got = got + more[head].astype(F32)
            other = others[bit][head]
            if bit == far - 1:
                got = jnp.concatenate([jnp.zeros((key, key), F32), got], 1)
                dpair[head] = jnp.where(uppers[bit], 0.0, got)
            else:
                as_low = mm_tn(other[:, :key], dpair[head]) + got
                as_high = mm_nt(dpair[head], other)
                as_high = jnp.concatenate([as_high, dpair[head][:, key:]], 1)
                dpair[head] = jnp.where(uppers[bit], as_high, as_low)
    moved_all, dmixed_all = [], []
    for head in all_heads:
        beta = column(pack, beta_col + head)
        growth = jnp.exp(column(pack, decay_col + head))
        both = jnp.concatenate([-growth * qkv_ref[1, head], qkv_ref[2, head]], 1)
        dmixed_all.append(mm_nt(both, dpair[head]))
        moved_all.append(mm(beta * mixed_ref[head].astype(F32), dpair[head]))
    dtail_all = [
        mm(trans_ref[head], column(pack, beta_col + head) * dmixed_all[head])
        for head in all_heads
    ]
    dlower_all = [-mm_nt(mixed_ref[head], dtail_all[head]) for head in all_heads]
    dcol = jnp.where(lane < decay_col, dcol_ref[...] + dfar_ref[...], dcol_ref[...])
    dcum_rows = []
    for head in all_heads:
        q_in, k_in = qkv_ref[0, head], qkv_ref[1, head]
        beta = column(pack, beta_col + head)
        cum_col = column(pack, decay_col + head)
        growth = jnp.exp(cum_col)
        last = cum_col[rows - 1 : rows, :]
        tail = jnp.exp(last - cum_col)
        dgrown = dgrown_ref[head] - moved_all[head][:, :key]
        dv = dqkv_ref[2, head] + moved_all[head][:, key:]
        dbeta_more = row_sum(mixed_ref[head].astype(F32) * dmixed_all[head])
        dtail = dtail_all[head]
        dbeta, dcum_col, dcum_row, dk_lower = lower_pull(
            dlower_all[head], base_ref[head], lower_ref[head], beta, decay_ref[head].astype(F32),
            strict, k_in
        )
        dcum_rows.append(-dcum_row)
        tail_pull = tail * row_sum(k_in * dtail)
        trace = col_sum(row_sum(dpair[head][:, :key] * eye_key))
        at_last = col_sum(tail_pull) + jnp.exp(last) * trace
        dcum_col = dcum_col + growth * row_sum(k_in * dgrown) - tail_pull
        dcum_col = dcum_col + jnp.where(last_row, at_last, 0.0)
        dk = dqkv_ref[1, head] + dk_lower + growth * dgrown + tail * dtail
        dq = dqkv_ref[0, head]
        dcol = dcol + jnp.where(lane == beta_col + head, dbeta + dbeta_more, 0.0)
        dcol = dcol + jnp.where(lane == decay_col + head, dcum_col, 0.0)
        for part, unit, dunit in ((0, q_in, dq), (1, k_in, dk)):
            scale = column(pack, norm_col + part * heads + head)
            back = scale * (dunit - unit * row_sum(unit * dunit))
            col = (part * heads + head) * key
            dproj[:, col : col + key] = back.astype(BF16)
        col = (2 * heads + head) * key
        dproj[:, col : col + key] = dv.astype(BF16)
    drow = drow_ref[...]
    drow = drow + jnp.concatenate(dcum_rows + [jnp.zeros((heads, rows), F32)], 0)
    drow = jnp.concatenate(
        [jnp.zeros((decay_col, rows), F32), drow,
         jnp.zeros((LANES - norm_col, rows), F32)], 0
    )
    dcol = dcol + drow.T
    rate, bias = rates_ref[0:1, :], rates_ref[1:2, :]
    switch = jax.nn.sigmoid(gate_ref[...] + bias)
    dlog = mm_ones((row_id <= col_id).astype(F32), dcol)
    slope = switch * (1.0 - switch)
    dgate = jnp.where(
        lane < decay_col,
        dcol * switch,
        jnp.where(lane < beta_col, -rate * dlog * slope, dcol * slope),
    )
    dgate_ref[...] = jnp.where(lane < norm_col, dgate, 0.0).astype(BF16)


def finish(place, arrays, others, arrived, levels):
    heads, rows, key = arrays[0].shape[1:]
    counts = tuple(len(group) for group in arrived)
    flat = [value for group in arrived for value in group]
    return local_call(
        functools.partial(finish_body, (heads, levels, len(others), counts)), "finish", 10,
        [kept((rows, 3 * heads * key), BF16), kept((rows, LANES), BF16)],
        [place], [*arrays, *others, *flat],
    )


def tokens_body(count, place_ref, dproj_ref, dgate_ref, wr_ref, small_ref, *refs):
    keep_ref, send_ref = refs[:2]
    direct_refs = refs[2:]
    size = wr_ref.shape[0] // count
    half = size // 2
    for mask in range(count):
        dest = place_ref[1] ^ mask
        span = pl.ds(pl.multiple_of(dest * size, size), size)
        part = mm_nt(dproj_ref[...], wr_ref[span, :]) + mm(dgate_ref[...], small_ref[:, span])
        direct_refs[mask][...] = part[:, :half].astype(BF16)
        target = send_ref if mask % 2 else keep_ref
        target[mask // 2] = part[:, half:].astype(BF16)


def pull_tokens(place, dproj, dgate, wr, small_t, count):
    rows = dproj.shape[0]
    half = wr.shape[0] // count // 2
    out_shape = [kept((count // 2, rows, half), BF16)] * 2 + [kept((rows, half), BF16)] * count
    got = local_call(
        functools.partial(tokens_body, count), "pull_tokens", 8, out_shape,
        [place], [dproj, dgate, wr, small_t],
    )
    return got[0], got[1], got[2:]


def swap(value, axis, mask):
    size = lax.axis_size(axis)
    return lax.ppermute(value, axis, [(at, at ^ mask) for at in range(size)])


def far_first(count):
    return sorted(range(1, count), key=lambda mask: mask < count // 2)


def halve_body(own_ref, got_ref, keep_ref, send_ref):
    for at in range(own_ref.shape[0]):
        total = own_ref[at].astype(F32) + got_ref[at].astype(F32)
        target = send_ref if at % 2 else keep_ref
        target[at // 2] = total.astype(target.dtype)


def halving(keep, send, axis, tied):
    mask = 1
    while keep.shape[0] > 1:
        got = swap(send, axis, mask)
        half = (keep.shape[0] // 2,) + keep.shape[1:]
        keep, send = local_call(
            halve_body, "halve", 6, [kept(half, F32), kept(half, BF16)], [], [keep, got]
        )
        send, tied = lax.optimization_barrier((send, tied))
        mask *= 2
    return keep, swap(send, axis, mask), tied


def sum_body(count, *refs):
    keep_ref, got_ref = refs[:2]
    out_ref = refs[-1]
    total = keep_ref[0].astype(F32) + got_ref[0].astype(F32)
    if count == 0:
        out_ref[...] = total.astype(BF16)
        return
    half = out_ref.shape[1] // 2
    out_ref[:, half:] = total.astype(BF16)
    total = refs[2][...].astype(F32)
    for ref in refs[3:-1]:
        total = total + ref[...].astype(F32)
    out_ref[:, :half] = total.astype(BF16)


def head_sum(keep, last, direct, got):
    rows, cols = keep.shape[1:]
    out = jax.ShapeDtypeStruct((rows, cols * (2 if direct else 1)), BF16)
    return local_call(
        functools.partial(sum_body, len(direct)), "head_sum", 6, [out], [],
        [keep, last, *direct[:1], *got],
    )[0]


def on_device(tokens, qkv_weight, small_weight, head_param, norm_gain, out_weight, grad_out):
    rows, width = tokens.shape
    heads, key = qkv_weight.shape[2:]
    levels = small_weight.shape[2] - 2
    bits = (rows // BLOCK).bit_length() - 1
    size = lax.axis_size("ctx")
    far = size.bit_length() - 1
    count = lax.axis_size("head")
    place = jnp.stack([lax.axis_index("ctx"), lax.axis_index("head")]).astype(jnp.int32)
    flat_w = qkv_weight.reshape(width * 3 * heads, key)
    small = jnp.transpose(small_weight, (2, 1, 0))
    rates = head_param.T
    flat_out = out_weight.reshape(heads * key, width)
    gain = norm_gain.reshape(1, key)

    (wr, query_w, value_w, small_t, qkv, gate, pack, pack_t, trans, mixed_t, decay, base, lower, rates_row,
     pair) = project(
        place, tokens, flat_w, small, rates, heads, levels
    )
    first = swap(pair, "ctx", 1)
    node = join_half(place, pair, first)
    mine = [swap(node, "ctx", 2 * at) for at in range(1, size // 2)]
    (attn, attn_t, prod_t, scores, mix, mixed, local_out, hat, hat_t, grad_normed, qkv, pack,
     wr) = local_part(
        [qkv, pack, pack_t, trans, mixed_t, decay, grad_out, flat_out, query_w, value_w, tokens],
        wr, levels, bits,
    )
    mine, local_out, grad_normed = lax.optimization_barrier((mine, local_out, grad_normed))
    theirs = [swap(value, "ctx", 1) for value in mine]
    out_parts, (unit, scale, found, prefix), nodes = reach(
        place, [gain, pack, local_out, hat, flat_out], first, (mine, theirs), bits, far, count
    )
    others = [first, *nodes]
    (dhat, dout), sends = return_states(
        place, [gain, pack, hat_t, grad_normed, unit, scale, found, prefix], others, bits
    )
    got = [swap(value, "ctx", 1) for value in sends]
    arrived = [[got[0]]]
    sums = add_all(sends[1:], got[1:])
    for bit in range(1, far):
        half = 1 << (bit - 1)
        arrived.append([swap(sums[bit - 1], "ctx", 2 * at) for at in range(half, 2 * half)])
    dqkv, dgrown, dcol, drow, dfar = pull_local(
        [qkv, pack, pack_t, trans, attn, attn_t, prod_t, scores, mix, decay, base, lower, dout,
         dhat, hat, found],
        levels, bits,
    )
    keep_out, last_out, dcol = halving(*out_parts, "head", dcol)
    arrays = [qkv, gate, pack, trans, mixed, decay, base, lower, dqkv, dgrown, dcol, drow, dfar,
              rates_row]
    dproj, dgate = finish(place, arrays, others, arrived, levels)
    keep, send, direct = pull_tokens(place, dproj, dgate, wr, small_t, count)
    direct, last_out = lax.optimization_barrier((direct, last_out))
    keep, last, late = halving(keep, send, "head", direct[1])
    direct = [direct[0], late, *direct[2:]]
    got = [swap(direct[mask], "head", mask) for mask in far_first(count)]
    return head_sum(keep_out, last_out, [], []), head_sum(keep, last, direct, got)


def solution(mesh):
    placed = (
        P("ctx", None),
        P(None, None, "head", None),
        P(None, "head", None),
        P("head", None),
        P(),
        P("head", None, None),
        P("ctx", None),
    )
    return jax.shard_map(
        on_device,
        mesh=mesh,
        in_specs=placed,
        out_specs=(P("ctx", "head"), P("ctx", "head")),
        check_vma=False,
    )
```

```python
import functools

import jax
import jax.numpy as jnp
from jax import lax
from jax.experimental import pallas as pl
from jax.experimental.pallas import tpu as pltpu
from jax.sharding import PartitionSpec as P

BLOCK = 64
LANES = 128
EPS = 1e-06
MIB = 1024 * 1024
F32 = jnp.float32
BF16 = jnp.bfloat16
WHOLE = pl.BlockSpec(memory_space=pltpu.VMEM)
SCALARS = pl.BlockSpec(memory_space=pltpu.SMEM)
HBM = pl.BlockSpec(memory_space=pltpu.HBM)


def contract(left, right, dim_left, dim_right):
    return lax.dot_general(
        left.astype(BF16),
        right.astype(BF16),
        (((dim_left,), (dim_right,)), ((), ())),
        preferred_element_type=F32,
    )


def mm(left, right):
    return contract(left, right, 1, 0)


def mm_nt(left, right):
    return contract(left, right, 1, 1)


def mm_tn(left, right):
    return contract(left, right, 0, 0)


def split(values):
    high = values.astype(BF16)
    return high, (values - high.astype(F32)).astype(BF16)


def mm_nt_fine(left, right):
    left_high, left_low = split(left)
    right_high, right_low = split(right)
    return mm_nt(left_high, right_high) + (mm_nt(left_low, right_high) + mm_nt(left_high, right_low))


def mm_full(left, right):
    return jnp.dot(left, right, precision=lax.Precision.HIGHEST, preferred_element_type=F32)


def mm_ones(ones, values):
    high = values.astype(BF16)
    rest = values - high.astype(F32)
    middle = rest.astype(BF16)
    low = (rest - middle.astype(F32)).astype(BF16)
    return mm(ones, high) + (mm(ones, middle) + mm(ones, low))


def pair_ids(count):
    row_id = lax.broadcasted_iota(jnp.int32, (count, count), 0)
    col_id = lax.broadcasted_iota(jnp.int32, (count, count), 1)
    return row_id, col_id


def row_sum(values):
    return jnp.sum(values, 1, keepdims=True)


def col_sum(values):
    return jnp.sum(values, 0, keepdims=True)


def lane_of(rows):
    return lax.broadcasted_iota(jnp.int32, (rows, LANES), 1)


def decay_of(pack, pack_t, col, inclusive):
    spread = pack[:, col : col + 1] - pack_t[col : col + 1, :]
    return jnp.where(inclusive, jnp.exp(jnp.minimum(spread, 0.0)), 0.0)


def kept(shape, dtype):
    return pltpu.VMEM(shape, dtype)


def stored(shape, dtype):
    return pltpu.HBM(shape, dtype)


def pin(values, space):
    return [pltpu.with_memory_space_constraint(value, space) for value in values]


def local_call(
    body, name, limit, out_shape, scalars, arrays, scratch=(), remote=(), out_specs=None, alias=None
):
    return pl.pallas_call(
        body,
        out_shape=tuple(out_shape),
        in_specs=[SCALARS] * len(scalars)
        + [WHOLE] * len(arrays)
        + [HBM] * len(remote),
        out_specs=tuple(out_specs or [WHOLE] * len(out_shape)),
        scratch_shapes=list(scratch),
        input_output_aliases=alias or {},
        compiler_params=pltpu.CompilerParams(vmem_limit_bytes=limit * MIB),
        name=name,
    )(*scalars, *pin(arrays, pltpu.VMEM), *pin(remote, pltpu.HBM))


def column(pack, at):
    return pack[:, at : at + 1]


def level_mix(pack, head, heads, bits, apart):
    block_bit = BLOCK.bit_length() - 1
    mixed = jnp.broadcast_to(column(pack, head), apart.shape)
    for level in range(1, bits + 1):
        here = (apart >> (block_bit + level - 1)) >= 1
        mixed = jnp.where(here, column(pack, level * heads + head), mixed)
    return mixed


def head_rows(hp_ref, heads, decay_col, beta_col):
    lane_row = lane_of(1)
    rate = jnp.zeros((1, LANES), F32)
    bias = jnp.zeros((1, LANES), F32)
    for head in range(heads):
        rate = jnp.where(lane_row == decay_col + head, hp_ref[0:1, head : head + 1], rate)
        bias = jnp.where(lane_row == beta_col + head, hp_ref[1:2, head : head + 1], bias)
    return rate, bias


def invert(lower_all, eye, apart, rows):
    trans_all = [(eye - jnp.where(apart == 1, lower, 0.0)).astype(BF16) for lower in lower_all]
    for bit in range(1, rows.bit_length() - 1):
        here = (apart >> bit) == 1
        edge = [jnp.where(here, lower, 0.0) for lower in lower_all]
        half = [mm(trans, part) for trans, part in zip(trans_all, edge)]
        trans_all = [
            trans - mm(part, trans).astype(BF16) for trans, part in zip(trans_all, half)
        ]
    rest_all = []
    for trans, lower in zip(trans_all, lower_all):
        high, low = split(lower)
        rest_all.append(eye - trans.astype(F32) - mm(high, trans) - mm(low, trans))
    return [
        (trans.astype(F32) + mm(trans, rest)).astype(BF16)
        for trans, rest in zip(trans_all, rest_all)
    ]


def project_body(sizes, place_ref, hp_hbm, tokens_hbm, w_hbm, small_hbm, *refs):
    heads, levels, chunks = sizes
    (wr_hbm, query_ref, value_ref, small_ref, qkv_ref, gate_ref, pack_ref, pack_t_ref, trans_ref, mixed_t_ref,
     decay_ref, base_ref, lower_ref, rates_ref, pair_ref) = refs[:15]
    tokens, wide_in, wide_even, wide_odd, key_ref, small_in, small_wide, acc, hp_ref = refs[15:24]
    sems, in_sems, out_sems = refs[24:]
    laid = (query_ref, key_ref, value_ref)
    rows, width = tokens.shape
    depth = width // chunks
    cols = 3 * heads
    fetch_tokens = pltpu.make_async_copy(tokens_hbm, tokens, sems.at[0])
    fetch_small = pltpu.make_async_copy(small_hbm, small_in, sems.at[1])
    fetch_rates = pltpu.make_async_copy(hp_hbm, hp_ref, sems.at[2])
    fetches, keeps = [], []
    for chunk in range(chunks):
        span = pl.ds(chunk * depth * cols, depth * cols)
        fetches.append(
            pltpu.make_async_copy(w_hbm.at[span, :], wide_in.at[span, :], in_sems.at[chunk])
        )
        span = pl.ds(chunk * depth, depth)
        block = wr_hbm.at[span, pl.ds(heads * LANES, heads * LANES)]
        keeps.append(pltpu.make_async_copy(key_ref.at[span, :], block, out_sems.at[chunk]))
    fetches[0].start()
    fetches[1].start(priority=1)
    fetch_tokens.start()
    fetch_small.start(priority=1)
    fetch_rates.start(priority=1)
    for chunk in range(2, chunks):
        fetches[chunk].start(priority=chunk % 2)

    def relay(chunk):
        fetches[chunk].wait()
        wide = wide_odd if chunk % 2 else wide_even
        at = chunk * depth
        wide[...] = wide_in[at * cols : (at + depth) * cols, :].astype(F32)
        for col in range(cols):
            value = wide[pl.ds(col, depth, stride=cols), :].astype(BF16)
            lanes = slice(col % heads * LANES, (col % heads + 1) * LANES)
            laid[col // heads][at : at + depth, lanes] = value

    def multiply(first, last):
        for part in (1, 2):
            span = slice((part * heads) * LANES, (part + 1) * heads * LANES)
            own = jnp.dot(
                tokens[:, first * depth : last * depth],
                laid[part][first * depth : last * depth, :],
                preferred_element_type=F32,
            )
            if first == 0:
                acc[:, span] = own
            else:
                acc[:, span] += own

    def lay(first, last):
        for chunk in range(first, last, 2):
            relay(chunk)
            relay(chunk + 1)
            if chunk == 0:
                fetch_tokens.wait()
            multiply(chunk, chunk + 2)

    decay_col = levels * heads
    beta_col = decay_col + heads
    norm_col = beta_col + heads
    lane = lane_of(rows)
    row_id, col_id = pair_ids(rows)
    inclusive = row_id >= col_id
    strict = row_id > col_id
    apart = row_id ^ col_id
    eye = (row_id == col_id).astype(F32)
    lay(0, chunks)
    for chunk, keep in enumerate(keeps):
        keep.start(priority=chunk % 2)
    fetch_small.wait()
    small_rows = small_in.shape[0] * heads
    for level in range(small_in.shape[0]):
        small_wide[level * heads : (level + 1) * heads, :] = small_in[level].astype(F32)
    small_wide[small_rows:, :] = jnp.zeros((LANES - small_rows, width), F32)
    small_ref[...] = small_wide[...].astype(BF16)
    fetch_rates.wait()
    rate, bias = head_rows(hp_ref, heads, decay_col, beta_col)
    rates_ref[0:1, :] = rate
    rates_ref[1:2, :] = bias
    gate = mm_nt(tokens[...], small_ref[...])
    gate_ref[...] = gate
    switch = jax.nn.sigmoid(gate + bias)
    lam = jnp.maximum(gate, 0.0) + jnp.log1p(jnp.exp(-jnp.abs(gate)))
    cum = mm_ones(inclusive.astype(F32), -rate * switch)
    pack = jnp.where(lane < decay_col, lam, jnp.where(lane < beta_col, cum, switch))
    pack_t = pack.T
    pack_t_ref[...] = pack_t

    def unit_of(part, head):
        col = (part * heads + head) * LANES
        raw = acc[:, col : col + LANES]
        scale = lax.rsqrt(row_sum(raw * raw) + EPS)
        qkv_ref[part, head] = raw * scale
        return raw * scale, jnp.where(lane == norm_col + part * heads + head, scale, 0.0)

    scales = jnp.zeros((rows, LANES), F32)
    k_all, lower_all = [], []
    for head in range(heads):
        unit, scale = unit_of(1, head)
        k_all.append(unit)
        scales = scales + scale
        decay = decay_of(pack, pack_t, decay_col + head, inclusive)
        decay_ref[head] = decay.astype(BF16)
        base = jnp.where(strict, decay * mm_nt(unit, unit), 0.0)
        base_ref[head] = base.astype(BF16)
        lower = column(pack, beta_col + head) * base
        lower_ref[head] = lower.astype(BF16)
        lower_all.append(lower)

    trans_all = invert(lower_all, eye, apart, rows)
    mixed_all = []
    for head in range(heads):
        trans_ref[head] = trans_all[head]
        cum_row = pack_t[decay_col + head : decay_col + head + 1, :]
        tail_t = k_all[head].T * jnp.exp(cum_row[:, rows - 1 :] - cum_row)
        mixed_all.append(mm(tail_t, trans_all[head]).astype(BF16))
    eye_key = eye[:LANES, :LANES]
    for head in range(heads):
        mixed_t_ref[head] = mixed_all[head]
        col = (2 * heads + head) * LANES
        v_in = acc[:, col : col + LANES]
        qkv_ref[2, head] = v_in
        cum_col = column(pack, decay_col + head)
        beta = column(pack, beta_col + head)
        grown = (beta * jnp.exp(cum_col)) * k_all[head]
        both = jnp.concatenate([-grown, beta * v_in], 1)
        pair = mm(mixed_all[head], both)
        last = jnp.exp(cum_col[rows - 1 : rows, :])
        pair_ref[head, :, :LANES] = (last * eye_key + pair[:, :LANES]).astype(BF16)
        pair_ref[head, :, LANES:] = pair[:, LANES:].astype(BF16)
    pack_ref[...] = jnp.where(lane < norm_col, pack, scales)
    for keep in keeps:
        keep.wait()


def project(place, tokens, flat_w, small, head_param, heads, levels):
    rows, width = tokens.shape
    chunks = 16
    cols = 3 * heads
    key = flat_w.shape[1]
    square = (heads, rows, rows)
    out_shape = (
        stored((width, cols * key), BF16),
        kept((width, heads * key), BF16),
        kept((width, heads * key), BF16),
        kept((LANES, width), BF16),
        kept((3, heads, rows, key), F32),
        kept((rows, LANES), F32),
        kept((rows, LANES), F32),
        kept((LANES, rows), F32),
        kept(square, BF16),
        kept((heads, key, rows), BF16),
        kept(square, BF16),
        kept(square, BF16),
        kept(square, BF16),
        kept((2, LANES), F32),
        kept((heads, key, 2 * key), BF16),
    )
    scratch = [
        pltpu.VMEM(tokens.shape, BF16),
        pltpu.VMEM(flat_w.shape, BF16),
        pltpu.VMEM((width // chunks * cols, key), F32),
        pltpu.VMEM((width // chunks * cols, key), F32),
        pltpu.VMEM((width, heads * key), BF16),
        pltpu.VMEM(small.shape, BF16),
        pltpu.VMEM((LANES, width), F32),
        pltpu.VMEM((rows, cols * key), F32),
        pltpu.VMEM(head_param.shape, F32),
        pltpu.SemaphoreType.DMA((3,)),
        pltpu.SemaphoreType.DMA((chunks,)),
        pltpu.SemaphoreType.DMA((chunks,)),
    ]
    return local_call(
        functools.partial(project_body, (heads, levels, chunks)), "project", 36, out_shape,
        [place], [], scratch, [head_param, tokens, flat_w, small], [HBM] + [WHOLE] * 14,
    )


def local_body(
    sizes, qkv_ref, pack_ref, pack_t_ref, trans_ref, mixed_t_ref, decay_ref, grad_ref, weight_ref,
    query_ref, value_ref, tokens_ref, wr_in, *outs
):
    heads, levels, bits = sizes
    (attn_ref, attn_t_ref, prod_t_ref, scores_ref, mix_ref, mixed_ref, local_ref, hat_ref,
     hat_t_ref, grad_normed_ref, qkv_out, pack_out, wr_hbm, sems) = outs
    del wr_in
    half, size = query_ref.shape[0] // 2, query_ref.shape[1]
    keeps = []
    for at in range(4):
        span = pl.ds(at % 2 * half, half)
        here, col = ((query_ref, 0), (value_ref, 2 * size))[at // 2]
        there = wr_hbm.at[span, pl.ds(col, size)]
        keeps.append(pltpu.make_async_copy(here.at[span, :], there, sems.at[at]))
        keeps[at].start(priority=at % 2)
    rows = pack_ref.shape[0]
    decay_col = levels * heads
    beta_col = decay_col + heads
    norm_col = beta_col + heads
    lane = lane_of(rows)
    raw_all = jnp.dot(tokens_ref[...], query_ref[...], preferred_element_type=F32)
    pack = pack_ref[...]
    q_all = []
    for head in range(heads):
        raw = raw_all[:, head * LANES : (head + 1) * LANES]
        scale = lax.rsqrt(row_sum(raw * raw) + EPS)
        q_all.append(raw * scale)
        qkv_out[0, head] = q_all[head]
        pack = jnp.where(lane == norm_col + head, scale, pack)
    pack_out[...] = pack
    grad_normed_ref[...] = mm_nt(grad_ref[...], weight_ref[...])
    pack_t = pack_t_ref[...]
    row_id, col_id = pair_ids(rows)
    apart = row_id ^ col_id
    for head in range(heads):
        scores = mm_nt_fine(q_all[head], qkv_ref[1, head]) * decay_ref[head].astype(F32)
        scores_ref[head] = scores.astype(BF16)
        mix_ref[head] = level_mix(pack, head, heads, bits, apart).astype(BF16)
        mixed_ref[head] = mixed_t_ref[head].astype(F32).T.astype(BF16)
    for head in range(heads):
        attn = mm(scores_ref[head], trans_ref[head])
        attn_ref[head] = attn.astype(BF16)
        attn_t_ref[head] = attn.T.astype(BF16)
        attn = attn * pack_t[beta_col + head : beta_col + head + 1, :]
        prod = attn * mix_ref[head].astype(F32)
        prod_t_ref[head] = prod.T.astype(BF16)
        growth = jnp.exp(column(pack, decay_col + head))
        local_ref[head] = mm(prod, qkv_ref[2, head])
        hat = growth * q_all[head] - mm(attn, growth * qkv_ref[1, head])
        hat_ref[head] = hat.astype(BF16)
        hat_t_ref[head] = hat.T.astype(BF16)
    for keep in keeps:
        keep.wait()


def local_part(arrays, wr, levels, bits):
    heads, rows, key = arrays[0].shape[1:]
    square = (heads, rows, rows)
    out_shape = (
        kept(square, BF16),
        kept(square, BF16),
        kept(square, BF16),
        kept(square, BF16),
        kept(square, BF16),
        kept((heads, rows, key), BF16),
        kept((heads, rows, key), F32),
        kept((heads, rows, key), BF16),
        kept((heads, key, rows), BF16),
        kept((rows, heads * key), F32),
        kept(arrays[0].shape, F32),
        kept(arrays[1].shape, F32),
        stored(wr.shape, BF16),
    )
    return local_call(
        functools.partial(local_body, (heads, levels, bits)), "local_part", 10, out_shape,
        [], arrays, [pltpu.SemaphoreType.DMA((4,))], [wr], [WHOLE] * 12 + [HBM],
        {0: 10, 1: 11, len(arrays): 12},
    )


def join_pair(upper, own, other):
    key = own.shape[0]
    low = jnp.where(upper, other, own)
    high = jnp.where(upper, own, other)
    moved = mm(high[:, :key], low)
    late = jnp.concatenate([jnp.zeros((key, key), F32), high[:, key:].astype(F32)], 1)
    return (moved + late).astype(BF16)


def join_body(place_ref, own_ref, other_ref, out_ref):
    half = out_ref.shape[0]
    upper = (place_ref[0] & 1) == 1
    for slot in range(half):
        head = (place_ref[0] & 1) * half + slot
        out_ref[slot] = join_pair(upper, own_ref[head], other_ref[head])


def join_half(place, own, other):
    half = (own.shape[0] // 2,) + own.shape[1:]
    return local_call(join_body, "join_half", 6, [kept(half, BF16)], [place], [own, other])[0]


def gather_node(head, bit, first, near, uppers):
    if bit == 0:
        mine, theirs = near[first]
        half = mine.shape[0]
        here = uppers[0] if head >= half else jnp.logical_not(uppers[0])
        return jnp.where(here, mine[head % half], theirs[head % half])
    own = gather_node(head, bit - 1, first, near, uppers)
    other = gather_node(head, bit - 1, first ^ (1 << (bit - 1)), near, uppers)
    return join_pair(uppers[bit], own, other)


def reach_body(
    sizes, place_ref, gain_ref, pack_ref, local_ref, hat_ref, weight_ref, *refs
):
    heads, bits, far, count, near_count = sizes
    first_ref = refs[0]
    near = [None] + [(refs[1 + at], refs[1 + near_count + at]) for at in range(near_count)]
    refs = refs[2 * near_count + 1 :]
    out_refs = refs[:2]
    summed_ref, scale_ref, found_ref, prefix_ref = refs[2:6]
    nodes = refs[6:-1]
    normed_ref = refs[-1]
    rows = pack_ref.shape[0]
    key = hat_ref.shape[2]
    pack = pack_ref[...]
    gain = gain_ref[...]
    lane = lane_of(rows)
    all_heads = range(heads)
    uppers = [((place_ref[0] >> bit) & 1) == 1 for bit in range(far)]
    others = []
    for bit in range(far):
        if bit == 0:
            others.append([first_ref[head] for head in all_heads])
        else:
            others.append(
                [gather_node(head, bit - 1, 1 << (bit - 1), near, uppers) for head in all_heads]
            )
            for head in all_heads:
                nodes[bit - 1][head] = others[bit][head]
    eye_key = jnp.where(pair_ids(key)[0] == pair_ids(key)[1], 1.0, 0.0).astype(BF16)
    prefix = [eye_key for head in all_heads]
    found = []
    for bit in range(far):
        for head in all_heads:
            prefix_ref[head, bit] = prefix[head]
        moved = [mm(prefix[head], others[bit][head]) for head in all_heads]
        found.append([jnp.where(uppers[bit], m[:, key:], 0.0).astype(BF16) for m in moved])
        prefix = [
            jnp.where(uppers[bit], moved[head][:, :key].astype(BF16), prefix[head])
            for head in all_heads
        ]
    found = [jnp.concatenate([found[bit][head] for bit in range(far)], 1) for head in all_heads]
    reached = [mm(hat_ref[head], found[head]) for head in all_heads]
    scales = jnp.zeros((rows, LANES), F32)
    for head in all_heads:
        found_ref[head] = found[head]
        summed = local_ref[head]
        for bit in range(far):
            part = reached[head][:, bit * key : (bit + 1) * key]
            summed = summed + column(pack, (bits + 1 + bit) * heads + head) * part
        scale = lax.rsqrt(jnp.mean(summed * summed, -1, keepdims=True) + EPS)
        unit = summed * scale
        normed_ref[:, head * key : (head + 1) * key] = (unit * gain).astype(BF16)
        summed_ref[head] = unit
        scales = jnp.where(lane == head, scale, scales)
    scale_ref[...] = scales
    size = weight_ref.shape[1] // count
    for mask in range(count):
        dest = place_ref[1] ^ mask
        cols = pl.ds(pl.multiple_of(dest * size, size), size)
        out_refs[mask % 2][mask // 2] = jnp.dot(
            normed_ref[...], weight_ref[:, cols], preferred_element_type=F32
        ).astype(BF16)


def reach(place, arrays, first, near, bits, far, count):
    gain, pack, local_out, hat, weight = arrays
    heads, rows, key = hat.shape
    nodes = tuple(kept(first.shape, BF16) for bit in range(1, far))
    size = weight.shape[1] // count
    out_shape = (kept((count // 2, rows, size), BF16),) * 2 + (
        kept((heads, rows, key), F32),
        kept((rows, LANES), F32),
        kept((heads, key, far * key), BF16),
        kept((heads, far, key, key), BF16),
    ) + nodes
    mine, theirs = near
    got = local_call(
        functools.partial(reach_body, (heads, bits, far, count, len(mine))), "reach", 10, out_shape,
        [place], [*arrays, first, *mine, *theirs], [pltpu.VMEM((rows, heads * key), BF16)],
    )
    return got[:2], got[2:6], got[6:]


def return_body(
    sizes, place_ref, gain_ref, pack_ref, hat_t_ref, grad_ref, unit_ref, scale_ref,
    found_ref, prefix_ref, *refs
):
    heads, bits, far = sizes
    others = refs[:far]
    dhat_ref, dout_ref = refs[far : far + 2]
    sends = refs[far + 2 :]
    gain, scales = gain_ref[...], scale_ref[...]
    key = hat_t_ref.shape[1]
    pack = pack_ref[...]
    all_heads = range(heads)
    uppers = [((place_ref[0] >> bit) & 1) == 1 for bit in range(far)]
    spread = []
    for head in all_heads:
        unit = unit_ref[head]
        pulled = grad_ref[:, head * key : (head + 1) * key] * gain
        mean = jnp.mean(pulled * unit, -1, keepdims=True)
        dout = column(scales, head) * (pulled - unit * mean)
        dout_ref[head] = dout
        parts = []
        for bit in range(far):
            col = (bits + 1 + bit) * heads + head
            parts.append((column(pack, col) * dout).astype(BF16))
        spread.append(jnp.concatenate(parts, 1))
    dfound = [mm(hat_t_ref[head], spread[head]) for head in all_heads]
    for head in all_heads:
        dhat_ref[head] = mm_nt(spread[head], found_ref[head])
    dprefix = [jnp.zeros((key, key), F32) for head in all_heads]
    for bit in reversed(range(far)):
        dfree = [
            jnp.where(uppers[bit], d[:, bit * key : (bit + 1) * key], 0.0) for d in dfound
        ]
        both = [
            jnp.concatenate([jnp.where(uppers[bit], dprefix[head], 0.0), dfree[head]], 1)
            for head in all_heads
        ]
        for head in all_heads:
            sent = dfree[head] if bit == far - 1 else both[head]
            sends[bit][head] = mm_tn(prefix_ref[head, bit], sent).astype(BF16)
        if bit > 0:
            moved = [mm_nt(both[head], others[bit][head]) for head in all_heads]
            dprefix = [
                jnp.where(uppers[bit], moved[head], dprefix[head]) for head in all_heads
            ]


def return_states(place, arrays, others, bits):
    heads, key, rows = arrays[2].shape
    far = len(others)
    sends = tuple(
        kept((heads, key, (1 if bit == far - 1 else 2) * key), BF16) for bit in range(far)
    )
    wide = kept((heads, rows, key), F32)
    got = local_call(
        functools.partial(return_body, (heads, bits, far)), "return_states", 8,
        (wide, wide) + sends, [place], [*arrays, *others],
    )
    return got[:2], got[2:]


def add_body(*refs):
    count = len(refs) // 3
    for at in range(count):
        left, right = refs[at][...].astype(F32), refs[count + at][...].astype(F32)
        refs[2 * count + at][...] = (left + right).astype(BF16)


def add_all(left, right):
    out_shape = [kept(value.shape, BF16) for value in left]
    return local_call(add_body, "add_all", 6, out_shape, [], [*left, *right])


def lower_pull(dlower, base, lower, beta, decay, strict, k_in):
    dlower = jnp.where(strict, dlower, 0.0)
    dbeta = row_sum(dlower * base.astype(F32))
    dgram = dlower * (beta * decay)
    dkey = mm(dgram, k_in) + mm_tn(dgram, k_in)
    return dbeta, beta * dbeta, col_sum(dlower * lower.astype(F32)), dkey


def pull_body(sizes, *refs):
    heads, levels, bits = sizes
    (qkv_ref, pack_ref, pack_t_ref, trans_ref, attn_ref, attn_t_ref, prod_t_ref, scores_ref,
     mix_ref, decay_ref, base_ref, lower_ref, dout_ref, dhat_ref, hat_ref, found_ref) = refs[:16]
    dqkv_ref, dgrown_ref, dcol_ref, drow_ref, dfar_ref = refs[16:]
    rows = pack_ref.shape[0]
    decay_col = levels * heads
    beta_col = decay_col + heads
    block_bit = BLOCK.bit_length() - 1
    pack = pack_ref[...]
    pack_t = pack_t_ref[...]
    row_id, col_id = pair_ids(rows)
    strict = row_id > col_id
    apart = row_id ^ col_id
    lane = lane_of(rows)
    all_heads = range(heads)
    dcol = jnp.zeros((rows, LANES), F32)
    dbeta_rows, dcum_rows, dattn_all = [], [], []
    key = hat_ref.shape[2]
    dfar = jnp.zeros((rows, LANES), F32)
    for head in all_heads:
        reached = mm(hat_ref[head], found_ref[head])
        for bit in range(reached.shape[1] // key):
            here = row_sum(dout_ref[head] * reached[:, bit * key : (bit + 1) * key])
            dfar = jnp.where(lane == (bits + 1 + bit) * heads + head, here, dfar)
    dfar_ref[...] = dfar
    for head in all_heads:
        high, low = split(dout_ref[head])
        v_in = qkv_ref[2, head].astype(BF16)
        dprod = mm_nt(high, v_in) + mm_nt(low, v_in)
        dqkv_ref[2, head] = mm(prod_t_ref[head], high)
        beta_row = pack_t[beta_col + head : beta_col + head + 1, :]
        growth = jnp.exp(column(pack, decay_col + head))
        attn0 = attn_ref[head].astype(F32)
        touched = dprod * (attn0 * beta_row)
        for level in range(bits + 1):
            if level == 0:
                here = (apart >> block_bit) == 0
            else:
                here = (apart >> (block_bit + level - 1)) == 1
            dcol = jnp.where(
                lane == level * heads + head, row_sum(jnp.where(here, touched, 0.0)), dcol
            )
        dattn = dprod * mix_ref[head].astype(F32) - mm_nt(dhat_ref[head], growth * qkv_ref[1, head])
        dbeta_rows.append(col_sum(dattn * attn0))
        dattn_all.append((dattn * beta_row).astype(BF16))
    dscore_all = [mm_nt(dattn_all[head], trans_ref[head]) for head in all_heads]
    moved_all = []
    for head in all_heads:
        both = jnp.concatenate(
            [dscore_all[head].astype(BF16), dhat_ref[head].astype(BF16)], 1
        )
        moved_all.append(mm(attn_t_ref[head], both))
    for head in all_heads:
        q_in, k_in = qkv_ref[0, head], qkv_ref[1, head]
        beta = column(pack, beta_col + head)
        growth = jnp.exp(column(pack, decay_col + head))
        dscore = dscore_all[head]
        decay = decay_ref[head].astype(F32)
        dprobs = dscore * decay
        shift = dscore * scores_ref[head].astype(F32)
        dgrown_ref[head] = -beta * moved_all[head][:, rows:]
        dbeta, dcum_col, dcum_row, dk_lower = lower_pull(
            -moved_all[head][:, :rows], base_ref[head], lower_ref[head], beta, decay, strict, k_in
        )
        dhat = dhat_ref[head]
        dqkv_ref[0, head] = growth * dhat + mm(dprobs, k_in)
        dqkv_ref[1, head] = mm_tn(dprobs, q_in) + dk_lower
        dcum_col = dcum_col + row_sum(shift) + growth * row_sum(q_in * dhat)
        dcum_rows.append(-dcum_row - col_sum(shift))
        dcol = jnp.where(lane == beta_col + head, dbeta, dcol)
        dcol = jnp.where(lane == decay_col + head, dcum_col, dcol)
    dcol_ref[...] = dcol
    drow_ref[...] = jnp.concatenate(dcum_rows + dbeta_rows, 0)


def pull_local(arrays, levels, bits):
    heads, rows, key = arrays[0].shape[1:]
    out_shape = (
        kept((3, heads, rows, key), F32),
        kept((heads, rows, key), F32),
        kept((rows, LANES), F32),
        kept((2 * heads, rows), F32),
        kept((rows, LANES), F32),
    )
    return local_call(
        functools.partial(pull_body, (heads, levels, bits)), "pull_local", 12, out_shape, [], arrays
    )


def finish_body(sizes, place_ref, *refs):
    heads, levels, far, arrived_counts = sizes
    (qkv_ref, gate_ref, pack_ref, trans_ref, mixed_ref, decay_ref, base_ref, lower_ref,
     dqkv_ref, dgrown_ref, dcol_ref, drow_ref, dfar_ref, rates_ref) = refs[:14]
    others = refs[14 : 14 + far]
    refs = refs[14 + far :]
    arrived = []
    for found in arrived_counts:
        arrived.append(refs[:found])
        refs = refs[found:]
    dproj, dgate_ref = refs
    rows = pack_ref.shape[0]
    key = qkv_ref.shape[3]
    decay_col = levels * heads
    beta_col = decay_col + heads
    norm_col = beta_col + heads
    place = place_ref[0]
    all_heads = range(heads)
    uppers = [((place >> bit) & 1) == 1 for bit in range(far)]
    pack = pack_ref[...]
    row_id, col_id = pair_ids(rows)
    strict = row_id > col_id
    lane = lane_of(rows)
    last_row = lax.broadcasted_iota(jnp.int32, (rows, 1), 0) == rows - 1
    eye_key = (pair_ids(key)[0] == pair_ids(key)[1]).astype(F32)
    dpair = [jnp.zeros((key, 2 * key), F32) for head in all_heads]
    for bit in reversed(range(far)):
        for head in all_heads:
            got = arrived[bit][0][head].astype(F32)
            for more in arrived[bit][1:]:
                got = got + more[head].astype(F32)
            other = others[bit][head]
            if bit == far - 1:
                got = jnp.concatenate([jnp.zeros((key, key), F32), got], 1)
                dpair[head] = jnp.where(uppers[bit], 0.0, got)
            else:
                as_low = mm_tn(other[:, :key], dpair[head]) + got
                as_high = mm_nt(dpair[head], other)
                as_high = jnp.concatenate([as_high, dpair[head][:, key:]], 1)
                dpair[head] = jnp.where(uppers[bit], as_high, as_low)
    moved_all, dmixed_all = [], []
    for head in all_heads:
        beta = column(pack, beta_col + head)
        growth = jnp.exp(column(pack, decay_col + head))
        both = jnp.concatenate([-growth * qkv_ref[1, head], qkv_ref[2, head]], 1)
        dmixed_all.append(mm_nt(both, dpair[head]))
        moved_all.append(mm(beta * mixed_ref[head].astype(F32), dpair[head]))
    dtail_all = [
        mm(trans_ref[head], column(pack, beta_col + head) * dmixed_all[head])
        for head in all_heads
    ]
    dlower_all = [-mm_nt(mixed_ref[head], dtail_all[head]) for head in all_heads]
    dcol = jnp.where(lane < decay_col, dcol_ref[...] + dfar_ref[...], dcol_ref[...])
    dcum_rows = []
    for head in all_heads:
        q_in, k_in = qkv_ref[0, head], qkv_ref[1, head]
        beta = column(pack, beta_col + head)
        cum_col = column(pack, decay_col + head)
        growth = jnp.exp(cum_col)
        last = cum_col[rows - 1 : rows, :]
        tail = jnp.exp(last - cum_col)
        dgrown = dgrown_ref[head] - moved_all[head][:, :key]
        dv = dqkv_ref[2, head] + moved_all[head][:, key:]
        dbeta_more = row_sum(mixed_ref[head].astype(F32) * dmixed_all[head])
        dtail = dtail_all[head]
        dbeta, dcum_col, dcum_row, dk_lower = lower_pull(
            dlower_all[head], base_ref[head], lower_ref[head], beta, decay_ref[head].astype(F32),
            strict, k_in
        )
        dcum_rows.append(-dcum_row)
        tail_pull = tail * row_sum(k_in * dtail)
        trace = col_sum(row_sum(dpair[head][:, :key] * eye_key))
        at_last = col_sum(tail_pull) + jnp.exp(last) * trace
        dcum_col = dcum_col + growth * row_sum(k_in * dgrown) - tail_pull
        dcum_col = dcum_col + jnp.where(last_row, at_last, 0.0)
        dk = dqkv_ref[1, head] + dk_lower + growth * dgrown + tail * dtail
        dq = dqkv_ref[0, head]
        dcol = dcol + jnp.where(lane == beta_col + head, dbeta + dbeta_more, 0.0)
        dcol = dcol + jnp.where(lane == decay_col + head, dcum_col, 0.0)
        for part, unit, dunit in ((0, q_in, dq), (1, k_in, dk)):
            scale = column(pack, norm_col + part * heads + head)
            back = scale * (dunit - unit * row_sum(unit * dunit))
            col = (part * heads + head) * key
            dproj[:, col : col + key] = back.astype(BF16)
        col = (2 * heads + head) * key
        dproj[:, col : col + key] = dv.astype(BF16)
    drow = drow_ref[...]
    drow = drow + jnp.concatenate(dcum_rows + [jnp.zeros((heads, rows), F32)], 0)
    drow = jnp.concatenate(
        [jnp.zeros((decay_col, rows), F32), drow,
         jnp.zeros((LANES - norm_col, rows), F32)], 0
    )
    dcol = dcol + drow.T
    rate, bias = rates_ref[0:1, :], rates_ref[1:2, :]
    switch = jax.nn.sigmoid(gate_ref[...] + bias)
    dlog = mm_ones((row_id <= col_id).astype(F32), dcol)
    slope = switch * (1.0 - switch)
    dgate = jnp.where(
        lane < decay_col,
        dcol * switch,
        jnp.where(lane < beta_col, -rate * dlog * slope, dcol * slope),
    )
    dgate_ref[...] = jnp.where(lane < norm_col, dgate, 0.0).astype(BF16)


def finish(place, arrays, others, arrived, levels):
    heads, rows, key = arrays[0].shape[1:]
    counts = tuple(len(group) for group in arrived)
    flat = [value for group in arrived for value in group]
    return local_call(
        functools.partial(finish_body, (heads, levels, len(others), counts)), "finish", 10,
        [kept((rows, 3 * heads * key), BF16), kept((rows, LANES), BF16)],
        [place], [*arrays, *others, *flat],
    )


def tokens_body(count, place_ref, dproj_ref, dgate_ref, wr_ref, small_ref, *refs):
    keep_ref, send_ref = refs[:2]
    direct_refs = refs[2:]
    size = wr_ref.shape[0] // count
    half = size // 2
    for mask in range(count):
        dest = place_ref[1] ^ mask
        span = pl.ds(pl.multiple_of(dest * size, size), size)
        part = mm_nt(dproj_ref[...], wr_ref[span, :]) + mm(dgate_ref[...], small_ref[:, span])
        direct_refs[mask][...] = part[:, :half].astype(BF16)
        target = send_ref if mask % 2 else keep_ref
        target[mask // 2] = part[:, half:].astype(BF16)


def pull_tokens(place, dproj, dgate, wr, small_t, count):
    rows = dproj.shape[0]
    half = wr.shape[0] // count // 2
    out_shape = [kept((count // 2, rows, half), BF16)] * 2 + [kept((rows, half), BF16)] * count
    got = local_call(
        functools.partial(tokens_body, count), "pull_tokens", 8, out_shape,
        [place], [dproj, dgate, wr, small_t],
    )
    return got[0], got[1], got[2:]


def swap(value, axis, mask):
    size = lax.axis_size(axis)
    return lax.ppermute(value, axis, [(at, at ^ mask) for at in range(size)])


def far_first(count):
    return sorted(range(1, count), key=lambda mask: mask < count // 2)


def halve_body(own_ref, got_ref, keep_ref, send_ref):
    for at in range(own_ref.shape[0]):
        total = own_ref[at].astype(F32) + got_ref[at].astype(F32)
        target = send_ref if at % 2 else keep_ref
        target[at // 2] = total.astype(target.dtype)


def halving(keep, send, axis, tied):
    mask = 1
    while keep.shape[0] > 1:
        got = swap(send, axis, mask)
        half = (keep.shape[0] // 2,) + keep.shape[1:]
        keep, send = local_call(
            halve_body, "halve", 6, [kept(half, F32), kept(half, BF16)], [], [keep, got]
        )
        send, tied = lax.optimization_barrier((send, tied))
        mask *= 2
    return keep, swap(send, axis, mask), tied


def sum_body(count, *refs):
    keep_ref, got_ref = refs[:2]
    out_ref = refs[-1]
    total = keep_ref[0].astype(F32) + got_ref[0].astype(F32)
    if count == 0:
        out_ref[...] = total.astype(BF16)
        return
    half = out_ref.shape[1] // 2
    out_ref[:, half:] = total.astype(BF16)
    total = refs[2][...].astype(F32)
    for ref in refs[3:-1]:
        total = total + ref[...].astype(F32)
    out_ref[:, :half] = total.astype(BF16)


def head_sum(keep, last, direct, got):
    rows, cols = keep.shape[1:]
    out = jax.ShapeDtypeStruct((rows, cols * (2 if direct else 1)), BF16)
    return local_call(
        functools.partial(sum_body, len(direct)), "head_sum", 6, [out], [],
        [keep, last, *direct[:1], *got],
    )[0]


def on_device(tokens, qkv_weight, small_weight, head_param, norm_gain, out_weight, grad_out):
    rows, width = tokens.shape
    heads, key = qkv_weight.shape[2:]
    levels = small_weight.shape[2] - 2
    bits = (rows // BLOCK).bit_length() - 1
    size = lax.axis_size("ctx")
    far = size.bit_length() - 1
    count = lax.axis_size("head")
    place = jnp.stack([lax.axis_index("ctx"), lax.axis_index("head")]).astype(jnp.int32)
    flat_w = qkv_weight.reshape(width * 3 * heads, key)
    small = jnp.transpose(small_weight, (2, 1, 0))
    rates = head_param.T
    flat_out = out_weight.reshape(heads * key, width)
    gain = norm_gain.reshape(1, key)

    (wr, query_w, value_w, small_t, qkv, gate, pack, pack_t, trans, mixed_t, decay, base, lower, rates_row,
     pair) = project(
        place, tokens, flat_w, small, rates, heads, levels
    )
    first = swap(pair, "ctx", 1)
    node = join_half(place, pair, first)
    mine = [swap(node, "ctx", 2 * at) for at in range(1, size // 2)]
    (attn, attn_t, prod_t, scores, mix, mixed, local_out, hat, hat_t, grad_normed, qkv, pack,
     wr) = local_part(
        [qkv, pack, pack_t, trans, mixed_t, decay, grad_out, flat_out, query_w, value_w, tokens],
        wr, levels, bits,
    )
    mine, local_out, grad_normed = lax.optimization_barrier((mine, local_out, grad_normed))
    theirs = [swap(value, "ctx", 1) for value in mine]
    out_parts, (unit, scale, found, prefix), nodes = reach(
        place, [gain, pack, local_out, hat, flat_out], first, (mine, theirs), bits, far, count
    )
    others = [first, *nodes]
    (dhat, dout), sends = return_states(
        place, [gain, pack, hat_t, grad_normed, unit, scale, found, prefix], others, bits
    )
    got = [swap(value, "ctx", 1) for value in sends]
    arrived = [[got[0]]]
    sums = add_all(sends[1:], got[1:])
    for bit in range(1, far):
        half = 1 << (bit - 1)
        arrived.append([swap(sums[bit - 1], "ctx", 2 * at) for at in range(half, 2 * half)])
    dqkv, dgrown, dcol, drow, dfar = pull_local(
        [qkv, pack, pack_t, trans, attn, attn_t, prod_t, scores, mix, decay, base, lower, dout,
         dhat, hat, found],
        levels, bits,
    )
    keep_out, last_out, dcol = halving(*out_parts, "head", dcol)
    arrays = [qkv, gate, pack, trans, mixed, decay, base, lower, dqkv, dgrown, dcol, drow, dfar,
              rates_row]
    dproj, dgate = finish(place, arrays, others, arrived, levels)
    keep, send, direct = pull_tokens(place, dproj, dgate, wr, small_t, count)
    direct, last_out = lax.optimization_barrier((direct, last_out))
    keep, last, late = halving(keep, send, "head", direct[1])
    direct = [direct[0], late, *direct[2:]]
    got = [swap(direct[mask], "head", mask) for mask in far_first(count)]
    return head_sum(keep_out, last_out, [], []), head_sum(keep, last, direct, got)


def solution(mesh):
    placed = (
        P("ctx", None),
        P(None, None, "head", None),
        P(None, "head", None),
        P("head", None),
        P(),
        P("head", None, None),
        P("ctx", None),
    )
    return jax.shard_map(
        on_device,
        mesh=mesh,
        in_specs=placed,
        out_specs=(P("ctx", "head"), P("ctx", "head")),
        check_vma=False,
    )
```
